32 devices in a mesh: grp: 4 (over z), tok: 8 (over y, x, core).
Axes of the slice: x: 2, y: 2, z: 4, core: 2. Of those that a mesh axis runs over, the one named last changes fastest.
Arguments:
- prompt_states: bfloat16 [8, 1024, 2048], P('grp', 'tok'), may hold values from -6 to 6
- answer_states: bfloat16 [32, 128, 2048], P(('grp', 'tok')), may hold values from -6 to 6
- answer_prompt: int32 [32], P('grp'), may hold values from 0 to 7, as said below
- prompt_teacher: bfloat16 [8, 1024, 2048], P('grp', 'tok'), may hold values from -6 to 6
- answer_teacher: bfloat16 [32, 128, 2048], P(('grp', 'tok')), may hold values from -6 to 6
- prompt_valid: int32 [8, 1024], P('grp', 'tok'), may hold values from 0 to 1
- answer_valid: int32 [32, 128], P(('grp', 'tok')), may hold values from 0 to 1, as said below
- first_gain: bfloat16 [2048], P(('grp', 'tok')), may hold values from 0.099609375 to 1.8984375
- first_shift: bfloat16 [2048], P(('grp', 'tok')), may hold values from -1.75 to 1.75
- query_weight: bfloat16 [2048, 2048], P('grp', 'tok'), may hold values from -0.125 to 0.125
- query_bias: bfloat16 [2048], P(('grp', 'tok')), may hold values from -1.75 to 1.75
- keyval_weight: bfloat16 [2048, 256], P(('grp', 'tok')), may hold values from -0.125 to 0.125
- value_bias: bfloat16 [128], replicated, may hold values from -3 to 3
- output_weight: bfloat16 [2048, 2048], P('grp', 'tok'), may hold values from -0.5 to 0.5
- output_bias: bfloat16 [2048], P(('grp', 'tok')), may hold values from -1.75 to 1.75
- second_gain: bfloat16 [2048], P(('grp', 'tok')), may hold values from 0.099609375 to 1.8984375
- second_shift: bfloat16 [2048], P(('grp', 'tok')), may hold values from -1.75 to 1.75
- up_weight: bfloat16 [2048, 8192], P('grp', 'tok'), may hold values from -0.125 to 0.125
- up_bias: bfloat16 [8192], P(('grp', 'tok')), may hold values from -3 to 3
- down_weight: bfloat16 [2048, 8192], P('grp', 'tok'), may hold values from -0.125 to 0.125
- down_bias: bfloat16 [2048], P(('grp', 'tok')), may hold values from -1.75 to 1.75
Outputs:
- prompt_out: bfloat16 [8, 1024, 2048], P('grp', 'tok')
- answer_out: bfloat16 [32, 128, 2048], P(('grp', 'tok'))
- prompt_grad: bfloat16 [8, 1024, 2048], P('grp', 'tok')
- answer_grad: bfloat16 [32, 128, 2048], P(('grp', 'tok'))
- grad_first_gain: float32 [2048], P(('grp', 'tok'))
- grad_first_shift: float32 [2048], P(('grp', 'tok'))
- grad_query_weight: float32 [2048, 2048], P('grp', 'tok')
- grad_query_bias: float32 [2048], P(('grp', 'tok'))
- grad_keyval_weight: float32 [2048, 256], P(('grp', 'tok'))
- grad_value_bias: float32 [128], replicated
- grad_output_weight: float32 [2048, 2048], P('grp', 'tok')
- grad_output_bias: float32 [2048], P(('grp', 'tok'))
- grad_second_gain: float32 [2048], P(('grp', 'tok'))
- grad_second_shift: float32 [2048], P(('grp', 'tok'))
- grad_up_weight: float32 [2048, 8192], P('grp', 'tok')
- grad_up_bias: float32 [8192], P(('grp', 'tok'))
- grad_down_weight: float32 [2048, 8192], P('grp', 'tok')
- grad_down_bias: float32 [2048], P(('grp', 'tok'))
- loss: float32 [], replicated
The draws below stay inside these ranges and needn't reach their ends.
Inputs may be any that keep to these rules, and one draw needn't show every extreme that they name: `answer_prompt`: answer a continues one of the 2 prompts a // 8 * 2 + k, k = 0 .. 1, and each prompt is continued by exactly 4 answers. `answer_valid`: the first token of every answer is valid.
All inputs are finite; a program needn't handle non-finite values.
Results may differ from the reference program's by a relative error of at most 0.018.
Values may be sent and summed in bfloat16 or wider, within the bound.
A program may use at most 512 MiB of HBM per device.

```python
import math
import jax
import jax.numpy as jnp
from jax import lax

D = 2048
FF = 8192
HEAD_WIDTH = 128
PROMPT_LEN = 1024
ANSWER_LEN = 128
PROMPT_DEV = 2
ANSWER_DEV = 1
ANSWER_GRP = 8
PROMPTS = 8
ANSWERS = 32
TOTAL_TOK = 12288


def valid_from(key, device, devices, shape):
    level = 250 + 500 * device // max(devices - 1, 1)
    return (jax.random.randint(key, shape, 0, 1000) < level).astype(jnp.int32)


def draw_answer_prompt(key, part):
    groups = ANSWERS // ANSWER_GRP
    group_keys = jax.random.split(key, groups)
    pattern = jnp.arange(ANSWER_GRP, dtype=jnp.int32) % PROMPT_DEV
    shuffled = jax.vmap(lambda sub_key: jax.random.permutation(sub_key, pattern))(group_keys)
    offsets = jnp.arange(groups, dtype=jnp.int32)[:, None] * PROMPT_DEV
    return (shuffled + offsets).reshape(ANSWERS).astype(jnp.int32)


def draw_answer_valid(key, part):
    devices = ANSWERS // ANSWER_DEV
    device = (jnp.arange(ANSWERS, dtype=jnp.int32) // ANSWER_DEV)[:, None]
    drawn = valid_from(key, device, devices, (ANSWERS, ANSWER_LEN))
    return drawn.at[:, 0].set(1).astype(jnp.int32)


def draw_prompt_valid(key, part):
    token_devices = ANSWER_GRP // ANSWER_DEV
    devices = PROMPTS // PROMPT_DEV * token_devices
    group_of = jnp.arange(PROMPTS, dtype=jnp.int32) // PROMPT_DEV
    block_of = jnp.arange(PROMPT_LEN, dtype=jnp.int32) // (PROMPT_LEN // token_devices)
    device = group_of[:, None] * token_devices + block_of[None, :]
    return valid_from(key, device, devices, (PROMPTS, PROMPT_LEN))


def block_levels(own_key, shape, cuts, low, top_value):
    factor_of = 1.0
    for dim, blocks in cuts:
        draws = jax.random.uniform(jax.random.fold_in(jax.random.fold_in(own_key, 6), dim), (blocks,), jnp.float32, low / len(cuts), top_value / len(cuts))
        factor_of = factor_of * jnp.repeat(jnp.exp(draws), shape[dim] // blocks).reshape((-1,) + (1,) * (len(shape) - 1 - dim))
    return factor_of


def gaussian(rng, extent, deviation, reach, pieces=(), kind=jnp.bfloat16):
    loudness = block_levels(rng, extent, pieces, -0.22, 0.18) if pieces else 1.0
    array = jax.random.normal(rng, extent, jnp.float32) * deviation * loudness
    return jnp.minimum(jnp.maximum(array, -reach), reach).astype(kind)


def setup_inputs(seed: int = 0) -> dict:
    streams_of = jax.random.split(jax.random.key(seed), 22)
    return {
        "prompt_states": gaussian(streams_of[0], (PROMPTS, PROMPT_LEN, D), 1.0, 6.0, ((0, 4), (1, 8))),
        "answer_states": gaussian(streams_of[1], (ANSWERS, ANSWER_LEN, D), 1.0, 6.0, ((0, 32),)),
        "answer_prompt": draw_answer_prompt(jax.random.fold_in(streams_of[21], 71), 0),
        "prompt_teacher": gaussian(streams_of[3], (PROMPTS, PROMPT_LEN, D), 1.0, 6.0, ((0, 4), (1, 8))),
        "answer_teacher": gaussian(streams_of[4], (ANSWERS, ANSWER_LEN, D), 1.0, 6.0, ((0, 32),)),
        "prompt_valid": draw_prompt_valid(jax.random.fold_in(streams_of[21], 71), 0),
        "answer_valid": draw_answer_valid(jax.random.fold_in(streams_of[21], 71), 0),
        "first_gain": jnp.clip(1.0 + 0.18 * jax.random.normal(streams_of[7], (D,), jnp.float32), 0.099609375, 1.8984375).astype(jnp.bfloat16),
        "first_shift": gaussian(streams_of[8], (D,), 0.3, 1.75, ((0, 32),)),
        "query_weight": gaussian(streams_of[9], (D, D), D ** -0.5, 0.125, ((0, 4), (1, 8))),
        "query_bias": gaussian(streams_of[10], (D,), 0.3, 1.75, ((0, 32),)),
        "keyval_weight": gaussian(streams_of[11], (D, 2 * HEAD_WIDTH), D ** -0.5, 0.125, ((0, 32),)),
        "value_bias": gaussian(streams_of[12], (HEAD_WIDTH,), 0.5, 3.0),
        "output_weight": gaussian(streams_of[13], (D, D), (D // 16) ** -0.5, 0.5, ((0, 4), (1, 8))),
        "output_bias": gaussian(streams_of[14], (D,), 0.3, 1.75, ((0, 32),)),
        "second_gain": jnp.clip(1.0 + 0.18 * jax.random.normal(streams_of[15], (D,), jnp.float32), 0.099609375, 1.8984375).astype(jnp.bfloat16),
        "second_shift": gaussian(streams_of[16], (D,), 0.3, 1.75, ((0, 32),)),
        "up_weight": gaussian(streams_of[17], (D, FF), D ** -0.5, 0.125, ((0, 4), (1, 8))),
        "up_bias": gaussian(streams_of[18], (FF,), 0.5, 3.0, ((0, 32),)),
        "down_weight": gaussian(streams_of[19], (D, FF), (FF // 4) ** -0.5, 0.125, ((0, 4), (1, 8))),
        "down_bias": gaussian(streams_of[20], (D,), 0.3, 1.75, ((0, 32),)),
    }


@jax.custom_vjp
def low(v):
    return lax.optimization_barrier(v.astype(jnp.bfloat16)).astype(jnp.float32)

@jax.custom_vjp
def low_back(v):
    return v

def low_keep(v):
    return (low(v), None)

def low_pass(kept, grad):
    return (grad,)

def back_keep(v):
    return (v, None)

def back_low(kept, grad):
    return (low(grad),)
low.defvjp(low_keep, low_pass)
low_back.defvjp(back_keep, back_low)
epsilon = 1e-05
masked = -1e+30

def layer_norm(values, gain, shift):
    center = values - lax.optimization_barrier(jnp.mean(values, axis=-1, keepdims=True))
    inverse = lax.rsqrt(lax.optimization_barrier(jnp.mean(center * center, axis=-1, keepdims=True)) + epsilon)
    return center * inverse * gain + shift

def matmul(left, right):
    return jnp.dot(left, right, precision=lax.Precision.HIGHEST, preferred_element_type=jnp.float32)

def attend(query_matrix, key_slice, value_slice, allowed):
    unscaled_scores = jnp.einsum('syzo,sno->syzn', query_matrix, key_slice, precision=lax.Precision.HIGHEST) * HEAD_WIDTH ** (-0.5)
    scores = jnp.where(allowed[:, :, None, :], low_back(unscaled_scores), masked)
    attention_weights = low(jax.nn.softmax(scores, axis=-1))
    return jnp.einsum('gcxz,gzj->gcxj', attention_weights, value_slice, precision=lax.Precision.HIGHEST)

def forward(prompt_float, answer_float, answer_prompt, first_gain, first_shift, query_weight, query_bias, keyval_weight, value_bias, output_weight, output_bias, second_gain, second_shift, up_weight, up_bias, down_weight, down_bias):
    head_count = D // HEAD_WIDTH
    prompt_total = PROMPTS * PROMPT_LEN
    token_rows = jnp.concatenate([prompt_float.reshape(-1, D), answer_float.reshape(-1, D)], axis=0)
    normed_one = low(layer_norm(token_rows, first_gain, first_shift))
    query_matrix = low(low_back(matmul(normed_one, query_weight) + query_bias))
    key_offset = jnp.concatenate([jnp.zeros((HEAD_WIDTH,), jnp.float32), value_bias])
    key_value_rows = low(low_back(matmul(normed_one, keyval_weight) + key_offset))
    prompt_queries = query_matrix[:prompt_total].reshape(PROMPTS, PROMPT_LEN, head_count, HEAD_WIDTH)
    prompt_keyvals = key_value_rows[:prompt_total].reshape(PROMPTS, PROMPT_LEN, 2 * HEAD_WIDTH)
    answer_queries = query_matrix[prompt_total:].reshape(ANSWERS // 8, 8, ANSWER_LEN, head_count, HEAD_WIDTH)
    answer_keyvals = key_value_rows[prompt_total:].reshape(ANSWERS // 8, 8, ANSWER_LEN, 2 * HEAD_WIDTH)
    owning = answer_prompt.reshape(ANSWERS // 8, 8).astype(jnp.int32)
    causal = jnp.arange(PROMPT_LEN)[:, None] >= jnp.arange(PROMPT_LEN)[None, :]

    def prompt_block(inputs):
        block_queries, block_keyvals = inputs
        return attend(block_queries[None], block_keyvals[None, :, :HEAD_WIDTH], block_keyvals[None, :, HEAD_WIDTH:], causal[None])[0]
    prompt_mixture = lax.map(jax.checkpoint(prompt_block), (prompt_queries, prompt_keyvals))
    own_causal = jnp.arange(ANSWER_LEN)[:, None] >= jnp.arange(ANSWER_LEN)[None, :]
    allowed = jnp.concatenate([jnp.ones((ANSWER_LEN, PROMPT_LEN), jnp.bool_), own_causal], axis=1)

    def answer_block(inputs):
        block_queries, block_keyvals, block_owning = inputs
        chosen = jnp.take(prompt_keyvals, block_owning, axis=0)
        joined = jnp.concatenate([chosen, block_keyvals], axis=1)
        return attend(block_queries, joined[..., :HEAD_WIDTH], joined[..., HEAD_WIDTH:], allowed[None])
    answer_mixture = lax.map(jax.checkpoint(answer_block), (answer_queries, answer_keyvals, owning))
    mixture = jnp.concatenate([prompt_mixture.reshape(-1, D), answer_mixture.reshape(-1, D)], axis=0)
    mixture = low(low_back(mixture))
    hidden = token_rows + low_back(matmul(mixture, output_weight.T) + output_bias)

    def feed_block(row_block):
        normed_two = low(layer_norm(row_block, second_gain, second_shift))
        pre_active = low_back(matmul(normed_two, up_weight) + up_bias)
        activated = low(jax.nn.gelu(pre_active, approximate=True))
        return row_block + low_back(matmul(activated, down_weight.T) + down_bias)
    block_rows = math.gcd(TOTAL_TOK, 4096)
    result_rows = lax.map(jax.checkpoint(feed_block), hidden.reshape(-1, block_rows, D))
    return result_rows.reshape(-1, D)

def reference(prompt_states, answer_states, answer_prompt, prompt_teacher, answer_teacher, prompt_valid, answer_valid, first_gain, first_shift, query_weight, query_bias, keyval_weight, value_bias, output_weight, output_bias, second_gain, second_shift, up_weight, up_bias, down_weight, down_bias):
    params = (first_gain, first_shift, query_weight, query_bias, keyval_weight, value_bias, output_weight, output_bias, second_gain, second_shift, up_weight, up_bias, down_weight, down_bias)
    teacher = jnp.concatenate([prompt_teacher.reshape(-1, D), answer_teacher.reshape(-1, D)], axis=0).astype(jnp.float32)
    valid_rows = jnp.concatenate([prompt_valid.reshape(-1), answer_valid.reshape(-1)]).astype(jnp.float32)
    valid_count = jnp.sum(valid_rows)

    def objective(prompt_float, answer_float, *weight_list):
        result_rows = forward(prompt_float, answer_float, answer_prompt, *weight_list)
        differ = result_rows - teacher
        squared_sum = jnp.sum(valid_rows[:, None] * differ * differ)
        return (squared_sum * (0.5 * TOTAL_TOK / valid_count), (result_rows, squared_sum))
    floats = [array_in.astype(jnp.float32) for array_in in (prompt_states, answer_states) + params]
    objective_value, backward, auxiliary = jax.vjp(objective, *floats, has_aux=True)
    gradients = backward(jnp.ones_like(objective_value))
    result_rows, squared_sum = auxiliary
    prompt_total = PROMPTS * PROMPT_LEN
    prompt_out = result_rows[:prompt_total].reshape(PROMPTS, PROMPT_LEN, D).astype(jnp.bfloat16)
    answer_out = result_rows[prompt_total:].reshape(ANSWERS, ANSWER_LEN, D).astype(jnp.bfloat16)
    loss = squared_sum / (valid_count * D)
    return (prompt_out, answer_out, gradients[0].astype(jnp.bfloat16), gradients[1].astype(jnp.bfloat16), gradients[2], gradients[3], gradients[4], gradients[5], gradients[6], gradients[7], gradients[8], gradients[9], gradients[10], gradients[11], gradients[12], gradients[13], gradients[14], gradients[15], loss)
```

```python
import functools

import jax
import jax.numpy as jnp
from jax import lax
from jax.experimental import pallas as pl
from jax.experimental.pallas import tpu as pltpu
from jax.sharding import PartitionSpec as P

HEAD_WIDTH = 128
epsilon = 1e-05
masked = -1e30
MESH = pl.DeviceIdType.MESH
VMEM_BYTES = 56 * 1024 * 1024
SMALL_ROWS = 16


def for_sending(value):
    return value.astype(jnp.bfloat16)


def plain_product(left, right):
    return jnp.dot(left, right, preferred_element_type=jnp.float32)


def transposed_product(left, right):
    return lax.dot_general(
        left, right, (((1,), (1,)), ((), ())), preferred_element_type=jnp.float32
    )


def weight_product(left, right):
    return lax.dot_general(
        left, right, (((0,), (0,)), ((), ())), preferred_element_type=jnp.float32
    )


def norm_stats(values):
    center = values - jnp.mean(values, axis=-1, keepdims=True)
    inverse = lax.rsqrt(jnp.mean(center * center, axis=-1, keepdims=True) + epsilon)
    return center * inverse, inverse


def norm_backward(grad_out, gain, scaled, inverse):
    weighted = grad_out * gain
    grad_in = inverse * (
        weighted
        - jnp.mean(weighted, axis=-1, keepdims=True)
        - scaled * jnp.mean(weighted * scaled, axis=-1, keepdims=True)
    )
    return (grad_in, jnp.sum(grad_out * scaled, axis=0), jnp.sum(grad_out, axis=0))


def column_sums(values):
    return jnp.sum(values.astype(jnp.float32), axis=0)


def block_of_eight():
    here = lax.axis_index("tok")
    core, across, along = here % 2, (here // 2) % 2, here // 4
    on_x = here + 2 - 4 * across
    on_y = here + 4 - 8 * along
    on_chip = here + 1 - 2 * core
    corner = on_x + 4 - 8 * along
    return here, on_x, on_y, on_chip, corner


def greet(devices):
    barrier = pltpu.get_barrier_semaphore()
    for device in devices:
        pl.semaphore_signal(barrier, inc=1, device_id={"tok": device}, device_id_type=MESH)
    pl.semaphore_wait(barrier, len(devices))


def gather_kernel(own_ref, out_ref, send_sem, recv_sem, local_sem):
    half = own_ref.shape[0] // 2
    here, on_x, on_y, on_chip, corner = block_of_eight()
    first, second = pl.ds(0, half), pl.ds(half, half)

    def copy(index, source, target, device):
        return pltpu.make_async_remote_copy(
            src_ref=source,
            dst_ref=target,
            send_sem=send_sem.at[index],
            recv_sem=recv_sem.at[index],
            device_id={"tok": device},
            device_id_type=MESH,
        )

    greet((on_x, on_y, on_chip))
    own = pltpu.make_async_copy(own_ref, out_ref.at[here], local_sem)
    copies = [
        copy(0, own_ref, out_ref.at[here], on_x),
        copy(1, own_ref, out_ref.at[here], on_y),
        copy(2, own_ref, out_ref.at[here], on_chip),
        copy(3, out_ref.at[on_x, first], out_ref.at[on_x, first], on_y),
        copy(4, out_ref.at[on_x], out_ref.at[on_x], on_chip),
        copy(5, out_ref.at[on_y, second], out_ref.at[on_y, second], on_x),
        copy(6, out_ref.at[on_y], out_ref.at[on_y], on_chip),
        copy(7, out_ref.at[corner, first], out_ref.at[corner, first], on_chip),
        copy(8, out_ref.at[corner, second], out_ref.at[corner, second], on_chip),
    ]
    for index in range(3):
        copies[index].start()
    own.start()
    copies[0].wait_recv()
    copies[3].start()
    copies[4].start()
    copies[1].wait_recv()
    copies[5].start()
    copies[6].start()
    copies[3].wait_recv()
    copies[7].start()
    copies[5].wait_recv()
    copies[8].start()
    for index in (2, 4, 6, 7, 8):
        copies[index].wait_recv()
    for each in copies:
        each.wait_send()
    own.wait()


def tok_gather(own, call_number, kernels):
    if not kernels:
        return lax.all_gather(own, "tok", axis=0)
    return pl.pallas_call(
        gather_kernel,
        out_shape=jax.ShapeDtypeStruct((8,) + own.shape, own.dtype),
        in_specs=[pl.BlockSpec(memory_space=pl.ANY)],
        out_specs=pl.BlockSpec(memory_space=pl.ANY),
        scratch_shapes=[
            pltpu.SemaphoreType.DMA((9,)),
            pltpu.SemaphoreType.DMA((9,)),
            pltpu.SemaphoreType.DMA,
        ],
        compiler_params=pltpu.CompilerParams(collective_id=call_number, has_side_effects=True),
        cost_estimate=pl.CostEstimate(
            flops=0, bytes_accessed=own.size * 2 * 100, transcendentals=0
        ),
        name="tok_gather",
    )(own)


def reduce_kernel(part_ref, out_ref, mine, theirs, relayed, final, send_sem, recv_sem, load_sem):
    rows = part_ref.shape[1]
    half = rows // 2
    here, on_x, on_y, on_chip, corner = block_of_eight()
    shift = on_chip - here
    first, second = pl.ds(0, half), pl.ds(half, half)

    def copy(index, source, target, device):
        return pltpu.make_async_remote_copy(
            src_ref=source,
            dst_ref=target,
            send_sem=send_sem.at[index],
            recv_sem=recv_sem.at[index],
            device_id={"tok": device},
            device_id_type=MESH,
        )

    places = (corner, on_x, on_y, here)
    greet((on_x, on_y, on_chip))
    to_chip = [
        copy(index, part_ref.at[places[index] + shift], theirs.at[index], on_chip)
        for index in range(4)
    ]
    loads = [
        pltpu.make_async_copy(part_ref.at[places[index]], mine.at[index], load_sem.at[index])
        for index in range(4)
    ]
    for index in range(4):
        to_chip[index].start()
        loads[index].start()

    step = 16

    def add_into(target, other, start, count):
        @pl.loop(0, count // step)
        def _(turn):
            at = pl.ds(pl.multiple_of(start + turn * step, step), step)
            come = pl.ds(pl.multiple_of(turn * step, step), step)
            total = target[at, :].astype(jnp.float32) + other(at, come).astype(jnp.float32)
            target[at, :] = total.astype(target.dtype)

    def join(index):
        to_chip[index].wait_recv()
        loads[index].wait()
        if index < 3:
            add_into(mine.at[index], lambda at, come: theirs[index, at, :], 0, rows)

    join(0)
    corner_x = copy(4, mine.at[0, first], relayed.at[0], on_x)
    corner_y = copy(5, mine.at[0, second], relayed.at[1], on_y)
    corner_x.start()
    corner_y.start()
    join(1)
    x_first = copy(6, mine.at[1, first], final.at[0, first], on_x)
    x_first.start()
    join(2)
    y_second = copy(7, mine.at[2, second], final.at[1, second], on_y)
    y_second.start()
    corner_y.wait_recv()
    add_into(mine.at[1], lambda at, come: relayed[1, come, :], half, half)
    x_second = copy(8, mine.at[1, second], final.at[0, second], on_x)
    x_second.start()
    corner_x.wait_recv()
    add_into(mine.at[2], lambda at, come: relayed[0, come, :], 0, half)
    y_first = copy(9, mine.at[2, first], final.at[1, first], on_y)
    y_first.start()
    join(3)
    for each in (x_first, y_second, x_second, y_first):
        each.wait_recv()

    @pl.loop(0, rows // step)
    def _(turn):
        at = pl.ds(pl.multiple_of(turn * step, step), step)
        total = mine[3, at, :].astype(jnp.float32) + theirs[3, at, :].astype(jnp.float32)
        total = total + final[0, at, :].astype(jnp.float32) + final[1, at, :].astype(jnp.float32)
        out_ref[at, :] = total.astype(out_ref.dtype)

    for each in to_chip + [corner_x, corner_y, x_first, y_second, x_second, y_first]:
        each.wait_send()


def tok_reduce(parts, call_number, kernels, out_type=jnp.float32):
    if not kernels:
        return lax.psum_scatter(parts, "tok", scatter_dimension=0, tiled=False).astype(out_type)
    _, rows, columns = parts.shape
    kind = parts.dtype
    return pl.pallas_call(
        reduce_kernel,
        out_shape=jax.ShapeDtypeStruct((rows, columns), out_type),
        in_specs=[pl.BlockSpec(memory_space=pl.ANY)],
        out_specs=pl.BlockSpec(memory_space=pltpu.VMEM),
        scratch_shapes=[
            pltpu.VMEM((4, rows, columns), kind),
            pltpu.VMEM((4, rows, columns), kind),
            pltpu.VMEM((2, rows // 2, columns), kind),
            pltpu.VMEM((2, rows, columns), kind),
            pltpu.SemaphoreType.DMA((10,)),
            pltpu.SemaphoreType.DMA((10,)),
            pltpu.SemaphoreType.DMA((4,)),
        ],
        compiler_params=pltpu.CompilerParams(
            collective_id=call_number, has_side_effects=True, vmem_limit_bytes=VMEM_BYTES
        ),
        cost_estimate=pl.CostEstimate(
            flops=0, bytes_accessed=rows * columns * 2 * 100, transcendentals=0
        ),
        name="tok_reduce",
    )(parts)


def peers_of(count):
    here = lax.axis_index("tok")
    return here, [(here + step) % count for step in range(1, count)]


def small_gather_kernel(count, own_ref, out_ref, send_sem, recv_sem, local_sem):
    here, peers = peers_of(count)
    rows = own_ref.shape[1]
    place = pl.ds(pl.multiple_of(here * rows, rows), rows)
    greet(peers)
    own = pltpu.make_async_copy(own_ref, out_ref.at[:, place, :], local_sem)
    copies = [
        pltpu.make_async_remote_copy(
            src_ref=own_ref,
            dst_ref=out_ref.at[:, place, :],
            send_sem=send_sem.at[index],
            recv_sem=recv_sem.at[index],
            device_id={"tok": peers[index]},
            device_id_type=MESH,
        )
        for index in range(count - 1)
    ]
    for each in copies:
        each.start()
    own.start()
    for each in copies:
        each.wait_recv()
    for each in copies:
        each.wait_send()
    own.wait()


def tok_gather_small(own, call_number, kernels):
    if not kernels:
        return lax.all_gather(own, "tok", axis=1, tiled=True)
    count = 8
    prompts, rows, columns = own.shape
    return pl.pallas_call(
        functools.partial(small_gather_kernel, count),
        out_shape=jax.ShapeDtypeStruct((prompts, count * rows, columns), own.dtype),
        in_specs=[pl.BlockSpec(memory_space=pl.ANY)],
        out_specs=pl.BlockSpec(memory_space=pl.ANY),
        scratch_shapes=[
            pltpu.SemaphoreType.DMA((count - 1,)),
            pltpu.SemaphoreType.DMA((count - 1,)),
            pltpu.SemaphoreType.DMA,
        ],
        compiler_params=pltpu.CompilerParams(collective_id=call_number, has_side_effects=True),
        name="tok_gather_small",
    )(own)


def small_reduce_kernel(count, part_ref, out_ref, come, send_sem, recv_sem):
    here, peers = peers_of(count)
    rows = come.shape[2]

    def place(device):
        return pl.ds(pl.multiple_of(device * rows, rows), rows)

    greet(peers)
    copies = [
        pltpu.make_async_remote_copy(
            src_ref=part_ref.at[:, place(peers[index]), :],
            dst_ref=come.at[index],
            send_sem=send_sem.at[index],
            recv_sem=recv_sem.at[index],
            device_id={"tok": peers[index]},
            device_id_type=MESH,
        )
        for index in range(count - 1)
    ]
    for each in copies:
        each.start()
    total = part_ref[:, place(here), :].astype(jnp.float32)
    for index in range(count - 1):
        copies[index].wait_recv()
        total = total + come[index].astype(jnp.float32)
    out_ref[...] = total.astype(out_ref.dtype)
    for each in copies:
        each.wait_send()


def tok_reduce_small(parts, call_number, kernels):
    if not kernels:
        return lax.psum_scatter(parts, "tok", scatter_dimension=1, tiled=True).astype(jnp.float32)
    count = 8
    prompts, rows, columns = parts.shape
    rows = rows // count
    return pl.pallas_call(
        functools.partial(small_reduce_kernel, count),
        out_shape=jax.ShapeDtypeStruct((prompts, rows, columns), jnp.float32),
        in_specs=[pl.BlockSpec(memory_space=pltpu.VMEM)],
        out_specs=pl.BlockSpec(memory_space=pltpu.VMEM),
        scratch_shapes=[
            pltpu.VMEM((count - 1, prompts, rows, columns), parts.dtype),
            pltpu.SemaphoreType.DMA((count - 1,)),
            pltpu.SemaphoreType.DMA((count - 1,)),
        ],
        compiler_params=pltpu.CompilerParams(
            collective_id=call_number, has_side_effects=True, vmem_limit_bytes=VMEM_BYTES
        ),
        name="tok_reduce_small",
    )(parts)


def stack_heads(values, heads):
    return jnp.concatenate(
        [values[:, head * HEAD_WIDTH : (head + 1) * HEAD_WIDTH] for head in range(heads)], axis=0
    )


def unstack_heads(values, heads):
    rows = values.shape[0] // heads
    return jnp.concatenate(
        [values[head * rows : (head + 1) * rows, :] for head in range(heads)], axis=1
    )


def part_rows(part, prompts, answers, token_ref, answer_ref):
    answer_rows = answer_ref.shape[0] // answers
    prompt_rows = (token_ref.shape[0] - answer_ref.shape[0]) // prompts
    if part < prompts:
        return slice(part * prompt_rows, (part + 1) * prompt_rows), prompt_rows
    start = prompts * prompt_rows + (part - prompts) * answer_rows
    return slice(start, start + answer_rows), answer_rows


def as_row(column):
    wide = jnp.broadcast_to(column, (column.shape[0], HEAD_WIDTH))
    return jnp.transpose(wide)[0:1, :]


def attention_forward_kernel(
    prompts,
    answers,
    heads,
    scale,
    place_ref,
    owner_ref,
    normed_ref,
    query_ref,
    bias_ref,
    prompt_kv_ref,
    answer_kv_ref,
    output_ref,
    states_ref,
    offset_ref,
    gain_ref,
    shift_ref,
    queries_ref,
    mixture_ref,
    log_ref,
    hidden_ref,
    second_ref,
):
    step = pl.program_id(0)
    width = HEAD_WIDTH
    length = prompt_kv_ref.shape[1]
    query_block = query_ref[0].reshape(-1, query_ref.shape[-1])
    output_block = output_ref[0].reshape(-1, output_ref.shape[-1])
    queries = (plain_product(normed_ref[...], query_block) + bias_ref[0]).astype(jnp.bfloat16)
    queries_ref[...] = queries

    pieces = []
    for part in range(prompts + answers):
        here, rows = part_rows(part, prompts, answers, normed_ref, answer_kv_ref)
        token = lax.broadcasted_iota(jnp.int32, (heads * rows, 1), 0) % rows
        stacked = stack_heads(queries[here, :], heads)
        if part < prompts:
            keys = prompt_kv_ref[part, :, :width]
            values = prompt_kv_ref[part, :, width:]
            scores = transposed_product(stacked, keys)
            place = lax.broadcasted_iota(jnp.int32, (1, length), 1)
            scores = jnp.where(place <= place_ref[0] + token, scores, masked)
            top = jnp.max(scores, axis=-1, keepdims=True)
            exponent = jnp.exp((scores - top) * scale)
            total = jnp.sum(exponent, axis=-1, keepdims=True)
            mixed = plain_product(exponent.astype(jnp.bfloat16), values)
        else:
            answer = part - prompts
            owner = owner_ref[answer]
            own = slice(answer * rows, (answer + 1) * rows)
            keys = prompt_kv_ref[owner, :, :width]
            values = prompt_kv_ref[owner, :, width:]
            scores = transposed_product(stacked, keys)
            own_scores = transposed_product(stacked, answer_kv_ref[own, :width])
            place = lax.broadcasted_iota(jnp.int32, (1, rows), 1)
            own_scores = jnp.where(place <= token, own_scores, masked)
            top = jnp.maximum(
                jnp.max(scores, axis=-1, keepdims=True),
                jnp.max(own_scores, axis=-1, keepdims=True),
            )
            exponent = jnp.exp((scores - top) * scale)
            own_exponent = jnp.exp((own_scores - top) * scale)
            total = jnp.sum(exponent, axis=-1, keepdims=True) + jnp.sum(
                own_exponent, axis=-1, keepdims=True
            )
            mixed = plain_product(exponent.astype(jnp.bfloat16), values) + plain_product(
                own_exponent.astype(jnp.bfloat16), answer_kv_ref[own, width:]
            )
        pieces.append(unstack_heads((mixed / total).astype(jnp.bfloat16), heads))
        log_row = as_row(top * scale + jnp.log(total))
        for head in range(heads):
            log_ref[0, head : head + 1, here] = log_row[:, head * rows : (head + 1) * rows]
    mixture = jnp.concatenate(pieces, axis=0)
    mixture_ref[...] = mixture

    @pl.when(step == 0)
    def _():
        hidden_ref[...] = states_ref[...].astype(jnp.float32) + offset_ref[...]

    hidden_ref[...] += transposed_product(mixture, output_block)

    @pl.when(step == pl.num_programs(0) - 1)
    def _():
        scaled, _ = norm_stats(hidden_ref[...])
        second_ref[...] = (scaled * gain_ref[...] + shift_ref[...]).astype(jnp.bfloat16)


def attention_forward(
    place,
    owning,
    normed,
    packed,
    weight_rows,
    query_offset,
    prompt_kv,
    answer_kv,
    states,
    output_offset,
    gain,
    shift,
    prompts,
    answers,
):
    token_rows, model_width = normed.shape
    steps, groups, _, block = packed.shape
    heads = block // HEAD_WIDTH
    length = prompt_kv.shape[1]
    whole = lambda *shape: pl.BlockSpec(shape, lambda step, *_: (0,) * len(shape))
    scores = heads * token_rows * length
    return pl.pallas_call(
        functools.partial(
            attention_forward_kernel, prompts, answers, heads, HEAD_WIDTH ** (-0.5)
        ),
        out_shape=(
            jax.ShapeDtypeStruct((token_rows, model_width), jnp.bfloat16),
            jax.ShapeDtypeStruct((token_rows, model_width), jnp.bfloat16),
            jax.ShapeDtypeStruct((steps, heads, token_rows), jnp.float32),
            jax.ShapeDtypeStruct((token_rows, model_width), jnp.float32),
            jax.ShapeDtypeStruct((token_rows, model_width), jnp.bfloat16),
        ),
        grid_spec=pltpu.PrefetchScalarGridSpec(
            num_scalar_prefetch=2,
            grid=(steps,),
            in_specs=[
                whole(token_rows, model_width),
                pl.BlockSpec(
                    (1, groups, weight_rows, block), lambda step, *_: (step, 0, 0, 0)
                ),
                pl.BlockSpec((1, 1, block), lambda step, *_: (step, 0, 0)),
                whole(*prompt_kv.shape),
                whole(*answer_kv.shape),
                pl.BlockSpec(
                    (1, groups, weight_rows, block), lambda step, *_: (step, 0, 1, 0)
                ),
                whole(token_rows, model_width),
                whole(1, model_width),
                whole(1, model_width),
                whole(1, model_width),
            ],
            out_specs=(
                pl.BlockSpec((token_rows, block), lambda step, *_: (0, step)),
                pl.BlockSpec((token_rows, block), lambda step, *_: (0, step)),
                pl.BlockSpec((1, heads, token_rows), lambda step, *_: (step, 0, 0)),
                whole(token_rows, model_width),
                whole(token_rows, model_width),
            ),
        ),
        compiler_params=pltpu.CompilerParams(vmem_limit_bytes=VMEM_BYTES),
        cost_estimate=pl.CostEstimate(
            flops=steps * (4 * token_rows * model_width * block + 8 * scores * HEAD_WIDTH),
            bytes_accessed=8 * steps * model_width * block,
            transcendentals=steps * scores,
        ),
        name="attention_forward",
    )(
        place,
        owning,
        normed,
        packed,
        query_offset.reshape(steps, 1, block),
        prompt_kv,
        answer_kv,
        packed,
        states,
        output_offset.reshape(1, -1),
        gain.reshape(1, -1),
        shift.reshape(1, -1),
    )


def attention_backward_kernel(
    prompts,
    answers,
    heads,
    scale,
    place_ref,
    owner_ref,
    normed_ref,
    query_ref,
    prompt_kv_ref,
    answer_kv_ref,
    output_ref,
    branch_ref,
    queries_ref,
    mixture_ref,
    log_ref,
    grad_weights_ref,
    grad_normed_ref,
    grad_prompt_ref,
    grad_answer_ref,
    grad_bias_ref,
    normed_across,
    branch_across,
    key_sums,
    own_sums,
):
    step = pl.program_id(0)
    width = HEAD_WIDTH
    length = prompt_kv_ref.shape[1]
    block = queries_ref.shape[1]

    @pl.when(step == 0)
    def _():
        normed_across[...] = jnp.transpose(normed_ref[...])
        branch_across[...] = jnp.transpose(branch_ref[...])
        key_sums[...] = jnp.zeros_like(key_sums)
        own_sums[...] = jnp.zeros_like(own_sums)
        grad_normed_ref[...] = jnp.zeros_like(grad_normed_ref)

    query_block = query_ref[0].reshape(-1, block)
    output_block = output_ref[0].reshape(-1, block)
    weight_shape = query_ref.shape[1:]
    grad_weights_ref[0, :, 1] = (
        plain_product(branch_across[...], mixture_ref[...])
        .astype(jnp.bfloat16)
        .reshape(weight_shape)
    )
    grad_mixture = plain_product(branch_ref[...], output_block).astype(jnp.bfloat16)
    queries = queries_ref[...]
    mixture = mixture_ref[...]

    def backward(keys, values, stacked, grad_stacked, log_row, inner_row, allowed):
        scores = transposed_product(keys, stacked)
        probs = jnp.exp(scores * scale - log_row)
        if allowed is not None:
            probs = jnp.where(allowed, probs, 0.0)
        grad_values = plain_product(probs.astype(jnp.bfloat16), grad_stacked)
        grad_probs = transposed_product(values, grad_stacked)
        grad_scores = (probs * (grad_probs - inner_row)).astype(jnp.bfloat16)
        grad_keys = plain_product(grad_scores, stacked)
        grad_queries = weight_product(grad_scores, keys)
        return grad_queries, grad_keys, grad_values

    pieces = []
    for part in range(prompts + answers):
        here, rows = part_rows(part, prompts, answers, normed_ref, answer_kv_ref)
        token = lax.broadcasted_iota(jnp.int32, (1, heads * rows), 1) % rows
        stacked = stack_heads(queries[here, :], heads)
        grad_stacked = stack_heads(grad_mixture[here, :], heads)
        mixed = stack_heads(mixture[here, :], heads)
        product = grad_stacked.astype(jnp.float32) * mixed.astype(jnp.float32)
        inner_row = jnp.sum(jnp.transpose(product), axis=0, keepdims=True)
        log_row = jnp.concatenate(
            [log_ref[0, head : head + 1, here] for head in range(heads)], axis=1
        )
        if part < prompts:
            place = lax.broadcasted_iota(jnp.int32, (length, 1), 0)
            grad_queries, grad_keys, grad_values = backward(
                prompt_kv_ref[part, :, :width],
                prompt_kv_ref[part, :, width:],
                stacked,
                grad_stacked,
                log_row,
                inner_row,
                place <= place_ref[0] + token,
            )
            key_sums[part, :, :width] += grad_keys
            key_sums[part, :, width:] += grad_values
        else:
            answer = part - prompts
            owner = owner_ref[answer]
            own = slice(answer * rows, (answer + 1) * rows)
            grad_queries, grad_keys, grad_values = backward(
                prompt_kv_ref[owner, :, :width],
                prompt_kv_ref[owner, :, width:],
                stacked,
                grad_stacked,
                log_row,
                inner_row,
                None,
            )
            key_sums[owner, :, :width] += grad_keys
            key_sums[owner, :, width:] += grad_values
            place = lax.broadcasted_iota(jnp.int32, (rows, 1), 0)
            own_queries, own_keys, own_values = backward(
                answer_kv_ref[own, :width],
                answer_kv_ref[own, width:],
                stacked,
                grad_stacked,
                log_row,
                inner_row,
                place <= token,
            )
            grad_queries = grad_queries + own_queries
            own_sums[own, :width] += own_keys
            own_sums[own, width:] += own_values
        pieces.append(unstack_heads((grad_queries * scale).astype(jnp.bfloat16), heads))
    grad_queries = jnp.concatenate(pieces, axis=0)
    grad_weights_ref[0, :, 0] = (
        plain_product(normed_across[...], grad_queries).astype(jnp.bfloat16).reshape(weight_shape)
    )
    grad_normed_ref[...] += transposed_product(grad_queries, query_block)
    grad_bias_ref[0] = jnp.sum(grad_queries.astype(jnp.float32), axis=0, keepdims=True)

    @pl.when(step == pl.num_programs(0) - 1)
    def _():
        grad_prompt_ref[:, :, :width] = (key_sums[:, :, :width] * scale).astype(jnp.bfloat16)
        grad_prompt_ref[:, :, width:] = key_sums[:, :, width:].astype(jnp.bfloat16)
        grad_answer_ref[:, :width] = own_sums[:, :width] * scale
        grad_answer_ref[:, width:] = own_sums[:, width:]


def attention_backward(
    place,
    owning,
    normed,
    packed,
    weight_rows,
    prompt_kv,
    answer_kv,
    branch,
    queries,
    mixture,
    log_total,
    prompts,
    answers,
):
    token_rows, model_width = normed.shape
    steps, groups, _, block = packed.shape
    heads = block // HEAD_WIDTH
    length = prompt_kv.shape[1]
    whole = lambda *shape: pl.BlockSpec(shape, lambda step, *_: (0,) * len(shape))
    columns = lambda: pl.BlockSpec((token_rows, block), lambda step, *_: (0, step))
    scores = heads * token_rows * length
    return pl.pallas_call(
        functools.partial(
            attention_backward_kernel, prompts, answers, heads, HEAD_WIDTH ** (-0.5)
        ),
        out_shape=(
            jax.ShapeDtypeStruct((steps, groups, 2, weight_rows, block), jnp.bfloat16),
            jax.ShapeDtypeStruct((token_rows, model_width), jnp.float32),
            jax.ShapeDtypeStruct(prompt_kv.shape, jnp.bfloat16),
            jax.ShapeDtypeStruct(answer_kv.shape, jnp.float32),
            jax.ShapeDtypeStruct((steps, 1, block), jnp.float32),
        ),
        grid_spec=pltpu.PrefetchScalarGridSpec(
            num_scalar_prefetch=2,
            grid=(steps,),
            in_specs=[
                whole(token_rows, model_width),
                pl.BlockSpec(
                    (1, groups, weight_rows, block), lambda step, *_: (step, 0, 0, 0)
                ),
                whole(*prompt_kv.shape),
                whole(*answer_kv.shape),
                pl.BlockSpec(
                    (1, groups, weight_rows, block), lambda step, *_: (step, 0, 1, 0)
                ),
                whole(token_rows, model_width),
                columns(),
                columns(),
                pl.BlockSpec((1, heads, token_rows), lambda step, *_: (step, 0, 0)),
            ],
            out_specs=(
                pl.BlockSpec(
                    (1, groups, 2, weight_rows, block), lambda step, *_: (step, 0, 0, 0, 0)
                ),
                whole(token_rows, model_width),
                whole(*prompt_kv.shape),
                whole(*answer_kv.shape),
                pl.BlockSpec((1, 1, block), lambda step, *_: (step, 0, 0)),
            ),
            scratch_shapes=[
                pltpu.VMEM((model_width, token_rows), jnp.bfloat16),
                pltpu.VMEM((model_width, token_rows), jnp.bfloat16),
                pltpu.VMEM(prompt_kv.shape, jnp.float32),
                pltpu.VMEM(answer_kv.shape, jnp.float32),
            ],
        ),
        compiler_params=pltpu.CompilerParams(vmem_limit_bytes=VMEM_BYTES),
        cost_estimate=pl.CostEstimate(
            flops=steps * (8 * token_rows * model_width * block + 20 * scores * HEAD_WIDTH),
            bytes_accessed=16 * steps * model_width * block,
            transcendentals=steps * scores,
        ),
        name="attention_backward",
    )(
        place,
        owning,
        normed,
        packed,
        prompt_kv,
        answer_kv,
        packed,
        branch,
        queries,
        mixture,
        log_total,
    )


def by_group(values):
    return jnp.swapaxes(values, 0, 1).reshape(-1)


def body(
    kernels,
    prompt_states,
    answer_states,
    answer_prompt,
    prompt_teacher,
    answer_teacher,
    prompt_valid,
    answer_valid,
    first_gain,
    first_shift,
    query_weight,
    query_bias,
    keyval_weight,
    value_bias,
    output_weight,
    output_bias,
    second_gain,
    second_shift,
    up_weight,
    up_bias,
    down_weight,
    down_bias,
):
    prompt_count, prompt_rows, model_width = prompt_states.shape
    answer_count, answer_len, _ = answer_states.shape
    groups = lax.axis_size("grp")
    token_devices = lax.axis_size("tok")
    token_index = lax.axis_index("tok")
    group_index = lax.axis_index("grp")
    own_prompt = prompt_rows * prompt_count
    token_rows = own_prompt + answer_count * answer_len
    hidden_units = up_bias.shape[0] * groups * token_devices
    ff_here = hidden_units // token_devices
    ff_start = token_index * ff_here
    share = first_gain.shape[0]
    block = query_weight.shape[1]
    weight_rows = query_weight.shape[0]
    keyval_rows, keyval_width = keyval_weight.shape

    def own_rows(prompt_part, answer_part):
        return jnp.concatenate(
            [prompt_part.reshape(own_prompt, -1), answer_part.reshape(-1, prompt_part.shape[-1])],
            axis=0,
        )

    states = own_rows(prompt_states, answer_states)
    inputs = states.astype(jnp.float32)
    valid_rows = jnp.concatenate([prompt_valid.reshape(-1), answer_valid.reshape(-1)])
    own_count = jnp.sum(valid_rows)
    valid_rows = valid_rows.astype(jnp.float32)

    up_cols = lax.all_gather(up_weight, "grp", axis=0, tiled=True)
    down_cols = lax.all_gather(down_weight, "grp", axis=0, tiled=True)

    count_parts = jnp.stack([own_count // 128, own_count % 128]).astype(jnp.bfloat16)
    smalls = jnp.concatenate(
        [
            first_gain,
            first_shift,
            query_bias,
            output_bias,
            second_gain,
            second_shift,
            down_bias,
            up_bias,
            count_parts,
        ]
    )
    smalls = jnp.pad(smalls, (0, SMALL_ROWS * block - smalls.shape[0])).reshape(SMALL_ROWS, block)
    pack = jnp.concatenate(
        [query_weight, output_weight, keyval_weight.reshape(-1, block), smalls], axis=0
    )
    pack_rows = pack.shape[0]
    packed = lax.all_gather(pack, "grp", axis=0, tiled=True)
    packed = tok_gather(packed, 0, kernels).reshape(token_devices, groups, pack_rows, block)
    keyval_start = 2 * weight_rows
    keyval_end = pack_rows - SMALL_ROWS
    keyval_full = jnp.swapaxes(
        packed[:, :, keyval_start:keyval_end].reshape(
            token_devices, groups, keyval_rows, keyval_width
        ),
        0,
        1,
    ).reshape(model_width, keyval_width)
    small_full = packed[:, :, keyval_end:].reshape(token_devices, groups, SMALL_ROWS * block)
    small_full = jnp.swapaxes(small_full.astype(jnp.float32), 0, 1)

    def vector(start, size):
        return small_full[:, :, start : start + size].reshape(-1)

    gain_one, shift_one, query_offset, output_offset, gain_two, shift_two, down_offset = (
        vector(index * share, share) for index in range(7)
    )
    up_offset = vector(7 * share, up_bias.shape[0])
    count_at = 7 * share + up_bias.shape[0]
    counts = small_full[:, :, count_at : count_at + 2]
    valid_count = jnp.sum(counts[:, :, 0]) * 128.0 + jnp.sum(counts[:, :, 1])
    up_here = lax.dynamic_slice_in_dim(up_offset, ff_start, ff_here)

    scaled_one, inverse_one = norm_stats(inputs)
    normed_one = (scaled_one * gain_one + shift_one).astype(jnp.bfloat16)
    key_offset = jnp.concatenate(
        [jnp.zeros((HEAD_WIDTH,), jnp.float32), value_bias.astype(jnp.float32)]
    )
    key_value_rows = (plain_product(normed_one, keyval_full) + key_offset).astype(jnp.bfloat16)
    prompt_kv = tok_gather_small(
        key_value_rows[:own_prompt].reshape(prompt_count, prompt_rows, -1), 1, kernels
    )
    answer_kv = key_value_rows[own_prompt:]
    owning = answer_prompt - group_index * prompt_count
    owning = lax.dynamic_slice_in_dim(owning, token_index * answer_count, answer_count)
    place = jnp.reshape(token_index * prompt_rows, (1,)).astype(jnp.int32)
    queries, mixture, log_total, hidden, normed_two = attention_forward(
        place,
        owning,
        normed_one,
        packed,
        weight_rows,
        query_offset,
        prompt_kv,
        answer_kv,
        states,
        output_offset,
        gain_two,
        shift_two,
        prompt_count,
        answer_count,
    )

    group_two = tok_gather(normed_two, 2, kernels).reshape(-1, model_width)
    pre_active = plain_product(group_two, up_cols) + up_here
    activated = jax.nn.gelu(pre_active, approximate=True).astype(jnp.bfloat16)
    feed_term = for_sending(transposed_product(activated, down_cols))
    feed_term = tok_reduce(feed_term.reshape(token_devices, token_rows, model_width), 3, kernels)
    result_rows = hidden + feed_term + down_offset

    teacher = own_rows(prompt_teacher, answer_teacher).astype(jnp.float32)
    differ = result_rows - teacher
    own_squares = jnp.sum(valid_rows[:, None] * differ * differ)
    every_token = token_rows * groups * token_devices
    grad_result = every_token / valid_count * valid_rows[:, None] * differ
    grad_branch_two = grad_result.astype(jnp.bfloat16)

    group_grad_two = tok_gather(grad_branch_two, 4, kernels).reshape(-1, model_width)
    grad_activated = plain_product(group_grad_two, down_cols)
    _, gelu_back = jax.vjp(lambda argument: jax.nn.gelu(argument, approximate=True), pre_active)
    grad_pre_active = gelu_back(grad_activated)[0].astype(jnp.bfloat16)
    grad_normed_two = for_sending(transposed_product(grad_pre_active, up_cols))
    grad_normed_two = tok_reduce(
        grad_normed_two.reshape(token_devices, token_rows, model_width), 5, kernels
    )
    grad_down_cols = for_sending(weight_product(group_grad_two, activated))
    grad_down_weight = lax.psum_scatter(grad_down_cols, "grp", scatter_dimension=0, tiled=True)
    grad_up_cols = for_sending(weight_product(group_two, grad_pre_active))
    grad_up_weight = lax.psum_scatter(grad_up_cols, "grp", scatter_dimension=0, tiled=True)
    grad_down_offset = column_sums(grad_branch_two)
    grad_up_offset = column_sums(grad_pre_active)
    scaled_two, inverse_two = norm_stats(hidden)
    grad_norm_two, grad_gain_two, grad_shift_two = norm_backward(
        grad_normed_two, gain_two, scaled_two, inverse_two
    )
    grad_hidden = grad_result + grad_norm_two
    grad_branch_one = grad_hidden.astype(jnp.bfloat16)
    grad_output_offset = column_sums(grad_branch_one)

    grad_weights, grad_normed_one, grad_prompt_kv, grad_answer_kv, grad_query_offset = (
        attention_backward(
            place,
            owning,
            normed_one,
            packed,
            weight_rows,
            prompt_kv,
            answer_kv,
            grad_branch_one,
            queries,
            mixture,
            log_total,
            prompt_count,
            answer_count,
        )
    )
    grad_prompt_kv = tok_reduce_small(grad_prompt_kv, 6, kernels)
    grad_keyvals = jnp.concatenate(
        [grad_prompt_kv.reshape(own_prompt, -1), grad_answer_kv], axis=0
    ).astype(jnp.bfloat16)
    grad_keyval_full = weight_product(normed_one, grad_keyvals)
    grad_value_offset = column_sums(grad_keyvals[:, HEAD_WIDTH:])
    grad_normed_one = grad_normed_one + transposed_product(grad_keyvals, keyval_full)
    grad_norm_one, grad_gain_one, grad_shift_one = norm_backward(
        grad_normed_one, gain_one, scaled_one, inverse_one
    )
    grad_inputs = grad_hidden + grad_norm_one

    grad_weights = grad_weights.reshape(token_devices, -1, block)
    grad_weights = tok_reduce(grad_weights, 7, kernels, jnp.bfloat16)
    grad_weights = lax.psum_scatter(grad_weights, "grp", scatter_dimension=0, tiled=True)
    grad_weights = grad_weights.astype(jnp.float32).reshape(2, weight_rows, block)
    grad_keyval_own = lax.psum_scatter(
        grad_keyval_full, ("grp", "tok"), scatter_dimension=0, tiled=True
    )
    small_grads = jnp.concatenate(
        [
            vector_grad.reshape(groups * token_devices, -1)
            for vector_grad in (
                grad_gain_one,
                grad_shift_one,
                grad_query_offset.reshape(-1),
                grad_output_offset,
                grad_gain_two,
                grad_shift_two,
                grad_down_offset,
                lax.dynamic_update_slice_in_dim(
                    jnp.zeros((hidden_units,), jnp.float32), grad_up_offset, ff_start, 0
                ),
            )
        ],
        axis=1,
    ).reshape(-1)
    small_size = small_grads.shape[0]
    small_grads = lax.psum(
        jnp.concatenate([small_grads, grad_value_offset, own_squares.reshape(1)]), ("grp", "tok")
    )
    value_total = small_grads[small_size : small_size + HEAD_WIDTH]
    squared_sum = small_grads[small_size + HEAD_WIDTH]
    own_small = lax.dynamic_slice_in_dim(
        small_grads[:small_size].reshape(groups * token_devices, -1),
        group_index * token_devices + token_index,
        1,
    ).reshape(-1)
    loss_value = squared_sum / (valid_count * model_width)

    def split_rows(values):
        values = values.astype(jnp.bfloat16)
        return (
            values[:own_prompt].reshape(prompt_states.shape),
            values[own_prompt:].reshape(answer_states.shape),
        )

    prompt_out, answer_out = split_rows(result_rows)
    prompt_grad, answer_grad = split_rows(grad_inputs)
    pieces = [own_small[index * share : (index + 1) * share] for index in range(7)]
    return (
        prompt_out,
        answer_out,
        prompt_grad,
        answer_grad,
        pieces[0],
        pieces[1],
        grad_weights[0],
        pieces[2],
        grad_keyval_own,
        value_total,
        grad_weights[1],
        pieces[3],
        pieces[4],
        pieces[5],
        grad_up_weight.astype(jnp.float32),
        own_small[7 * share :],
        grad_down_weight.astype(jnp.float32),
        pieces[6],
        loss_value,
    )


def solution(mesh):
    rows = P(("grp", "tok"))
    table = P(("grp", "tok"), None)
    matrix = P("grp", "tok")
    prompt_part = P("grp", "tok", None)
    answer_part = P(("grp", "tok"), None, None)
    in_specs = (
        prompt_part,
        answer_part,
        P("grp"),
        prompt_part,
        answer_part,
        P("grp", "tok"),
        table,
        rows,
        rows,
        matrix,
        rows,
        table,
        P(),
        matrix,
        rows,
        rows,
        rows,
        matrix,
        rows,
        matrix,
        rows,
    )
    out_specs = (
        prompt_part,
        answer_part,
        prompt_part,
        answer_part,
        rows,
        rows,
        matrix,
        rows,
        table,
        P(),
        matrix,
        rows,
        rows,
        rows,
        matrix,
        rows,
        matrix,
        rows,
        P(),
    )
    kernels = mesh.shape["tok"] == 8
    return jax.shard_map(
        functools.partial(body, kernels),
        mesh=mesh,
        in_specs=in_specs,
        out_specs=out_specs,
        check_vma=False,
    )
```

```python
import functools

import jax
import jax.numpy as jnp
from jax import lax
from jax.experimental import pallas as pl
from jax.experimental.pallas import tpu as pltpu
from jax.sharding import PartitionSpec as P

HEAD_WIDTH = 128
epsilon = 1e-05
masked = -1e30
MESH = pl.DeviceIdType.MESH
VMEM_BYTES = 56 * 1024 * 1024
SMALL_ROWS = 16
SMALL_SUMS = 1024


def for_sending(value):
    return value.astype(jnp.bfloat16)


def plain_product(left, right):
    return jnp.dot(left, right, preferred_element_type=jnp.float32)


def transposed_product(left, right):
    return lax.dot_general(
        left, right, (((1,), (1,)), ((), ())), preferred_element_type=jnp.float32
    )


def weight_product(left, right):
    return lax.dot_general(
        left, right, (((0,), (0,)), ((), ())), preferred_element_type=jnp.float32
    )


def norm_stats(values):
    center = values - jnp.mean(values, axis=-1, keepdims=True)
    inverse = lax.rsqrt(jnp.mean(center * center, axis=-1, keepdims=True) + epsilon)
    return center * inverse, inverse


def norm_backward(grad_out, gain, scaled, inverse):
    weighted = grad_out * gain
    grad_in = inverse * (
        weighted
        - jnp.mean(weighted, axis=-1, keepdims=True)
        - scaled * jnp.mean(weighted * scaled, axis=-1, keepdims=True)
    )
    return (grad_in, jnp.sum(grad_out * scaled, axis=0), jnp.sum(grad_out, axis=0))


def column_sums(values):
    return jnp.sum(values.astype(jnp.float32), axis=0)


def block_of_eight():
    here = lax.axis_index("tok")
    core, across, along = here % 2, (here // 2) % 2, here // 4
    on_x = here + 2 - 4 * across
    on_y = here + 4 - 8 * along
    on_chip = here + 1 - 2 * core
    corner = on_x + 4 - 8 * along
    return here, on_x, on_y, on_chip, corner


def greet(devices):
    barrier = pltpu.get_barrier_semaphore()
    for device in devices:
        pl.semaphore_signal(barrier, inc=1, device_id={"tok": device}, device_id_type=MESH)
    pl.semaphore_wait(barrier, len(devices))


def gather_kernel(own_ref, out_ref, send_sem, recv_sem, local_sem):
    half = own_ref.shape[0] // 2
    here, on_x, on_y, on_chip, corner = block_of_eight()
    first, second = pl.ds(0, half), pl.ds(half, half)

    def copy(index, source, target, device):
        return pltpu.make_async_remote_copy(
            src_ref=source,
            dst_ref=target,
            send_sem=send_sem.at[index],
            recv_sem=recv_sem.at[index],
            device_id={"tok": device},
            device_id_type=MESH,
        )

    greet((on_x, on_y, on_chip))
    own = pltpu.make_async_copy(own_ref, out_ref.at[here], local_sem)
    copies = [
        copy(0, own_ref, out_ref.at[here], on_x),
        copy(1, own_ref, out_ref.at[here], on_y),
        copy(2, own_ref, out_ref.at[here], on_chip),
        copy(3, out_ref.at[on_x, first], out_ref.at[on_x, first], on_y),
        copy(4, out_ref.at[on_x], out_ref.at[on_x], on_chip),
        copy(5, out_ref.at[on_y, second], out_ref.at[on_y, second], on_x),
        copy(6, out_ref.at[on_y], out_ref.at[on_y], on_chip),
        copy(7, out_ref.at[corner, first], out_ref.at[corner, first], on_chip),
        copy(8, out_ref.at[corner, second], out_ref.at[corner, second], on_chip),
    ]
    for index in range(3):
        copies[index].start()
    own.start()
    copies[0].wait_recv()
    copies[3].start()
    copies[4].start()
    copies[1].wait_recv()
    copies[5].start()
    copies[6].start()
    copies[3].wait_recv()
    copies[7].start()
    copies[5].wait_recv()
    copies[8].start()
    for index in (2, 4, 6, 7, 8):
        copies[index].wait_recv()
    for each in copies:
        each.wait_send()
    own.wait()


def tok_gather(own, call_number, kernels):
    if not kernels:
        return lax.all_gather(own, "tok", axis=0)
    return pl.pallas_call(
        gather_kernel,
        out_shape=jax.ShapeDtypeStruct((8,) + own.shape, own.dtype),
        in_specs=[pl.BlockSpec(memory_space=pl.ANY)],
        out_specs=pl.BlockSpec(memory_space=pl.ANY),
        scratch_shapes=[
            pltpu.SemaphoreType.DMA((9,)),
            pltpu.SemaphoreType.DMA((9,)),
            pltpu.SemaphoreType.DMA,
        ],
        compiler_params=pltpu.CompilerParams(collective_id=call_number, has_side_effects=True),
        cost_estimate=pl.CostEstimate(
            flops=0, bytes_accessed=own.size * 2 * 100, transcendentals=0
        ),
        name="tok_gather",
    )(own)


def reduce_kernel(part_ref, out_ref, mine, theirs, relayed, final, send_sem, recv_sem, load_sem):
    rows = part_ref.shape[1]
    half = rows // 2
    here, on_x, on_y, on_chip, corner = block_of_eight()
    shift = on_chip - here
    first, second = pl.ds(0, half), pl.ds(half, half)

    def copy(index, source, target, device):
        return pltpu.make_async_remote_copy(
            src_ref=source,
            dst_ref=target,
            send_sem=send_sem.at[index],
            recv_sem=recv_sem.at[index],
            device_id={"tok": device},
            device_id_type=MESH,
        )

    places = (corner, on_x, on_y, here)
    greet((on_x, on_y, on_chip))
    to_chip = [
        copy(index, part_ref.at[places[index] + shift], theirs.at[index], on_chip)
        for index in range(4)
    ]
    loads = [
        pltpu.make_async_copy(part_ref.at[places[index]], mine.at[index], load_sem.at[index])
        for index in range(4)
    ]
    for index in range(4):
        to_chip[index].start()
        loads[index].start()

    step = 16

    def add_into(target, other, start, count):
        @pl.loop(0, count // step)
        def _(turn):
            at = pl.ds(pl.multiple_of(start + turn * step, step), step)
            come = pl.ds(pl.multiple_of(turn * step, step), step)
            total = target[at, :].astype(jnp.float32) + other(at, come).astype(jnp.float32)
            target[at, :] = total.astype(target.dtype)

    def join(index):
        to_chip[index].wait_recv()
        loads[index].wait()
        if index < 3:
            add_into(mine.at[index], lambda at, come: theirs[index, at, :], 0, rows)

    join(0)
    corner_x = copy(4, mine.at[0, first], relayed.at[0], on_x)
    corner_y = copy(5, mine.at[0, second], relayed.at[1], on_y)
    corner_x.start()
    corner_y.start()
    join(1)
    x_first = copy(6, mine.at[1, first], final.at[0, first], on_x)
    x_first.start()
    join(2)
    y_second = copy(7, mine.at[2, second], final.at[1, second], on_y)
    y_second.start()
    corner_y.wait_recv()
    add_into(mine.at[1], lambda at, come: relayed[1, come, :], half, half)
    x_second = copy(8, mine.at[1, second], final.at[0, second], on_x)
    x_second.start()
    corner_x.wait_recv()
    add_into(mine.at[2], lambda at, come: relayed[0, come, :], 0, half)
    y_first = copy(9, mine.at[2, first], final.at[1, first], on_y)
    y_first.start()
    join(3)
    for each in (x_first, y_second, x_second, y_first):
        each.wait_recv()

    @pl.loop(0, rows // step)
    def _(turn):
        at = pl.ds(pl.multiple_of(turn * step, step), step)
        total = mine[3, at, :].astype(jnp.float32) + theirs[3, at, :].astype(jnp.float32)
        total = total + final[0, at, :].astype(jnp.float32) + final[1, at, :].astype(jnp.float32)
        out_ref[at, :] = total.astype(out_ref.dtype)

    for each in to_chip + [corner_x, corner_y, x_first, y_second, x_second, y_first]:
        each.wait_send()


def tok_reduce(parts, call_number, kernels, out_type=jnp.float32):
    if not kernels:
        return lax.psum_scatter(parts, "tok", scatter_dimension=0, tiled=False).astype(out_type)
    _, rows, columns = parts.shape
    kind = parts.dtype
    return pl.pallas_call(
        reduce_kernel,
        out_shape=jax.ShapeDtypeStruct((rows, columns), out_type),
        in_specs=[pl.BlockSpec(memory_space=pl.ANY)],
        out_specs=pl.BlockSpec(memory_space=pltpu.VMEM),
        scratch_shapes=[
            pltpu.VMEM((4, rows, columns), kind),
            pltpu.VMEM((4, rows, columns), kind),
            pltpu.VMEM((2, rows // 2, columns), kind),
            pltpu.VMEM((2, rows, columns), kind),
            pltpu.SemaphoreType.DMA((10,)),
            pltpu.SemaphoreType.DMA((10,)),
            pltpu.SemaphoreType.DMA((4,)),
        ],
        compiler_params=pltpu.CompilerParams(
            collective_id=call_number, has_side_effects=True, vmem_limit_bytes=VMEM_BYTES
        ),
        cost_estimate=pl.CostEstimate(
            flops=0, bytes_accessed=rows * columns * 2 * 100, transcendentals=0
        ),
        name="tok_reduce",
    )(parts)


def peers_of(count):
    here = lax.axis_index("tok")
    return here, [(here + step) % count for step in range(1, count)]


def small_gather_kernel(count, own_ref, out_ref, send_sem, recv_sem, local_sem):
    here, peers = peers_of(count)
    rows = own_ref.shape[1]
    place = pl.ds(pl.multiple_of(here * rows, rows), rows)
    greet(peers)
    own = pltpu.make_async_copy(own_ref, out_ref.at[:, place, :], local_sem)
    copies = [
        pltpu.make_async_remote_copy(
            src_ref=own_ref,
            dst_ref=out_ref.at[:, place, :],
            send_sem=send_sem.at[index],
            recv_sem=recv_sem.at[index],
            device_id={"tok": peers[index]},
            device_id_type=MESH,
        )
        for index in range(count - 1)
    ]
    for each in copies:
        each.start()
    own.start()
    for each in copies:
        each.wait_recv()
    for each in copies:
        each.wait_send()
    own.wait()


def tok_gather_small(own, call_number, kernels):
    if not kernels:
        return lax.all_gather(own, "tok", axis=1, tiled=True)
    count = 8
    prompts, rows, columns = own.shape
    return pl.pallas_call(
        functools.partial(small_gather_kernel, count),
        out_shape=jax.ShapeDtypeStruct((prompts, count * rows, columns), own.dtype),
        in_specs=[pl.BlockSpec(memory_space=pl.ANY)],
        out_specs=pl.BlockSpec(memory_space=pl.ANY),
        scratch_shapes=[
            pltpu.SemaphoreType.DMA((count - 1,)),
            pltpu.SemaphoreType.DMA((count - 1,)),
            pltpu.SemaphoreType.DMA,
        ],
        compiler_params=pltpu.CompilerParams(collective_id=call_number, has_side_effects=True),
        name="tok_gather_small",
    )(own)


def small_reduce_kernel(count, part_ref, out_ref, come, send_sem, recv_sem):
    here, peers = peers_of(count)
    rows = come.shape[2]

    def place(device):
        return pl.ds(pl.multiple_of(device * rows, rows), rows)

    greet(peers)
    copies = [
        pltpu.make_async_remote_copy(
            src_ref=part_ref.at[:, place(peers[index]), :],
            dst_ref=come.at[index],
            send_sem=send_sem.at[index],
            recv_sem=recv_sem.at[index],
            device_id={"tok": peers[index]},
            device_id_type=MESH,
        )
        for index in range(count - 1)
    ]
    for each in copies:
        each.start()
    total = part_ref[:, place(here), :].astype(jnp.float32)
    for index in range(count - 1):
        copies[index].wait_recv()
        total = total + come[index].astype(jnp.float32)
    out_ref[...] = total.astype(out_ref.dtype)
    for each in copies:
        each.wait_send()


def tok_reduce_small(parts, call_number, kernels):
    if not kernels:
        return lax.psum_scatter(parts, "tok", scatter_dimension=1, tiled=True).astype(jnp.float32)
    count = 8
    prompts, rows, columns = parts.shape
    rows = rows // count
    return pl.pallas_call(
        functools.partial(small_reduce_kernel, count),
        out_shape=jax.ShapeDtypeStruct((prompts, rows, columns), jnp.float32),
        in_specs=[pl.BlockSpec(memory_space=pltpu.VMEM)],
        out_specs=pl.BlockSpec(memory_space=pltpu.VMEM),
        scratch_shapes=[
            pltpu.VMEM((count - 1, prompts, rows, columns), parts.dtype),
            pltpu.SemaphoreType.DMA((count - 1,)),
            pltpu.SemaphoreType.DMA((count - 1,)),
        ],
        compiler_params=pltpu.CompilerParams(
            collective_id=call_number, has_side_effects=True, vmem_limit_bytes=VMEM_BYTES
        ),
        name="tok_reduce_small",
    )(parts)


def final_reduce_kernel(
    groups,
    part_ref,
    small_ref,
    out_ref,
    small_out_ref,
    mine,
    theirs,
    relayed,
    final,
    come,
    small_come,
    small_total,
    small_across,
    send_sem,
    recv_sem,
    load_sem,
    across_send,
    across_recv,
    small_send,
    small_recv,
    small_across_send,
    small_across_recv,
):
    rows = part_ref.shape[1] // groups
    half = rows // 2
    small_rows = small_ref.shape[1] // groups
    here, on_x, on_y, on_chip, corner = block_of_eight()
    group = lax.axis_index("grp")
    shift = on_chip - here
    _, peers = peers_of(8)
    other_groups = [(group + turn) % groups for turn in range(1, groups)]
    step = 16

    barrier = pltpu.get_barrier_semaphore()
    for peer in peers:
        pl.semaphore_signal(barrier, inc=1, device_id={"tok": peer}, device_id_type=MESH)
    for other in other_groups:
        pl.semaphore_signal(barrier, inc=1, device_id={"grp": other}, device_id_type=MESH)
    pl.semaphore_wait(barrier, len(peers) + len(other_groups))

    def copy(chunk, index, source, target, device):
        return pltpu.make_async_remote_copy(
            src_ref=source,
            dst_ref=target,
            send_sem=send_sem.at[chunk, index],
            recv_sem=recv_sem.at[chunk, index],
            device_id={"tok": device},
            device_id_type=MESH,
        )

    def add_into(target, other, start, count):
        @pl.loop(0, count // step)
        def _(turn):
            at = pl.ds(pl.multiple_of(start + turn * step, step), step)
            from_here = pl.ds(pl.multiple_of(turn * step, step), step)
            total = target[at, :].astype(jnp.float32) + other[from_here, :].astype(jnp.float32)
            target[at, :] = total.astype(target.dtype)

    places = (corner, on_x, on_y, here)
    first, second = pl.ds(0, half), pl.ds(half, half)
    to_chip, loads, others = [], [], []
    for chunk in range(groups):
        owner = (group + 1 + chunk) % groups
        span = pl.ds(pl.multiple_of(owner * rows, rows), rows)
        to_chip.append(
            [
                copy(
                    chunk,
                    index,
                    part_ref.at[places[index] + shift, span],
                    theirs.at[chunk, index],
                    on_chip,
                )
                for index in range(4)
            ]
        )
        loads.append(
            [
                pltpu.make_async_copy(
                    part_ref.at[places[index], span],
                    mine.at[chunk, index],
                    load_sem.at[chunk, index],
                )
                for index in range(4)
            ]
        )
        own, two = mine.at[chunk], final.at[chunk]
        others.append(
            {
                "corner_x": copy(chunk, 4, own.at[0, first], relayed.at[chunk, 0], on_x),
                "corner_y": copy(chunk, 5, own.at[0, second], relayed.at[chunk, 1], on_y),
                "x_first": copy(chunk, 6, own.at[1, first], two.at[0, first], on_x),
                "y_second": copy(chunk, 7, own.at[2, second], two.at[1, second], on_y),
                "x_second": copy(chunk, 8, own.at[1, second], two.at[0, second], on_x),
                "y_first": copy(chunk, 9, own.at[2, first], two.at[1, first], on_y),
            }
        )
    small_copies = [
        pltpu.make_async_remote_copy(
            src_ref=small_ref.at[peers[index]],
            dst_ref=small_come.at[index],
            send_sem=small_send.at[index],
            recv_sem=small_recv.at[index],
            device_id={"tok": peers[index]},
            device_id_type=MESH,
        )
        for index in range(len(peers))
    ]
    across = [
        pltpu.make_async_remote_copy(
            src_ref=mine.at[chunk, 3],
            dst_ref=come.at[chunk],
            send_sem=across_send.at[chunk],
            recv_sem=across_recv.at[chunk],
            device_id={"grp": other_groups[chunk]},
            device_id_type=MESH,
        )
        for chunk in range(groups - 1)
    ]
    small_over = [
        pltpu.make_async_remote_copy(
            src_ref=small_total.at[other_groups[chunk]],
            dst_ref=small_across.at[chunk],
            send_sem=small_across_send.at[chunk],
            recv_sem=small_across_recv.at[chunk],
            device_id={"grp": other_groups[chunk]},
            device_id_type=MESH,
        )
        for chunk in range(groups - 1)
    ]

    for chunk in range(groups):
        for index in range(4):
            to_chip[chunk][index].start()
            loads[chunk][index].start()
        if chunk == 0:
            for each in small_copies:
                each.start()

    def join(chunk, index):
        to_chip[chunk][index].wait_recv()
        loads[chunk][index].wait()
        add_into(mine.at[chunk, index], theirs.at[chunk, index], 0, rows)

    def open_chunk(chunk):
        join(chunk, 0)
        others[chunk]["corner_x"].start()
        others[chunk]["corner_y"].start()
        join(chunk, 1)
        others[chunk]["x_first"].start()
        join(chunk, 2)
        others[chunk]["y_second"].start()

    def relay_chunk(chunk):
        others[chunk]["corner_y"].wait_recv()
        add_into(mine.at[chunk, 1], relayed.at[chunk, 1], half, half)
        others[chunk]["x_second"].start()
        others[chunk]["corner_x"].wait_recv()
        add_into(mine.at[chunk, 2], relayed.at[chunk, 0], 0, half)
        others[chunk]["y_first"].start()

    def close_chunk(chunk):
        join(chunk, 3)
        for name in ("x_first", "y_second", "x_second", "y_first"):
            others[chunk][name].wait_recv()

        @pl.loop(0, rows // step)
        def _(turn):
            at = pl.ds(pl.multiple_of(turn * step, step), step)
            total = mine[chunk, 3, at, :].astype(jnp.float32)
            total = total + final[chunk, 0, at, :].astype(jnp.float32)
            total = total + final[chunk, 1, at, :].astype(jnp.float32)
            mine[chunk, 3, at, :] = total.astype(mine.dtype)

        if chunk < groups - 1:
            across[chunk].start()

    open_chunk(0)
    for chunk in range(1, groups):
        open_chunk(chunk)
        relay_chunk(chunk - 1)
        if chunk == 1:
            sums = small_ref[here]
            for index in range(len(peers)):
                small_copies[index].wait_recv()
                sums = sums + small_come[index]
            small_total[...] = sums.reshape(small_total.shape)
            for each in small_over:
                each.start()
        if chunk >= 2:
            close_chunk(chunk - 2)
    relay_chunk(groups - 1)
    close_chunk(groups - 2)
    close_chunk(groups - 1)
    for each in across:
        each.wait_recv()

    @pl.loop(0, rows // step)
    def _(turn):
        at = pl.ds(pl.multiple_of(turn * step, step), step)
        total = mine[groups - 1, 3, at, :].astype(jnp.float32)
        for chunk in range(groups - 1):
            total = total + come[chunk, at, :].astype(jnp.float32)
        out_ref[at, :] = total

    small_sum = small_total[group]
    for chunk in range(groups - 1):
        small_over[chunk].wait_recv()
        small_sum = small_sum + small_across[chunk]
    small_out_ref[...] = small_sum
    for chunk in range(groups):
        for each in to_chip[chunk] + list(others[chunk].values()):
            each.wait_send()
    for each in small_copies + across + small_over:
        each.wait_send()


def final_reduce(parts, small_parts, groups, call_number, kernels):
    if not kernels:
        sums = lax.psum_scatter(parts, "tok", scatter_dimension=0, tiled=False)
        sums = lax.psum_scatter(sums, "grp", scatter_dimension=0, tiled=True)
        small_sums = lax.psum_scatter(small_parts, "tok", scatter_dimension=0, tiled=False)
        small_sums = lax.psum_scatter(small_sums, "grp", scatter_dimension=0, tiled=True)
        return sums.astype(jnp.float32), small_sums
    _, rows, columns = parts.shape
    rows = rows // groups
    small_rows, small_columns = small_parts.shape[1] // groups, small_parts.shape[2]
    kind = parts.dtype
    dma = pltpu.SemaphoreType.DMA
    small = (small_rows, small_columns)
    return pl.pallas_call(
        functools.partial(final_reduce_kernel, groups),
        out_shape=(
            jax.ShapeDtypeStruct((rows, columns), jnp.float32),
            jax.ShapeDtypeStruct(small, jnp.float32),
        ),
        in_specs=[
            pl.BlockSpec(memory_space=pl.ANY),
            pl.BlockSpec(memory_space=pltpu.VMEM),
        ],
        out_specs=(
            pl.BlockSpec(memory_space=pltpu.VMEM),
            pl.BlockSpec(memory_space=pltpu.VMEM),
        ),
        scratch_shapes=[
            pltpu.VMEM((groups, 4, rows, columns), kind),
            pltpu.VMEM((groups, 4, rows, columns), kind),
            pltpu.VMEM((groups, 2, rows // 2, columns), kind),
            pltpu.VMEM((groups, 2, rows, columns), kind),
            pltpu.VMEM((groups - 1, rows, columns), kind),
            pltpu.VMEM((7, groups * small_rows, small_columns), jnp.float32),
            pltpu.VMEM((groups,) + small, jnp.float32),
            pltpu.VMEM((groups - 1,) + small, jnp.float32),
            dma((groups, 10)),
            dma((groups, 10)),
            dma((groups, 4)),
            dma((groups - 1,)),
            dma((groups - 1,)),
            dma((7,)),
            dma((7,)),
            dma((groups - 1,)),
            dma((groups - 1,)),
        ],
        compiler_params=pltpu.CompilerParams(
            collective_id=call_number, has_side_effects=True, vmem_limit_bytes=VMEM_BYTES
        ),
        name="final_reduce",
    )(parts, small_parts)


def stack_heads(values, heads):
    return jnp.concatenate(
        [values[:, head * HEAD_WIDTH : (head + 1) * HEAD_WIDTH] for head in range(heads)], axis=0
    )


def unstack_heads(values, heads):
    rows = values.shape[0] // heads
    return jnp.concatenate(
        [values[head * rows : (head + 1) * rows, :] for head in range(heads)], axis=1
    )


def part_rows(part, prompts, answers, token_ref, answer_ref):
    answer_rows = answer_ref.shape[0] // answers
    prompt_rows = (token_ref.shape[0] - answer_ref.shape[0]) // prompts
    if part < prompts:
        return slice(part * prompt_rows, (part + 1) * prompt_rows), prompt_rows
    start = prompts * prompt_rows + (part - prompts) * answer_rows
    return slice(start, start + answer_rows), answer_rows


def as_row(column):
    wide = jnp.broadcast_to(column, (column.shape[0], HEAD_WIDTH))
    return jnp.transpose(wide)[0:1, :]


def attention_forward_kernel(
    prompts,
    answers,
    heads,
    scale,
    place_ref,
    owner_ref,
    normed_ref,
    query_ref,
    bias_ref,
    prompt_kv_ref,
    answer_kv_ref,
    output_ref,
    states_ref,
    offset_ref,
    gain_ref,
    shift_ref,
    queries_ref,
    mixture_ref,
    log_ref,
    hidden_ref,
    second_ref,
):
    step = pl.program_id(0)
    width = HEAD_WIDTH
    length = prompt_kv_ref.shape[1]
    query_block = query_ref[0].reshape(-1, query_ref.shape[-1])
    output_block = output_ref[0].reshape(-1, output_ref.shape[-1])
    queries = (plain_product(normed_ref[...], query_block) + bias_ref[0]).astype(jnp.bfloat16)
    queries_ref[...] = queries

    pieces = []
    for part in range(prompts + answers):
        here, rows = part_rows(part, prompts, answers, normed_ref, answer_kv_ref)
        token = lax.broadcasted_iota(jnp.int32, (heads * rows, 1), 0) % rows
        stacked = stack_heads(queries[here, :], heads)
        if part < prompts:
            keys = prompt_kv_ref[part, :, :width]
            values = prompt_kv_ref[part, :, width:]
            scores = transposed_product(stacked, keys)
            place = lax.broadcasted_iota(jnp.int32, (1, length), 1)
            scores = jnp.where(place <= place_ref[0] + token, scores, masked)
            top = jnp.max(scores, axis=-1, keepdims=True)
            exponent = jnp.exp((scores - top) * scale)
            total = jnp.sum(exponent, axis=-1, keepdims=True)
            mixed = plain_product(exponent.astype(jnp.bfloat16), values)
        else:
            answer = part - prompts
            owner = owner_ref[answer]
            own = slice(answer * rows, (answer + 1) * rows)
            keys = prompt_kv_ref[owner, :, :width]
            values = prompt_kv_ref[owner, :, width:]
            scores = transposed_product(stacked, keys)
            own_scores = transposed_product(stacked, answer_kv_ref[own, :width])
            place = lax.broadcasted_iota(jnp.int32, (1, rows), 1)
            own_scores = jnp.where(place <= token, own_scores, masked)
            top = jnp.maximum(
                jnp.max(scores, axis=-1, keepdims=True),
                jnp.max(own_scores, axis=-1, keepdims=True),
            )
            exponent = jnp.exp((scores - top) * scale)
            own_exponent = jnp.exp((own_scores - top) * scale)
            total = jnp.sum(exponent, axis=-1, keepdims=True) + jnp.sum(
                own_exponent, axis=-1, keepdims=True
            )
            mixed = plain_product(exponent.astype(jnp.bfloat16), values) + plain_product(
                own_exponent.astype(jnp.bfloat16), answer_kv_ref[own, width:]
            )
        pieces.append(unstack_heads((mixed / total).astype(jnp.bfloat16), heads))
        log_row = as_row(top * scale + jnp.log(total))
        for head in range(heads):
            log_ref[0, head : head + 1, here] = log_row[:, head * rows : (head + 1) * rows]
    mixture = jnp.concatenate(pieces, axis=0)
    mixture_ref[...] = mixture

    @pl.when(step == 0)
    def _():
        hidden_ref[...] = states_ref[...].astype(jnp.float32) + offset_ref[...]

    hidden_ref[...] += transposed_product(mixture, output_block)

    @pl.when(step == pl.num_programs(0) - 1)
    def _():
        scaled, _ = norm_stats(hidden_ref[...])
        second_ref[...] = (scaled * gain_ref[...] + shift_ref[...]).astype(jnp.bfloat16)


def attention_forward(
    place,
    owning,
    normed,
    packed,
    weight_rows,
    query_offset,
    prompt_kv,
    answer_kv,
    states,
    output_offset,
    gain,
    shift,
    prompts,
    answers,
):
    token_rows, model_width = normed.shape
    steps, groups, _, block = packed.shape
    heads = block // HEAD_WIDTH
    length = prompt_kv.shape[1]
    whole = lambda *shape: pl.BlockSpec(shape, lambda step, *_: (0,) * len(shape))
    scores = heads * token_rows * length
    return pl.pallas_call(
        functools.partial(
            attention_forward_kernel, prompts, answers, heads, HEAD_WIDTH ** (-0.5)
        ),
        out_shape=(
            jax.ShapeDtypeStruct((token_rows, model_width), jnp.bfloat16),
            jax.ShapeDtypeStruct((token_rows, model_width), jnp.bfloat16),
            jax.ShapeDtypeStruct((steps, heads, token_rows), jnp.float32),
            jax.ShapeDtypeStruct((token_rows, model_width), jnp.float32),
            jax.ShapeDtypeStruct((token_rows, model_width), jnp.bfloat16),
        ),
        grid_spec=pltpu.PrefetchScalarGridSpec(
            num_scalar_prefetch=2,
            grid=(steps,),
            in_specs=[
                whole(token_rows, model_width),
                pl.BlockSpec(
                    (1, groups, weight_rows, block), lambda step, *_: (step, 0, 0, 0)
                ),
                pl.BlockSpec((1, 1, block), lambda step, *_: (step, 0, 0)),
                whole(*prompt_kv.shape),
                whole(*answer_kv.shape),
                pl.BlockSpec(
                    (1, groups, weight_rows, block), lambda step, *_: (step, 0, 1, 0)
                ),
                whole(token_rows, model_width),
                whole(1, model_width),
                whole(1, model_width),
                whole(1, model_width),
            ],
            out_specs=(
                pl.BlockSpec((token_rows, block), lambda step, *_: (0, step)),
                pl.BlockSpec((token_rows, block), lambda step, *_: (0, step)),
                pl.BlockSpec((1, heads, token_rows), lambda step, *_: (step, 0, 0)),
                whole(token_rows, model_width),
                whole(token_rows, model_width),
            ),
        ),
        compiler_params=pltpu.CompilerParams(vmem_limit_bytes=VMEM_BYTES),
        cost_estimate=pl.CostEstimate(
            flops=steps * (4 * token_rows * model_width * block + 8 * scores * HEAD_WIDTH),
            bytes_accessed=8 * steps * model_width * block,
            transcendentals=steps * scores,
        ),
        name="attention_forward",
    )(
        place,
        owning,
        normed,
        packed,
        query_offset.reshape(steps, 1, block),
        prompt_kv,
        answer_kv,
        packed,
        states,
        output_offset.reshape(1, -1),
        gain.reshape(1, -1),
        shift.reshape(1, -1),
    )


def attention_backward_kernel(
    prompts,
    answers,
    heads,
    scale,
    place_ref,
    owner_ref,
    normed_ref,
    query_ref,
    prompt_kv_ref,
    answer_kv_ref,
    output_ref,
    branch_ref,
    queries_ref,
    mixture_ref,
    log_ref,
    grad_weights_ref,
    grad_normed_ref,
    grad_prompt_ref,
    grad_answer_ref,
    grad_bias_ref,
    normed_across,
    branch_across,
    key_sums,
    own_sums,
):
    step = pl.program_id(0)
    width = HEAD_WIDTH
    length = prompt_kv_ref.shape[1]
    block = queries_ref.shape[1]

    @pl.when(step == 0)
    def _():
        normed_across[...] = jnp.transpose(normed_ref[...])
        branch_across[...] = jnp.transpose(branch_ref[...])
        key_sums[...] = jnp.zeros_like(key_sums)
        own_sums[...] = jnp.zeros_like(own_sums)
        grad_normed_ref[...] = jnp.zeros_like(grad_normed_ref)

    query_block = query_ref[0].reshape(-1, block)
    output_block = output_ref[0].reshape(-1, block)
    weight_shape = query_ref.shape[1:]
    weight_rows = weight_shape[1]
    grad_weights_ref[0, :, weight_rows : 2 * weight_rows] = (
        plain_product(branch_across[...], mixture_ref[...])
        .astype(jnp.bfloat16)
        .reshape(weight_shape)
    )
    grad_mixture = plain_product(branch_ref[...], output_block).astype(jnp.bfloat16)
    queries = queries_ref[...]
    mixture = mixture_ref[...]

    def backward(keys, values, stacked, grad_stacked, log_row, inner_row, allowed):
        scores = transposed_product(keys, stacked)
        probs = jnp.exp(scores * scale - log_row)
        if allowed is not None:
            probs = jnp.where(allowed, probs, 0.0)
        grad_values = plain_product(probs.astype(jnp.bfloat16), grad_stacked)
        grad_probs = transposed_product(values, grad_stacked)
        grad_scores = (probs * (grad_probs - inner_row)).astype(jnp.bfloat16)
        grad_keys = plain_product(grad_scores, stacked)
        grad_queries = weight_product(grad_scores, keys)
        return grad_queries, grad_keys, grad_values

    pieces = []
    for part in range(prompts + answers):
        here, rows = part_rows(part, prompts, answers, normed_ref, answer_kv_ref)
        token = lax.broadcasted_iota(jnp.int32, (1, heads * rows), 1) % rows
        stacked = stack_heads(queries[here, :], heads)
        grad_stacked = stack_heads(grad_mixture[here, :], heads)
        mixed = stack_heads(mixture[here, :], heads)
        product = grad_stacked.astype(jnp.float32) * mixed.astype(jnp.float32)
        inner_row = jnp.sum(jnp.transpose(product), axis=0, keepdims=True)
        log_row = jnp.concatenate(
            [log_ref[0, head : head + 1, here] for head in range(heads)], axis=1
        )
        if part < prompts:
            place = lax.broadcasted_iota(jnp.int32, (length, 1), 0)
            grad_queries, grad_keys, grad_values = backward(
                prompt_kv_ref[part, :, :width],
                prompt_kv_ref[part, :, width:],
                stacked,
                grad_stacked,
                log_row,
                inner_row,
                place <= place_ref[0] + token,
            )
            key_sums[part, :, :width] += grad_keys
            key_sums[part, :, width:] += grad_values
        else:
            answer = part - prompts
            owner = owner_ref[answer]
            own = slice(answer * rows, (answer + 1) * rows)
            grad_queries, grad_keys, grad_values = backward(
                prompt_kv_ref[owner, :, :width],
                prompt_kv_ref[owner, :, width:],
                stacked,
                grad_stacked,
                log_row,
                inner_row,
                None,
            )
            key_sums[owner, :, :width] += grad_keys
            key_sums[owner, :, width:] += grad_values
            place = lax.broadcasted_iota(jnp.int32, (rows, 1), 0)
            own_queries, own_keys, own_values = backward(
                answer_kv_ref[own, :width],
                answer_kv_ref[own, width:],
                stacked,
                grad_stacked,
                log_row,
                inner_row,
                place <= token,
            )
            grad_queries = grad_queries + own_queries
            own_sums[own, :width] += own_keys
            own_sums[own, width:] += own_values
        pieces.append(unstack_heads((grad_queries * scale).astype(jnp.bfloat16), heads))
    grad_queries = jnp.concatenate(pieces, axis=0)
    grad_weights_ref[0, :, :weight_rows] = (
        plain_product(normed_across[...], grad_queries).astype(jnp.bfloat16).reshape(weight_shape)
    )
    grad_normed_ref[...] += transposed_product(grad_queries, query_block)
    grad_bias_ref[0] = jnp.sum(grad_queries.astype(jnp.float32), axis=0, keepdims=True)

    @pl.when(step == pl.num_programs(0) - 1)
    def _():
        grad_prompt_ref[:, :, :width] = (key_sums[:, :, :width] * scale).astype(jnp.bfloat16)
        grad_prompt_ref[:, :, width:] = key_sums[:, :, width:].astype(jnp.bfloat16)
        grad_answer_ref[:, :width] = own_sums[:, :width] * scale
        grad_answer_ref[:, width:] = own_sums[:, width:]


def attention_backward(
    place,
    owning,
    normed,
    packed,
    weight_rows,
    grad_rows,
    prompt_kv,
    answer_kv,
    branch,
    queries,
    mixture,
    log_total,
    prompts,
    answers,
):
    token_rows, model_width = normed.shape
    steps, groups, _, block = packed.shape
    heads = block // HEAD_WIDTH
    length = prompt_kv.shape[1]
    whole = lambda *shape: pl.BlockSpec(shape, lambda step, *_: (0,) * len(shape))
    columns = lambda: pl.BlockSpec((token_rows, block), lambda step, *_: (0, step))
    scores = heads * token_rows * length
    return pl.pallas_call(
        functools.partial(
            attention_backward_kernel, prompts, answers, heads, HEAD_WIDTH ** (-0.5)
        ),
        out_shape=(
            jax.ShapeDtypeStruct((steps, groups, grad_rows, block), jnp.bfloat16),
            jax.ShapeDtypeStruct((token_rows, model_width), jnp.float32),
            jax.ShapeDtypeStruct(prompt_kv.shape, jnp.bfloat16),
            jax.ShapeDtypeStruct(answer_kv.shape, jnp.float32),
            jax.ShapeDtypeStruct((steps, 1, block), jnp.float32),
        ),
        grid_spec=pltpu.PrefetchScalarGridSpec(
            num_scalar_prefetch=2,
            grid=(steps,),
            in_specs=[
                whole(token_rows, model_width),
                pl.BlockSpec(
                    (1, groups, weight_rows, block), lambda step, *_: (step, 0, 0, 0)
                ),
                whole(*prompt_kv.shape),
                whole(*answer_kv.shape),
                pl.BlockSpec(
                    (1, groups, weight_rows, block), lambda step, *_: (step, 0, 1, 0)
                ),
                whole(token_rows, model_width),
                columns(),
                columns(),
                pl.BlockSpec((1, heads, token_rows), lambda step, *_: (step, 0, 0)),
            ],
            out_specs=(
                pl.BlockSpec(
                    (1, groups, grad_rows, block), lambda step, *_: (step, 0, 0, 0)
                ),
                whole(token_rows, model_width),
                whole(*prompt_kv.shape),
                whole(*answer_kv.shape),
                pl.BlockSpec((1, 1, block), lambda step, *_: (step, 0, 0)),
            ),
            scratch_shapes=[
                pltpu.VMEM((model_width, token_rows), jnp.bfloat16),
                pltpu.VMEM((model_width, token_rows), jnp.bfloat16),
                pltpu.VMEM(prompt_kv.shape, jnp.float32),
                pltpu.VMEM(answer_kv.shape, jnp.float32),
            ],
        ),
        compiler_params=pltpu.CompilerParams(vmem_limit_bytes=VMEM_BYTES),
        cost_estimate=pl.CostEstimate(
            flops=steps * (8 * token_rows * model_width * block + 20 * scores * HEAD_WIDTH),
            bytes_accessed=16 * steps * model_width * block,
            transcendentals=steps * scores,
        ),
        name="attention_backward",
    )(
        place,
        owning,
        normed,
        packed,
        prompt_kv,
        answer_kv,
        packed,
        branch,
        queries,
        mixture,
        log_total,
    )


def by_group(values):
    return jnp.swapaxes(values, 0, 1).reshape(-1)


def body(
    kernels,
    prompt_states,
    answer_states,
    answer_prompt,
    prompt_teacher,
    answer_teacher,
    prompt_valid,
    answer_valid,
    first_gain,
    first_shift,
    query_weight,
    query_bias,
    keyval_weight,
    value_bias,
    output_weight,
    output_bias,
    second_gain,
    second_shift,
    up_weight,
    up_bias,
    down_weight,
    down_bias,
):
    prompt_count, prompt_rows, model_width = prompt_states.shape
    answer_count, answer_len, _ = answer_states.shape
    groups = lax.axis_size("grp")
    token_devices = lax.axis_size("tok")
    token_index = lax.axis_index("tok")
    group_index = lax.axis_index("grp")
    own_prompt = prompt_rows * prompt_count
    token_rows = own_prompt + answer_count * answer_len
    hidden_units = up_bias.shape[0] * groups * token_devices
    ff_here = hidden_units // token_devices
    ff_start = token_index * ff_here
    share = first_gain.shape[0]
    block = query_weight.shape[1]
    weight_rows = query_weight.shape[0]
    keyval_rows, keyval_width = keyval_weight.shape

    def own_rows(prompt_part, answer_part):
        return jnp.concatenate(
            [prompt_part.reshape(own_prompt, -1), answer_part.reshape(-1, prompt_part.shape[-1])],
            axis=0,
        )

    states = own_rows(prompt_states, answer_states)
    inputs = states.astype(jnp.float32)
    valid_rows = jnp.concatenate([prompt_valid.reshape(-1), answer_valid.reshape(-1)])
    own_count = jnp.sum(valid_rows)
    valid_rows = valid_rows.astype(jnp.float32)

    up_cols = lax.all_gather(up_weight, "grp", axis=0, tiled=True)
    down_cols = lax.all_gather(down_weight, "grp", axis=0, tiled=True)

    count_parts = jnp.stack([own_count // 128, own_count % 128]).astype(jnp.bfloat16)
    smalls = jnp.concatenate(
        [
            first_gain,
            first_shift,
            query_bias,
            output_bias,
            second_gain,
            second_shift,
            down_bias,
            up_bias,
            count_parts,
        ]
    )
    smalls = jnp.pad(smalls, (0, SMALL_ROWS * block - smalls.shape[0])).reshape(SMALL_ROWS, block)
    pack = jnp.concatenate(
        [query_weight, output_weight, keyval_weight.reshape(-1, block), smalls], axis=0
    )
    pack_rows = pack.shape[0]
    packed = lax.all_gather(pack, "grp", axis=0, tiled=True)
    packed = tok_gather(packed, 0, kernels).reshape(token_devices, groups, pack_rows, block)
    keyval_start = 2 * weight_rows
    keyval_end = pack_rows - SMALL_ROWS
    keyval_full = jnp.swapaxes(
        packed[:, :, keyval_start:keyval_end].reshape(
            token_devices, groups, keyval_rows, keyval_width
        ),
        0,
        1,
    ).reshape(model_width, keyval_width)
    small_full = packed[:, :, keyval_end:].reshape(token_devices, groups, SMALL_ROWS * block)
    small_full = jnp.swapaxes(small_full.astype(jnp.float32), 0, 1)

    def vector(start, size):
        return small_full[:, :, start : start + size].reshape(-1)

    gain_one, shift_one, query_offset, output_offset, gain_two, shift_two, down_offset = (
        vector(index * share, share) for index in range(7)
    )
    up_offset = vector(7 * share, up_bias.shape[0])
    count_at = 7 * share + up_bias.shape[0]
    counts = small_full[:, :, count_at : count_at + 2]
    valid_count = jnp.sum(counts[:, :, 0]) * 128.0 + jnp.sum(counts[:, :, 1])
    up_here = lax.dynamic_slice_in_dim(up_offset, ff_start, ff_here)

    scaled_one, inverse_one = norm_stats(inputs)
    normed_one = (scaled_one * gain_one + shift_one).astype(jnp.bfloat16)
    key_offset = jnp.concatenate(
        [jnp.zeros((HEAD_WIDTH,), jnp.float32), value_bias.astype(jnp.float32)]
    )
    key_value_rows = (plain_product(normed_one, keyval_full) + key_offset).astype(jnp.bfloat16)
    prompt_kv = tok_gather_small(
        key_value_rows[:own_prompt].reshape(prompt_count, prompt_rows, -1), 1, kernels
    )
    answer_kv = key_value_rows[own_prompt:]
    owning = answer_prompt - group_index * prompt_count
    owning = lax.dynamic_slice_in_dim(owning, token_index * answer_count, answer_count)
    place = jnp.reshape(token_index * prompt_rows, (1,)).astype(jnp.int32)
    queries, mixture, log_total, hidden, normed_two = attention_forward(
        place,
        owning,
        normed_one,
        packed,
        weight_rows,
        query_offset,
        prompt_kv,
        answer_kv,
        states,
        output_offset,
        gain_two,
        shift_two,
        prompt_count,
        answer_count,
    )

    group_two = tok_gather(normed_two, 2, kernels).reshape(-1, model_width)
    pre_active = plain_product(group_two, up_cols) + up_here
    activated = jax.nn.gelu(pre_active, approximate=True).astype(jnp.bfloat16)
    feed_term = for_sending(transposed_product(activated, down_cols))
    feed_term = tok_reduce(feed_term.reshape(token_devices, token_rows, model_width), 3, kernels)
    result_rows = hidden + feed_term + down_offset

    teacher = own_rows(prompt_teacher, answer_teacher).astype(jnp.float32)
    differ = result_rows - teacher
    own_squares = jnp.sum(valid_rows[:, None] * differ * differ)
    every_token = token_rows * groups * token_devices
    grad_result = every_token / valid_count * valid_rows[:, None] * differ
    grad_branch_two = grad_result.astype(jnp.bfloat16)

    group_grad_two = tok_gather(grad_branch_two, 4, kernels).reshape(-1, model_width)
    grad_activated = plain_product(group_grad_two, down_cols)
    _, gelu_back = jax.vjp(lambda argument: jax.nn.gelu(argument, approximate=True), pre_active)
    grad_pre_active = gelu_back(grad_activated)[0].astype(jnp.bfloat16)
    grad_normed_two = for_sending(transposed_product(grad_pre_active, up_cols))
    grad_down_cols = for_sending(weight_product(group_grad_two, activated))
    grad_up_cols = for_sending(weight_product(group_two, grad_pre_active))
    grad_normed_two, grad_down_cols, grad_up_cols = lax.optimization_barrier(
        (grad_normed_two, grad_down_cols, grad_up_cols)
    )
    grad_down_weight = lax.psum_scatter(grad_down_cols, "grp", scatter_dimension=0, tiled=True)
    grad_up_weight = lax.psum_scatter(grad_up_cols, "grp", scatter_dimension=0, tiled=True)
    grad_normed_two = tok_reduce(
        grad_normed_two.reshape(token_devices, token_rows, model_width), 5, kernels
    )
    grad_down_offset = column_sums(grad_branch_two)
    grad_up_offset = column_sums(grad_pre_active)
    scaled_two, inverse_two = norm_stats(hidden)
    grad_norm_two, grad_gain_two, grad_shift_two = norm_backward(
        grad_normed_two, gain_two, scaled_two, inverse_two
    )
    grad_hidden = grad_result + grad_norm_two
    grad_branch_one = grad_hidden.astype(jnp.bfloat16)
    grad_output_offset = column_sums(grad_branch_one)

    grad_rows = keyval_end
    grad_weights, grad_normed_one, grad_prompt_kv, grad_answer_kv, grad_query_offset = (
        attention_backward(
            place,
            owning,
            normed_one,
            packed,
            weight_rows,
            grad_rows,
            prompt_kv,
            answer_kv,
            grad_branch_one,
            queries,
            mixture,
            log_total,
            prompt_count,
            answer_count,
        )
    )
    grad_prompt_kv = tok_reduce_small(grad_prompt_kv, 6, kernels)
    grad_keyvals = jnp.concatenate(
        [grad_prompt_kv.reshape(own_prompt, -1), grad_answer_kv], axis=0
    ).astype(jnp.bfloat16)
    grad_keyval_full = weight_product(normed_one, grad_keyvals)
    grad_value_offset = column_sums(grad_keyvals[:, HEAD_WIDTH:])
    grad_normed_one = grad_normed_one + transposed_product(grad_keyvals, keyval_full)
    grad_norm_one, grad_gain_one, grad_shift_one = norm_backward(
        grad_normed_one, gain_one, scaled_one, inverse_one
    )
    grad_inputs = grad_hidden + grad_norm_one

    grad_keyval_blocks = jnp.swapaxes(
        grad_keyval_full.astype(jnp.bfloat16).reshape(groups, token_devices, -1, block), 0, 1
    )
    grad_weights = lax.dynamic_update_slice(
        grad_weights, grad_keyval_blocks, (0, 0, keyval_start, 0)
    )
    vectors = (
        grad_gain_one,
        grad_shift_one,
        grad_query_offset.reshape(-1),
        grad_output_offset,
        grad_gain_two,
        grad_shift_two,
        grad_down_offset,
        lax.dynamic_update_slice_in_dim(
            jnp.zeros((hidden_units,), jnp.float32), grad_up_offset, ff_start, 0
        ),
    )
    totals = jnp.concatenate([grad_value_offset, own_squares.reshape(1)])
    blocks = jnp.concatenate(
        [each.reshape(groups, token_devices, -1) for each in vectors]
        + [jnp.broadcast_to(totals, (groups, token_devices, totals.shape[0]))],
        axis=2,
    )
    blocks = jnp.pad(blocks, ((0, 0), (0, 0), (0, SMALL_SUMS - blocks.shape[2])))
    blocks = jnp.swapaxes(blocks, 0, 1).reshape(token_devices, -1, HEAD_WIDTH)
    grad_weights, small_sums = final_reduce(
        grad_weights.reshape(token_devices, -1, block), blocks, groups, 7, kernels
    )
    small_sums = small_sums.reshape(-1)
    up_share = up_bias.shape[0]
    totals_at = 7 * share + up_share
    value_total = small_sums[totals_at : totals_at + HEAD_WIDTH]
    squared_sum = small_sums[totals_at + HEAD_WIDTH]
    loss_value = squared_sum / (valid_count * model_width)

    def split_rows(values):
        values = values.astype(jnp.bfloat16)
        return (
            values[:own_prompt].reshape(prompt_states.shape),
            values[own_prompt:].reshape(answer_states.shape),
        )

    prompt_out, answer_out = split_rows(result_rows)
    prompt_grad, answer_grad = split_rows(grad_inputs)
    pieces = [small_sums[index * share : (index + 1) * share] for index in range(7)]
    return (
        prompt_out,
        answer_out,
        prompt_grad,
        answer_grad,
        pieces[0],
        pieces[1],
        grad_weights[:weight_rows],
        pieces[2],
        grad_weights[keyval_start:].reshape(keyval_rows, keyval_width),
        value_total,
        grad_weights[weight_rows:keyval_start],
        pieces[3],
        pieces[4],
        pieces[5],
        grad_up_weight.astype(jnp.float32),
        small_sums[7 * share : totals_at],
        grad_down_weight.astype(jnp.float32),
        pieces[6],
        loss_value,
    )


def solution(mesh):
    rows = P(("grp", "tok"))
    table = P(("grp", "tok"), None)
    matrix = P("grp", "tok")
    prompt_part = P("grp", "tok", None)
    answer_part = P(("grp", "tok"), None, None)
    in_specs = (
        prompt_part,
        answer_part,
        P("grp"),
        prompt_part,
        answer_part,
        P("grp", "tok"),
        table,
        rows,
        rows,
        matrix,
        rows,
        table,
        P(),
        matrix,
        rows,
        rows,
        rows,
        matrix,
        rows,
        matrix,
        rows,
    )
    out_specs = (
        prompt_part,
        answer_part,
        prompt_part,
        answer_part,
        rows,
        rows,
        matrix,
        rows,
        table,
        P(),
        matrix,
        rows,
        rows,
        rows,
        matrix,
        rows,
        matrix,
        rows,
        P(),
    )
    kernels = mesh.shape["tok"] == 8
    return jax.shard_map(
        functools.partial(body, kernels),
        mesh=mesh,
        in_specs=in_specs,
        out_specs=out_specs,
        check_vma=False,
    )
```

```python
import functools

import jax
import jax.numpy as jnp
from jax import lax
from jax.experimental import pallas as pl
from jax.experimental.pallas import tpu as pltpu
from jax.sharding import PartitionSpec as P

HEAD_WIDTH = 128
epsilon = 1e-05
masked = -1e30
MESH = pl.DeviceIdType.MESH
VMEM_BYTES = 56 * 1024 * 1024
SMALL_ROWS = 16
SMALL_SUMS = 1024


def for_sending(value):
    return value.astype(jnp.bfloat16)


def plain_product(left, right):
    return jnp.dot(left, right, preferred_element_type=jnp.float32)


def transposed_product(left, right):
    return lax.dot_general(
        left, right, (((1,), (1,)), ((), ())), preferred_element_type=jnp.float32
    )


def weight_product(left, right):
    return lax.dot_general(
        left, right, (((0,), (0,)), ((), ())), preferred_element_type=jnp.float32
    )


def norm_stats(values):
    center = values - jnp.mean(values, axis=-1, keepdims=True)
    inverse = lax.rsqrt(jnp.mean(center * center, axis=-1, keepdims=True) + epsilon)
    return center * inverse, inverse


def norm_backward(grad_out, gain, scaled, inverse):
    weighted = grad_out * gain
    grad_in = inverse * (
        weighted
        - jnp.mean(weighted, axis=-1, keepdims=True)
        - scaled * jnp.mean(weighted * scaled, axis=-1, keepdims=True)
    )
    return (grad_in, jnp.sum(grad_out * scaled, axis=0), jnp.sum(grad_out, axis=0))


def column_sums(values):
    return jnp.sum(values.astype(jnp.float32), axis=0)


def block_of_eight():
    here = lax.axis_index("tok")
    core, across, along = here % 2, (here // 2) % 2, here // 4
    on_x = here + 2 - 4 * across
    on_y = here + 4 - 8 * along
    on_chip = here + 1 - 2 * core
    corner = on_x + 4 - 8 * along
    return here, on_x, on_y, on_chip, corner


def greet(devices):
    barrier = pltpu.get_barrier_semaphore()
    for device in devices:
        pl.semaphore_signal(barrier, inc=1, device_id={"tok": device}, device_id_type=MESH)
    pl.semaphore_wait(barrier, len(devices))


def gather_kernel(own_ref, out_ref, send_sem, recv_sem, local_sem):
    half = own_ref.shape[0] // 2
    here, on_x, on_y, on_chip, corner = block_of_eight()
    first, second = pl.ds(0, half), pl.ds(half, half)

    def copy(index, source, target, device):
        return pltpu.make_async_remote_copy(
            src_ref=source,
            dst_ref=target,
            send_sem=send_sem.at[index],
            recv_sem=recv_sem.at[index],
            device_id={"tok": device},
            device_id_type=MESH,
        )

    greet((on_x, on_y, on_chip))
    own = pltpu.make_async_copy(own_ref, out_ref.at[here], local_sem)
    copies = [
        copy(0, own_ref, out_ref.at[here], on_x),
        copy(1, own_ref, out_ref.at[here], on_y),
        copy(2, own_ref, out_ref.at[here], on_chip),
        copy(3, out_ref.at[on_x, first], out_ref.at[on_x, first], on_y),
        copy(4, out_ref.at[on_x], out_ref.at[on_x], on_chip),
        copy(5, out_ref.at[on_y, second], out_ref.at[on_y, second], on_x),
        copy(6, out_ref.at[on_y], out_ref.at[on_y], on_chip),
        copy(7, out_ref.at[corner, first], out_ref.at[corner, first], on_chip),
        copy(8, out_ref.at[corner, second], out_ref.at[corner, second], on_chip),
    ]
    for index in range(3):
        copies[index].start()
    own.start()
    copies[0].wait_recv()
    copies[3].start()
    copies[4].start()
    copies[1].wait_recv()
    copies[5].start()
    copies[6].start()
    copies[3].wait_recv()
    copies[7].start()
    copies[5].wait_recv()
    copies[8].start()
    for index in (2, 4, 6, 7, 8):
        copies[index].wait_recv()
    for each in copies:
        each.wait_send()
    own.wait()


def tok_gather(own, call_number, kernels):
    if not kernels:
        return lax.all_gather(own, "tok", axis=0)
    return pl.pallas_call(
        gather_kernel,
        out_shape=jax.ShapeDtypeStruct((8,) + own.shape, own.dtype),
        in_specs=[pl.BlockSpec(memory_space=pl.ANY)],
        out_specs=pl.BlockSpec(memory_space=pl.ANY),
        scratch_shapes=[
            pltpu.SemaphoreType.DMA((9,)),
            pltpu.SemaphoreType.DMA((9,)),
            pltpu.SemaphoreType.DMA,
        ],
        compiler_params=pltpu.CompilerParams(collective_id=call_number, has_side_effects=True),
        cost_estimate=pl.CostEstimate(
            flops=0, bytes_accessed=own.size * 2 * 100, transcendentals=0
        ),
        name="tok_gather",
    )(own)


def remote(index, source, target, device, send_sem, recv_sem):
    return pltpu.make_async_remote_copy(
        src_ref=source,
        dst_ref=target,
        send_sem=send_sem.at[index],
        recv_sem=recv_sem.at[index],
        device_id={"tok": device},
        device_id_type=MESH,
    )


def chunk_of(index, size):
    return pl.ds(pl.multiple_of(index * size, size), size)


CHUNK = 256
LINEAR = 0.7978845608
CUBIC = 0.044715


def gather_beside(own_ref, out_ref, send_sem, recv_sem, local_sem, use):
    half = own_ref.shape[0] // 2
    here, on_x, on_y, on_chip, corner = block_of_eight()
    shift = on_chip - here
    first, second = pl.ds(0, half), pl.ds(half, half)

    def copy(index, source, target, device):
        return remote(index, source, target, device, send_sem, recv_sem)

    greet((on_x, on_y, on_chip))
    own = pltpu.make_async_copy(own_ref, out_ref.at[here], local_sem)
    copies = [
        copy(0, own_ref, out_ref.at[here], on_x),
        copy(1, own_ref, out_ref.at[here], on_y),
        copy(2, own_ref, out_ref.at[here], on_chip),
        copy(3, out_ref.at[on_x, first], out_ref.at[on_x, first], on_y),
        copy(4, out_ref.at[on_x], out_ref.at[on_x], on_chip),
        copy(5, out_ref.at[on_y, second], out_ref.at[on_y, second], on_x),
        copy(6, out_ref.at[on_y], out_ref.at[on_y], on_chip),
        copy(7, out_ref.at[corner, first], out_ref.at[corner, first], on_chip),
        copy(8, out_ref.at[corner, second], out_ref.at[corner, second], on_chip),
    ]
    for index in range(3):
        copies[index].start()
    own.start()
    use(0, here)
    copies[2].wait_recv()
    use(1, on_chip)
    copies[0].wait_recv()
    copies[3].start()
    copies[4].start()
    copies[1].wait_recv()
    copies[5].start()
    copies[6].start()
    use(2, on_x)
    use(3, on_y)
    copies[4].wait_recv()
    use(4, on_x + shift)
    copies[6].wait_recv()
    use(5, on_y + shift)
    copies[3].wait_recv()
    copies[7].start()
    copies[5].wait_recv()
    copies[8].start()
    use(6, corner)
    copies[7].wait_recv()
    copies[8].wait_recv()
    use(7, corner + shift)
    own.wait()
    for each in copies:
        each.wait_send()


def up_kernel(
    own_ref,
    up_hbm,
    bias_ref,
    rows_ref,
    active_ref,
    slope_ref,
    up,
    rows,
    active,
    slope,
    send_sem,
    recv_sem,
    local_sem,
    weight_sem,
    row_sem,
    store_sem,
):
    weights = pltpu.make_async_copy(up_hbm, up, weight_sem)
    weights.start()
    stores = {}

    def use(place, block):
        slot = place % 2
        load = pltpu.make_async_copy(
            rows_ref.at[block] if place else own_ref, rows, row_sem
        )
        load.start()
        if place == 0:
            weights.wait()
        for each in stores.pop(slot, ()):
            each.wait()
        load.wait()

        @pl.loop(0, up.shape[1] // CHUNK)
        def _(turn):
            at = chunk_of(turn, CHUNK)
            value = plain_product(rows[...], up[:, at]) + bias_ref[:, at]
            square = value * value
            bent = jnp.tanh(value * (LINEAR + (LINEAR * CUBIC) * square))
            level = 0.5 + 0.5 * bent
            active[slot, :, at] = (value * level).astype(jnp.bfloat16)
            slope[slot, :, at] = (
                level
                + (0.5 * value)
                * (1.0 - bent * bent)
                * (LINEAR + (3.0 * LINEAR * CUBIC) * square)
            ).astype(jnp.bfloat16)

        stores[slot] = (
            pltpu.make_async_copy(active.at[slot], active_ref.at[block], store_sem.at[slot, 0]),
            pltpu.make_async_copy(slope.at[slot], slope_ref.at[block], store_sem.at[slot, 1]),
        )
        for each in stores[slot]:
            each.start()

    gather_beside(own_ref, rows_ref, send_sem, recv_sem, local_sem, use)
    for slot in (0, 1):
        for each in stores[slot]:
            each.wait()


def gather_and_up(own, up_cols, bias, call_number):
    token_rows, model_width = own.shape
    width = up_cols.shape[1]
    hidden = jax.ShapeDtypeStruct((8, token_rows, width), jnp.bfloat16)
    anywhere = pl.BlockSpec(memory_space=pl.ANY)
    dma = pltpu.SemaphoreType.DMA
    return pl.pallas_call(
        up_kernel,
        out_shape=(
            jax.ShapeDtypeStruct((8, token_rows, model_width), jnp.bfloat16),
            hidden,
            hidden,
        ),
        in_specs=[anywhere, anywhere, pl.BlockSpec(memory_space=pltpu.VMEM)],
        out_specs=(anywhere, anywhere, anywhere),
        scratch_shapes=[
            pltpu.VMEM(up_cols.shape, jnp.bfloat16),
            pltpu.VMEM((token_rows, model_width), jnp.bfloat16),
            pltpu.VMEM((2, token_rows, width), jnp.bfloat16),
            pltpu.VMEM((2, token_rows, width), jnp.bfloat16),
            dma((9,)),
            dma((9,)),
            dma,
            dma,
            dma,
            dma((2, 2)),
        ],
        compiler_params=pltpu.CompilerParams(
            collective_id=call_number, has_side_effects=True, vmem_limit_bytes=VMEM_BYTES
        ),
        cost_estimate=pl.CostEstimate(
            flops=16 * token_rows * model_width * width,
            bytes_accessed=150 * 1000 * 1000,
            transcendentals=0,
        ),
        name="gather_and_up",
    )(own, up_cols, bias.reshape(1, -1))


def grad_kernel(
    own_ref,
    down_hbm,
    active_ref,
    slope_ref,
    rows_ref,
    grad_ref,
    weight_ref,
    bias_ref,
    down,
    rows,
    across,
    active,
    slope,
    grads,
    sums,
    narrow,
    send_sem,
    recv_sem,
    local_sem,
    weight_sem,
    row_sem,
    load_sem,
    store_sem,
):
    weights = pltpu.make_async_copy(down_hbm, down, weight_sem)
    weights.start()
    stores = {}

    def use(place, block):
        slot = place % 2
        load = pltpu.make_async_copy(
            rows_ref.at[block] if place else own_ref, rows, row_sem
        )
        load.start()
        loads = (
            pltpu.make_async_copy(active_ref.at[block], active, load_sem.at[0]),
            pltpu.make_async_copy(slope_ref.at[block], slope, load_sem.at[1]),
        )
        for each in loads:
            each.start()
        if place == 0:
            weights.wait()
        if slot in stores:
            stores.pop(slot).wait()
        load.wait()
        for each in loads:
            each.wait()
        across[...] = jnp.transpose(rows[...])

        @pl.loop(0, down.shape[1] // CHUNK)
        def _(turn):
            at = chunk_of(turn, CHUNK)
            value = plain_product(rows[...], down[:, at]) * slope[:, at].astype(jnp.float32)
            value = value.astype(jnp.bfloat16)
            grads[slot, :, at] = value
            total = jnp.sum(value.astype(jnp.float32), axis=0, keepdims=True)
            weight = plain_product(across[...], active[:, at])
            if place == 0:
                bias_ref[:, at] = total
                sums[:, at] = weight
            elif place < 7:
                bias_ref[:, at] += total
                sums[:, at] += weight
            else:
                bias_ref[:, at] += total
                narrow[:, at] = (sums[:, at] + weight).astype(jnp.bfloat16)

        stores[slot] = pltpu.make_async_copy(
            grads.at[slot], grad_ref.at[block], store_sem.at[slot]
        )
        stores[slot].start()

    gather_beside(own_ref, rows_ref, send_sem, recv_sem, local_sem, use)
    last = pltpu.make_async_copy(narrow, weight_ref, weight_sem)
    last.start()
    for slot in (0, 1):
        stores[slot].wait()
    last.wait()


def gather_and_grad(own, down_cols, active, slope, call_number):
    token_rows, model_width = own.shape
    width = down_cols.shape[1]
    anywhere = pl.BlockSpec(memory_space=pl.ANY)
    dma = pltpu.SemaphoreType.DMA
    return pl.pallas_call(
        grad_kernel,
        out_shape=(
            jax.ShapeDtypeStruct((8, token_rows, model_width), jnp.bfloat16),
            jax.ShapeDtypeStruct((8, token_rows, width), jnp.bfloat16),
            jax.ShapeDtypeStruct((model_width, width), jnp.bfloat16),
            jax.ShapeDtypeStruct((1, width), jnp.float32),
        ),
        in_specs=[anywhere] * 4,
        out_specs=(anywhere, anywhere, anywhere, pl.BlockSpec(memory_space=pltpu.VMEM)),
        scratch_shapes=[
            pltpu.VMEM(down_cols.shape, jnp.bfloat16),
            pltpu.VMEM((token_rows, model_width), jnp.bfloat16),
            pltpu.VMEM((model_width, token_rows), jnp.bfloat16),
            pltpu.VMEM((token_rows, width), jnp.bfloat16),
            pltpu.VMEM((token_rows, width), jnp.bfloat16),
            pltpu.VMEM((2, token_rows, width), jnp.bfloat16),
            pltpu.VMEM((model_width, width), jnp.float32),
            pltpu.VMEM((model_width, width), jnp.bfloat16),
            dma((9,)),
            dma((9,)),
            dma,
            dma,
            dma,
            dma((2,)),
            dma((2,)),
        ],
        compiler_params=pltpu.CompilerParams(
            collective_id=call_number, has_side_effects=True, vmem_limit_bytes=VMEM_BYTES
        ),
        cost_estimate=pl.CostEstimate(
            flops=32 * token_rows * model_width * width,
            bytes_accessed=150 * 1000 * 1000,
            transcendentals=0,
        ),
        name="gather_and_grad",
    )(own, down_cols, active, slope)


def product_reduce_kernel(
    with_grad,
    narrow_ref,
    weight_hbm,
    *refs,
):
    if with_grad:
        wide_ref, out_ref, grad_ref, *refs = refs
        *refs, wide, across, sums, wide_sem = refs
    else:
        out_ref, *refs = refs
    (
        weight,
        narrow,
        sent,
        mine,
        theirs,
        relayed,
        final,
        send_sem,
        recv_sem,
        weight_sem,
        narrow_sem,
    ) = refs
    rows = narrow.shape[1]
    half = rows // 2
    here, on_x, on_y, on_chip, corner = block_of_eight()
    shift = on_chip - here
    first, second = pl.ds(0, half), pl.ds(half, half)
    load_weight = pltpu.make_async_copy(weight_hbm, weight, weight_sem)
    load_weight.start()

    def copy(index, source, target, device):
        return remote(index, source, target, device, send_sem, recv_sem)

    places = (corner, on_x, on_y, here)
    order = []
    for place in places:
        order += [place + shift, place]

    def fetch(turn):
        return pltpu.make_async_copy(
            narrow_ref.at[order[turn]], narrow.at[turn % 2], narrow_sem.at[turn % 2]
        )

    fetch(0).start()
    greet((on_x, on_y, on_chip))
    to_chip = [copy(index, sent.at[index], theirs.at[index], on_chip) for index in range(4)]
    step = 16

    def add_into(target, other, start, count):
        @pl.loop(0, count // step)
        def _(turn):
            at = pl.ds(pl.multiple_of(start + turn * step, step), step)
            come = pl.ds(pl.multiple_of(turn * step, step), step)
            total = target[at, :].astype(jnp.float32) + other[come, :].astype(jnp.float32)
            target[at, :] = total.astype(target.dtype)

    def join(index):
        to_chip[index].wait_recv()
        add_into(mine.at[index], theirs.at[index], 0, rows)

    corner_x = copy(4, mine.at[0, first], relayed.at[0], on_x)
    corner_y = copy(5, mine.at[0, second], relayed.at[1], on_y)
    x_first = copy(6, mine.at[1, first], final.at[0, first], on_x)
    y_second = copy(7, mine.at[2, second], final.at[1, second], on_y)
    x_second = copy(8, mine.at[1, second], final.at[0, second], on_x)
    y_first = copy(9, mine.at[2, first], final.at[1, first], on_y)

    for turn in range(8):
        pair, own = turn // 2, turn % 2
        if turn < 7:
            fetch(turn + 1).start()
        fetch(turn).wait()
        if turn == 0:
            load_weight.wait()
        target = mine.at[pair] if own else sent.at[pair]

        @pl.loop(0, weight.shape[0] // CHUNK)
        def _(piece):
            at = chunk_of(piece, CHUNK)
            target[:, at] = transposed_product(narrow[turn % 2], weight[at, :]).astype(
                jnp.bfloat16
            )

        if not own:
            to_chip[pair].start()
        if turn == 2:
            join(0)
            corner_x.start()
            corner_y.start()
        if turn == 4:
            join(1)
            x_first.start()
        if turn == 6:
            join(2)
            y_second.start()
    corner_y.wait_recv()
    add_into(mine.at[1], relayed.at[1], half, half)
    x_second.start()
    corner_x.wait_recv()
    add_into(mine.at[2], relayed.at[0], 0, half)
    y_first.start()
    join(3)

    if with_grad:
        def fetch_wide(turn):
            return pltpu.make_async_copy(
                wide_ref.at[order[turn]], wide.at[turn % 2], wide_sem.at[turn % 2]
            )

        fetch_wide(0).start()
        fetch(0).start()
        for turn in range(8):
            if turn < 7:
                fetch_wide(turn + 1).start()
                fetch(turn + 1).start()
            fetch_wide(turn).wait()
            fetch(turn).wait()
            across[...] = jnp.transpose(wide[turn % 2])

            @pl.loop(0, sums.shape[1] // CHUNK)
            def _(piece):
                at = chunk_of(piece, CHUNK)
                value = plain_product(across[...], narrow[turn % 2, :, at])
                if turn == 0:
                    sums[:, at] = value
                elif turn < 7:
                    sums[:, at] += value
                else:
                    weight[:, at] = (sums[:, at] + value).astype(jnp.bfloat16)

        store = pltpu.make_async_copy(weight, grad_ref, weight_sem)
        store.start()

    for each in (x_first, y_second, x_second, y_first):
        each.wait_recv()

    @pl.loop(0, rows // step)
    def _(turn):
        at = pl.ds(pl.multiple_of(turn * step, step), step)
        total = mine[3, at, :].astype(jnp.float32) + final[0, at, :].astype(jnp.float32)
        out_ref[at, :] = total + final[1, at, :].astype(jnp.float32)

    if with_grad:
        store.wait()
    for each in to_chip + [corner_x, corner_y, x_first, y_second, x_second, y_first]:
        each.wait_send()


def product_and_reduce(narrow, weight, wide, call_number):
    _, token_rows, width = narrow.shape
    model_width = weight.shape[0]
    with_grad = wide is not None
    anywhere = pl.BlockSpec(memory_space=pl.ANY)
    inside = pl.BlockSpec(memory_space=pltpu.VMEM)
    dma = pltpu.SemaphoreType.DMA
    block = (token_rows, model_width)
    kind = jnp.bfloat16
    out_shape = [jax.ShapeDtypeStruct(block, jnp.float32)]
    scratch = [
        pltpu.VMEM(weight.shape, kind),
        pltpu.VMEM((2, token_rows, width), kind),
        pltpu.VMEM((4,) + block, kind),
        pltpu.VMEM((4,) + block, kind),
        pltpu.VMEM((4,) + block, kind),
        pltpu.VMEM((2, token_rows // 2, model_width), kind),
        pltpu.VMEM((2,) + block, kind),
        dma((10,)),
        dma((10,)),
        dma,
        dma((2,)),
    ]
    operands = [narrow, weight]
    if with_grad:
        out_shape.append(jax.ShapeDtypeStruct(weight.shape, kind))
        scratch += [
            pltpu.VMEM((2,) + block, kind),
            pltpu.VMEM((model_width, token_rows), kind),
            pltpu.VMEM(weight.shape, jnp.float32),
            dma((2,)),
        ]
        operands.append(wide)
    return pl.pallas_call(
        functools.partial(product_reduce_kernel, with_grad),
        out_shape=tuple(out_shape),
        in_specs=[anywhere] * len(operands),
        out_specs=(inside, anywhere)[: len(out_shape)],
        scratch_shapes=scratch,
        compiler_params=pltpu.CompilerParams(
            collective_id=call_number, has_side_effects=True, vmem_limit_bytes=VMEM_BYTES
        ),
        cost_estimate=pl.CostEstimate(
            flops=(32 if with_grad else 16) * token_rows * model_width * width,
            bytes_accessed=150 * 1000 * 1000,
            transcendentals=0,
        ),
        name="product_and_reduce",
    )(*operands)


def peers_of(count):
    here = lax.axis_index("tok")
    return here, [(here + step) % count for step in range(1, count)]


def small_gather_kernel(count, own_ref, out_ref, send_sem, recv_sem, local_sem):
    here, peers = peers_of(count)
    rows = own_ref.shape[1]
    place = pl.ds(pl.multiple_of(here * rows, rows), rows)
    greet(peers)
    own = pltpu.make_async_copy(own_ref, out_ref.at[:, place, :], local_sem)
    copies = [
        pltpu.make_async_remote_copy(
            src_ref=own_ref,
            dst_ref=out_ref.at[:, place, :],
            send_sem=send_sem.at[index],
            recv_sem=recv_sem.at[index],
            device_id={"tok": peers[index]},
            device_id_type=MESH,
        )
        for index in range(count - 1)
    ]
    for each in copies:
        each.start()
    own.start()
    for each in copies:
        each.wait_recv()
    for each in copies:
        each.wait_send()
    own.wait()


def tok_gather_small(own, call_number, kernels):
    if not kernels:
        return lax.all_gather(own, "tok", axis=1, tiled=True)
    count = 8
    prompts, rows, columns = own.shape
    return pl.pallas_call(
        functools.partial(small_gather_kernel, count),
        out_shape=jax.ShapeDtypeStruct((prompts, count * rows, columns), own.dtype),
        in_specs=[pl.BlockSpec(memory_space=pl.ANY)],
        out_specs=pl.BlockSpec(memory_space=pl.ANY),
        scratch_shapes=[
            pltpu.SemaphoreType.DMA((count - 1,)),
            pltpu.SemaphoreType.DMA((count - 1,)),
            pltpu.SemaphoreType.DMA,
        ],
        compiler_params=pltpu.CompilerParams(collective_id=call_number, has_side_effects=True),
        name="tok_gather_small",
    )(own)


def small_reduce_kernel(count, part_ref, out_ref, come, send_sem, recv_sem):
    here, peers = peers_of(count)
    rows = come.shape[2]

    def place(device):
        return pl.ds(pl.multiple_of(device * rows, rows), rows)

    greet(peers)
    copies = [
        pltpu.make_async_remote_copy(
            src_ref=part_ref.at[:, place(peers[index]), :],
            dst_ref=come.at[index],
            send_sem=send_sem.at[index],
            recv_sem=recv_sem.at[index],
            device_id={"tok": peers[index]},
            device_id_type=MESH,
        )
        for index in range(count - 1)
    ]
    for each in copies:
        each.start()
    total = part_ref[:, place(here), :].astype(jnp.float32)
    for index in range(count - 1):
        copies[index].wait_recv()
        total = total + come[index].astype(jnp.float32)
    out_ref[...] = total.astype(out_ref.dtype)
    for each in copies:
        each.wait_send()


def tok_reduce_small(parts, call_number, kernels):
    if not kernels:
        return lax.psum_scatter(parts, "tok", scatter_dimension=1, tiled=True).astype(jnp.float32)
    count = 8
    prompts, rows, columns = parts.shape
    rows = rows // count
    return pl.pallas_call(
        functools.partial(small_reduce_kernel, count),
        out_shape=jax.ShapeDtypeStruct((prompts, rows, columns), jnp.float32),
        in_specs=[pl.BlockSpec(memory_space=pltpu.VMEM)],
        out_specs=pl.BlockSpec(memory_space=pltpu.VMEM),
        scratch_shapes=[
            pltpu.VMEM((count - 1, prompts, rows, columns), parts.dtype),
            pltpu.SemaphoreType.DMA((count - 1,)),
            pltpu.SemaphoreType.DMA((count - 1,)),
        ],
        compiler_params=pltpu.CompilerParams(
            collective_id=call_number, has_side_effects=True, vmem_limit_bytes=VMEM_BYTES
        ),
        name="tok_reduce_small",
    )(parts)


def final_reduce_kernel(
    groups,
    part_ref,
    small_ref,
    out_ref,
    small_out_ref,
    mine,
    theirs,
    relayed,
    final,
    come,
    small_come,
    small_total,
    small_across,
    send_sem,
    recv_sem,
    load_sem,
    across_send,
    across_recv,
    small_send,
    small_recv,
    small_across_send,
    small_across_recv,
):
    rows = part_ref.shape[1] // groups
    half = rows // 2
    small_rows = small_ref.shape[1] // groups
    here, on_x, on_y, on_chip, corner = block_of_eight()
    group = lax.axis_index("grp")
    shift = on_chip - here
    _, peers = peers_of(8)
    other_groups = [(group + turn) % groups for turn in range(1, groups)]
    step = 16

    barrier = pltpu.get_barrier_semaphore()
    for peer in peers:
        pl.semaphore_signal(barrier, inc=1, device_id={"tok": peer}, device_id_type=MESH)
    for other in other_groups:
        pl.semaphore_signal(barrier, inc=1, device_id={"grp": other}, device_id_type=MESH)
    pl.semaphore_wait(barrier, len(peers) + len(other_groups))

    def copy(chunk, index, source, target, device):
        return pltpu.make_async_remote_copy(
            src_ref=source,
            dst_ref=target,
            send_sem=send_sem.at[chunk, index],
            recv_sem=recv_sem.at[chunk, index],
            device_id={"tok": device},
            device_id_type=MESH,
        )

    def add_into(target, other, start, count):
        @pl.loop(0, count // step)
        def _(turn):
            at = pl.ds(pl.multiple_of(start + turn * step, step), step)
            from_here = pl.ds(pl.multiple_of(turn * step, step), step)
            total = target[at, :].astype(jnp.float32) + other[from_here, :].astype(jnp.float32)
            target[at, :] = total.astype(target.dtype)

    places = (corner, on_x, on_y, here)
    first, second = pl.ds(0, half), pl.ds(half, half)
    to_chip, loads, others = [], [], []
    for chunk in range(groups):
        owner = (group + 1 + chunk) % groups
        span = pl.ds(pl.multiple_of(owner * rows, rows), rows)
        to_chip.append(
            [
                copy(
                    chunk,
                    index,
                    part_ref.at[places[index] + shift, span],
                    theirs.at[chunk, index],
                    on_chip,
                )
                for index in range(4)
            ]
        )
        loads.append(
            [
                pltpu.make_async_copy(
                    part_ref.at[places[index], span],
                    mine.at[chunk, index],
                    load_sem.at[chunk, index],
                )
                for index in range(4)
            ]
        )
        own, two = mine.at[chunk], final.at[chunk]
        others.append(
            {
                "corner_x": copy(chunk, 4, own.at[0, first], relayed.at[chunk, 0], on_x),
                "corner_y": copy(chunk, 5, own.at[0, second], relayed.at[chunk, 1], on_y),
                "x_first": copy(chunk, 6, own.at[1, first], two.at[0, first], on_x),
                "y_second": copy(chunk, 7, own.at[2, second], two.at[1, second], on_y),
                "x_second": copy(chunk, 8, own.at[1, second], two.at[0, second], on_x),
                "y_first": copy(chunk, 9, own.at[2, first], two.at[1, first], on_y),
            }
        )
    small_copies = [
        pltpu.make_async_remote_copy(
            src_ref=small_ref.at[peers[index]],
            dst_ref=small_come.at[index],
            send_sem=small_send.at[index],
            recv_sem=small_recv.at[index],
            device_id={"tok": peers[index]},
            device_id_type=MESH,
        )
        for index in range(len(peers))
    ]
    across = [
        pltpu.make_async_remote_copy(
            src_ref=mine.at[chunk, 3],
            dst_ref=come.at[chunk],
            send_sem=across_send.at[chunk],
            recv_sem=across_recv.at[chunk],
            device_id={"grp": other_groups[chunk]},
            device_id_type=MESH,
        )
        for chunk in range(groups - 1)
    ]
    small_over = [
        pltpu.make_async_remote_copy(
            src_ref=small_total.at[other_groups[chunk]],
            dst_ref=small_across.at[chunk],
            send_sem=small_across_send.at[chunk],
            recv_sem=small_across_recv.at[chunk],
            device_id={"grp": other_groups[chunk]},
            device_id_type=MESH,
        )
        for chunk in range(groups - 1)
    ]

    for chunk in range(groups):
        for index in range(4):
            to_chip[chunk][index].start()
            loads[chunk][index].start()
        if chunk == 0:
            for each in small_copies:
                each.start()

    def join(chunk, index):
        to_chip[chunk][index].wait_recv()
        loads[chunk][index].wait()
        add_into(mine.at[chunk, index], theirs.at[chunk, index], 0, rows)

    def open_chunk(chunk):
        join(chunk, 0)
        others[chunk]["corner_x"].start()
        others[chunk]["corner_y"].start()
        join(chunk, 1)
        others[chunk]["x_first"].start()
        join(chunk, 2)
        others[chunk]["y_second"].start()

    def relay_chunk(chunk):
        others[chunk]["corner_y"].wait_recv()
        add_into(mine.at[chunk, 1], relayed.at[chunk, 1], half, half)
        others[chunk]["x_second"].start()
        others[chunk]["corner_x"].wait_recv()
        add_into(mine.at[chunk, 2], relayed.at[chunk, 0], 0, half)
        others[chunk]["y_first"].start()

    def close_chunk(chunk):
        join(chunk, 3)
        for name in ("x_first", "y_second", "x_second", "y_first"):
            others[chunk][name].wait_recv()

        @pl.loop(0, rows // step)
        def _(turn):
            at = pl.ds(pl.multiple_of(turn * step, step), step)
            total = mine[chunk, 3, at, :].astype(jnp.float32)
            total = total + final[chunk, 0, at, :].astype(jnp.float32)
            total = total + final[chunk, 1, at, :].astype(jnp.float32)
            mine[chunk, 3, at, :] = total.astype(mine.dtype)

        if chunk < groups - 1:
            across[chunk].start()

    open_chunk(0)
    for chunk in range(1, groups):
        open_chunk(chunk)
        relay_chunk(chunk - 1)
        if chunk == 1:
            sums = small_ref[here]
            for index in range(len(peers)):
                small_copies[index].wait_recv()
                sums = sums + small_come[index]
            small_total[...] = sums.reshape(small_total.shape)
            for each in small_over:
                each.start()
        if chunk >= 2:
            close_chunk(chunk - 2)
    relay_chunk(groups - 1)
    close_chunk(groups - 2)
    close_chunk(groups - 1)
    for each in across:
        each.wait_recv()

    @pl.loop(0, rows // step)
    def _(turn):
        at = pl.ds(pl.multiple_of(turn * step, step), step)
        total = mine[groups - 1, 3, at, :].astype(jnp.float32)
        for chunk in range(groups - 1):
            total = total + come[chunk, at, :].astype(jnp.float32)
        out_ref[at, :] = total

    small_sum = small_total[group]
    for chunk in range(groups - 1):
        small_over[chunk].wait_recv()
        small_sum = small_sum + small_across[chunk]
    small_out_ref[...] = small_sum
    for chunk in range(groups):
        for each in to_chip[chunk] + list(others[chunk].values()):
            each.wait_send()
    for each in small_copies + across + small_over:
        each.wait_send()


def final_reduce(parts, small_parts, groups, call_number, kernels):
    if not kernels:
        sums = lax.psum_scatter(parts, "tok", scatter_dimension=0, tiled=False)
        sums = lax.psum_scatter(sums, "grp", scatter_dimension=0, tiled=True)
        small_sums = lax.psum_scatter(small_parts, "tok", scatter_dimension=0, tiled=False)
        small_sums = lax.psum_scatter(small_sums, "grp", scatter_dimension=0, tiled=True)
        return sums.astype(jnp.float32), small_sums
    _, rows, columns = parts.shape
    rows = rows // groups
    small_rows, small_columns = small_parts.shape[1] // groups, small_parts.shape[2]
    kind = parts.dtype
    dma = pltpu.SemaphoreType.DMA
    small = (small_rows, small_columns)
    return pl.pallas_call(
        functools.partial(final_reduce_kernel, groups),
        out_shape=(
            jax.ShapeDtypeStruct((rows, columns), jnp.float32),
            jax.ShapeDtypeStruct(small, jnp.float32),
        ),
        in_specs=[
            pl.BlockSpec(memory_space=pl.ANY),
            pl.BlockSpec(memory_space=pltpu.VMEM),
        ],
        out_specs=(
            pl.BlockSpec(memory_space=pltpu.VMEM),
            pl.BlockSpec(memory_space=pltpu.VMEM),
        ),
        scratch_shapes=[
            pltpu.VMEM((groups, 4, rows, columns), kind),
            pltpu.VMEM((groups, 4, rows, columns), kind),
            pltpu.VMEM((groups, 2, rows // 2, columns), kind),
            pltpu.VMEM((groups, 2, rows, columns), kind),
            pltpu.VMEM((groups - 1, rows, columns), kind),
            pltpu.VMEM((7, groups * small_rows, small_columns), jnp.float32),
            pltpu.VMEM((groups,) + small, jnp.float32),
            pltpu.VMEM((groups - 1,) + small, jnp.float32),
            dma((groups, 10)),
            dma((groups, 10)),
            dma((groups, 4)),
            dma((groups - 1,)),
            dma((groups - 1,)),
            dma((7,)),
            dma((7,)),
            dma((groups - 1,)),
            dma((groups - 1,)),
        ],
        compiler_params=pltpu.CompilerParams(
            collective_id=call_number, has_side_effects=True, vmem_limit_bytes=VMEM_BYTES
        ),
        name="final_reduce",
    )(parts, small_parts)


def stack_heads(values, heads):
    return jnp.concatenate(
        [values[:, head * HEAD_WIDTH : (head + 1) * HEAD_WIDTH] for head in range(heads)], axis=0
    )


def unstack_heads(values, heads):
    rows = values.shape[0] // heads
    return jnp.concatenate(
        [values[head * rows : (head + 1) * rows, :] for head in range(heads)], axis=1
    )


def part_rows(part, prompts, answers, token_ref, answer_ref):
    answer_rows = answer_ref.shape[0] // answers
    prompt_rows = (token_ref.shape[0] - answer_ref.shape[0]) // prompts
    if part < prompts:
        return slice(part * prompt_rows, (part + 1) * prompt_rows), prompt_rows
    start = prompts * prompt_rows + (part - prompts) * answer_rows
    return slice(start, start + answer_rows), answer_rows


def as_row(column):
    wide = jnp.broadcast_to(column, (column.shape[0], HEAD_WIDTH))
    return jnp.transpose(wide)[0:1, :]


def attention_forward_kernel(
    prompts,
    answers,
    heads,
    scale,
    place_ref,
    owner_ref,
    normed_ref,
    query_ref,
    bias_ref,
    prompt_kv_ref,
    answer_kv_ref,
    output_ref,
    states_ref,
    offset_ref,
    gain_ref,
    shift_ref,
    queries_ref,
    mixture_ref,
    log_ref,
    hidden_ref,
    second_ref,
):
    step = pl.program_id(0)
    width = HEAD_WIDTH
    length = prompt_kv_ref.shape[1]
    query_block = query_ref[0].reshape(-1, query_ref.shape[-1])
    output_block = output_ref[0].reshape(-1, output_ref.shape[-1])
    queries = (plain_product(normed_ref[...], query_block) + bias_ref[0]).astype(jnp.bfloat16)
    queries_ref[...] = queries

    pieces = []
    for part in range(prompts + answers):
        here, rows = part_rows(part, prompts, answers, normed_ref, answer_kv_ref)
        token = lax.broadcasted_iota(jnp.int32, (heads * rows, 1), 0) % rows
        stacked = stack_heads(queries[here, :], heads)
        if part < prompts:
            keys = prompt_kv_ref[part, :, :width]
            values = prompt_kv_ref[part, :, width:]
            scores = transposed_product(stacked, keys)
            place = lax.broadcasted_iota(jnp.int32, (1, length), 1)
            scores = jnp.where(place <= place_ref[0] + token, scores, masked)
            top = jnp.max(scores, axis=-1, keepdims=True)
            exponent = jnp.exp((scores - top) * scale)
            total = jnp.sum(exponent, axis=-1, keepdims=True)
            mixed = plain_product(exponent.astype(jnp.bfloat16), values)
        else:
            answer = part - prompts
            owner = owner_ref[answer]
            own = slice(answer * rows, (answer + 1) * rows)
            keys = prompt_kv_ref[owner, :, :width]
            values = prompt_kv_ref[owner, :, width:]
            scores = transposed_product(stacked, keys)
            own_scores = transposed_product(stacked, answer_kv_ref[own, :width])
            place = lax.broadcasted_iota(jnp.int32, (1, rows), 1)
            own_scores = jnp.where(place <= token, own_scores, masked)
            top = jnp.maximum(
                jnp.max(scores, axis=-1, keepdims=True),
                jnp.max(own_scores, axis=-1, keepdims=True),
            )
            exponent = jnp.exp((scores - top) * scale)
            own_exponent = jnp.exp((own_scores - top) * scale)
            total = jnp.sum(exponent, axis=-1, keepdims=True) + jnp.sum(
                own_exponent, axis=-1, keepdims=True
            )
            mixed = plain_product(exponent.astype(jnp.bfloat16), values) + plain_product(
                own_exponent.astype(jnp.bfloat16), answer_kv_ref[own, width:]
            )
        pieces.append(unstack_heads((mixed / total).astype(jnp.bfloat16), heads))
        log_row = as_row(top * scale + jnp.log(total))
        for head in range(heads):
            log_ref[0, head : head + 1, here] = log_row[:, head * rows : (head + 1) * rows]
    mixture = jnp.concatenate(pieces, axis=0)
    mixture_ref[...] = mixture

    @pl.when(step == 0)
    def _():
        hidden_ref[...] = states_ref[...].astype(jnp.float32) + offset_ref[...]

    hidden_ref[...] += transposed_product(mixture, output_block)

    @pl.when(step == pl.num_programs(0) - 1)
    def _():
        scaled, _ = norm_stats(hidden_ref[...])
        second_ref[...] = (scaled * gain_ref[...] + shift_ref[...]).astype(jnp.bfloat16)


def attention_forward(
    place,
    owning,
    normed,
    packed,
    weight_rows,
    query_offset,
    prompt_kv,
    answer_kv,
    states,
    output_offset,
    gain,
    shift,
    prompts,
    answers,
):
    token_rows, model_width = normed.shape
    steps, groups, _, block = packed.shape
    heads = block // HEAD_WIDTH
    length = prompt_kv.shape[1]
    whole = lambda *shape: pl.BlockSpec(shape, lambda step, *_: (0,) * len(shape))
    scores = heads * token_rows * length
    return pl.pallas_call(
        functools.partial(
            attention_forward_kernel, prompts, answers, heads, HEAD_WIDTH ** (-0.5)
        ),
        out_shape=(
            jax.ShapeDtypeStruct((token_rows, model_width), jnp.bfloat16),
            jax.ShapeDtypeStruct((token_rows, model_width), jnp.bfloat16),
            jax.ShapeDtypeStruct((steps, heads, token_rows), jnp.float32),
            jax.ShapeDtypeStruct((token_rows, model_width), jnp.float32),
            jax.ShapeDtypeStruct((token_rows, model_width), jnp.bfloat16),
        ),
        grid_spec=pltpu.PrefetchScalarGridSpec(
            num_scalar_prefetch=2,
            grid=(steps,),
            in_specs=[
                whole(token_rows, model_width),
                pl.BlockSpec(
                    (1, groups, weight_rows, block), lambda step, *_: (step, 0, 0, 0)
                ),
                pl.BlockSpec((1, 1, block), lambda step, *_: (step, 0, 0)),
                whole(*prompt_kv.shape),
                whole(*answer_kv.shape),
                pl.BlockSpec(
                    (1, groups, weight_rows, block), lambda step, *_: (step, 0, 1, 0)
                ),
                whole(token_rows, model_width),
                whole(1, model_width),
                whole(1, model_width),
                whole(1, model_width),
            ],
            out_specs=(
                pl.BlockSpec((token_rows, block), lambda step, *_: (0, step)),
                pl.BlockSpec((token_rows, block), lambda step, *_: (0, step)),
                pl.BlockSpec((1, heads, token_rows), lambda step, *_: (step, 0, 0)),
                whole(token_rows, model_width),
                whole(token_rows, model_width),
            ),
        ),
        compiler_params=pltpu.CompilerParams(vmem_limit_bytes=VMEM_BYTES),
        cost_estimate=pl.CostEstimate(
            flops=steps * (4 * token_rows * model_width * block + 8 * scores * HEAD_WIDTH),
            bytes_accessed=8 * steps * model_width * block,
            transcendentals=steps * scores,
        ),
        name="attention_forward",
    )(
        place,
        owning,
        normed,
        packed,
        query_offset.reshape(steps, 1, block),
        prompt_kv,
        answer_kv,
        packed,
        states,
        output_offset.reshape(1, -1),
        gain.reshape(1, -1),
        shift.reshape(1, -1),
    )


def attention_backward_kernel(
    prompts,
    answers,
    heads,
    scale,
    place_ref,
    owner_ref,
    normed_ref,
    query_ref,
    prompt_kv_ref,
    answer_kv_ref,
    output_ref,
    branch_ref,
    queries_ref,
    mixture_ref,
    log_ref,
    grad_weights_ref,
    grad_normed_ref,
    grad_prompt_ref,
    grad_answer_ref,
    grad_bias_ref,
    normed_across,
    branch_across,
    key_sums,
    own_sums,
):
    step = pl.program_id(0)
    width = HEAD_WIDTH
    length = prompt_kv_ref.shape[1]
    block = queries_ref.shape[1]

    @pl.when(step == 0)
    def _():
        normed_across[...] = jnp.transpose(normed_ref[...])
        branch_across[...] = jnp.transpose(branch_ref[...])
        key_sums[...] = jnp.zeros_like(key_sums)
        own_sums[...] = jnp.zeros_like(own_sums)
        grad_normed_ref[...] = jnp.zeros_like(grad_normed_ref)

    query_block = query_ref[0].reshape(-1, block)
    output_block = output_ref[0].reshape(-1, block)
    weight_shape = query_ref.shape[1:]
    weight_rows = weight_shape[1]
    grad_weights_ref[0, :, weight_rows : 2 * weight_rows] = (
        plain_product(branch_across[...], mixture_ref[...])
        .astype(jnp.bfloat16)
        .reshape(weight_shape)
    )
    grad_mixture = plain_product(branch_ref[...], output_block).astype(jnp.bfloat16)
    queries = queries_ref[...]
    mixture = mixture_ref[...]

    def backward(keys, values, stacked, grad_stacked, log_row, inner_row, allowed):
        scores = transposed_product(keys, stacked)
        probs = jnp.exp(scores * scale - log_row)
        if allowed is not None:
            probs = jnp.where(allowed, probs, 0.0)
        grad_values = plain_product(probs.astype(jnp.bfloat16), grad_stacked)
        grad_probs = transposed_product(values, grad_stacked)
        grad_scores = (probs * (grad_probs - inner_row)).astype(jnp.bfloat16)
        grad_keys = plain_product(grad_scores, stacked)
        grad_queries = weight_product(grad_scores, keys)
        return grad_queries, grad_keys, grad_values

    pieces = []
    for part in range(prompts + answers):
        here, rows = part_rows(part, prompts, answers, normed_ref, answer_kv_ref)
        token = lax.broadcasted_iota(jnp.int32, (1, heads * rows), 1) % rows
        stacked = stack_heads(queries[here, :], heads)
        grad_stacked = stack_heads(grad_mixture[here, :], heads)
        mixed = stack_heads(mixture[here, :], heads)
        product = grad_stacked.astype(jnp.float32) * mixed.astype(jnp.float32)
        inner_row = jnp.sum(jnp.transpose(product), axis=0, keepdims=True)
        log_row = jnp.concatenate(
            [log_ref[0, head : head + 1, here] for head in range(heads)], axis=1
        )
        if part < prompts:
            place = lax.broadcasted_iota(jnp.int32, (length, 1), 0)
            grad_queries, grad_keys, grad_values = backward(
                prompt_kv_ref[part, :, :width],
                prompt_kv_ref[part, :, width:],
                stacked,
                grad_stacked,
                log_row,
                inner_row,
                place <= place_ref[0] + token,
            )
            key_sums[part, :, :width] += grad_keys
            key_sums[part, :, width:] += grad_values
        else:
            answer = part - prompts
            owner = owner_ref[answer]
            own = slice(answer * rows, (answer + 1) * rows)
            grad_queries, grad_keys, grad_values = backward(
                prompt_kv_ref[owner, :, :width],
                prompt_kv_ref[owner, :, width:],
                stacked,
                grad_stacked,
                log_row,
                inner_row,
                None,
            )
            key_sums[owner, :, :width] += grad_keys
            key_sums[owner, :, width:] += grad_values
            place = lax.broadcasted_iota(jnp.int32, (rows, 1), 0)
            own_queries, own_keys, own_values = backward(
                answer_kv_ref[own, :width],
                answer_kv_ref[own, width:],
                stacked,
                grad_stacked,
                log_row,
                inner_row,
                place <= token,
            )
            grad_queries = grad_queries + own_queries
            own_sums[own, :width] += own_keys
            own_sums[own, width:] += own_values
        pieces.append(unstack_heads((grad_queries * scale).astype(jnp.bfloat16), heads))
    grad_queries = jnp.concatenate(pieces, axis=0)
    grad_weights_ref[0, :, :weight_rows] = (
        plain_product(normed_across[...], grad_queries).astype(jnp.bfloat16).reshape(weight_shape)
    )
    grad_normed_ref[...] += transposed_product(grad_queries, query_block)
    grad_bias_ref[0] = jnp.sum(grad_queries.astype(jnp.float32), axis=0, keepdims=True)

    @pl.when(step == pl.num_programs(0) - 1)
    def _():
        grad_prompt_ref[:, :, :width] = (key_sums[:, :, :width] * scale).astype(jnp.bfloat16)
        grad_prompt_ref[:, :, width:] = key_sums[:, :, width:].astype(jnp.bfloat16)
        grad_answer_ref[:, :width] = own_sums[:, :width] * scale
        grad_answer_ref[:, width:] = own_sums[:, width:]


def attention_backward(
    place,
    owning,
    normed,
    packed,
    weight_rows,
    grad_rows,
    prompt_kv,
    answer_kv,
    branch,
    queries,
    mixture,
    log_total,
    prompts,
    answers,
):
    token_rows, model_width = normed.shape
    steps, groups, _, block = packed.shape
    heads = block // HEAD_WIDTH
    length = prompt_kv.shape[1]
    whole = lambda *shape: pl.BlockSpec(shape, lambda step, *_: (0,) * len(shape))
    columns = lambda: pl.BlockSpec((token_rows, block), lambda step, *_: (0, step))
    scores = heads * token_rows * length
    return pl.pallas_call(
        functools.partial(
            attention_backward_kernel, prompts, answers, heads, HEAD_WIDTH ** (-0.5)
        ),
        out_shape=(
            jax.ShapeDtypeStruct((steps, groups, grad_rows, block), jnp.bfloat16),
            jax.ShapeDtypeStruct((token_rows, model_width), jnp.float32),
            jax.ShapeDtypeStruct(prompt_kv.shape, jnp.bfloat16),
            jax.ShapeDtypeStruct(answer_kv.shape, jnp.float32),
            jax.ShapeDtypeStruct((steps, 1, block), jnp.float32),
        ),
        grid_spec=pltpu.PrefetchScalarGridSpec(
            num_scalar_prefetch=2,
            grid=(steps,),
            in_specs=[
                whole(token_rows, model_width),
                pl.BlockSpec(
                    (1, groups, weight_rows, block), lambda step, *_: (step, 0, 0, 0)
                ),
                whole(*prompt_kv.shape),
                whole(*answer_kv.shape),
                pl.BlockSpec(
                    (1, groups, weight_rows, block), lambda step, *_: (step, 0, 1, 0)
                ),
                whole(token_rows, model_width),
                columns(),
                columns(),
                pl.BlockSpec((1, heads, token_rows), lambda step, *_: (step, 0, 0)),
            ],
            out_specs=(
                pl.BlockSpec(
                    (1, groups, grad_rows, block), lambda step, *_: (step, 0, 0, 0)
                ),
                whole(token_rows, model_width),
                whole(*prompt_kv.shape),
                whole(*answer_kv.shape),
                pl.BlockSpec((1, 1, block), lambda step, *_: (step, 0, 0)),
            ),
            scratch_shapes=[
                pltpu.VMEM((model_width, token_rows), jnp.bfloat16),
                pltpu.VMEM((model_width, token_rows), jnp.bfloat16),
                pltpu.VMEM(prompt_kv.shape, jnp.float32),
                pltpu.VMEM(answer_kv.shape, jnp.float32),
            ],
        ),
        compiler_params=pltpu.CompilerParams(vmem_limit_bytes=VMEM_BYTES),
        cost_estimate=pl.CostEstimate(
            flops=steps * (8 * token_rows * model_width * block + 20 * scores * HEAD_WIDTH),
            bytes_accessed=16 * steps * model_width * block,
            transcendentals=steps * scores,
        ),
        name="attention_backward",
    )(
        place,
        owning,
        normed,
        packed,
        prompt_kv,
        answer_kv,
        packed,
        branch,
        queries,
        mixture,
        log_total,
    )


def by_group(values):
    return jnp.swapaxes(values, 0, 1).reshape(-1)


def body(
    kernels,
    prompt_states,
    answer_states,
    answer_prompt,
    prompt_teacher,
    answer_teacher,
    prompt_valid,
    answer_valid,
    first_gain,
    first_shift,
    query_weight,
    query_bias,
    keyval_weight,
    value_bias,
    output_weight,
    output_bias,
    second_gain,
    second_shift,
    up_weight,
    up_bias,
    down_weight,
    down_bias,
):
    prompt_count, prompt_rows, model_width = prompt_states.shape
    answer_count, answer_len, _ = answer_states.shape
    groups = lax.axis_size("grp")
    token_devices = lax.axis_size("tok")
    token_index = lax.axis_index("tok")
    group_index = lax.axis_index("grp")
    own_prompt = prompt_rows * prompt_count
    token_rows = own_prompt + answer_count * answer_len
    hidden_units = up_bias.shape[0] * groups * token_devices
    ff_here = hidden_units // token_devices
    ff_start = token_index * ff_here
    share = first_gain.shape[0]
    block = query_weight.shape[1]
    weight_rows = query_weight.shape[0]
    keyval_rows, keyval_width = keyval_weight.shape

    def own_rows(prompt_part, answer_part):
        return jnp.concatenate(
            [prompt_part.reshape(own_prompt, -1), answer_part.reshape(-1, prompt_part.shape[-1])],
            axis=0,
        )

    states = own_rows(prompt_states, answer_states)
    inputs = states.astype(jnp.float32)
    valid_rows = jnp.concatenate([prompt_valid.reshape(-1), answer_valid.reshape(-1)])
    own_count = jnp.sum(valid_rows)
    valid_rows = valid_rows.astype(jnp.float32)

    up_cols = lax.all_gather(up_weight, "grp", axis=0, tiled=True)
    down_cols = lax.all_gather(down_weight, "grp", axis=0, tiled=True)

    count_parts = jnp.stack([own_count // 128, own_count % 128]).astype(jnp.bfloat16)
    smalls = jnp.concatenate(
        [
            first_gain,
            first_shift,
            query_bias,
            output_bias,
            second_gain,
            second_shift,
            down_bias,
            up_bias,
            count_parts,
        ]
    )
    smalls = jnp.pad(smalls, (0, SMALL_ROWS * block - smalls.shape[0])).reshape(SMALL_ROWS, block)
    pack = jnp.concatenate(
        [query_weight, output_weight, keyval_weight.reshape(-1, block), smalls], axis=0
    )
    pack_rows = pack.shape[0]
    packed = lax.all_gather(pack, "grp", axis=0, tiled=True)
    packed = tok_gather(packed, 0, kernels).reshape(token_devices, groups, pack_rows, block)
    keyval_start = 2 * weight_rows
    keyval_end = pack_rows - SMALL_ROWS
    keyval_full = jnp.swapaxes(
        packed[:, :, keyval_start:keyval_end].reshape(
            token_devices, groups, keyval_rows, keyval_width
        ),
        0,
        1,
    ).reshape(model_width, keyval_width)
    small_full = packed[:, :, keyval_end:].reshape(token_devices, groups, SMALL_ROWS * block)
    small_full = jnp.swapaxes(small_full.astype(jnp.float32), 0, 1)

    def vector(start, size):
        return small_full[:, :, start : start + size].reshape(-1)

    gain_one, shift_one, query_offset, output_offset, gain_two, shift_two, down_offset = (
        vector(index * share, share) for index in range(7)
    )
    up_offset = vector(7 * share, up_bias.shape[0])
    count_at = 7 * share + up_bias.shape[0]
    counts = small_full[:, :, count_at : count_at + 2]
    valid_count = jnp.sum(counts[:, :, 0]) * 128.0 + jnp.sum(counts[:, :, 1])
    up_here = lax.dynamic_slice_in_dim(up_offset, ff_start, ff_here)

    scaled_one, inverse_one = norm_stats(inputs)
    normed_one = (scaled_one * gain_one + shift_one).astype(jnp.bfloat16)
    key_offset = jnp.concatenate(
        [jnp.zeros((HEAD_WIDTH,), jnp.float32), value_bias.astype(jnp.float32)]
    )
    key_value_rows = (plain_product(normed_one, keyval_full) + key_offset).astype(jnp.bfloat16)
    prompt_kv = tok_gather_small(
        key_value_rows[:own_prompt].reshape(prompt_count, prompt_rows, -1), 1, kernels
    )
    answer_kv = key_value_rows[own_prompt:]
    owning = answer_prompt - group_index * prompt_count
    owning = lax.dynamic_slice_in_dim(owning, token_index * answer_count, answer_count)
    place = jnp.reshape(token_index * prompt_rows, (1,)).astype(jnp.int32)
    queries, mixture, log_total, hidden, normed_two = attention_forward(
        place,
        owning,
        normed_one,
        packed,
        weight_rows,
        query_offset,
        prompt_kv,
        answer_kv,
        states,
        output_offset,
        gain_two,
        shift_two,
        prompt_count,
        answer_count,
    )

    if kernels:
        group_two, activated, slope = gather_and_up(normed_two, up_cols, up_here, 2)
        (feed_term,) = product_and_reduce(activated, down_cols, None, 3)
    else:
        group_two = lax.all_gather(normed_two, "tok", axis=0, tiled=True)
        pre_active = plain_product(group_two, up_cols) + up_here
        activated = jax.nn.gelu(pre_active, approximate=True).astype(jnp.bfloat16)
        feed_term = for_sending(transposed_product(activated, down_cols))
        feed_term = lax.psum_scatter(feed_term, "tok", scatter_dimension=0, tiled=True)
        feed_term = feed_term.astype(jnp.float32)
    result_rows = hidden + feed_term + down_offset

    teacher = own_rows(prompt_teacher, answer_teacher).astype(jnp.float32)
    differ = result_rows - teacher
    own_squares = jnp.sum(valid_rows[:, None] * differ * differ)
    every_token = token_rows * groups * token_devices
    grad_result = every_token / valid_count * valid_rows[:, None] * differ
    grad_branch_two = grad_result.astype(jnp.bfloat16)

    if kernels:
        _, grad_pre_active, grad_down_cols, grad_up_offset = gather_and_grad(
            grad_branch_two, down_cols, activated, slope, 4
        )
        grad_normed_two, grad_up_cols = product_and_reduce(grad_pre_active, up_cols, group_two, 5)
        grad_up_offset = grad_up_offset.reshape(-1)
    else:
        group_grad_two = lax.all_gather(grad_branch_two, "tok", axis=0, tiled=True)
        grad_activated = plain_product(group_grad_two, down_cols)
        _, gelu_back = jax.vjp(
            lambda argument: jax.nn.gelu(argument, approximate=True), pre_active
        )
        grad_pre_active = gelu_back(grad_activated)[0].astype(jnp.bfloat16)
        grad_normed_two = for_sending(transposed_product(grad_pre_active, up_cols))
        grad_normed_two = lax.psum_scatter(
            grad_normed_two, "tok", scatter_dimension=0, tiled=True
        ).astype(jnp.float32)
        grad_down_cols = for_sending(weight_product(group_grad_two, activated))
        grad_up_cols = for_sending(weight_product(group_two, grad_pre_active))
        grad_up_offset = column_sums(grad_pre_active)
    grad_down_weight = lax.psum_scatter(grad_down_cols, "grp", scatter_dimension=0, tiled=True)
    grad_up_weight = lax.psum_scatter(grad_up_cols, "grp", scatter_dimension=0, tiled=True)
    grad_down_offset = column_sums(grad_branch_two)
    scaled_two, inverse_two = norm_stats(hidden)
    grad_norm_two, grad_gain_two, grad_shift_two = norm_backward(
        grad_normed_two, gain_two, scaled_two, inverse_two
    )
    grad_hidden = grad_result + grad_norm_two
    grad_branch_one = grad_hidden.astype(jnp.bfloat16)
    grad_output_offset = column_sums(grad_branch_one)

    grad_rows = keyval_end
    grad_weights, grad_normed_one, grad_prompt_kv, grad_answer_kv, grad_query_offset = (
        attention_backward(
            place,
            owning,
            normed_one,
            packed,
            weight_rows,
            grad_rows,
            prompt_kv,
            answer_kv,
            grad_branch_one,
            queries,
            mixture,
            log_total,
            prompt_count,
            answer_count,
        )
    )
    grad_prompt_kv = tok_reduce_small(grad_prompt_kv, 6, kernels)
    grad_keyvals = jnp.concatenate(
        [grad_prompt_kv.reshape(own_prompt, -1), grad_answer_kv], axis=0
    ).astype(jnp.bfloat16)
    grad_keyval_full = weight_product(normed_one, grad_keyvals)
    grad_value_offset = column_sums(grad_keyvals[:, HEAD_WIDTH:])
    grad_normed_one = grad_normed_one + transposed_product(grad_keyvals, keyval_full)
    grad_norm_one, grad_gain_one, grad_shift_one = norm_backward(
        grad_normed_one, gain_one, scaled_one, inverse_one
    )
    grad_inputs = grad_hidden + grad_norm_one

    grad_keyval_blocks = jnp.swapaxes(
        grad_keyval_full.astype(jnp.bfloat16).reshape(groups, token_devices, -1, block), 0, 1
    )
    grad_weights = lax.dynamic_update_slice(
        grad_weights, grad_keyval_blocks, (0, 0, keyval_start, 0)
    )
    vectors = (
        grad_gain_one,
        grad_shift_one,
        grad_query_offset.reshape(-1),
        grad_output_offset,
        grad_gain_two,
        grad_shift_two,
        grad_down_offset,
        lax.dynamic_update_slice_in_dim(
            jnp.zeros((hidden_units,), jnp.float32), grad_up_offset, ff_start, 0
        ),
    )
    totals = jnp.concatenate([grad_value_offset, own_squares.reshape(1)])
    blocks = jnp.concatenate(
        [each.reshape(groups, token_devices, -1) for each in vectors]
        + [jnp.broadcast_to(totals, (groups, token_devices, totals.shape[0]))],
        axis=2,
    )
    blocks = jnp.pad(blocks, ((0, 0), (0, 0), (0, SMALL_SUMS - blocks.shape[2])))
    blocks = jnp.swapaxes(blocks, 0, 1).reshape(token_devices, -1, HEAD_WIDTH)
    grad_weights, small_sums = final_reduce(
        grad_weights.reshape(token_devices, -1, block), blocks, groups, 7, kernels
    )
    small_sums = small_sums.reshape(-1)
    up_share = up_bias.shape[0]
    totals_at = 7 * share + up_share
    value_total = small_sums[totals_at : totals_at + HEAD_WIDTH]
    squared_sum = small_sums[totals_at + HEAD_WIDTH]
    loss_value = squared_sum / (valid_count * model_width)

    def split_rows(values):
        values = values.astype(jnp.bfloat16)
        return (
            values[:own_prompt].reshape(prompt_states.shape),
            values[own_prompt:].reshape(answer_states.shape),
        )

    prompt_out, answer_out = split_rows(result_rows)
    prompt_grad, answer_grad = split_rows(grad_inputs)
    pieces = [small_sums[index * share : (index + 1) * share] for index in range(7)]
    return (
        prompt_out,
        answer_out,
        prompt_grad,
        answer_grad,
        pieces[0],
        pieces[1],
        grad_weights[:weight_rows],
        pieces[2],
        grad_weights[keyval_start:].reshape(keyval_rows, keyval_width),
        value_total,
        grad_weights[weight_rows:keyval_start],
        pieces[3],
        pieces[4],
        pieces[5],
        grad_up_weight.astype(jnp.float32),
        small_sums[7 * share : totals_at],
        grad_down_weight.astype(jnp.float32),
        pieces[6],
        loss_value,
    )


def solution(mesh):
    rows = P(("grp", "tok"))
    table = P(("grp", "tok"), None)
    matrix = P("grp", "tok")
    prompt_part = P("grp", "tok", None)
    answer_part = P(("grp", "tok"), None, None)
    in_specs = (
        prompt_part,
        answer_part,
        P("grp"),
        prompt_part,
        answer_part,
        P("grp", "tok"),
        table,
        rows,
        rows,
        matrix,
        rows,
        table,
        P(),
        matrix,
        rows,
        rows,
        rows,
        matrix,
        rows,
        matrix,
        rows,
    )
    out_specs = (
        prompt_part,
        answer_part,
        prompt_part,
        answer_part,
        rows,
        rows,
        matrix,
        rows,
        table,
        P(),
        matrix,
        rows,
        rows,
        rows,
        matrix,
        rows,
        matrix,
        rows,
        P(),
    )
    kernels = mesh.shape["tok"] == 8
    return jax.shard_map(
        functools.partial(body, kernels),
        mesh=mesh,
        in_specs=in_specs,
        out_specs=out_specs,
        check_vma=False,
    )
```

```python
import functools

import jax
import jax.numpy as jnp
from jax import lax
from jax.experimental import pallas as pl
from jax.experimental.pallas import tpu as pltpu
from jax.sharding import PartitionSpec as P

HEAD_WIDTH = 128
epsilon = 1e-05
masked = -1e30
MESH = pl.DeviceIdType.MESH
VMEM_BYTES = 56 * 1024 * 1024
SMALL_ROWS = 16
SMALL_SUMS = 1024


def for_sending(value):
    return value.astype(jnp.bfloat16)


def plain_product(left, right):
    return jnp.dot(left, right, preferred_element_type=jnp.float32)


def transposed_product(left, right):
    return lax.dot_general(
        left, right, (((1,), (1,)), ((), ())), preferred_element_type=jnp.float32
    )


def weight_product(left, right):
    return lax.dot_general(
        left, right, (((0,), (0,)), ((), ())), preferred_element_type=jnp.float32
    )


def norm_stats(values):
    center = values - jnp.mean(values, axis=-1, keepdims=True)
    inverse = lax.rsqrt(jnp.mean(center * center, axis=-1, keepdims=True) + epsilon)
    return center * inverse, inverse


def norm_backward(grad_out, gain, scaled, inverse):
    weighted = grad_out * gain
    grad_in = inverse * (
        weighted
        - jnp.mean(weighted, axis=-1, keepdims=True)
        - scaled * jnp.mean(weighted * scaled, axis=-1, keepdims=True)
    )
    return (grad_in, jnp.sum(grad_out * scaled, axis=0), jnp.sum(grad_out, axis=0))


def column_sums(values):
    return jnp.sum(values.astype(jnp.float32), axis=0)


def block_of_eight():
    here = lax.axis_index("tok")
    core, across, along = here % 2, (here // 2) % 2, here // 4
    on_x = here + 2 - 4 * across
    on_y = here + 4 - 8 * along
    on_chip = here + 1 - 2 * core
    corner = on_x + 4 - 8 * along
    return here, on_x, on_y, on_chip, corner


def greet_all(peers, other_groups):
    barrier = pltpu.get_barrier_semaphore()
    for peer in peers:
        pl.semaphore_signal(barrier, inc=1, device_id={"tok": peer}, device_id_type=MESH)
    for other in other_groups:
        pl.semaphore_signal(barrier, inc=1, device_id={"grp": other}, device_id_type=MESH)
    pl.semaphore_wait(barrier, len(peers) + len(other_groups))


def greet(devices):
    barrier = pltpu.get_barrier_semaphore()
    for device in devices:
        pl.semaphore_signal(barrier, inc=1, device_id={"tok": device}, device_id_type=MESH)
    pl.semaphore_wait(barrier, len(devices))


def spread_kernel(groups, own_ref, out_ref, held, send_sem, recv_sem, over_send, over_recv):
    here, peers = peers_of(8)
    group = lax.axis_index("grp")
    other_groups = [(group + turn) % groups for turn in range(1, groups)]
    greet_all(peers, other_groups)
    over = [
        pltpu.make_async_remote_copy(
            src_ref=own_ref,
            dst_ref=held.at[group],
            send_sem=over_send.at[index],
            recv_sem=over_recv.at[index],
            device_id={"grp": other},
            device_id_type=MESH,
        )
        for index, other in enumerate(other_groups)
    ]
    for each in over:
        each.start()
    held[group] = own_ref[...]
    for each in over:
        each.wait_recv()
    copies = [
        remote(index, held, out_ref.at[here], peer, send_sem, recv_sem)
        for index, peer in enumerate(peers)
    ]
    for each in copies:
        each.start()
    out_ref[here] = held[...]
    for each in copies:
        each.wait_recv()
    for each in copies + over:
        each.wait_send()


def spread(own, groups, call_number, kernels):
    if not kernels:
        return lax.all_gather(lax.all_gather(own, "grp", axis=0), "tok", axis=0)
    inside = pl.BlockSpec(memory_space=pltpu.VMEM)
    dma = pltpu.SemaphoreType.DMA
    return pl.pallas_call(
        functools.partial(spread_kernel, groups),
        out_shape=jax.ShapeDtypeStruct((8, groups) + own.shape, own.dtype),
        in_specs=[inside],
        out_specs=inside,
        scratch_shapes=[
            pltpu.VMEM((groups,) + own.shape, own.dtype),
            dma((7,)),
            dma((7,)),
            dma((groups - 1,)),
            dma((groups - 1,)),
        ],
        compiler_params=pltpu.CompilerParams(collective_id=call_number, has_side_effects=True),
        name="spread",
    )(own)


def remote(index, source, target, device, send_sem, recv_sem):
    return pltpu.make_async_remote_copy(
        src_ref=source,
        dst_ref=target,
        send_sem=send_sem.at[index],
        recv_sem=recv_sem.at[index],
        device_id={"tok": device},
        device_id_type=MESH,
    )


def chunk_of(index, size):
    return pl.ds(pl.multiple_of(index * size, size), size)


CHUNK = 256
LINEAR = 0.7978845608
CUBIC = 0.044715


def gather_beside(own_ref, out_ref, send_sem, recv_sem, local_sem, use):
    half = own_ref.shape[0] // 2
    here, on_x, on_y, on_chip, corner = block_of_eight()
    shift = on_chip - here
    first, second = pl.ds(0, half), pl.ds(half, half)

    def copy(index, source, target, device):
        return remote(index, source, target, device, send_sem, recv_sem)

    greet((on_x, on_y, on_chip))
    own = pltpu.make_async_copy(own_ref, out_ref.at[here], local_sem)
    copies = [
        copy(0, own_ref, out_ref.at[here], on_x),
        copy(1, own_ref, out_ref.at[here], on_y),
        copy(2, own_ref, out_ref.at[here], on_chip),
        copy(3, out_ref.at[on_x, first], out_ref.at[on_x, first], on_y),
        copy(4, out_ref.at[on_x], out_ref.at[on_x], on_chip),
        copy(5, out_ref.at[on_y, second], out_ref.at[on_y, second], on_x),
        copy(6, out_ref.at[on_y], out_ref.at[on_y], on_chip),
        copy(7, out_ref.at[corner, first], out_ref.at[corner, first], on_chip),
        copy(8, out_ref.at[corner, second], out_ref.at[corner, second], on_chip),
    ]
    for index in range(3):
        copies[index].start()
    own.start()
    use(0, here)
    copies[2].wait_recv()
    use(1, on_chip)
    copies[0].wait_recv()
    copies[3].start()
    copies[4].start()
    copies[1].wait_recv()
    copies[5].start()
    copies[6].start()
    use(2, on_x)
    use(3, on_y)
    copies[4].wait_recv()
    use(4, on_x + shift)
    copies[6].wait_recv()
    use(5, on_y + shift)
    copies[3].wait_recv()
    copies[7].start()
    copies[5].wait_recv()
    copies[8].start()
    use(6, corner)
    copies[7].wait_recv()
    copies[8].wait_recv()
    use(7, corner + shift)
    own.wait()
    for each in copies:
        each.wait_send()


def up_kernel(
    own_ref,
    up_hbm,
    bias_ref,
    rows_ref,
    active_ref,
    slope_ref,
    up,
    rows,
    active,
    slope,
    send_sem,
    recv_sem,
    local_sem,
    weight_sem,
    row_sem,
    store_sem,
):
    weights = pltpu.make_async_copy(up_hbm, up, weight_sem)
    weights.start()
    stores = {}

    def use(place, block):
        slot = place % 2
        load = pltpu.make_async_copy(
            rows_ref.at[block] if place else own_ref, rows, row_sem
        )
        load.start()
        if place == 0:
            weights.wait()
        for each in stores.pop(slot, ()):
            each.wait()
        load.wait()

        @pl.loop(0, up.shape[1] // CHUNK)
        def _(turn):
            at = chunk_of(turn, CHUNK)
            value = plain_product(rows[...], up[:, at]) + bias_ref[:, at]
            square = value * value
            bent = jnp.tanh(value * (LINEAR + (LINEAR * CUBIC) * square))
            level = 0.5 + 0.5 * bent
            active[slot, :, at] = (value * level).astype(jnp.bfloat16)
            slope[slot, :, at] = (
                level
                + (0.5 * value)
                * (1.0 - bent * bent)
                * (LINEAR + (3.0 * LINEAR * CUBIC) * square)
            ).astype(jnp.bfloat16)

        stores[slot] = (
            pltpu.make_async_copy(active.at[slot], active_ref.at[block], store_sem.at[slot, 0]),
            pltpu.make_async_copy(slope.at[slot], slope_ref.at[block], store_sem.at[slot, 1]),
        )
        for each in stores[slot]:
            each.start()

    gather_beside(own_ref, rows_ref, send_sem, recv_sem, local_sem, use)
    for slot in (0, 1):
        for each in stores[slot]:
            each.wait()


def gather_and_up(own, up_cols, bias, call_number):
    token_rows, model_width = own.shape
    width = up_cols.shape[1]
    hidden = jax.ShapeDtypeStruct((8, token_rows, width), jnp.bfloat16)
    anywhere = pl.BlockSpec(memory_space=pl.ANY)
    dma = pltpu.SemaphoreType.DMA
    return pl.pallas_call(
        up_kernel,
        out_shape=(
            jax.ShapeDtypeStruct((8, token_rows, model_width), jnp.bfloat16),
            hidden,
            hidden,
        ),
        in_specs=[anywhere, anywhere, pl.BlockSpec(memory_space=pltpu.VMEM)],
        out_specs=(anywhere, anywhere, anywhere),
        scratch_shapes=[
            pltpu.VMEM(up_cols.shape, jnp.bfloat16),
            pltpu.VMEM((token_rows, model_width), jnp.bfloat16),
            pltpu.VMEM((2, token_rows, width), jnp.bfloat16),
            pltpu.VMEM((2, token_rows, width), jnp.bfloat16),
            dma((9,)),
            dma((9,)),
            dma,
            dma,
            dma,
            dma((2, 2)),
        ],
        compiler_params=pltpu.CompilerParams(
            collective_id=call_number, has_side_effects=True, vmem_limit_bytes=VMEM_BYTES
        ),
        cost_estimate=pl.CostEstimate(
            flops=16 * token_rows * model_width * width,
            bytes_accessed=150 * 1000 * 1000,
            transcendentals=0,
        ),
        name="gather_and_up",
    )(own, up_cols, bias.reshape(1, -1))


def grad_kernel(
    own_ref,
    down_hbm,
    active_ref,
    slope_ref,
    rows_ref,
    grad_ref,
    weight_ref,
    bias_ref,
    down,
    rows,
    across,
    active,
    slope,
    grads,
    sums,
    narrow,
    send_sem,
    recv_sem,
    local_sem,
    weight_sem,
    row_sem,
    load_sem,
    store_sem,
):
    weights = pltpu.make_async_copy(down_hbm, down, weight_sem)
    weights.start()
    stores = {}

    def use(place, block):
        slot = place % 2
        load = pltpu.make_async_copy(
            rows_ref.at[block] if place else own_ref, rows, row_sem
        )
        load.start()
        loads = (
            pltpu.make_async_copy(active_ref.at[block], active, load_sem.at[0]),
            pltpu.make_async_copy(slope_ref.at[block], slope, load_sem.at[1]),
        )
        for each in loads:
            each.start()
        if place == 0:
            weights.wait()
        if slot in stores:
            stores.pop(slot).wait()
        load.wait()
        for each in loads:
            each.wait()
        across[...] = jnp.transpose(rows[...])

        @pl.loop(0, down.shape[1] // CHUNK)
        def _(turn):
            at = chunk_of(turn, CHUNK)
            value = plain_product(rows[...], down[:, at]) * slope[:, at].astype(jnp.float32)
            value = value.astype(jnp.bfloat16)
            grads[slot, :, at] = value
            total = jnp.sum(value.astype(jnp.float32), axis=0, keepdims=True)
            weight = plain_product(across[...], active[:, at])
            if place == 0:
                bias_ref[:, at] = total
                sums[:, at] = weight
            elif place < 7:
                bias_ref[:, at] += total
                sums[:, at] += weight
            else:
                bias_ref[:, at] += total
                narrow[:, at] = (sums[:, at] + weight).astype(jnp.bfloat16)

        stores[slot] = pltpu.make_async_copy(
            grads.at[slot], grad_ref.at[block], store_sem.at[slot]
        )
        stores[slot].start()

    gather_beside(own_ref, rows_ref, send_sem, recv_sem, local_sem, use)
    last = pltpu.make_async_copy(narrow, weight_ref, weight_sem)
    last.start()
    for slot in (0, 1):
        stores[slot].wait()
    last.wait()


def gather_and_grad(own, down_cols, active, slope, call_number):
    token_rows, model_width = own.shape
    width = down_cols.shape[1]
    anywhere = pl.BlockSpec(memory_space=pl.ANY)
    dma = pltpu.SemaphoreType.DMA
    return pl.pallas_call(
        grad_kernel,
        out_shape=(
            jax.ShapeDtypeStruct((8, token_rows, model_width), jnp.bfloat16),
            jax.ShapeDtypeStruct((8, token_rows, width), jnp.bfloat16),
            jax.ShapeDtypeStruct((model_width, width), jnp.bfloat16),
            jax.ShapeDtypeStruct((1, width), jnp.float32),
        ),
        in_specs=[anywhere] * 4,
        out_specs=(anywhere, anywhere, anywhere, pl.BlockSpec(memory_space=pltpu.VMEM)),
        scratch_shapes=[
            pltpu.VMEM(down_cols.shape, jnp.bfloat16),
            pltpu.VMEM((token_rows, model_width), jnp.bfloat16),
            pltpu.VMEM((model_width, token_rows), jnp.bfloat16),
            pltpu.VMEM((token_rows, width), jnp.bfloat16),
            pltpu.VMEM((token_rows, width), jnp.bfloat16),
            pltpu.VMEM((2, token_rows, width), jnp.bfloat16),
            pltpu.VMEM((model_width, width), jnp.float32),
            pltpu.VMEM((model_width, width), jnp.bfloat16),
            dma((9,)),
            dma((9,)),
            dma,
            dma,
            dma,
            dma((2,)),
            dma((2,)),
        ],
        compiler_params=pltpu.CompilerParams(
            collective_id=call_number, has_side_effects=True, vmem_limit_bytes=VMEM_BYTES
        ),
        cost_estimate=pl.CostEstimate(
            flops=32 * token_rows * model_width * width,
            bytes_accessed=150 * 1000 * 1000,
            transcendentals=0,
        ),
        name="gather_and_grad",
    )(own, down_cols, active, slope)


def product_reduce_kernel(
    with_grad,
    narrow_ref,
    weight_hbm,
    *refs,
):
    if with_grad:
        wide_ref, out_ref, grad_ref, *refs = refs
        *refs, wide, across, sums, wide_sem = refs
    else:
        out_ref, *refs = refs
    (
        weight,
        narrow,
        sent,
        mine,
        theirs,
        relayed,
        final,
        send_sem,
        recv_sem,
        weight_sem,
        narrow_sem,
    ) = refs
    rows = narrow.shape[1]
    half = rows // 2
    here, on_x, on_y, on_chip, corner = block_of_eight()
    shift = on_chip - here
    first, second = pl.ds(0, half), pl.ds(half, half)
    load_weight = pltpu.make_async_copy(weight_hbm, weight, weight_sem)
    load_weight.start()

    def copy(index, source, target, device):
        return remote(index, source, target, device, send_sem, recv_sem)

    places = (corner, on_x, on_y, here)
    order = []
    for place in places:
        order += [place + shift, place]

    def fetch(turn):
        return pltpu.make_async_copy(
            narrow_ref.at[order[turn]], narrow.at[turn % 2], narrow_sem.at[turn % 2]
        )

    fetch(0).start()
    greet((on_x, on_y, on_chip))
    to_chip = [copy(index, sent.at[index], theirs.at[index], on_chip) for index in range(4)]
    step = 16

    def add_into(target, other, start, count):
        @pl.loop(0, count // step)
        def _(turn):
            at = pl.ds(pl.multiple_of(start + turn * step, step), step)
            come = pl.ds(pl.multiple_of(turn * step, step), step)
            total = target[at, :].astype(jnp.float32) + other[come, :].astype(jnp.float32)
            target[at, :] = total.astype(target.dtype)

    def join(index):
        to_chip[index].wait_recv()
        add_into(mine.at[index], theirs.at[index], 0, rows)

    corner_x = copy(4, mine.at[0, first], relayed.at[0], on_x)
    corner_y = copy(5, mine.at[0, second], relayed.at[1], on_y)
    x_first = copy(6, mine.at[1, first], final.at[0, first], on_x)
    y_second = copy(7, mine.at[2, second], final.at[1, second], on_y)
    x_second = copy(8, mine.at[1, second], final.at[0, second], on_x)
    y_first = copy(9, mine.at[2, first], final.at[1, first], on_y)

    for turn in range(8):
        pair, own = turn // 2, turn % 2
        if turn < 7:
            fetch(turn + 1).start()
        fetch(turn).wait()
        if turn == 0:
            load_weight.wait()
        target = mine.at[pair] if own else sent.at[pair]

        @pl.loop(0, weight.shape[0] // CHUNK)
        def _(piece):
            at = chunk_of(piece, CHUNK)
            target[:, at] = transposed_product(narrow[turn % 2], weight[at, :]).astype(
                jnp.bfloat16
            )

        if not own:
            to_chip[pair].start()
        if turn == 2:
            join(0)
            corner_x.start()
            corner_y.start()
        if turn == 4:
            join(1)
            x_first.start()
        if turn == 6:
            join(2)
            y_second.start()
    corner_y.wait_recv()
    add_into(mine.at[1], relayed.at[1], half, half)
    x_second.start()
    corner_x.wait_recv()
    add_into(mine.at[2], relayed.at[0], 0, half)
    y_first.start()
    join(3)

    if with_grad:
        def fetch_wide(turn):
            return pltpu.make_async_copy(
                wide_ref.at[order[turn]], wide.at[turn % 2], wide_sem.at[turn % 2]
            )

        fetch_wide(0).start()
        fetch(0).start()
        for turn in range(8):
            if turn < 7:
                fetch_wide(turn + 1).start()
                fetch(turn + 1).start()
            fetch_wide(turn).wait()
            fetch(turn).wait()
            across[...] = jnp.transpose(wide[turn % 2])

            @pl.loop(0, sums.shape[1] // CHUNK)
            def _(piece):
                at = chunk_of(piece, CHUNK)
                value = plain_product(across[...], narrow[turn % 2, :, at])
                if turn == 0:
                    sums[:, at] = value
                elif turn < 7:
                    sums[:, at] += value
                else:
                    weight[:, at] = (sums[:, at] + value).astype(jnp.bfloat16)

        store = pltpu.make_async_copy(weight, grad_ref, weight_sem)
        store.start()

    for each in (x_first, y_second, x_second, y_first):
        each.wait_recv()

    @pl.loop(0, rows // step)
    def _(turn):
        at = pl.ds(pl.multiple_of(turn * step, step), step)
        total = mine[3, at, :].astype(jnp.float32) + final[0, at, :].astype(jnp.float32)
        out_ref[at, :] = total + final[1, at, :].astype(jnp.float32)

    if with_grad:
        store.wait()
    for each in to_chip + [corner_x, corner_y, x_first, y_second, x_second, y_first]:
        each.wait_send()


def product_and_reduce(narrow, weight, wide, call_number):
    _, token_rows, width = narrow.shape
    model_width = weight.shape[0]
    with_grad = wide is not None
    anywhere = pl.BlockSpec(memory_space=pl.ANY)
    inside = pl.BlockSpec(memory_space=pltpu.VMEM)
    dma = pltpu.SemaphoreType.DMA
    block = (token_rows, model_width)
    kind = jnp.bfloat16
    out_shape = [jax.ShapeDtypeStruct(block, jnp.float32)]
    scratch = [
        pltpu.VMEM(weight.shape, kind),
        pltpu.VMEM((2, token_rows, width), kind),
        pltpu.VMEM((4,) + block, kind),
        pltpu.VMEM((4,) + block, kind),
        pltpu.VMEM((4,) + block, kind),
        pltpu.VMEM((2, token_rows // 2, model_width), kind),
        pltpu.VMEM((2,) + block, kind),
        dma((10,)),
        dma((10,)),
        dma,
        dma((2,)),
    ]
    operands = [narrow, weight]
    if with_grad:
        out_shape.append(jax.ShapeDtypeStruct(weight.shape, kind))
        scratch += [
            pltpu.VMEM((2,) + block, kind),
            pltpu.VMEM((model_width, token_rows), kind),
            pltpu.VMEM(weight.shape, jnp.float32),
            dma((2,)),
        ]
        operands.append(wide)
    return pl.pallas_call(
        functools.partial(product_reduce_kernel, with_grad),
        out_shape=tuple(out_shape),
        in_specs=[anywhere] * len(operands),
        out_specs=(inside, anywhere)[: len(out_shape)],
        scratch_shapes=scratch,
        compiler_params=pltpu.CompilerParams(
            collective_id=call_number, has_side_effects=True, vmem_limit_bytes=VMEM_BYTES
        ),
        cost_estimate=pl.CostEstimate(
            flops=(32 if with_grad else 16) * token_rows * model_width * width,
            bytes_accessed=150 * 1000 * 1000,
            transcendentals=0,
        ),
        name="product_and_reduce",
    )(*operands)


def peers_of(count):
    here = lax.axis_index("tok")
    return here, [(here + step) % count for step in range(1, count)]


def small_gather_kernel(count, own_ref, out_ref, send_sem, recv_sem, local_sem):
    here, peers = peers_of(count)
    rows = own_ref.shape[1]
    place = pl.ds(pl.multiple_of(here * rows, rows), rows)
    greet(peers)
    own = pltpu.make_async_copy(own_ref, out_ref.at[:, place, :], local_sem)
    copies = [
        pltpu.make_async_remote_copy(
            src_ref=own_ref,
            dst_ref=out_ref.at[:, place, :],
            send_sem=send_sem.at[index],
            recv_sem=recv_sem.at[index],
            device_id={"tok": peers[index]},
            device_id_type=MESH,
        )
        for index in range(count - 1)
    ]
    for each in copies:
        each.start()
    own.start()
    for each in copies:
        each.wait_recv()
    for each in copies:
        each.wait_send()
    own.wait()


def tok_gather_small(own, call_number, kernels):
    if not kernels:
        return lax.all_gather(own, "tok", axis=1, tiled=True)
    count = 8
    prompts, rows, columns = own.shape
    return pl.pallas_call(
        functools.partial(small_gather_kernel, count),
        out_shape=jax.ShapeDtypeStruct((prompts, count * rows, columns), own.dtype),
        in_specs=[pl.BlockSpec(memory_space=pl.ANY)],
        out_specs=pl.BlockSpec(memory_space=pl.ANY),
        scratch_shapes=[
            pltpu.SemaphoreType.DMA((count - 1,)),
            pltpu.SemaphoreType.DMA((count - 1,)),
            pltpu.SemaphoreType.DMA,
        ],
        compiler_params=pltpu.CompilerParams(collective_id=call_number, has_side_effects=True),
        name="tok_gather_small",
    )(own)


def small_reduce_kernel(count, part_ref, out_ref, come, send_sem, recv_sem):
    here, peers = peers_of(count)
    rows = come.shape[2]

    def place(device):
        return pl.ds(pl.multiple_of(device * rows, rows), rows)

    greet(peers)
    copies = [
        pltpu.make_async_remote_copy(
            src_ref=part_ref.at[:, place(peers[index]), :],
            dst_ref=come.at[index],
            send_sem=send_sem.at[index],
            recv_sem=recv_sem.at[index],
            device_id={"tok": peers[index]},
            device_id_type=MESH,
        )
        for index in range(count - 1)
    ]
    for each in copies:
        each.start()
    total = part_ref[:, place(here), :].astype(jnp.float32)
    for index in range(count - 1):
        copies[index].wait_recv()
        total = total + come[index].astype(jnp.float32)
    out_ref[...] = total.astype(out_ref.dtype)
    for each in copies:
        each.wait_send()


def tok_reduce_small(parts, call_number, kernels):
    if not kernels:
        return lax.psum_scatter(parts, "tok", scatter_dimension=1, tiled=True).astype(jnp.float32)
    count = 8
    prompts, rows, columns = parts.shape
    rows = rows // count
    return pl.pallas_call(
        functools.partial(small_reduce_kernel, count),
        out_shape=jax.ShapeDtypeStruct((prompts, rows, columns), jnp.float32),
        in_specs=[pl.BlockSpec(memory_space=pltpu.VMEM)],
        out_specs=pl.BlockSpec(memory_space=pltpu.VMEM),
        scratch_shapes=[
            pltpu.VMEM((count - 1, prompts, rows, columns), parts.dtype),
            pltpu.SemaphoreType.DMA((count - 1,)),
            pltpu.SemaphoreType.DMA((count - 1,)),
        ],
        compiler_params=pltpu.CompilerParams(
            collective_id=call_number, has_side_effects=True, vmem_limit_bytes=VMEM_BYTES
        ),
        name="tok_reduce_small",
    )(parts)


def final_reduce_kernel(
    groups,
    part_ref,
    small_ref,
    out_ref,
    small_out_ref,
    mine,
    theirs,
    relayed,
    final,
    come,
    small_come,
    small_total,
    small_across,
    send_sem,
    recv_sem,
    load_sem,
    across_send,
    across_recv,
    small_send,
    small_recv,
    small_across_send,
    small_across_recv,
):
    rows = part_ref.shape[1] // groups
    half = rows // 2
    small_rows = small_ref.shape[1] // groups
    here, on_x, on_y, on_chip, corner = block_of_eight()
    group = lax.axis_index("grp")
    shift = on_chip - here
    _, peers = peers_of(8)
    other_groups = [(group + turn) % groups for turn in range(1, groups)]
    step = 16

    greet_all(peers, other_groups)

    def copy(chunk, index, source, target, device):
        return pltpu.make_async_remote_copy(
            src_ref=source,
            dst_ref=target,
            send_sem=send_sem.at[chunk, index],
            recv_sem=recv_sem.at[chunk, index],
            device_id={"tok": device},
            device_id_type=MESH,
        )

    def add_into(target, other, start, count):
        @pl.loop(0, count // step)
        def _(turn):
            at = pl.ds(pl.multiple_of(start + turn * step, step), step)
            from_here = pl.ds(pl.multiple_of(turn * step, step), step)
            total = target[at, :].astype(jnp.float32) + other[from_here, :].astype(jnp.float32)
            target[at, :] = total.astype(target.dtype)

    places = (corner, on_x, on_y, here)
    first, second = pl.ds(0, half), pl.ds(half, half)
    to_chip, loads, others = [], [], []
    for chunk in range(groups):
        owner = (group + 1 + chunk) % groups
        span = pl.ds(pl.multiple_of(owner * rows, rows), rows)
        to_chip.append(
            [
                copy(
                    chunk,
                    index,
                    part_ref.at[places[index] + shift, span],
                    theirs.at[chunk, index],
                    on_chip,
                )
                for index in range(4)
            ]
        )
        loads.append(
            [
                pltpu.make_async_copy(
                    part_ref.at[places[index], span],
                    mine.at[chunk, index],
                    load_sem.at[chunk, index],
                )
                for index in range(4)
            ]
        )
        own, two = mine.at[chunk], final.at[chunk]
        others.append(
            {
                "corner_x": copy(chunk, 4, own.at[0, first], relayed.at[chunk, 0], on_x),
                "corner_y": copy(chunk, 5, own.at[0, second], relayed.at[chunk, 1], on_y),
                "x_first": copy(chunk, 6, own.at[1, first], two.at[0, first], on_x),
                "y_second": copy(chunk, 7, own.at[2, second], two.at[1, second], on_y),
                "x_second": copy(chunk, 8, own.at[1, second], two.at[0, second], on_x),
                "y_first": copy(chunk, 9, own.at[2, first], two.at[1, first], on_y),
            }
        )
    small_copies = [
        pltpu.make_async_remote_copy(
            src_ref=small_ref.at[peers[index]],
            dst_ref=small_come.at[index],
            send_sem=small_send.at[index],
            recv_sem=small_recv.at[index],
            device_id={"tok": peers[index]},
            device_id_type=MESH,
        )
        for index in range(len(peers))
    ]
    across = [
        pltpu.make_async_remote_copy(
            src_ref=mine.at[chunk, 3],
            dst_ref=come.at[chunk],
            send_sem=across_send.at[chunk],
            recv_sem=across_recv.at[chunk],
            device_id={"grp": other_groups[chunk]},
            device_id_type=MESH,
        )
        for chunk in range(groups - 1)
    ]
    small_over = [
        pltpu.make_async_remote_copy(
            src_ref=small_total.at[other_groups[chunk]],
            dst_ref=small_across.at[chunk],
            send_sem=small_across_send.at[chunk],
            recv_sem=small_across_recv.at[chunk],
            device_id={"grp": other_groups[chunk]},
            device_id_type=MESH,
        )
        for chunk in range(groups - 1)
    ]

    for chunk in range(groups):
        for index in range(4):
            to_chip[chunk][index].start()
            loads[chunk][index].start()
        if chunk == 0:
            for each in small_copies:
                each.start()

    def join(chunk, index):
        to_chip[chunk][index].wait_recv()
        loads[chunk][index].wait()
        add_into(mine.at[chunk, index], theirs.at[chunk, index], 0, rows)

    def open_chunk(chunk):
        join(chunk, 0)
        others[chunk]["corner_x"].start()
        others[chunk]["corner_y"].start()
        join(chunk, 1)
        others[chunk]["x_first"].start()
        join(chunk, 2)
        others[chunk]["y_second"].start()

    def relay_chunk(chunk):
        others[chunk]["corner_y"].wait_recv()
        add_into(mine.at[chunk, 1], relayed.at[chunk, 1], half, half)
        others[chunk]["x_second"].start()
        others[chunk]["corner_x"].wait_recv()
        add_into(mine.at[chunk, 2], relayed.at[chunk, 0], 0, half)
        others[chunk]["y_first"].start()

    def close_chunk(chunk):
        join(chunk, 3)
        for name in ("x_first", "y_second", "x_second", "y_first"):
            others[chunk][name].wait_recv()

        @pl.loop(0, rows // step)
        def _(turn):
            at = pl.ds(pl.multiple_of(turn * step, step), step)
            total = mine[chunk, 3, at, :].astype(jnp.float32)
            total = total + final[chunk, 0, at, :].astype(jnp.float32)
            total = total + final[chunk, 1, at, :].astype(jnp.float32)
            mine[chunk, 3, at, :] = total.astype(mine.dtype)

        if chunk < groups - 1:
            across[chunk].start()

    open_chunk(0)
    for chunk in range(1, groups):
        open_chunk(chunk)
        relay_chunk(chunk - 1)
        if chunk == 1:
            sums = small_ref[here]
            for index in range(len(peers)):
                small_copies[index].wait_recv()
                sums = sums + small_come[index]
            small_total[...] = sums.reshape(small_total.shape)
            for each in small_over:
                each.start()
        if chunk >= 2:
            close_chunk(chunk - 2)
    relay_chunk(groups - 1)
    close_chunk(groups - 2)
    close_chunk(groups - 1)
    for each in across:
        each.wait_recv()

    @pl.loop(0, rows // step)
    def _(turn):
        at = pl.ds(pl.multiple_of(turn * step, step), step)
        total = mine[groups - 1, 3, at, :].astype(jnp.float32)
        for chunk in range(groups - 1):
            total = total + come[chunk, at, :].astype(jnp.float32)
        out_ref[at, :] = total

    small_sum = small_total[group]
    for chunk in range(groups - 1):
        small_over[chunk].wait_recv()
        small_sum = small_sum + small_across[chunk]
    small_out_ref[...] = small_sum
    for chunk in range(groups):
        for each in to_chip[chunk] + list(others[chunk].values()):
            each.wait_send()
    for each in small_copies + across + small_over:
        each.wait_send()


def final_reduce(parts, small_parts, groups, call_number, kernels):
    if not kernels:
        sums = lax.psum_scatter(parts, "tok", scatter_dimension=0, tiled=False)
        sums = lax.psum_scatter(sums, "grp", scatter_dimension=0, tiled=True)
        small_sums = lax.psum_scatter(small_parts, "tok", scatter_dimension=0, tiled=False)
        small_sums = lax.psum_scatter(small_sums, "grp", scatter_dimension=0, tiled=True)
        return sums.astype(jnp.float32), small_sums
    _, rows, columns = parts.shape
    rows = rows // groups
    small_rows, small_columns = small_parts.shape[1] // groups, small_parts.shape[2]
    kind = parts.dtype
    dma = pltpu.SemaphoreType.DMA
    small = (small_rows, small_columns)
    return pl.pallas_call(
        functools.partial(final_reduce_kernel, groups),
        out_shape=(
            jax.ShapeDtypeStruct((rows, columns), jnp.float32),
            jax.ShapeDtypeStruct(small, jnp.float32),
        ),
        in_specs=[
            pl.BlockSpec(memory_space=pl.ANY),
            pl.BlockSpec(memory_space=pltpu.VMEM),
        ],
        out_specs=(
            pl.BlockSpec(memory_space=pltpu.VMEM),
            pl.BlockSpec(memory_space=pltpu.VMEM),
        ),
        scratch_shapes=[
            pltpu.VMEM((groups, 4, rows, columns), kind),
            pltpu.VMEM((groups, 4, rows, columns), kind),
            pltpu.VMEM((groups, 2, rows // 2, columns), kind),
            pltpu.VMEM((groups, 2, rows, columns), kind),
            pltpu.VMEM((groups - 1, rows, columns), kind),
            pltpu.VMEM((7, groups * small_rows, small_columns), jnp.float32),
            pltpu.VMEM((groups,) + small, jnp.float32),
            pltpu.VMEM((groups - 1,) + small, jnp.float32),
            dma((groups, 10)),
            dma((groups, 10)),
            dma((groups, 4)),
            dma((groups - 1,)),
            dma((groups - 1,)),
            dma((7,)),
            dma((7,)),
            dma((groups - 1,)),
            dma((groups - 1,)),
        ],
        compiler_params=pltpu.CompilerParams(
            collective_id=call_number, has_side_effects=True, vmem_limit_bytes=VMEM_BYTES
        ),
        name="final_reduce",
    )(parts, small_parts)


def stack_heads(values, heads):
    return jnp.concatenate(
        [values[:, head * HEAD_WIDTH : (head + 1) * HEAD_WIDTH] for head in range(heads)], axis=0
    )


def unstack_heads(values, heads):
    rows = values.shape[0] // heads
    return jnp.concatenate(
        [values[head * rows : (head + 1) * rows, :] for head in range(heads)], axis=1
    )


def part_rows(part, prompts, answers, token_ref, answer_ref):
    answer_rows = answer_ref.shape[0] // answers
    prompt_rows = (token_ref.shape[0] - answer_ref.shape[0]) // prompts
    if part < prompts:
        return slice(part * prompt_rows, (part + 1) * prompt_rows), prompt_rows
    start = prompts * prompt_rows + (part - prompts) * answer_rows
    return slice(start, start + answer_rows), answer_rows


def as_row(column):
    wide = jnp.broadcast_to(column, (column.shape[0], HEAD_WIDTH))
    return jnp.transpose(wide)[0:1, :]


def forward_block(
    prompts,
    answers,
    heads,
    start,
    owner_ref,
    normed_ref,
    query_block,
    bias,
    prompt_kv_ref,
    answer_kv_ref,
):
    width = HEAD_WIDTH
    scale = HEAD_WIDTH ** (-0.5)
    length = prompt_kv_ref.shape[1]
    queries = (plain_product(normed_ref[...], query_block) + bias).astype(jnp.bfloat16)
    pieces, logs = [], []
    for part in range(prompts + answers):
        here, rows = part_rows(part, prompts, answers, normed_ref, answer_kv_ref)
        token = lax.broadcasted_iota(jnp.int32, (heads * rows, 1), 0) % rows
        stacked = stack_heads(queries[here, :], heads)
        if part < prompts:
            keys = prompt_kv_ref[part, :, :width]
            values = prompt_kv_ref[part, :, width:]
            scores = transposed_product(stacked, keys)
            place = lax.broadcasted_iota(jnp.int32, (1, length), 1)
            scores = jnp.where(place <= start + token, scores, masked)
            top = jnp.max(scores, axis=-1, keepdims=True)
            exponent = jnp.exp((scores - top) * scale)
            total = jnp.sum(exponent, axis=-1, keepdims=True)
            mixed = plain_product(exponent.astype(jnp.bfloat16), values)
        else:
            answer = part - prompts
            owner = owner_ref[answer]
            own = slice(answer * rows, (answer + 1) * rows)
            keys = prompt_kv_ref[owner, :, :width]
            values = prompt_kv_ref[owner, :, width:]
            scores = transposed_product(stacked, keys)
            own_scores = transposed_product(stacked, answer_kv_ref[own, :width])
            place = lax.broadcasted_iota(jnp.int32, (1, rows), 1)
            own_scores = jnp.where(place <= token, own_scores, masked)
            top = jnp.maximum(
                jnp.max(scores, axis=-1, keepdims=True),
                jnp.max(own_scores, axis=-1, keepdims=True),
            )
            exponent = jnp.exp((scores - top) * scale)
            own_exponent = jnp.exp((own_scores - top) * scale)
            total = jnp.sum(exponent, axis=-1, keepdims=True) + jnp.sum(
                own_exponent, axis=-1, keepdims=True
            )
            mixed = plain_product(exponent.astype(jnp.bfloat16), values) + plain_product(
                own_exponent.astype(jnp.bfloat16), answer_kv_ref[own, width:]
            )
        pieces.append(unstack_heads((mixed / total).astype(jnp.bfloat16), heads))
        logs.append((here, rows, as_row(top * scale + jnp.log(total))))
    return queries, jnp.concatenate(pieces, axis=0), logs


def attention_forward_kernel(
    prompts,
    answers,
    heads,
    place_ref,
    owner_ref,
    normed_ref,
    query_ref,
    bias_ref,
    prompt_kv_ref,
    answer_kv_ref,
    output_ref,
    states_ref,
    offset_ref,
    gain_ref,
    shift_ref,
    queries_ref,
    mixture_ref,
    log_ref,
    hidden_ref,
    second_ref,
):
    step = pl.program_id(0)
    queries, mixture, logs = forward_block(
        prompts,
        answers,
        heads,
        place_ref[0],
        owner_ref,
        normed_ref,
        query_ref[0],
        bias_ref[0],
        prompt_kv_ref,
        answer_kv_ref,
    )
    queries_ref[0] = queries
    mixture_ref[0] = mixture
    for here, rows, log_row in logs:
        for head in range(heads):
            log_ref[0, head : head + 1, here] = log_row[:, head * rows : (head + 1) * rows]

    @pl.when(step == 0)
    def _():
        hidden_ref[...] = states_ref[...].astype(jnp.float32) + offset_ref[...]

    hidden_ref[...] += transposed_product(mixture, output_ref[0])

    @pl.when(step == pl.num_programs(0) - 1)
    def _():
        scaled, _ = norm_stats(hidden_ref[...])
        second_ref[...] = (scaled * gain_ref[...] + shift_ref[...]).astype(jnp.bfloat16)


def attention_forward(
    place,
    owning,
    normed,
    query_blocks,
    output_blocks,
    query_offset,
    prompt_kv,
    answer_kv,
    states,
    output_offset,
    gain,
    shift,
    prompts,
    answers,
):
    token_rows, model_width = normed.shape
    steps, _, block = query_blocks.shape
    heads = block // HEAD_WIDTH
    whole = lambda *shape: pl.BlockSpec(shape, lambda step, *_: (0,) * len(shape))
    one = lambda *shape: pl.BlockSpec((1,) + shape, lambda step, *_: (step, 0, 0))
    by_step = jax.ShapeDtypeStruct((steps, token_rows, block), jnp.bfloat16)
    return pl.pallas_call(
        functools.partial(attention_forward_kernel, prompts, answers, heads),
        out_shape=(
            by_step,
            by_step,
            jax.ShapeDtypeStruct((steps, heads, token_rows), jnp.float32),
            jax.ShapeDtypeStruct((token_rows, model_width), jnp.float32),
            jax.ShapeDtypeStruct((token_rows, model_width), jnp.bfloat16),
        ),
        grid_spec=pltpu.PrefetchScalarGridSpec(
            num_scalar_prefetch=2,
            grid=(steps,),
            in_specs=[
                whole(token_rows, model_width),
                one(model_width, block),
                one(1, block),
                whole(*prompt_kv.shape),
                whole(*answer_kv.shape),
                one(model_width, block),
                whole(token_rows, model_width),
                whole(1, model_width),
                whole(1, model_width),
                whole(1, model_width),
            ],
            out_specs=(
                one(token_rows, block),
                one(token_rows, block),
                one(heads, token_rows),
                whole(token_rows, model_width),
                whole(token_rows, model_width),
            ),
        ),
        compiler_params=pltpu.CompilerParams(vmem_limit_bytes=VMEM_BYTES),
        name="attention_forward",
    )(
        place,
        owning,
        normed,
        query_blocks,
        query_offset.reshape(steps, 1, block),
        prompt_kv,
        answer_kv,
        output_blocks,
        states,
        output_offset.reshape(1, -1),
        gain.reshape(1, -1),
        shift.reshape(1, -1),
    )


def bits_away(index):
    here = lax.axis_index("tok")
    core = (here + index) % 2
    across = (here // 2 + index // 2) % 2
    along = (here // 4 + index // 4) % 2
    return along * 4 + across * 2 + core


def gather_attention_kernel(
    prompts,
    answers,
    heads,
    prompt_rows,
    owner_ref,
    query_own_ref,
    output_own_ref,
    normed_ref,
    bias_ref,
    prompt_kv_ref,
    answer_kv_ref,
    states_ref,
    offset_ref,
    gain_ref,
    shift_ref,
    weights_ref,
    queries_ref,
    mixture_ref,
    log_ref,
    hidden_ref,
    second_ref,
    held,
    send_sem,
    recv_sem,
    local_sem,
    load_sem,
):
    here, on_x, on_y, on_chip, corner = block_of_eight()

    def copy(index, source, target, device):
        return remote(index, source, target, device, send_sem, recv_sem)

    own_refs = (query_own_ref, output_own_ref)
    to_x = [copy(0 + kind, own_refs[kind], weights_ref.at[here, kind], on_x) for kind in (0, 1)]
    to_y = [copy(2 + kind, own_refs[kind], weights_ref.at[here, kind], on_y) for kind in (0, 1)]
    to_chip = [
        copy(4 + kind, own_refs[kind], weights_ref.at[here, kind], on_chip) for kind in (0, 1)
    ]
    keep = [
        pltpu.make_async_copy(own_refs[kind], weights_ref.at[here, kind], local_sem.at[kind])
        for kind in (0, 1)
    ]
    x_to_y = copy(6, weights_ref.at[on_x, 0], weights_ref.at[on_x, 0], on_y)
    y_to_x = copy(7, weights_ref.at[on_y, 1], weights_ref.at[on_y, 1], on_x)
    x_to_chip = copy(8, weights_ref.at[on_x], weights_ref.at[on_x], on_chip)
    y_to_chip = copy(9, weights_ref.at[on_y], weights_ref.at[on_y], on_chip)
    corner_to_chip = [
        copy(10 + kind, weights_ref.at[corner, kind], weights_ref.at[corner, kind], on_chip)
        for kind in (0, 1)
    ]

    greet((on_x, on_y, on_chip))
    for each in (to_x[0], to_y[1], to_x[1], to_y[0], *to_chip, *keep):
        each.start()
    hidden_ref[...] = states_ref[...].astype(jnp.float32) + offset_ref[...]

    @pl.loop(0, 8)
    def _(turn):
        block = bits_away(turn)

        @pl.when(turn == 0)
        def _():
            for kind in (0, 1):
                load = pltpu.make_async_copy(own_refs[kind], held.at[kind], load_sem.at[kind])
                load.start()
                load.wait()

        @pl.when(turn == 1)
        def _():
            for each in to_chip:
                each.wait_recv()

        @pl.when(turn == 2)
        def _():
            to_x[0].wait_recv()
            x_to_y.start()
            to_y[1].wait_recv()
            y_to_x.start()
            to_x[1].wait_recv()
            x_to_chip.start()
            to_y[0].wait_recv()
            y_to_chip.start()

        @pl.when(turn == 3)
        def _():
            x_to_chip.wait_recv()

        @pl.when(turn == 5)
        def _():
            y_to_chip.wait_recv()

        @pl.when(turn == 6)
        def _():
            x_to_y.wait_recv()
            corner_to_chip[0].start()
            y_to_x.wait_recv()
            corner_to_chip[1].start()

        @pl.when(turn == 7)
        def _():
            for each in corner_to_chip:
                each.wait_recv()

        @pl.when(turn > 0)
        def _():
            for kind in (0, 1):
                pltpu.make_async_copy(
                    weights_ref.at[block, kind], held.at[kind], load_sem.at[kind]
                ).start()
            for kind in (0, 1):
                pltpu.make_async_copy(
                    weights_ref.at[block, kind], held.at[kind], load_sem.at[kind]
                ).wait()

        queries, mixture, logs = forward_block(
            prompts,
            answers,
            heads,
            here * prompt_rows,
            owner_ref,
            normed_ref,
            held[0],
            bias_ref[block],
            prompt_kv_ref,
            answer_kv_ref,
        )
        queries_ref[block] = queries
        mixture_ref[block] = mixture
        for place, rows, log_row in logs:
            for head in range(heads):
                log_ref[block, head : head + 1, place] = log_row[
                    :, head * rows : (head + 1) * rows
                ]
        hidden_ref[...] += transposed_product(mixture, held[1])

    scaled, _ = norm_stats(hidden_ref[...])
    second_ref[...] = (scaled * gain_ref[...] + shift_ref[...]).astype(jnp.bfloat16)
    for each in (*to_x, *to_y, *to_chip, x_to_y, y_to_x, x_to_chip, y_to_chip, *corner_to_chip):
        each.wait_send()
    for each in keep:
        each.wait()


def gather_attention(
    owning,
    query_own,
    output_own,
    normed,
    query_offset,
    prompt_kv,
    answer_kv,
    states,
    output_offset,
    gain,
    shift,
    prompts,
    answers,
    prompt_rows,
    call_number,
):
    token_rows, model_width = normed.shape
    block = query_own.shape[1]
    heads = block // HEAD_WIDTH
    inside = pl.BlockSpec(memory_space=pltpu.VMEM)
    anywhere = pl.BlockSpec(memory_space=pl.ANY)
    dma = pltpu.SemaphoreType.DMA
    by_step = jax.ShapeDtypeStruct((8, token_rows, block), jnp.bfloat16)
    return pl.pallas_call(
        functools.partial(gather_attention_kernel, prompts, answers, heads, prompt_rows),
        out_shape=(
            jax.ShapeDtypeStruct((8, 2, model_width, block), jnp.bfloat16),
            by_step,
            by_step,
            jax.ShapeDtypeStruct((8, heads, token_rows), jnp.float32),
            jax.ShapeDtypeStruct((token_rows, model_width), jnp.float32),
            jax.ShapeDtypeStruct((token_rows, model_width), jnp.bfloat16),
        ),
        in_specs=[pl.BlockSpec(memory_space=pltpu.SMEM), anywhere, anywhere] + [inside] * 8,
        out_specs=(anywhere,) + (inside,) * 5,
        scratch_shapes=[
            pltpu.VMEM((2, model_width, block), jnp.bfloat16),
            dma((12,)),
            dma((12,)),
            dma((2,)),
            dma((2,)),
        ],
        compiler_params=pltpu.CompilerParams(
            collective_id=call_number, has_side_effects=True, vmem_limit_bytes=VMEM_BYTES
        ),
        cost_estimate=pl.CostEstimate(
            flops=64 * token_rows * model_width * block,
            bytes_accessed=250 * 1000 * 1000,
            transcendentals=0,
        ),
        name="gather_attention",
    )(
        owning,
        query_own,
        output_own,
        normed,
        query_offset.reshape(8, 1, block),
        prompt_kv,
        answer_kv,
        states,
        output_offset.reshape(1, -1),
        gain.reshape(1, -1),
        shift.reshape(1, -1),
    )


def attention_backward_kernel(
    prompts,
    answers,
    heads,
    scale,
    place_ref,
    owner_ref,
    normed_ref,
    query_ref,
    prompt_kv_ref,
    answer_kv_ref,
    output_ref,
    branch_ref,
    queries_ref,
    mixture_ref,
    log_ref,
    grad_weights_ref,
    grad_normed_ref,
    grad_prompt_ref,
    grad_answer_ref,
    grad_bias_ref,
    normed_across,
    branch_across,
    key_sums,
    own_sums,
):
    step = pl.program_id(0)
    width = HEAD_WIDTH
    length = prompt_kv_ref.shape[1]
    block = queries_ref.shape[2]

    @pl.when(step == 0)
    def _():
        normed_across[...] = jnp.transpose(normed_ref[...])
        branch_across[...] = jnp.transpose(branch_ref[...])
        key_sums[...] = jnp.zeros_like(key_sums)
        own_sums[...] = jnp.zeros_like(own_sums)
        grad_normed_ref[...] = jnp.zeros_like(grad_normed_ref)

    query_block, output_block = query_ref[0, 0], output_ref[0, 0]
    weight_shape = (grad_weights_ref.shape[1], -1, block)
    weight_rows = query_block.shape[0] // grad_weights_ref.shape[1]
    grad_weights_ref[0, :, weight_rows : 2 * weight_rows] = (
        plain_product(branch_across[...], mixture_ref[0])
        .astype(jnp.bfloat16)
        .reshape(weight_shape)
    )
    grad_mixture = plain_product(branch_ref[...], output_block).astype(jnp.bfloat16)
    queries = queries_ref[0]
    mixture = mixture_ref[0]

    def backward(keys, values, stacked, grad_stacked, log_row, inner_row, allowed):
        scores = transposed_product(keys, stacked)
        probs = jnp.exp(scores * scale - log_row)
        if allowed is not None:
            probs = jnp.where(allowed, probs, 0.0)
        grad_values = plain_product(probs.astype(jnp.bfloat16), grad_stacked)
        grad_probs = transposed_product(values, grad_stacked)
        grad_scores = (probs * (grad_probs - inner_row)).astype(jnp.bfloat16)
        grad_keys = plain_product(grad_scores, stacked)
        grad_queries = weight_product(grad_scores, keys)
        return grad_queries, grad_keys, grad_values

    pieces = []
    for part in range(prompts + answers):
        here, rows = part_rows(part, prompts, answers, normed_ref, answer_kv_ref)
        token = lax.broadcasted_iota(jnp.int32, (1, heads * rows), 1) % rows
        stacked = stack_heads(queries[here, :], heads)
        grad_stacked = stack_heads(grad_mixture[here, :], heads)
        mixed = stack_heads(mixture[here, :], heads)
        product = grad_stacked.astype(jnp.float32) * mixed.astype(jnp.float32)
        inner_row = jnp.sum(jnp.transpose(product), axis=0, keepdims=True)
        log_row = jnp.concatenate(
            [log_ref[0, head : head + 1, here] for head in range(heads)], axis=1
        )
        if part < prompts:
            place = lax.broadcasted_iota(jnp.int32, (length, 1), 0)
            grad_queries, grad_keys, grad_values = backward(
                prompt_kv_ref[part, :, :width],
                prompt_kv_ref[part, :, width:],
                stacked,
                grad_stacked,
                log_row,
                inner_row,
                place <= place_ref[0] + token,
            )
            key_sums[part, :, :width] += grad_keys
            key_sums[part, :, width:] += grad_values
        else:
            answer = part - prompts
            owner = owner_ref[answer]
            own = slice(answer * rows, (answer + 1) * rows)
            grad_queries, grad_keys, grad_values = backward(
                prompt_kv_ref[owner, :, :width],
                prompt_kv_ref[owner, :, width:],
                stacked,
                grad_stacked,
                log_row,
                inner_row,
                None,
            )
            key_sums[owner, :, :width] += grad_keys
            key_sums[owner, :, width:] += grad_values
            place = lax.broadcasted_iota(jnp.int32, (rows, 1), 0)
            own_queries, own_keys, own_values = backward(
                answer_kv_ref[own, :width],
                answer_kv_ref[own, width:],
                stacked,
                grad_stacked,
                log_row,
                inner_row,
                place <= token,
            )
            grad_queries = grad_queries + own_queries
            own_sums[own, :width] += own_keys
            own_sums[own, width:] += own_values
        pieces.append(unstack_heads((grad_queries * scale).astype(jnp.bfloat16), heads))
    grad_queries = jnp.concatenate(pieces, axis=0)
    grad_weights_ref[0, :, :weight_rows] = (
        plain_product(normed_across[...], grad_queries).astype(jnp.bfloat16).reshape(weight_shape)
    )
    grad_normed_ref[...] += transposed_product(grad_queries, query_block)
    grad_bias_ref[0] = jnp.sum(grad_queries.astype(jnp.float32), axis=0, keepdims=True)

    @pl.when(step == pl.num_programs(0) - 1)
    def _():
        grad_prompt_ref[:, :, :width] = (key_sums[:, :, :width] * scale).astype(jnp.bfloat16)
        grad_prompt_ref[:, :, width:] = key_sums[:, :, width:].astype(jnp.bfloat16)
        grad_answer_ref[:, :width] = own_sums[:, :width] * scale
        grad_answer_ref[:, width:] = own_sums[:, width:]


def attention_backward(
    place,
    owning,
    normed,
    weights,
    groups,
    grad_rows,
    prompt_kv,
    answer_kv,
    branch,
    queries,
    mixture,
    log_total,
    prompts,
    answers,
):
    token_rows, model_width = normed.shape
    steps, _, _, block = weights.shape
    heads = block // HEAD_WIDTH
    length = prompt_kv.shape[1]
    whole = lambda *shape: pl.BlockSpec(shape, lambda step, *_: (0,) * len(shape))
    columns = lambda: pl.BlockSpec((1, token_rows, block), lambda step, *_: (step, 0, 0))
    kind = lambda which: pl.BlockSpec(
        (1, 1, model_width, block), lambda step, *_: (step, which, 0, 0)
    )
    scores = heads * token_rows * length
    return pl.pallas_call(
        functools.partial(
            attention_backward_kernel, prompts, answers, heads, HEAD_WIDTH ** (-0.5)
        ),
        out_shape=(
            jax.ShapeDtypeStruct((steps, groups, grad_rows, block), jnp.bfloat16),
            jax.ShapeDtypeStruct((token_rows, model_width), jnp.float32),
            jax.ShapeDtypeStruct(prompt_kv.shape, jnp.bfloat16),
            jax.ShapeDtypeStruct(answer_kv.shape, jnp.float32),
            jax.ShapeDtypeStruct((steps, 1, block), jnp.float32),
        ),
        grid_spec=pltpu.PrefetchScalarGridSpec(
            num_scalar_prefetch=2,
            grid=(steps,),
            in_specs=[
                whole(token_rows, model_width),
                kind(0),
                whole(*prompt_kv.shape),
                whole(*answer_kv.shape),
                kind(1),
                whole(token_rows, model_width),
                columns(),
                columns(),
                pl.BlockSpec((1, heads, token_rows), lambda step, *_: (step, 0, 0)),
            ],
            out_specs=(
                pl.BlockSpec(
                    (1, groups, grad_rows, block), lambda step, *_: (step, 0, 0, 0)
                ),
                whole(token_rows, model_width),
                whole(*prompt_kv.shape),
                whole(*answer_kv.shape),
                pl.BlockSpec((1, 1, block), lambda step, *_: (step, 0, 0)),
            ),
            scratch_shapes=[
                pltpu.VMEM((model_width, token_rows), jnp.bfloat16),
                pltpu.VMEM((model_width, token_rows), jnp.bfloat16),
                pltpu.VMEM(prompt_kv.shape, jnp.float32),
                pltpu.VMEM(answer_kv.shape, jnp.float32),
            ],
        ),
        compiler_params=pltpu.CompilerParams(vmem_limit_bytes=VMEM_BYTES),
        cost_estimate=pl.CostEstimate(
            flops=steps * (8 * token_rows * model_width * block + 20 * scores * HEAD_WIDTH),
            bytes_accessed=16 * steps * model_width * block,
            transcendentals=steps * scores,
        ),
        name="attention_backward",
    )(
        place,
        owning,
        normed,
        weights,
        prompt_kv,
        answer_kv,
        weights,
        branch,
        queries,
        mixture,
        log_total,
    )


def by_group(values):
    return jnp.swapaxes(values, 0, 1).reshape(-1)


def body(
    kernels,
    prompt_states,
    answer_states,
    answer_prompt,
    prompt_teacher,
    answer_teacher,
    prompt_valid,
    answer_valid,
    first_gain,
    first_shift,
    query_weight,
    query_bias,
    keyval_weight,
    value_bias,
    output_weight,
    output_bias,
    second_gain,
    second_shift,
    up_weight,
    up_bias,
    down_weight,
    down_bias,
):
    prompt_count, prompt_rows, model_width = prompt_states.shape
    answer_count, answer_len, _ = answer_states.shape
    groups = lax.axis_size("grp")
    token_devices = lax.axis_size("tok")
    token_index = lax.axis_index("tok")
    group_index = lax.axis_index("grp")
    own_prompt = prompt_rows * prompt_count
    token_rows = own_prompt + answer_count * answer_len
    hidden_units = up_bias.shape[0] * groups * token_devices
    ff_here = hidden_units // token_devices
    ff_start = token_index * ff_here
    share = first_gain.shape[0]
    block = query_weight.shape[1]
    weight_rows = query_weight.shape[0]
    keyval_rows, keyval_width = keyval_weight.shape

    def own_rows(prompt_part, answer_part):
        return jnp.concatenate(
            [prompt_part.reshape(own_prompt, -1), answer_part.reshape(-1, prompt_part.shape[-1])],
            axis=0,
        )

    states = own_rows(prompt_states, answer_states)
    inputs = states.astype(jnp.float32)
    valid_rows = jnp.concatenate([prompt_valid.reshape(-1), answer_valid.reshape(-1)])
    own_count = jnp.sum(valid_rows)
    valid_rows = valid_rows.astype(jnp.float32)

    up_cols = lax.all_gather(up_weight, "grp", axis=0, tiled=True)
    down_cols = lax.all_gather(down_weight, "grp", axis=0, tiled=True)

    query_own = lax.all_gather(query_weight, "grp", axis=0, tiled=True)
    output_own = lax.all_gather(output_weight, "grp", axis=0, tiled=True)
    count_parts = jnp.stack([own_count // 128, own_count % 128]).astype(jnp.bfloat16)
    smalls = jnp.concatenate(
        [
            first_gain,
            first_shift,
            query_bias,
            output_bias,
            second_gain,
            second_shift,
            down_bias,
            up_bias,
            count_parts,
        ]
    )
    smalls = jnp.pad(smalls, (0, SMALL_ROWS * block - smalls.shape[0])).reshape(SMALL_ROWS, block)
    pack = jnp.concatenate([keyval_weight.reshape(-1, block), smalls], axis=0)
    packed = spread(pack, groups, 0, kernels)
    keyval_pack = pack.shape[0] - SMALL_ROWS
    keyval_start = 2 * weight_rows
    keyval_full = jnp.swapaxes(
        packed[:, :, :keyval_pack].reshape(token_devices, groups, keyval_rows, keyval_width),
        0,
        1,
    ).reshape(model_width, keyval_width)
    small_full = packed[:, :, keyval_pack:].reshape(token_devices, groups, SMALL_ROWS * block)
    small_full = jnp.swapaxes(small_full.astype(jnp.float32), 0, 1)

    def vector(start, size):
        return small_full[:, :, start : start + size].reshape(-1)

    gain_one, shift_one, query_offset, output_offset, gain_two, shift_two, down_offset = (
        vector(index * share, share) for index in range(7)
    )
    up_offset = vector(7 * share, up_bias.shape[0])
    count_at = 7 * share + up_bias.shape[0]
    counts = small_full[:, :, count_at : count_at + 2]
    valid_count = jnp.sum(counts[:, :, 0]) * 128.0 + jnp.sum(counts[:, :, 1])
    up_here = lax.dynamic_slice_in_dim(up_offset, ff_start, ff_here)

    scaled_one, inverse_one = norm_stats(inputs)
    normed_one = (scaled_one * gain_one + shift_one).astype(jnp.bfloat16)
    key_offset = jnp.concatenate(
        [jnp.zeros((HEAD_WIDTH,), jnp.float32), value_bias.astype(jnp.float32)]
    )
    key_value_rows = (plain_product(normed_one, keyval_full) + key_offset).astype(jnp.bfloat16)
    prompt_kv = tok_gather_small(
        key_value_rows[:own_prompt].reshape(prompt_count, prompt_rows, -1), 1, kernels
    )
    answer_kv = key_value_rows[own_prompt:]
    owning = answer_prompt - group_index * prompt_count
    owning = lax.dynamic_slice_in_dim(owning, token_index * answer_count, answer_count)
    place = jnp.reshape(token_index * prompt_rows, (1,)).astype(jnp.int32)
    if kernels:
        weights, queries, mixture, log_total, hidden, normed_two = gather_attention(
            owning,
            query_own,
            output_own,
            normed_one,
            query_offset,
            prompt_kv,
            answer_kv,
            states,
            output_offset,
            gain_two,
            shift_two,
            prompt_count,
            answer_count,
            prompt_rows,
            8,
        )
    else:
        weights = lax.all_gather(jnp.stack([query_own, output_own]), "tok", axis=0)
        queries, mixture, log_total, hidden, normed_two = attention_forward(
            place,
            owning,
            normed_one,
            weights[:, 0],
            weights[:, 1],
            query_offset,
            prompt_kv,
            answer_kv,
            states,
            output_offset,
            gain_two,
            shift_two,
            prompt_count,
            answer_count,
        )

    if kernels:
        group_two, activated, slope = gather_and_up(normed_two, up_cols, up_here, 2)
        (feed_term,) = product_and_reduce(activated, down_cols, None, 3)
    else:
        group_two = lax.all_gather(normed_two, "tok", axis=0, tiled=True)
        pre_active = plain_product(group_two, up_cols) + up_here
        activated = jax.nn.gelu(pre_active, approximate=True).astype(jnp.bfloat16)
        feed_term = for_sending(transposed_product(activated, down_cols))
        feed_term = lax.psum_scatter(feed_term, "tok", scatter_dimension=0, tiled=True)
        feed_term = feed_term.astype(jnp.float32)
    result_rows = hidden + feed_term + down_offset

    teacher = own_rows(prompt_teacher, answer_teacher).astype(jnp.float32)
    differ = result_rows - teacher
    own_squares = jnp.sum(valid_rows[:, None] * differ * differ)
    every_token = token_rows * groups * token_devices
    grad_result = every_token / valid_count * valid_rows[:, None] * differ
    grad_branch_two = grad_result.astype(jnp.bfloat16)

    if kernels:
        _, grad_pre_active, grad_down_cols, grad_up_offset = gather_and_grad(
            grad_branch_two, down_cols, activated, slope, 4
        )
        grad_normed_two, grad_up_cols = product_and_reduce(grad_pre_active, up_cols, group_two, 5)
        grad_up_offset = grad_up_offset.reshape(-1)
    else:
        group_grad_two = lax.all_gather(grad_branch_two, "tok", axis=0, tiled=True)
        grad_activated = plain_product(group_grad_two, down_cols)
        _, gelu_back = jax.vjp(
            lambda argument: jax.nn.gelu(argument, approximate=True), pre_active
        )
        grad_pre_active = gelu_back(grad_activated)[0].astype(jnp.bfloat16)
        grad_normed_two = for_sending(transposed_product(grad_pre_active, up_cols))
        grad_normed_two = lax.psum_scatter(
            grad_normed_two, "tok", scatter_dimension=0, tiled=True
        ).astype(jnp.float32)
        grad_down_cols = for_sending(weight_product(group_grad_two, activated))
        grad_up_cols = for_sending(weight_product(group_two, grad_pre_active))
        grad_up_offset = column_sums(grad_pre_active)
    grad_down_weight = lax.psum_scatter(grad_down_cols, "grp", scatter_dimension=0, tiled=True)
    grad_up_weight = lax.psum_scatter(grad_up_cols, "grp", scatter_dimension=0, tiled=True)
    grad_down_offset = column_sums(grad_branch_two)
    scaled_two, inverse_two = norm_stats(hidden)
    grad_norm_two, grad_gain_two, grad_shift_two = norm_backward(
        grad_normed_two, gain_two, scaled_two, inverse_two
    )
    grad_hidden = grad_result + grad_norm_two
    grad_branch_one = grad_hidden.astype(jnp.bfloat16)
    grad_output_offset = column_sums(grad_branch_one)

    grad_rows = keyval_start + keyval_pack
    grad_weights, grad_normed_one, grad_prompt_kv, grad_answer_kv, grad_query_offset = (
        attention_backward(
            place,
            owning,
            normed_one,
            weights,
            groups,
            grad_rows,
            prompt_kv,
            answer_kv,
            grad_branch_one,
            queries,
            mixture,
            log_total,
            prompt_count,
            answer_count,
        )
    )
    grad_prompt_kv = tok_reduce_small(grad_prompt_kv, 6, kernels)
    grad_keyvals = jnp.concatenate(
        [grad_prompt_kv.reshape(own_prompt, -1), grad_answer_kv], axis=0
    ).astype(jnp.bfloat16)
    grad_keyval_full = weight_product(normed_one, grad_keyvals)
    grad_value_offset = column_sums(grad_keyvals[:, HEAD_WIDTH:])
    grad_normed_one = grad_normed_one + transposed_product(grad_keyvals, keyval_full)
    grad_norm_one, grad_gain_one, grad_shift_one = norm_backward(
        grad_normed_one, gain_one, scaled_one, inverse_one
    )
    grad_inputs = grad_hidden + grad_norm_one

    grad_keyval_blocks = jnp.swapaxes(
        grad_keyval_full.astype(jnp.bfloat16).reshape(groups, token_devices, -1, block), 0, 1
    )
    grad_weights = lax.dynamic_update_slice(
        grad_weights, grad_keyval_blocks, (0, 0, keyval_start, 0)
    )
    vectors = (
        grad_gain_one,
        grad_shift_one,
        grad_query_offset.reshape(-1),
        grad_output_offset,
        grad_gain_two,
        grad_shift_two,
        grad_down_offset,
        lax.dynamic_update_slice_in_dim(
            jnp.zeros((hidden_units,), jnp.float32), grad_up_offset, ff_start, 0
        ),
    )
    totals = jnp.concatenate([grad_value_offset, own_squares.reshape(1)])
    blocks = jnp.concatenate(
        [each.reshape(groups, token_devices, -1) for each in vectors]
        + [jnp.broadcast_to(totals, (groups, token_devices, totals.shape[0]))],
        axis=2,
    )
    blocks = jnp.pad(blocks, ((0, 0), (0, 0), (0, SMALL_SUMS - blocks.shape[2])))
    blocks = jnp.swapaxes(blocks, 0, 1).reshape(token_devices, -1, HEAD_WIDTH)
    grad_weights, small_sums = final_reduce(
        grad_weights.reshape(token_devices, -1, block), blocks, groups, 7, kernels
    )
    small_sums = small_sums.reshape(-1)
    up_share = up_bias.shape[0]
    totals_at = 7 * share + up_share
    value_total = small_sums[totals_at : totals_at + HEAD_WIDTH]
    squared_sum = small_sums[totals_at + HEAD_WIDTH]
    loss_value = squared_sum / (valid_count * model_width)

    def split_rows(values):
        values = values.astype(jnp.bfloat16)
        return (
            values[:own_prompt].reshape(prompt_states.shape),
            values[own_prompt:].reshape(answer_states.shape),
        )

    prompt_out, answer_out = split_rows(result_rows)
    prompt_grad, answer_grad = split_rows(grad_inputs)
    pieces = [small_sums[index * share : (index + 1) * share] for index in range(7)]
    return (
        prompt_out,
        answer_out,
        prompt_grad,
        answer_grad,
        pieces[0],
        pieces[1],
        grad_weights[:weight_rows],
        pieces[2],
        grad_weights[keyval_start:].reshape(keyval_rows, keyval_width),
        value_total,
        grad_weights[weight_rows:keyval_start],
        pieces[3],
        pieces[4],
        pieces[5],
        grad_up_weight.astype(jnp.float32),
        small_sums[7 * share : totals_at],
        grad_down_weight.astype(jnp.float32),
        pieces[6],
        loss_value,
    )


def solution(mesh):
    rows = P(("grp", "tok"))
    table = P(("grp", "tok"), None)
    matrix = P("grp", "tok")
    prompt_part = P("grp", "tok", None)
    answer_part = P(("grp", "tok"), None, None)
    in_specs = (
        prompt_part,
        answer_part,
        P("grp"),
        prompt_part,
        answer_part,
        P("grp", "tok"),
        table,
        rows,
        rows,
        matrix,
        rows,
        table,
        P(),
        matrix,
        rows,
        rows,
        rows,
        matrix,
        rows,
        matrix,
        rows,
    )
    out_specs = (
        prompt_part,
        answer_part,
        prompt_part,
        answer_part,
        rows,
        rows,
        matrix,
        rows,
        table,
        P(),
        matrix,
        rows,
        rows,
        rows,
        matrix,
        rows,
        matrix,
        rows,
        P(),
    )
    kernels = mesh.shape["tok"] == 8
    return jax.shard_map(
        functools.partial(body, kernels),
        mesh=mesh,
        in_specs=in_specs,
        out_specs=out_specs,
        check_vma=False,
    )
```

```python
import functools

import jax
import jax.numpy as jnp
from jax import lax
from jax.experimental import pallas as pl
from jax.experimental.pallas import tpu as pltpu
from jax.sharding import PartitionSpec as P

HEAD_WIDTH = 128
epsilon = 1e-05
masked = -1e30
MESH = pl.DeviceIdType.MESH
VMEM_BYTES = 56 * 1024 * 1024
SMALL_ROWS = 16
SMALL_SUMS = 1024


def for_sending(value):
    return value.astype(jnp.bfloat16)


def plain_product(left, right):
    return jnp.dot(left, right, preferred_element_type=jnp.float32)


def transposed_product(left, right):
    return lax.dot_general(
        left, right, (((1,), (1,)), ((), ())), preferred_element_type=jnp.float32
    )


def weight_product(left, right):
    return lax.dot_general(
        left, right, (((0,), (0,)), ((), ())), preferred_element_type=jnp.float32
    )


def norm_stats(values):
    center = values - jnp.mean(values, axis=-1, keepdims=True)
    inverse = lax.rsqrt(jnp.mean(center * center, axis=-1, keepdims=True) + epsilon)
    return center * inverse, inverse


def norm_backward(grad_out, gain, scaled, inverse):
    weighted = grad_out * gain
    grad_in = inverse * (
        weighted
        - jnp.mean(weighted, axis=-1, keepdims=True)
        - scaled * jnp.mean(weighted * scaled, axis=-1, keepdims=True)
    )
    return (grad_in, jnp.sum(grad_out * scaled, axis=0), jnp.sum(grad_out, axis=0))


def column_sums(values):
    return jnp.sum(values.astype(jnp.float32), axis=0)


def block_of_eight():
    here = lax.axis_index("tok")
    core, across, along = here % 2, (here // 2) % 2, here // 4
    on_x = here + 2 - 4 * across
    on_y = here + 4 - 8 * along
    on_chip = here + 1 - 2 * core
    corner = on_x + 4 - 8 * along
    return here, on_x, on_y, on_chip, corner


def greet_all(peers, other_groups):
    barrier = pltpu.get_barrier_semaphore()
    for peer in peers:
        pl.semaphore_signal(barrier, inc=1, device_id={"tok": peer}, device_id_type=MESH)
    for other in other_groups:
        pl.semaphore_signal(barrier, inc=1, device_id={"grp": other}, device_id_type=MESH)
    pl.semaphore_wait(barrier, len(peers) + len(other_groups))


def greet(devices):
    barrier = pltpu.get_barrier_semaphore()
    for device in devices:
        pl.semaphore_signal(barrier, inc=1, device_id={"tok": device}, device_id_type=MESH)
    pl.semaphore_wait(barrier, len(devices))


def spread_kernel(groups, own_ref, out_ref, held, send_sem, recv_sem, over_send, over_recv):
    here, peers = peers_of(8)
    group = lax.axis_index("grp")
    other_groups = [(group + turn) % groups for turn in range(1, groups)]
    greet_all(peers, other_groups)
    over = [
        pltpu.make_async_remote_copy(
            src_ref=own_ref,
            dst_ref=held.at[group],
            send_sem=over_send.at[index],
            recv_sem=over_recv.at[index],
            device_id={"grp": other},
            device_id_type=MESH,
        )
        for index, other in enumerate(other_groups)
    ]
    for each in over:
        each.start()
    held[group] = own_ref[...]
    for each in over:
        each.wait_recv()
    copies = [
        remote(index, held, out_ref.at[here], peer, send_sem, recv_sem)
        for index, peer in enumerate(peers)
    ]
    for each in copies:
        each.start()
    out_ref[here] = held[...]
    for each in copies:
        each.wait_recv()
    for each in copies + over:
        each.wait_send()


def spread(own, groups, call_number, kernels):
    if not kernels:
        return lax.all_gather(lax.all_gather(own, "grp", axis=0), "tok", axis=0)
    inside = pl.BlockSpec(memory_space=pltpu.VMEM)
    dma = pltpu.SemaphoreType.DMA
    return pl.pallas_call(
        functools.partial(spread_kernel, groups),
        out_shape=jax.ShapeDtypeStruct((8, groups) + own.shape, own.dtype),
        in_specs=[inside],
        out_specs=inside,
        scratch_shapes=[
            pltpu.VMEM((groups,) + own.shape, own.dtype),
            dma((7,)),
            dma((7,)),
            dma((groups - 1,)),
            dma((groups - 1,)),
        ],
        compiler_params=pltpu.CompilerParams(collective_id=call_number, has_side_effects=True),
        name="spread",
    )(own)


def remote(index, source, target, device, send_sem, recv_sem):
    return pltpu.make_async_remote_copy(
        src_ref=source,
        dst_ref=target,
        send_sem=send_sem.at[index],
        recv_sem=recv_sem.at[index],
        device_id={"tok": device},
        device_id_type=MESH,
    )


def chunk_of(index, size):
    return pl.ds(pl.multiple_of(index * size, size), size)


CHUNK = 512
LINEAR = 0.7978845608
CUBIC = 0.044715


def gather_beside(own_ref, out_ref, send_sem, recv_sem, local_sem, use):
    rows = own_ref.shape[0]
    half, quarter = rows // 2, rows // 4
    here, on_x, on_y, on_chip, corner = block_of_eight()
    shift = on_chip - here
    counter = iter(range(GATHER_COPIES))

    def copy(source, block, start, count, device):
        place = pl.ds(start, count)
        return remote(
            next(counter),
            source.at[place] if source is own_ref else source.at[block, place],
            out_ref.at[block, place],
            device,
            send_sem,
            recv_sem,
        )

    greet((on_x, on_y, on_chip))
    own = pltpu.make_async_copy(own_ref, out_ref.at[here], local_sem)
    x_low = copy(own_ref, here, 0, half, on_x)
    y_high = copy(own_ref, here, half, half, on_y)
    x_high = copy(own_ref, here, half, half, on_x)
    y_low = copy(own_ref, here, 0, half, on_y)
    to_chip = copy(own_ref, here, 0, rows, on_chip)
    to_y = [copy(out_ref, on_x, turn * quarter, quarter, on_y) for turn in (0, 1)]
    to_x = [copy(out_ref, on_y, half + turn * quarter, quarter, on_x) for turn in (0, 1)]
    chip_x = [copy(out_ref, on_x, turn * half, half, on_chip) for turn in (0, 1)]
    chip_y = [copy(out_ref, on_y, turn * half, half, on_chip) for turn in (0, 1)]
    chip_corner = [copy(out_ref, corner, turn * quarter, quarter, on_chip) for turn in range(4)]
    for each in (x_low, y_high, x_high, y_low, to_chip, own):
        each.start()
    use(0, [(here, 0, rows)])
    to_chip.wait_recv()
    use(1, [(on_chip, 0, rows)])
    x_low.wait_recv()
    for each in (*to_y, chip_x[0]):
        each.start()
    y_high.wait_recv()
    for each in (*to_x, chip_y[1]):
        each.start()
    use(2, [(on_x, 0, half), (on_y, half, half)])
    chip_x[0].wait_recv()
    chip_y[1].wait_recv()
    use(3, [(on_x + shift, 0, half), (on_y + shift, half, half)])
    x_high.wait_recv()
    chip_x[1].start()
    y_low.wait_recv()
    chip_y[0].start()
    use(4, [(on_x, half, half), (on_y, 0, half)])
    chip_x[1].wait_recv()
    chip_y[0].wait_recv()
    use(5, [(on_x + shift, half, half), (on_y + shift, 0, half)])
    for turn in (0, 1):
        to_y[turn].wait_recv()
        chip_corner[turn].start()
        to_x[turn].wait_recv()
        chip_corner[2 + turn].start()
        chip_corner[turn].wait_recv()
        chip_corner[2 + turn].wait_recv()
        use(
            6 + turn,
            [
                (block, start + turn * quarter, quarter)
                for block in (corner, corner + shift)
                for start in (0, half)
            ],
        )
    own.wait()
    for each in (x_low, y_high, x_high, y_low, to_chip, *to_y, *to_x, *chip_x, *chip_y, *chip_corner):
        each.wait_send()


GATHER_COPIES = 17


def moves(outside, inside, pieces, semaphores, outward):
    done, copies = 0, []
    for index, (block, start, count) in enumerate(pieces):
        away = outside.at[block, pl.ds(start, count)]
        near = inside.at[pl.ds(done, count)]
        pair = (near, away) if outward else (away, near)
        copies.append(pltpu.make_async_copy(*pair, semaphores.at[index]))
        done += count
    return copies


def up_kernel(
    own_ref,
    up_hbm,
    bias_ref,
    rows_ref,
    active_ref,
    slope_ref,
    up,
    rows,
    active,
    slope,
    send_sem,
    recv_sem,
    local_sem,
    weight_sem,
    row_sem,
    store_sem,
):
    weights = pltpu.make_async_copy(up_hbm, up, weight_sem)
    weights.start()
    stores = {}

    def use(place, pieces):
        slot = place % 2
        if place:
            loads = moves(rows_ref, rows, pieces, row_sem, False)
        else:
            loads = [pltpu.make_async_copy(own_ref, rows, row_sem.at[0])]
        for each in loads:
            each.start()
        if place == 0:
            weights.wait()
        for each in stores.pop(slot, ()):
            each.wait()
        for each in loads:
            each.wait()

        @pl.loop(0, up.shape[1] // CHUNK)
        def _(turn):
            at = chunk_of(turn, CHUNK)
            value = plain_product(rows[...], up[:, at]) + bias_ref[:, at]
            square = value * value
            bent = jnp.tanh(value * (LINEAR + (LINEAR * CUBIC) * square))
            level = 0.5 + 0.5 * bent
            active[slot, :, at] = (value * level).astype(jnp.bfloat16)
            slope[slot, :, at] = (
                level
                + (0.5 * value)
                * (1.0 - bent * bent)
                * (LINEAR + (3.0 * LINEAR * CUBIC) * square)
            ).astype(jnp.bfloat16)

        stores[slot] = moves(
            active_ref, active.at[slot], pieces, store_sem.at[slot, 0], True
        ) + moves(slope_ref, slope.at[slot], pieces, store_sem.at[slot, 1], True)
        for each in stores[slot]:
            each.start()

    gather_beside(own_ref, rows_ref, send_sem, recv_sem, local_sem, use)
    for slot in (0, 1):
        for each in stores[slot]:
            each.wait()


def gather_and_up(own, up_cols, bias, call_number):
    token_rows, model_width = own.shape
    width = up_cols.shape[1]
    hidden = jax.ShapeDtypeStruct((8, token_rows, width), jnp.bfloat16)
    anywhere = pl.BlockSpec(memory_space=pl.ANY)
    dma = pltpu.SemaphoreType.DMA
    return pl.pallas_call(
        up_kernel,
        out_shape=(
            jax.ShapeDtypeStruct((8, token_rows, model_width), jnp.bfloat16),
            hidden,
            hidden,
        ),
        in_specs=[anywhere, anywhere, pl.BlockSpec(memory_space=pltpu.VMEM)],
        out_specs=(anywhere, anywhere, anywhere),
        scratch_shapes=[
            pltpu.VMEM(up_cols.shape, jnp.bfloat16),
            pltpu.VMEM((token_rows, model_width), jnp.bfloat16),
            pltpu.VMEM((2, token_rows, width), jnp.bfloat16),
            pltpu.VMEM((2, token_rows, width), jnp.bfloat16),
            dma((GATHER_COPIES,)),
            dma((GATHER_COPIES,)),
            dma,
            dma,
            dma((4,)),
            dma((2, 2, 4)),
        ],
        compiler_params=pltpu.CompilerParams(
            collective_id=call_number, has_side_effects=True, vmem_limit_bytes=VMEM_BYTES
        ),
        cost_estimate=pl.CostEstimate(
            flops=16 * token_rows * model_width * width,
            bytes_accessed=150 * 1000 * 1000,
            transcendentals=0,
        ),
        name="gather_and_up",
    )(own, up_cols, bias.reshape(1, -1))


def grad_kernel(
    own_ref,
    down_hbm,
    active_ref,
    slope_ref,
    rows_ref,
    grad_ref,
    weight_ref,
    bias_ref,
    down,
    rows,
    active,
    slope,
    grads,
    sums,
    narrow,
    send_sem,
    recv_sem,
    local_sem,
    weight_sem,
    row_sem,
    load_sem,
    store_sem,
):
    weights = pltpu.make_async_copy(down_hbm, down, weight_sem)
    weights.start()
    stores = {}

    def use(place, pieces):
        slot = place % 2
        if place:
            loads = moves(rows_ref, rows, pieces, row_sem, False)
        else:
            loads = [pltpu.make_async_copy(own_ref, rows, row_sem.at[0])]
        loads += moves(active_ref, active, pieces, load_sem.at[0], False)
        loads += moves(slope_ref, slope, pieces, load_sem.at[1], False)
        for each in loads:
            each.start()
        if place == 0:
            weights.wait()
        for each in stores.pop(slot, ()):
            each.wait()
        for each in loads:
            each.wait()

        @pl.loop(0, down.shape[1] // CHUNK)
        def _(turn):
            at = chunk_of(turn, CHUNK)
            value = plain_product(rows[...], down[:, at]) * slope[:, at].astype(jnp.float32)
            value = value.astype(jnp.bfloat16)
            grads[slot, :, at] = value
            total = jnp.sum(value.astype(jnp.float32), axis=0, keepdims=True)
            weight = weight_product(rows[...], active[:, at])
            if place == 0:
                bias_ref[:, at] = total
                sums[:, at] = weight
            elif place < 7:
                bias_ref[:, at] += total
                sums[:, at] += weight
            else:
                bias_ref[:, at] += total
                narrow[:, at] = (sums[:, at] + weight).astype(jnp.bfloat16)

        stores[slot] = moves(grad_ref, grads.at[slot], pieces, store_sem.at[slot], True)
        for each in stores[slot]:
            each.start()

    gather_beside(own_ref, rows_ref, send_sem, recv_sem, local_sem, use)
    last = pltpu.make_async_copy(narrow, weight_ref, weight_sem)
    last.start()
    for slot in (0, 1):
        for each in stores[slot]:
            each.wait()
    last.wait()


def gather_and_grad(own, down_cols, active, slope, call_number):
    token_rows, model_width = own.shape
    width = down_cols.shape[1]
    anywhere = pl.BlockSpec(memory_space=pl.ANY)
    dma = pltpu.SemaphoreType.DMA
    return pl.pallas_call(
        grad_kernel,
        out_shape=(
            jax.ShapeDtypeStruct((8, token_rows, model_width), jnp.bfloat16),
            jax.ShapeDtypeStruct((8, token_rows, width), jnp.bfloat16),
            jax.ShapeDtypeStruct((model_width, width), jnp.bfloat16),
            jax.ShapeDtypeStruct((1, width), jnp.float32),
        ),
        in_specs=[anywhere] * 4,
        out_specs=(anywhere, anywhere, anywhere, pl.BlockSpec(memory_space=pltpu.VMEM)),
        scratch_shapes=[
            pltpu.VMEM(down_cols.shape, jnp.bfloat16),
            pltpu.VMEM((token_rows, model_width), jnp.bfloat16),
            pltpu.VMEM((token_rows, width), jnp.bfloat16),
            pltpu.VMEM((token_rows, width), jnp.bfloat16),
            pltpu.VMEM((2, token_rows, width), jnp.bfloat16),
            pltpu.VMEM((model_width, width), jnp.float32),
            pltpu.VMEM((model_width, width), jnp.bfloat16),
            dma((GATHER_COPIES,)),
            dma((GATHER_COPIES,)),
            dma,
            dma,
            dma((4,)),
            dma((2, 4)),
            dma((2, 4)),
        ],
        compiler_params=pltpu.CompilerParams(
            collective_id=call_number, has_side_effects=True, vmem_limit_bytes=VMEM_BYTES
        ),
        cost_estimate=pl.CostEstimate(
            flops=32 * token_rows * model_width * width,
            bytes_accessed=150 * 1000 * 1000,
            transcendentals=0,
        ),
        name="gather_and_grad",
    )(own, down_cols, active, slope)


def product_reduce_kernel(
    with_grad,
    narrow_ref,
    weight_hbm,
    *refs,
):
    if with_grad:
        wide_ref, out_ref, grad_ref, *refs = refs
        *refs, wide, across, sums, wide_sem = refs
    else:
        out_ref, *refs = refs
    (
        weight,
        narrow,
        sent,
        mine,
        theirs,
        relayed,
        final,
        send_sem,
        recv_sem,
        weight_sem,
        narrow_sem,
    ) = refs
    rows = narrow.shape[1]
    half = rows // 2
    here, on_x, on_y, on_chip, corner = block_of_eight()
    shift = on_chip - here
    first, second = pl.ds(0, half), pl.ds(half, half)
    load_weight = pltpu.make_async_copy(weight_hbm, weight, weight_sem)
    load_weight.start()

    def copy(index, source, target, device):
        return remote(index, source, target, device, send_sem, recv_sem)

    places = (corner, on_x, on_y, here)
    order = []
    for place in places:
        order += [place + shift, place]

    def fetch(turn):
        return pltpu.make_async_copy(
            narrow_ref.at[order[turn]], narrow.at[turn % 2], narrow_sem.at[turn % 2]
        )

    fetch(0).start()
    greet((on_x, on_y, on_chip))
    to_chip = [copy(index, sent.at[index], theirs.at[index], on_chip) for index in range(4)]
    step = 16

    def add_into(target, other, start, count):
        @pl.loop(0, count // step)
        def _(turn):
            at = pl.ds(pl.multiple_of(start + turn * step, step), step)
            come = pl.ds(pl.multiple_of(turn * step, step), step)
            total = target[at, :].astype(jnp.float32) + other[come, :].astype(jnp.float32)
            target[at, :] = total.astype(target.dtype)

    def join(index):
        to_chip[index].wait_recv()
        add_into(mine.at[index], theirs.at[index], 0, rows)

    corner_x = copy(4, mine.at[0, first], relayed.at[0], on_x)
    corner_y = copy(5, mine.at[0, second], relayed.at[1], on_y)
    x_first = copy(6, mine.at[1, first], final.at[0, first], on_x)
    y_second = copy(7, mine.at[2, second], final.at[1, second], on_y)
    x_second = copy(8, mine.at[1, second], final.at[0, second], on_x)
    y_first = copy(9, mine.at[2, first], final.at[1, first], on_y)

    for turn in range(8):
        pair, own = turn // 2, turn % 2
        if turn < 7:
            fetch(turn + 1).start()
        fetch(turn).wait()
        if turn == 0:
            load_weight.wait()
        target = mine.at[pair] if own else sent.at[pair]

        @pl.loop(0, weight.shape[0] // CHUNK)
        def _(piece):
            at = chunk_of(piece, CHUNK)
            target[:, at] = transposed_product(narrow[turn % 2], weight[at, :]).astype(
                jnp.bfloat16
            )

        if not own:
            to_chip[pair].start()
        if turn == 2:
            join(0)
            corner_x.start()
            corner_y.start()
        if turn == 4:
            join(1)
            x_first.start()
        if turn == 6:
            join(2)
            y_second.start()
    corner_y.wait_recv()
    add_into(mine.at[1], relayed.at[1], half, half)
    x_second.start()
    corner_x.wait_recv()
    add_into(mine.at[2], relayed.at[0], 0, half)
    y_first.start()
    join(3)

    if with_grad:
        def fetch_wide(turn):
            return pltpu.make_async_copy(
                wide_ref.at[order[turn]], wide.at[turn % 2], wide_sem.at[turn % 2]
            )

        fetch_wide(0).start()
        fetch(0).start()
        for turn in range(8):
            if turn < 7:
                fetch_wide(turn + 1).start()
                fetch(turn + 1).start()
            fetch_wide(turn).wait()
            fetch(turn).wait()
            across[...] = jnp.transpose(wide[turn % 2])

            @pl.loop(0, sums.shape[1] // CHUNK)
            def _(piece):
                at = chunk_of(piece, CHUNK)
                value = plain_product(across[...], narrow[turn % 2, :, at])
                if turn == 0:
                    sums[:, at] = value
                elif turn < 7:
                    sums[:, at] += value
                else:
                    weight[:, at] = (sums[:, at] + value).astype(jnp.bfloat16)

        store = pltpu.make_async_copy(weight, grad_ref, weight_sem)
        store.start()

    for each in (x_first, y_second, x_second, y_first):
        each.wait_recv()

    @pl.loop(0, rows // step)
    def _(turn):
        at = pl.ds(pl.multiple_of(turn * step, step), step)
        total = mine[3, at, :].astype(jnp.float32) + final[0, at, :].astype(jnp.float32)
        out_ref[at, :] = total + final[1, at, :].astype(jnp.float32)

    if with_grad:
        store.wait()
    for each in to_chip + [corner_x, corner_y, x_first, y_second, x_second, y_first]:
        each.wait_send()


def product_and_reduce(narrow, weight, wide, call_number):
    _, token_rows, width = narrow.shape
    model_width = weight.shape[0]
    with_grad = wide is not None
    anywhere = pl.BlockSpec(memory_space=pl.ANY)
    inside = pl.BlockSpec(memory_space=pltpu.VMEM)
    dma = pltpu.SemaphoreType.DMA
    block = (token_rows, model_width)
    kind = jnp.bfloat16
    out_shape = [jax.ShapeDtypeStruct(block, jnp.float32)]
    scratch = [
        pltpu.VMEM(weight.shape, kind),
        pltpu.VMEM((2, token_rows, width), kind),
        pltpu.VMEM((4,) + block, kind),
        pltpu.VMEM((4,) + block, kind),
        pltpu.VMEM((4,) + block, kind),
        pltpu.VMEM((2, token_rows // 2, model_width), kind),
        pltpu.VMEM((2,) + block, kind),
        dma((10,)),
        dma((10,)),
        dma,
        dma((2,)),
    ]
    operands = [narrow, weight]
    if with_grad:
        out_shape.append(jax.ShapeDtypeStruct(weight.shape, kind))
        scratch += [
            pltpu.VMEM((2,) + block, kind),
            pltpu.VMEM((model_width, token_rows), kind),
            pltpu.VMEM(weight.shape, jnp.float32),
            dma((2,)),
        ]
        operands.append(wide)
    return pl.pallas_call(
        functools.partial(product_reduce_kernel, with_grad),
        out_shape=tuple(out_shape),
        in_specs=[anywhere] * len(operands),
        out_specs=(inside, anywhere)[: len(out_shape)],
        scratch_shapes=scratch,
        compiler_params=pltpu.CompilerParams(
            collective_id=call_number, has_side_effects=True, vmem_limit_bytes=VMEM_BYTES
        ),
        cost_estimate=pl.CostEstimate(
            flops=(32 if with_grad else 16) * token_rows * model_width * width,
            bytes_accessed=150 * 1000 * 1000,
            transcendentals=0,
        ),
        name="product_and_reduce",
    )(*operands)


def peers_of(count):
    here = lax.axis_index("tok")
    return here, [(here + step) % count for step in range(1, count)]


def small_gather_kernel(count, own_ref, out_ref, send_sem, recv_sem, local_sem):
    here, peers = peers_of(count)
    rows = own_ref.shape[1]
    place = pl.ds(pl.multiple_of(here * rows, rows), rows)
    greet(peers)
    own = pltpu.make_async_copy(own_ref, out_ref.at[:, place, :], local_sem)
    copies = [
        pltpu.make_async_remote_copy(
            src_ref=own_ref,
            dst_ref=out_ref.at[:, place, :],
            send_sem=send_sem.at[index],
            recv_sem=recv_sem.at[index],
            device_id={"tok": peers[index]},
            device_id_type=MESH,
        )
        for index in range(count - 1)
    ]
    for each in copies:
        each.start()
    own.start()
    for each in copies:
        each.wait_recv()
    for each in copies:
        each.wait_send()
    own.wait()


def tok_gather_small(own, call_number, kernels):
    if not kernels:
        return lax.all_gather(own, "tok", axis=1, tiled=True)
    count = 8
    prompts, rows, columns = own.shape
    return pl.pallas_call(
        functools.partial(small_gather_kernel, count),
        out_shape=jax.ShapeDtypeStruct((prompts, count * rows, columns), own.dtype),
        in_specs=[pl.BlockSpec(memory_space=pl.ANY)],
        out_specs=pl.BlockSpec(memory_space=pl.ANY),
        scratch_shapes=[
            pltpu.SemaphoreType.DMA((count - 1,)),
            pltpu.SemaphoreType.DMA((count - 1,)),
            pltpu.SemaphoreType.DMA,
        ],
        compiler_params=pltpu.CompilerParams(collective_id=call_number, has_side_effects=True),
        name="tok_gather_small",
    )(own)


def stack_heads(values, heads):
    return jnp.concatenate(
        [values[:, head * HEAD_WIDTH : (head + 1) * HEAD_WIDTH] for head in range(heads)], axis=0
    )


def unstack_heads(values, heads):
    rows = values.shape[0] // heads
    return jnp.concatenate(
        [values[head * rows : (head + 1) * rows, :] for head in range(heads)], axis=1
    )


def part_rows(part, prompts, answers, token_ref, answer_ref):
    answer_rows = answer_ref.shape[0] // answers
    prompt_rows = (token_ref.shape[0] - answer_ref.shape[0]) // prompts
    if part < prompts:
        return slice(part * prompt_rows, (part + 1) * prompt_rows), prompt_rows
    start = prompts * prompt_rows + (part - prompts) * answer_rows
    return slice(start, start + answer_rows), answer_rows


def as_row(column):
    wide = jnp.broadcast_to(column, (column.shape[0], HEAD_WIDTH))
    return jnp.transpose(wide)[0:1, :]


def forward_block(
    prompts,
    answers,
    heads,
    start,
    owner_ref,
    normed_ref,
    query_block,
    bias,
    prompt_kv_ref,
    answer_kv_ref,
):
    width = HEAD_WIDTH
    scale = HEAD_WIDTH ** (-0.5)
    length = prompt_kv_ref.shape[1]
    queries = (plain_product(normed_ref[...], query_block) + bias).astype(jnp.bfloat16)
    pieces, logs = [], []
    for part in range(prompts + answers):
        here, rows = part_rows(part, prompts, answers, normed_ref, answer_kv_ref)
        token = lax.broadcasted_iota(jnp.int32, (heads * rows, 1), 0) % rows
        stacked = stack_heads(queries[here, :], heads)
        if part < prompts:
            keys = prompt_kv_ref[part, :, :width]
            values = prompt_kv_ref[part, :, width:]
            scores = transposed_product(stacked, keys)
            place = lax.broadcasted_iota(jnp.int32, (1, length), 1)
            scores = jnp.where(place <= start + token, scores, masked)
            top = jnp.max(scores, axis=-1, keepdims=True)
            exponent = jnp.exp((scores - top) * scale)
            total = jnp.sum(exponent, axis=-1, keepdims=True)
            mixed = plain_product(exponent.astype(jnp.bfloat16), values)
        else:
            answer = part - prompts
            owner = owner_ref[answer]
            own = slice(answer * rows, (answer + 1) * rows)
            keys = prompt_kv_ref[owner, :, :width]
            values = prompt_kv_ref[owner, :, width:]
            scores = transposed_product(stacked, keys)
            own_scores = transposed_product(stacked, answer_kv_ref[own, :width])
            place = lax.broadcasted_iota(jnp.int32, (1, rows), 1)
            own_scores = jnp.where(place <= token, own_scores, masked)
            top = jnp.maximum(
                jnp.max(scores, axis=-1, keepdims=True),
                jnp.max(own_scores, axis=-1, keepdims=True),
            )
            exponent = jnp.exp((scores - top) * scale)
            own_exponent = jnp.exp((own_scores - top) * scale)
            total = jnp.sum(exponent, axis=-1, keepdims=True) + jnp.sum(
                own_exponent, axis=-1, keepdims=True
            )
            mixed = plain_product(exponent.astype(jnp.bfloat16), values) + plain_product(
                own_exponent.astype(jnp.bfloat16), answer_kv_ref[own, width:]
            )
        pieces.append(unstack_heads((mixed / total).astype(jnp.bfloat16), heads))
        logs.append((here, rows, as_row(top * scale + jnp.log(total))))
    return queries, jnp.concatenate(pieces, axis=0), logs


def attention_forward_kernel(
    prompts,
    answers,
    heads,
    place_ref,
    owner_ref,
    normed_ref,
    query_ref,
    bias_ref,
    prompt_kv_ref,
    answer_kv_ref,
    output_ref,
    states_ref,
    offset_ref,
    gain_ref,
    shift_ref,
    queries_ref,
    mixture_ref,
    log_ref,
    hidden_ref,
    second_ref,
):
    step = pl.program_id(0)
    queries, mixture, logs = forward_block(
        prompts,
        answers,
        heads,
        place_ref[0],
        owner_ref,
        normed_ref,
        query_ref[0],
        bias_ref[0],
        prompt_kv_ref,
        answer_kv_ref,
    )
    queries_ref[0] = queries
    mixture_ref[0] = mixture
    for here, rows, log_row in logs:
        for head in range(heads):
            log_ref[0, head : head + 1, here] = log_row[:, head * rows : (head + 1) * rows]

    @pl.when(step == 0)
    def _():
        hidden_ref[...] = states_ref[...].astype(jnp.float32) + offset_ref[...]

    hidden_ref[...] += transposed_product(mixture, output_ref[0])

    @pl.when(step == pl.num_programs(0) - 1)
    def _():
        scaled, _ = norm_stats(hidden_ref[...])
        second_ref[...] = (scaled * gain_ref[...] + shift_ref[...]).astype(jnp.bfloat16)


def attention_forward(
    place,
    owning,
    normed,
    query_blocks,
    output_blocks,
    query_offset,
    prompt_kv,
    answer_kv,
    states,
    output_offset,
    gain,
    shift,
    prompts,
    answers,
):
    token_rows, model_width = normed.shape
    steps, _, block = query_blocks.shape
    heads = block // HEAD_WIDTH
    whole = lambda *shape: pl.BlockSpec(shape, lambda step, *_: (0,) * len(shape))
    one = lambda *shape: pl.BlockSpec((1,) + shape, lambda step, *_: (step, 0, 0))
    by_step = jax.ShapeDtypeStruct((steps, token_rows, block), jnp.bfloat16)
    return pl.pallas_call(
        functools.partial(attention_forward_kernel, prompts, answers, heads),
        out_shape=(
            by_step,
            by_step,
            jax.ShapeDtypeStruct((steps, heads, token_rows), jnp.float32),
            jax.ShapeDtypeStruct((token_rows, model_width), jnp.float32),
            jax.ShapeDtypeStruct((token_rows, model_width), jnp.bfloat16),
        ),
        grid_spec=pltpu.PrefetchScalarGridSpec(
            num_scalar_prefetch=2,
            grid=(steps,),
            in_specs=[
                whole(token_rows, model_width),
                one(model_width, block),
                one(1, block),
                whole(*prompt_kv.shape),
                whole(*answer_kv.shape),
                one(model_width, block),
                whole(token_rows, model_width),
                whole(1, model_width),
                whole(1, model_width),
                whole(1, model_width),
            ],
            out_specs=(
                one(token_rows, block),
                one(token_rows, block),
                one(heads, token_rows),
                whole(token_rows, model_width),
                whole(token_rows, model_width),
            ),
        ),
        compiler_params=pltpu.CompilerParams(vmem_limit_bytes=VMEM_BYTES),
        name="attention_forward",
    )(
        place,
        owning,
        normed,
        query_blocks,
        query_offset.reshape(steps, 1, block),
        prompt_kv,
        answer_kv,
        output_blocks,
        states,
        output_offset.reshape(1, -1),
        gain.reshape(1, -1),
        shift.reshape(1, -1),
    )


def bits_away(index):
    here = lax.axis_index("tok")
    core = (here + index) % 2
    across = (here // 2 + index // 2) % 2
    along = (here // 4 + index // 4) % 2
    return along * 4 + across * 2 + core


def gather_attention_kernel(
    prompts,
    answers,
    heads,
    prompt_rows,
    owner_ref,
    query_own_ref,
    output_own_ref,
    normed_ref,
    bias_ref,
    prompt_kv_ref,
    answer_kv_ref,
    states_ref,
    offset_ref,
    gain_ref,
    shift_ref,
    weights_ref,
    queries_ref,
    mixture_ref,
    log_ref,
    hidden_ref,
    second_ref,
    held,
    send_sem,
    recv_sem,
    local_sem,
    load_sem,
):
    here, on_x, on_y, on_chip, corner = block_of_eight()

    def copy(index, source, target, device):
        return remote(index, source, target, device, send_sem, recv_sem)

    own_refs = (query_own_ref, output_own_ref)
    to_x = [copy(0 + kind, own_refs[kind], weights_ref.at[here, kind], on_x) for kind in (0, 1)]
    to_y = [copy(2 + kind, own_refs[kind], weights_ref.at[here, kind], on_y) for kind in (0, 1)]
    to_chip = [
        copy(4 + kind, own_refs[kind], weights_ref.at[here, kind], on_chip) for kind in (0, 1)
    ]
    keep = [
        pltpu.make_async_copy(own_refs[kind], weights_ref.at[here, kind], local_sem.at[kind])
        for kind in (0, 1)
    ]
    x_to_y = copy(6, weights_ref.at[on_x, 0], weights_ref.at[on_x, 0], on_y)
    y_to_x = copy(7, weights_ref.at[on_y, 1], weights_ref.at[on_y, 1], on_x)
    x_to_chip = copy(8, weights_ref.at[on_x], weights_ref.at[on_x], on_chip)
    y_to_chip = copy(9, weights_ref.at[on_y], weights_ref.at[on_y], on_chip)
    corner_to_chip = [
        copy(10 + kind, weights_ref.at[corner, kind], weights_ref.at[corner, kind], on_chip)
        for kind in (0, 1)
    ]

    greet((on_x, on_y, on_chip))
    for each in (to_x[0], to_y[1], to_x[1], to_y[0], *to_chip, *keep):
        each.start()
    hidden_ref[...] = states_ref[...].astype(jnp.float32) + offset_ref[...]

    @pl.loop(0, 8)
    def _(turn):
        block = bits_away(turn)

        @pl.when(turn == 0)
        def _():
            for kind in (0, 1):
                load = pltpu.make_async_copy(own_refs[kind], held.at[kind], load_sem.at[kind])
                load.start()
                load.wait()

        @pl.when(turn == 1)
        def _():
            for each in to_chip:
                each.wait_recv()

        @pl.when(turn == 2)
        def _():
            to_x[0].wait_recv()
            x_to_y.start()
            to_y[1].wait_recv()
            y_to_x.start()
            to_x[1].wait_recv()
            x_to_chip.start()
            to_y[0].wait_recv()
            y_to_chip.start()

        @pl.when(turn == 3)
        def _():
            x_to_chip.wait_recv()

        @pl.when(turn == 5)
        def _():
            y_to_chip.wait_recv()

        @pl.when(turn == 6)
        def _():
            x_to_y.wait_recv()
            corner_to_chip[0].start()
            y_to_x.wait_recv()
            corner_to_chip[1].start()

        @pl.when(turn == 7)
        def _():
            for each in corner_to_chip:
                each.wait_recv()

        @pl.when(turn > 0)
        def _():
            for kind in (0, 1):
                pltpu.make_async_copy(
                    weights_ref.at[block, kind], held.at[kind], load_sem.at[kind]
                ).start()
            for kind in (0, 1):
                pltpu.make_async_copy(
                    weights_ref.at[block, kind], held.at[kind], load_sem.at[kind]
                ).wait()

        queries, mixture, logs = forward_block(
            prompts,
            answers,
            heads,
            here * prompt_rows,
            owner_ref,
            normed_ref,
            held[0],
            bias_ref[block],
            prompt_kv_ref,
            answer_kv_ref,
        )
        queries_ref[block] = queries
        mixture_ref[block] = mixture
        for place, rows, log_row in logs:
            for head in range(heads):
                log_ref[block, head : head + 1, place] = log_row[
                    :, head * rows : (head + 1) * rows
                ]
        hidden_ref[...] += transposed_product(mixture, held[1])

    scaled, _ = norm_stats(hidden_ref[...])
    second_ref[...] = (scaled * gain_ref[...] + shift_ref[...]).astype(jnp.bfloat16)
    for each in (*to_x, *to_y, *to_chip, x_to_y, y_to_x, x_to_chip, y_to_chip, *corner_to_chip):
        each.wait_send()
    for each in keep:
        each.wait()


def gather_attention(
    owning,
    query_own,
    output_own,
    normed,
    query_offset,
    prompt_kv,
    answer_kv,
    states,
    output_offset,
    gain,
    shift,
    prompts,
    answers,
    prompt_rows,
    call_number,
):
    token_rows, model_width = normed.shape
    block = query_own.shape[1]
    heads = block // HEAD_WIDTH
    inside = pl.BlockSpec(memory_space=pltpu.VMEM)
    anywhere = pl.BlockSpec(memory_space=pl.ANY)
    dma = pltpu.SemaphoreType.DMA
    by_step = jax.ShapeDtypeStruct((8, token_rows, block), jnp.bfloat16)
    return pl.pallas_call(
        functools.partial(gather_attention_kernel, prompts, answers, heads, prompt_rows),
        out_shape=(
            jax.ShapeDtypeStruct((8, 2, model_width, block), jnp.bfloat16),
            by_step,
            by_step,
            jax.ShapeDtypeStruct((8, heads, token_rows), jnp.float32),
            jax.ShapeDtypeStruct((token_rows, model_width), jnp.float32),
            jax.ShapeDtypeStruct((token_rows, model_width), jnp.bfloat16),
        ),
        in_specs=[pl.BlockSpec(memory_space=pltpu.SMEM), anywhere, anywhere] + [inside] * 8,
        out_specs=(anywhere,) + (inside,) * 5,
        scratch_shapes=[
            pltpu.VMEM((2, model_width, block), jnp.bfloat16),
            dma((12,)),
            dma((12,)),
            dma((2,)),
            dma((2,)),
        ],
        compiler_params=pltpu.CompilerParams(
            collective_id=call_number, has_side_effects=True, vmem_limit_bytes=VMEM_BYTES
        ),
        cost_estimate=pl.CostEstimate(
            flops=64 * token_rows * model_width * block,
            bytes_accessed=250 * 1000 * 1000,
            transcendentals=0,
        ),
        name="gather_attention",
    )(
        owning,
        query_own,
        output_own,
        normed,
        query_offset.reshape(8, 1, block),
        prompt_kv,
        answer_kv,
        states,
        output_offset.reshape(1, -1),
        gain.reshape(1, -1),
        shift.reshape(1, -1),
    )


def backward_block(
    prompts,
    answers,
    heads,
    start,
    owner_ref,
    share_ref,
    normed_ref,
    branch_ref,
    query_block,
    output_block,
    queries,
    mixture,
    log_ref,
    prompt_kv_ref,
    answer_kv_ref,
    normed_across,
    branch_across,
    key_sums,
    own_sums,
    grad_normed_ref,
):
    width = HEAD_WIDTH
    scale = HEAD_WIDTH ** (-0.5)
    length = prompt_kv_ref.shape[1]
    grad_output_block = plain_product(branch_across[...], mixture).astype(jnp.bfloat16)
    grad_mixture = plain_product(branch_ref[...], output_block).astype(jnp.bfloat16)

    def backward(keys, values, stacked, grad_stacked, log_row, inner_row, allowed):
        scores = transposed_product(keys, stacked)
        probs = jnp.exp(scores * scale - log_row)
        if allowed is not None:
            probs = jnp.where(allowed, probs, 0.0)
        grad_values = plain_product(probs.astype(jnp.bfloat16), grad_stacked)
        grad_probs = transposed_product(values, grad_stacked)
        grad_scores = (probs * (grad_probs - inner_row)).astype(jnp.bfloat16)
        grad_keys = plain_product(grad_scores, stacked)
        grad_queries = weight_product(grad_scores, keys)
        return grad_queries, grad_keys, grad_values

    pieces = []
    for part in range(prompts + answers):
        here, rows = part_rows(part, prompts, answers, normed_ref, answer_kv_ref)
        token = lax.broadcasted_iota(jnp.int32, (1, heads * rows), 1) % rows
        stacked = stack_heads(queries[here, :], heads)
        grad_stacked = stack_heads(grad_mixture[here, :], heads)
        mixed = stack_heads(mixture[here, :], heads)
        product = grad_stacked.astype(jnp.float32) * mixed.astype(jnp.float32)
        inner_row = jnp.sum(jnp.transpose(product), axis=0, keepdims=True)
        log_row = jnp.concatenate([log_ref[head : head + 1, here] for head in range(heads)], axis=1)
        if part < prompts:
            place = lax.broadcasted_iota(jnp.int32, (length, 1), 0)
            grad_queries, grad_keys, grad_values = backward(
                prompt_kv_ref[part, :, :width],
                prompt_kv_ref[part, :, width:],
                stacked,
                grad_stacked,
                log_row,
                inner_row,
                place <= start + token,
            )
            key_sums[part, :, :width] += grad_keys
            key_sums[part, :, width:] += grad_values
        else:
            answer = part - prompts
            owner = owner_ref[answer]
            own = slice(answer * rows, (answer + 1) * rows)
            grad_queries, grad_keys, grad_values = backward(
                prompt_kv_ref[owner, :, :width],
                prompt_kv_ref[owner, :, width:],
                stacked,
                grad_stacked,
                log_row,
                inner_row,
                None,
            )
            for prompt in range(prompts):
                share = share_ref[answer * prompts + prompt]
                key_sums[prompt, :, :width] += share * grad_keys
                key_sums[prompt, :, width:] += share * grad_values
            place = lax.broadcasted_iota(jnp.int32, (rows, 1), 0)
            own_queries, own_keys, own_values = backward(
                answer_kv_ref[own, :width],
                answer_kv_ref[own, width:],
                stacked,
                grad_stacked,
                log_row,
                inner_row,
                place <= token,
            )
            grad_queries = grad_queries + own_queries
            own_sums[own, :width] += own_keys
            own_sums[own, width:] += own_values
        pieces.append(unstack_heads((grad_queries * scale).astype(jnp.bfloat16), heads))
    grad_queries = jnp.concatenate(pieces, axis=0)
    grad_query_block = plain_product(normed_across[...], grad_queries).astype(jnp.bfloat16)
    grad_normed_ref[...] += transposed_product(grad_queries, query_block)
    grad_bias = jnp.sum(grad_queries.astype(jnp.float32), axis=0, keepdims=True)
    return grad_query_block, grad_output_block, grad_bias


def attention_backward_kernel(
    prompts,
    answers,
    heads,
    place_ref,
    owner_ref,
    share_ref,
    normed_ref,
    query_ref,
    prompt_kv_ref,
    answer_kv_ref,
    output_ref,
    branch_ref,
    queries_ref,
    mixture_ref,
    log_ref,
    grad_weights_ref,
    grad_normed_ref,
    grad_prompt_ref,
    grad_answer_ref,
    grad_bias_ref,
    normed_across,
    branch_across,
    key_sums,
    own_sums,
):
    step = pl.program_id(0)
    width = HEAD_WIDTH
    scale = HEAD_WIDTH ** (-0.5)
    block = queries_ref.shape[2]

    @pl.when(step == 0)
    def _():
        normed_across[...] = jnp.transpose(normed_ref[...])
        branch_across[...] = jnp.transpose(branch_ref[...])
        key_sums[...] = jnp.zeros_like(key_sums)
        own_sums[...] = jnp.zeros_like(own_sums)
        grad_normed_ref[...] = jnp.zeros_like(grad_normed_ref)

    query_block, output_block = query_ref[0, 0], output_ref[0, 0]
    groups = grad_weights_ref.shape[1]
    weight_rows = query_block.shape[0] // groups
    grad_query_block, grad_output_block, grad_bias = backward_block(
        prompts,
        answers,
        heads,
        place_ref[0],
        owner_ref,
        share_ref,
        normed_ref,
        branch_ref,
        query_block,
        output_block,
        queries_ref[0],
        mixture_ref[0],
        log_ref.at[0],
        prompt_kv_ref,
        answer_kv_ref,
        normed_across,
        branch_across,
        key_sums,
        own_sums,
        grad_normed_ref,
    )
    grad_weights_ref[0, :, :weight_rows] = grad_query_block.reshape(groups, weight_rows, block)
    grad_weights_ref[0, :, weight_rows : 2 * weight_rows] = grad_output_block.reshape(
        groups, weight_rows, block
    )
    grad_bias_ref[0] = grad_bias

    @pl.when(step == pl.num_programs(0) - 1)
    def _():
        grad_prompt_ref[:, :, :width] = (key_sums[:, :, :width] * scale).astype(jnp.bfloat16)
        grad_prompt_ref[:, :, width:] = key_sums[:, :, width:].astype(jnp.bfloat16)
        grad_answer_ref[:, :width] = own_sums[:, :width] * scale
        grad_answer_ref[:, width:] = own_sums[:, width:]


def attention_backward(
    place,
    owning,
    share,
    normed,
    weights,
    groups,
    grad_rows,
    prompt_kv,
    answer_kv,
    branch,
    queries,
    mixture,
    log_total,
    prompts,
    answers,
):
    token_rows, model_width = normed.shape
    steps, _, _, block = weights.shape
    heads = block // HEAD_WIDTH
    length = prompt_kv.shape[1]
    whole = lambda *shape: pl.BlockSpec(shape, lambda step, *_: (0,) * len(shape))
    columns = lambda: pl.BlockSpec((1, token_rows, block), lambda step, *_: (step, 0, 0))
    kind = lambda which: pl.BlockSpec(
        (1, 1, model_width, block), lambda step, *_: (step, which, 0, 0)
    )
    scores = heads * token_rows * length
    return pl.pallas_call(
        functools.partial(
            attention_backward_kernel, prompts, answers, heads
        ),
        out_shape=(
            jax.ShapeDtypeStruct((steps, groups, grad_rows, block), jnp.bfloat16),
            jax.ShapeDtypeStruct((token_rows, model_width), jnp.float32),
            jax.ShapeDtypeStruct(prompt_kv.shape, jnp.bfloat16),
            jax.ShapeDtypeStruct(answer_kv.shape, jnp.float32),
            jax.ShapeDtypeStruct((steps, 1, block), jnp.float32),
        ),
        grid_spec=pltpu.PrefetchScalarGridSpec(
            num_scalar_prefetch=3,
            grid=(steps,),
            in_specs=[
                whole(token_rows, model_width),
                kind(0),
                whole(*prompt_kv.shape),
                whole(*answer_kv.shape),
                kind(1),
                whole(token_rows, model_width),
                columns(),
                columns(),
                pl.BlockSpec((1, heads, token_rows), lambda step, *_: (step, 0, 0)),
            ],
            out_specs=(
                pl.BlockSpec(
                    (1, groups, grad_rows, block), lambda step, *_: (step, 0, 0, 0)
                ),
                whole(token_rows, model_width),
                whole(*prompt_kv.shape),
                whole(*answer_kv.shape),
                pl.BlockSpec((1, 1, block), lambda step, *_: (step, 0, 0)),
            ),
            scratch_shapes=[
                pltpu.VMEM((model_width, token_rows), jnp.bfloat16),
                pltpu.VMEM((model_width, token_rows), jnp.bfloat16),
                pltpu.VMEM(prompt_kv.shape, jnp.float32),
                pltpu.VMEM(answer_kv.shape, jnp.float32),
            ],
        ),
        compiler_params=pltpu.CompilerParams(vmem_limit_bytes=VMEM_BYTES),
        cost_estimate=pl.CostEstimate(
            flops=steps * (8 * token_rows * model_width * block + 20 * scores * HEAD_WIDTH),
            bytes_accessed=16 * steps * model_width * block,
            transcendentals=steps * scores,
        ),
        name="attention_backward",
    )(
        place,
        owning,
        share,
        normed,
        weights,
        prompt_kv,
        answer_kv,
        weights,
        branch,
        queries,
        mixture,
        log_total,
    )


VECTOR_ROWS = 16
KNOWN_ROWS = 8


def backward_reduce_kernel(
    prompts,
    answers,
    heads,
    groups,
    prompt_rows,
    owner_ref,
    share_ref,
    weights_ref,
    queries_ref,
    mixture_ref,
    hidden_hbm,
    normed_ref,
    branch_ref,
    log_ref,
    prompt_kv_ref,
    answer_kv_ref,
    states_ref,
    gain_ref,
    keyval_ref,
    known_ref,
    grad_query_ref,
    grad_output_ref,
    grad_keyval_ref,
    vectors_ref,
    grad_input_ref,
    normed_across,
    branch_across,
    key_sums,
    own_sums,
    grad_normed,
    grad_hidden,
    held,
    pair,
    kept,
    theirs,
    relayed,
    final,
    come,
    kv_part,
    kv_come,
    kv_rows,
    keyval_part,
    keyval_come,
    keyval_sum,
    keyval_over,
    vectors,
    vector_come,
    vector_sum,
    vector_over,
    send_sem,
    recv_sem,
    over_send,
    over_recv,
    peer_send,
    peer_recv,
    load_sem,
    hidden_sem,
):
    width = HEAD_WIDTH
    scale = HEAD_WIDTH ** (-0.5)
    here, on_x, on_y, on_chip, corner = block_of_eight()
    _, peers = peers_of(8)
    group = lax.axis_index("grp")
    other_groups = [(group + turn) % groups for turn in range(1, groups)]
    model_width, block = held.shape[1:]
    chunk_rows = model_width // groups
    step = 64
    counter = iter(range(4 + 6 * groups))

    def copy(source, target, device):
        return remote(next(counter), source, target, device, send_sem, recv_sem)

    def over(index, source, target, turn):
        return pltpu.make_async_remote_copy(
            src_ref=source,
            dst_ref=target,
            send_sem=over_send.at[index],
            recv_sem=over_recv.at[index],
            device_id={"grp": other_groups[turn]},
            device_id_type=MESH,
        )

    def to_peers(row, source, target):
        return [
            pltpu.make_async_remote_copy(
                src_ref=source(peers[index]),
                dst_ref=target(index),
                send_sem=peer_send.at[row, index],
                recv_sem=peer_recv.at[row, index],
                device_id={"tok": peers[index]},
                device_id_type=MESH,
            )
            for index in range(len(peers))
        ]

    spans = [
        pl.ds(pl.multiple_of(((group + 1 + chunk) % groups) * chunk_rows, chunk_rows), chunk_rows)
        for chunk in range(groups)
    ]
    chunks = range(groups)
    to_chip = [copy(kept.at[turn % 2], theirs.at[turn], on_chip) for turn in range(4)]
    corner_x = [copy(kept.at[2, 0, span], relayed.at[0, span], on_x) for span in spans]
    corner_y = [copy(kept.at[2, 1, span], relayed.at[1, span], on_y) for span in spans]
    x_first = [copy(kept.at[4, 0, span], final.at[0, 0, span], on_x) for span in spans]
    y_second = [copy(kept.at[3, 1, span], final.at[1, 1, span], on_y) for span in spans]
    x_second = [copy(kept.at[4, 1, span], final.at[0, 1, span], on_x) for span in spans]
    y_first = [copy(kept.at[3, 0, span], final.at[1, 0, span], on_y) for span in spans]
    across = [
        [over(2 * turn + kind, kept.at[5, kind, spans[turn]], come.at[turn, kind], turn) for kind in (0, 1)]
        for turn in range(groups - 1)
    ]

    def lanes(device):
        return pl.ds(pl.multiple_of(device * block, block), block)

    def prompt_place(device):
        return pl.ds(pl.multiple_of(device * prompt_rows, prompt_rows), prompt_rows)

    kv_copies = to_peers(
        0, lambda peer: kv_part.at[:, prompt_place(peer), :], lambda index: kv_come.at[index]
    )
    keyval_copies = to_peers(
        1, lambda peer: keyval_part.at[:, peer], lambda index: keyval_come.at[index]
    )
    vector_copies = to_peers(
        2, lambda peer: vectors.at[:, lanes(peer)], lambda index: vector_come.at[index]
    )
    vector_out = to_peers(
        3, lambda peer: vector_sum, lambda index: vectors_ref.at[:, lanes(here)]
    )
    first_over = 2 * (groups - 1)
    keyval_across = [
        over(first_over + turn, keyval_sum.at[other_groups[turn]], keyval_over.at[turn], turn)
        for turn in range(groups - 1)
    ]
    vector_across = [
        over(first_over + groups - 1 + turn, vectors.at[:, lanes(here)], vector_over.at[turn], turn)
        for turn in range(groups - 1)
    ]

    load_hidden = pltpu.make_async_copy(hidden_hbm, grad_hidden, hidden_sem)
    load_hidden.start()
    greet_all(peers, other_groups)
    normed_across[...] = jnp.transpose(normed_ref[...])
    branch_across[...] = jnp.transpose(branch_ref[...])
    key_sums[...] = jnp.zeros_like(key_sums)
    own_sums[...] = jnp.zeros_like(own_sums)
    grad_normed[...] = jnp.zeros_like(grad_normed)
    vectors[:KNOWN_ROWS, :] = known_ref[:KNOWN_ROWS, :]
    vectors[KNOWN_ROWS:, :] = known_ref[KNOWN_ROWS:, :]

    def add_into(target, other, rows):
        @pl.loop(0, rows // step)
        def _(turn):
            at = chunk_of(turn, step)
            total = target[at, :].astype(jnp.float32) + other[at, :].astype(jnp.float32)
            target[at, :] = total.astype(target.dtype)

    def join(turn):
        to_chip[turn].wait_recv()
        for kind in (0, 1):
            add_into(kept.at[2 + turn, kind], theirs.at[turn, kind], model_width)

    @pl.loop(0, 8)
    def _(turn):
        source = bits_away(7 - turn)
        slot = (turn % 2) * (2 + turn // 2) + (1 - turn % 2) * ((turn // 2) % 2)
        loads = (
            pltpu.make_async_copy(weights_ref.at[source], held, load_sem.at[0]),
            pltpu.make_async_copy(queries_ref.at[source], pair.at[0], load_sem.at[1]),
            pltpu.make_async_copy(mixture_ref.at[source], pair.at[1], load_sem.at[2]),
        )
        for each in loads:
            each.start()
        for index in (2, 3):

            @pl.when(turn == 2 * index)
            def _():
                to_chip[index - 2].wait_send()

        for each in loads:
            each.wait()
        grad_query_block, grad_output_block, grad_bias = backward_block(
            prompts,
            answers,
            heads,
            here * prompt_rows,
            owner_ref,
            share_ref,
            normed_ref,
            branch_ref,
            held[0],
            held[1],
            pair[0],
            pair[1],
            log_ref.at[source],
            prompt_kv_ref,
            answer_kv_ref,
            normed_across,
            branch_across,
            key_sums,
            own_sums,
            grad_normed,
        )
        kept[slot, 0] = grad_query_block
        kept[slot, 1] = grad_output_block
        vectors[10:11, lanes(source)] = grad_bias
        for index in range(4):

            @pl.when(turn == 2 * index)
            def _():
                to_chip[index].start()

        @pl.when(turn == 2)
        def _():
            join(0)
            for chunk in chunks:
                corner_x[chunk].start()
                corner_y[chunk].start()

        @pl.when(turn == 4)
        def _():
            join(1)
            for chunk in chunks[:2]:
                y_second[chunk].start()

        @pl.when(turn == 6)
        def _():
            join(2)
            for chunk in chunks[:2]:
                x_first[chunk].start()

    kv_part[:, :, :width] = (key_sums[:, :, :width] * scale).astype(jnp.bfloat16)
    kv_part[:, :, width:] = key_sums[:, :, width:].astype(jnp.bfloat16)
    for each in kv_copies:
        each.start()
    for chunk in chunks:
        span = spans[chunk]
        corner_y[chunk].wait_recv()
        add_into(kept.at[4, 1, span], relayed.at[1, span], chunk_rows)
        x_second[chunk].start()
        corner_x[chunk].wait_recv()
        add_into(kept.at[3, 0, span], relayed.at[0, span], chunk_rows)
        y_first[chunk].start()
        if chunk + 2 < groups:
            x_first[chunk + 2].start()
            y_second[chunk + 2].start()
    join(3)

    def close(chunk):
        span = spans[chunk]
        for kind, parts in ((0, (x_first, y_first)), (1, (x_second, y_second))):
            for part in parts:
                part[chunk].wait_recv()
            for turn in (0, 1):
                add_into(kept.at[5, kind, span], final.at[turn, kind, span], chunk_rows)
            if chunk < groups - 1:
                across[chunk][kind].start()

    for each in kv_copies:
        each.wait_recv()
    own_prompt = prompts * prompt_rows
    for prompt in range(prompts):
        total = kv_part[prompt, prompt_place(here), :].astype(jnp.float32)
        for index in range(len(peers)):
            total = total + kv_come[index, prompt].astype(jnp.float32)
        kv_rows[prompt * prompt_rows : (prompt + 1) * prompt_rows, :] = total.astype(jnp.bfloat16)
    kv_rows[own_prompt:, :width] = (own_sums[:, :width] * scale).astype(jnp.bfloat16)
    kv_rows[own_prompt:, width:] = own_sums[:, width:].astype(jnp.bfloat16)
    keyval_part[...] = (
        plain_product(normed_across[...], kv_rows[...])
        .astype(jnp.bfloat16)
        .reshape(keyval_part.shape)
    )
    for each in keyval_copies:
        each.start()
    close(0)
    load_hidden.wait()
    vectors[11:12, :width] = jnp.sum(
        kv_rows[:, width:].astype(jnp.float32), axis=0, keepdims=True
    )
    piece = 64
    vectors[8:10, :] = jnp.zeros((2, model_width), jnp.float32)

    @pl.loop(0, states_ref.shape[0] // piece)
    def _(turn):
        at = chunk_of(turn, piece)
        scaled, inverse = norm_stats(states_ref[at, :].astype(jnp.float32))
        grad_out = grad_normed[at, :] + transposed_product(kv_rows[at, :], keyval_ref[...])
        weighted = grad_out * gain_ref[...]
        grad_in = inverse * (
            weighted
            - jnp.mean(weighted, axis=-1, keepdims=True)
            - scaled * jnp.mean(weighted * scaled, axis=-1, keepdims=True)
        )
        grad_input_ref[at, :] = (grad_hidden[at, :] + grad_in).astype(jnp.bfloat16)
        vectors[8:9, :] += jnp.sum(grad_out * scaled, axis=0, keepdims=True)
        vectors[9:10, :] += jnp.sum(grad_out, axis=0, keepdims=True)

    for each in vector_copies:
        each.start()
    close(1)
    for each in keyval_copies:
        each.wait_recv()
    for other in range(groups):
        total = keyval_part[other, here].astype(jnp.float32)
        for index in range(len(peers)):
            total = total + keyval_come[index, other].astype(jnp.float32)
        keyval_sum[other] = total.astype(jnp.bfloat16)
    for each in keyval_across:
        each.start()
    for each in vector_copies:
        each.wait_recv()
    total = vectors[:, lanes(here)]
    for index in range(len(peers)):
        total = total + vector_come[index]
    vectors[:, lanes(here)] = total
    for each in vector_across:
        each.start()
    close(2)
    for each in vector_across:
        each.wait_recv()
    total = vectors[:, lanes(here)]
    for turn in range(groups - 1):
        total = total + vector_over[turn]
    vector_sum[...] = total
    for each in vector_out:
        each.start()
    vectors_ref[:, lanes(here)] = vector_sum[...]
    for chunk in chunks[3:]:
        close(chunk)
    for each in keyval_across:
        each.wait_recv()
    total = keyval_sum[group].astype(jnp.float32)
    for turn in range(groups - 1):
        total = total + keyval_over[turn].astype(jnp.float32)
    grad_keyval_ref[...] = total
    for kind, out_ref in ((0, grad_query_ref), (1, grad_output_ref)):
        for turn in range(groups - 1):
            across[turn][kind].wait_recv()
        own = pl.multiple_of(group * chunk_rows, chunk_rows)

        @pl.loop(0, chunk_rows // step)
        def _(turn):
            at = chunk_of(turn, step)
            total = kept[5, kind, pl.ds(own + turn * step, step), :].astype(jnp.float32)
            for other in range(groups - 1):
                total = total + come[other, kind, at, :].astype(jnp.float32)
            out_ref[at, :] = total

    for each in vector_out:
        each.wait_recv()
    for each in to_chip[2:] + corner_x + corner_y + x_first + y_second + x_second + y_first:
        each.wait_send()
    for each in kv_copies + keyval_copies + vector_copies + vector_out:
        each.wait_send()
    for each in sum(across, []) + keyval_across + vector_across:
        each.wait_send()


def backward_reduce(
    owning,
    share,
    weights,
    queries,
    mixture,
    grad_hidden,
    normed,
    branch,
    log_total,
    prompt_kv,
    answer_kv,
    states,
    gain,
    keyval_full,
    known,
    groups,
    prompts,
    answers,
    prompt_rows,
    call_number,
):
    token_rows, model_width = normed.shape
    block = weights.shape[3]
    heads = block // HEAD_WIDTH
    keyval_width = keyval_full.shape[1]
    weight_rows = model_width // groups
    keyval_rows = model_width // groups // 8
    kind, wide = jnp.bfloat16, jnp.float32
    inside = pl.BlockSpec(memory_space=pltpu.VMEM)
    anywhere = pl.BlockSpec(memory_space=pl.ANY)
    scalars = pl.BlockSpec(memory_space=pltpu.SMEM)
    dma = pltpu.SemaphoreType.DMA
    others = groups - 1
    return pl.pallas_call(
        functools.partial(backward_reduce_kernel, prompts, answers, heads, groups, prompt_rows),
        out_shape=(
            jax.ShapeDtypeStruct((weight_rows, block), wide),
            jax.ShapeDtypeStruct((weight_rows, block), wide),
            jax.ShapeDtypeStruct((keyval_rows, keyval_width), wide),
            jax.ShapeDtypeStruct((VECTOR_ROWS, model_width), wide),
            jax.ShapeDtypeStruct((token_rows, model_width), kind),
        ),
        in_specs=[scalars] * 2 + [anywhere] * 4 + [inside] * 9,
        out_specs=(inside,) * 5,
        scratch_shapes=[
            pltpu.VMEM((model_width, token_rows), kind),
            pltpu.VMEM((model_width, token_rows), kind),
            pltpu.VMEM(prompt_kv.shape, wide),
            pltpu.VMEM(answer_kv.shape, wide),
            pltpu.VMEM((token_rows, model_width), wide),
            pltpu.VMEM((token_rows, model_width), wide),
            pltpu.VMEM((2, model_width, block), kind),
            pltpu.VMEM((2, token_rows, block), kind),
            pltpu.VMEM((6, 2, model_width, block), kind),
            pltpu.VMEM((4, 2, model_width, block), kind),
            pltpu.VMEM((2, model_width, block), kind),
            pltpu.VMEM((2, 2, model_width, block), kind),
            pltpu.VMEM((others, 2, weight_rows, block), kind),
            pltpu.VMEM(prompt_kv.shape, kind),
            pltpu.VMEM((7, prompts, prompt_rows, keyval_width), kind),
            pltpu.VMEM((token_rows, keyval_width), kind),
            pltpu.VMEM((groups, 8, keyval_rows, keyval_width), kind),
            pltpu.VMEM((7, groups, keyval_rows, keyval_width), kind),
            pltpu.VMEM((groups, keyval_rows, keyval_width), kind),
            pltpu.VMEM((others, keyval_rows, keyval_width), kind),
            pltpu.VMEM((VECTOR_ROWS, model_width), wide),
            pltpu.VMEM((7, VECTOR_ROWS, block), wide),
            pltpu.VMEM((VECTOR_ROWS, block), wide),
            pltpu.VMEM((others, VECTOR_ROWS, block), wide),
            dma((4 + 6 * groups,)),
            dma((4 + 6 * groups,)),
            dma((4 * others,)),
            dma((4 * others,)),
            dma((4, 7)),
            dma((4, 7)),
            dma((3,)),
            dma,
        ],
        compiler_params=pltpu.CompilerParams(
            collective_id=call_number,
            has_side_effects=True,
            vmem_limit_bytes=63 * 1024 * 1024,
        ),
        cost_estimate=pl.CostEstimate(
            flops=100 * token_rows * model_width * block,
            bytes_accessed=250 * 1000 * 1000,
            transcendentals=0,
        ),
        name="backward_reduce",
    )(
        owning,
        share,
        weights,
        queries,
        mixture,
        grad_hidden,
        normed,
        branch,
        log_total,
        prompt_kv,
        answer_kv,
        states,
        gain.reshape(1, -1),
        keyval_full,
        known,
    )


def by_group(values):
    return jnp.swapaxes(values, 0, 1).reshape(-1)


def body(
    kernels,
    prompt_states,
    answer_states,
    answer_prompt,
    prompt_teacher,
    answer_teacher,
    prompt_valid,
    answer_valid,
    first_gain,
    first_shift,
    query_weight,
    query_bias,
    keyval_weight,
    value_bias,
    output_weight,
    output_bias,
    second_gain,
    second_shift,
    up_weight,
    up_bias,
    down_weight,
    down_bias,
):
    prompt_count, prompt_rows, model_width = prompt_states.shape
    answer_count, answer_len, _ = answer_states.shape
    groups = lax.axis_size("grp")
    token_devices = lax.axis_size("tok")
    token_index = lax.axis_index("tok")
    group_index = lax.axis_index("grp")
    own_prompt = prompt_rows * prompt_count
    token_rows = own_prompt + answer_count * answer_len
    hidden_units = up_bias.shape[0] * groups * token_devices
    ff_here = hidden_units // token_devices
    ff_start = token_index * ff_here
    share_size = first_gain.shape[0]
    block = query_weight.shape[1]
    weight_rows = query_weight.shape[0]
    keyval_rows, keyval_width = keyval_weight.shape

    def own_rows(prompt_part, answer_part):
        return jnp.concatenate(
            [prompt_part.reshape(own_prompt, -1), answer_part.reshape(-1, prompt_part.shape[-1])],
            axis=0,
        )

    states = own_rows(prompt_states, answer_states)
    inputs = states.astype(jnp.float32)
    valid_rows = jnp.concatenate([prompt_valid.reshape(-1), answer_valid.reshape(-1)])
    own_count = jnp.sum(valid_rows)
    valid_rows = valid_rows.astype(jnp.float32)

    up_cols = lax.all_gather(up_weight, "grp", axis=0, tiled=True)
    down_cols = lax.all_gather(down_weight, "grp", axis=0, tiled=True)

    query_own = lax.all_gather(query_weight, "grp", axis=0, tiled=True)
    output_own = lax.all_gather(output_weight, "grp", axis=0, tiled=True)
    count_parts = jnp.stack([own_count // 128, own_count % 128]).astype(jnp.bfloat16)
    smalls = jnp.concatenate(
        [
            first_gain,
            first_shift,
            query_bias,
            output_bias,
            second_gain,
            second_shift,
            down_bias,
            up_bias,
            count_parts,
        ]
    )
    smalls = jnp.pad(smalls, (0, SMALL_ROWS * block - smalls.shape[0])).reshape(SMALL_ROWS, block)
    pack = jnp.concatenate([keyval_weight.reshape(-1, block), smalls], axis=0)
    packed = spread(pack, groups, 0, kernels)
    keyval_pack = pack.shape[0] - SMALL_ROWS
    keyval_start = 2 * weight_rows
    keyval_full = jnp.swapaxes(
        packed[:, :, :keyval_pack].reshape(token_devices, groups, keyval_rows, keyval_width),
        0,
        1,
    ).reshape(model_width, keyval_width)
    small_full = packed[:, :, keyval_pack:].reshape(token_devices, groups, SMALL_ROWS * block)
    small_full = jnp.swapaxes(small_full.astype(jnp.float32), 0, 1)

    def vector(start, size):
        return small_full[:, :, start : start + size].reshape(-1)

    gain_one, shift_one, query_offset, output_offset, gain_two, shift_two, down_offset = (
        vector(index * share_size, share_size) for index in range(7)
    )
    up_offset = vector(7 * share_size, up_bias.shape[0])
    count_at = 7 * share_size + up_bias.shape[0]
    counts = small_full[:, :, count_at : count_at + 2]
    valid_count = jnp.sum(counts[:, :, 0]) * 128.0 + jnp.sum(counts[:, :, 1])
    up_here = lax.dynamic_slice_in_dim(up_offset, ff_start, ff_here)

    scaled_one, inverse_one = norm_stats(inputs)
    normed_one = (scaled_one * gain_one + shift_one).astype(jnp.bfloat16)
    key_offset = jnp.concatenate(
        [jnp.zeros((HEAD_WIDTH,), jnp.float32), value_bias.astype(jnp.float32)]
    )
    key_value_rows = (plain_product(normed_one, keyval_full) + key_offset).astype(jnp.bfloat16)
    prompt_kv = tok_gather_small(
        key_value_rows[:own_prompt].reshape(prompt_count, prompt_rows, -1), 1, kernels
    )
    answer_kv = key_value_rows[own_prompt:]
    owning = answer_prompt - group_index * prompt_count
    owning = lax.dynamic_slice_in_dim(owning, token_index * answer_count, answer_count)
    place = jnp.reshape(token_index * prompt_rows, (1,)).astype(jnp.int32)
    if kernels:
        weights, queries, mixture, log_total, hidden, normed_two = gather_attention(
            owning,
            query_own,
            output_own,
            normed_one,
            query_offset,
            prompt_kv,
            answer_kv,
            states,
            output_offset,
            gain_two,
            shift_two,
            prompt_count,
            answer_count,
            prompt_rows,
            8,
        )
    else:
        weights = lax.all_gather(jnp.stack([query_own, output_own]), "tok", axis=0)
        queries, mixture, log_total, hidden, normed_two = attention_forward(
            place,
            owning,
            normed_one,
            weights[:, 0],
            weights[:, 1],
            query_offset,
            prompt_kv,
            answer_kv,
            states,
            output_offset,
            gain_two,
            shift_two,
            prompt_count,
            answer_count,
        )

    if kernels:
        group_two, activated, slope = gather_and_up(normed_two, up_cols, up_here, 2)
        (feed_term,) = product_and_reduce(activated, down_cols, None, 3)
    else:
        group_two = lax.all_gather(normed_two, "tok", axis=0, tiled=True)
        pre_active = plain_product(group_two, up_cols) + up_here
        activated = jax.nn.gelu(pre_active, approximate=True).astype(jnp.bfloat16)
        feed_term = for_sending(transposed_product(activated, down_cols))
        feed_term = lax.psum_scatter(feed_term, "tok", scatter_dimension=0, tiled=True)
        feed_term = feed_term.astype(jnp.float32)
    result_rows = hidden + feed_term + down_offset

    teacher = own_rows(prompt_teacher, answer_teacher).astype(jnp.float32)
    differ = result_rows - teacher
    own_squares = jnp.sum(valid_rows[:, None] * differ * differ)
    every_token = token_rows * groups * token_devices
    grad_result = every_token / valid_count * valid_rows[:, None] * differ
    grad_branch_two = grad_result.astype(jnp.bfloat16)

    if kernels:
        _, grad_pre_active, grad_down_cols, grad_up_offset = gather_and_grad(
            grad_branch_two, down_cols, activated, slope, 4
        )
        grad_normed_two, grad_up_cols = product_and_reduce(grad_pre_active, up_cols, group_two, 5)
        grad_up_offset = grad_up_offset.reshape(-1)
    else:
        group_grad_two = lax.all_gather(grad_branch_two, "tok", axis=0, tiled=True)
        grad_activated = plain_product(group_grad_two, down_cols)
        _, gelu_back = jax.vjp(
            lambda argument: jax.nn.gelu(argument, approximate=True), pre_active
        )
        grad_pre_active = gelu_back(grad_activated)[0].astype(jnp.bfloat16)
        grad_normed_two = for_sending(transposed_product(grad_pre_active, up_cols))
        grad_normed_two = lax.psum_scatter(
            grad_normed_two, "tok", scatter_dimension=0, tiled=True
        ).astype(jnp.float32)
        grad_down_cols = for_sending(weight_product(group_grad_two, activated))
        grad_up_cols = for_sending(weight_product(group_two, grad_pre_active))
        grad_up_offset = column_sums(grad_pre_active)
    grad_down_weight = lax.psum_scatter(grad_down_cols, "grp", scatter_dimension=0, tiled=True)
    grad_down_offset = column_sums(grad_branch_two)
    scaled_two, inverse_two = norm_stats(hidden)
    grad_norm_two, grad_gain_two, grad_shift_two = norm_backward(
        grad_normed_two, gain_two, scaled_two, inverse_two
    )
    grad_hidden = grad_result + grad_norm_two
    grad_branch_one = grad_hidden.astype(jnp.bfloat16)
    grad_down_weight, grad_up_cols, grad_branch_one = lax.optimization_barrier(
        (grad_down_weight, grad_up_cols, grad_branch_one)
    )
    grad_up_weight = lax.psum_scatter(grad_up_cols, "grp", scatter_dimension=0, tiled=True)
    grad_output_offset = column_sums(grad_branch_one)

    share = (owning[:, None] == jnp.arange(prompt_count)[None, :]).astype(jnp.float32).reshape(-1)
    grad_up_place = lax.dynamic_update_slice_in_dim(
        jnp.zeros((hidden_units,), jnp.float32), grad_up_offset, ff_start, 0
    )
    if kernels:
        known = jnp.concatenate(
            [
                grad_up_place,
                grad_output_offset,
                grad_gain_two,
                grad_shift_two,
                grad_down_offset,
                jnp.zeros((3 * model_width + HEAD_WIDTH,), jnp.float32),
                own_squares.reshape(1),
            ]
        )
        known = jnp.pad(known, (0, VECTOR_ROWS * model_width - known.shape[0]))
        grad_query_own, grad_output_own, grad_keyval_own, vectors, grad_inputs = backward_reduce(
            owning,
            share,
            weights,
            queries,
            mixture,
            grad_hidden,
            normed_one,
            grad_branch_one,
            log_total,
            prompt_kv,
            answer_kv,
            states,
            gain_one,
            keyval_full,
            known.reshape(VECTOR_ROWS, model_width),
            groups,
            prompt_count,
            answer_count,
            prompt_rows,
            6,
        )
        value_total = vectors[11, :HEAD_WIDTH]
        squared_sum = vectors[11, HEAD_WIDTH]
        device = group_index * token_devices + token_index
        mine = lax.dynamic_slice_in_dim(
            vectors.reshape(VECTOR_ROWS, -1, share_size), device, 1, axis=1
        )[:, 0]
        own_vectors = [mine[row] for row in (8, 9, 10, 4, 5, 6, 7)]
        grad_up_own = lax.dynamic_slice_in_dim(
            vectors[: hidden_units // model_width].reshape(-1),
            device * up_bias.shape[0],
            up_bias.shape[0],
        )
    else:
        grad_rows = keyval_start + keyval_pack
        grad_weights, grad_normed_one, grad_prompt_kv, grad_answer_kv, grad_query_offset = (
            attention_backward(
                place,
                owning,
                share,
                normed_one,
                weights,
                groups,
                grad_rows,
                prompt_kv,
                answer_kv,
                grad_branch_one,
                queries,
                mixture,
                log_total,
                prompt_count,
                answer_count,
            )
        )
        grad_prompt_kv = lax.psum_scatter(
            grad_prompt_kv, "tok", scatter_dimension=1, tiled=True
        ).astype(jnp.float32)
        grad_keyvals = jnp.concatenate(
            [grad_prompt_kv.reshape(own_prompt, -1), grad_answer_kv], axis=0
        ).astype(jnp.bfloat16)
        grad_keyval_full = weight_product(normed_one, grad_keyvals)
        grad_value_offset = column_sums(grad_keyvals[:, HEAD_WIDTH:])
        grad_normed_one = grad_normed_one + transposed_product(grad_keyvals, keyval_full)
        grad_norm_one, grad_gain_one, grad_shift_one = norm_backward(
            grad_normed_one, gain_one, scaled_one, inverse_one
        )
        grad_inputs = grad_hidden + grad_norm_one

        grad_keyval_blocks = jnp.swapaxes(
            grad_keyval_full.astype(jnp.bfloat16).reshape(groups, token_devices, -1, block), 0, 1
        )
        grad_weights = lax.dynamic_update_slice(
            grad_weights, grad_keyval_blocks, (0, 0, keyval_start, 0)
        )
        vectors = (
            grad_gain_one,
            grad_shift_one,
            grad_query_offset.reshape(-1),
            grad_output_offset,
            grad_gain_two,
            grad_shift_two,
            grad_down_offset,
            grad_up_place,
        )
        totals = jnp.concatenate([grad_value_offset, own_squares.reshape(1)])
        blocks = jnp.concatenate(
            [each.reshape(groups, token_devices, -1) for each in vectors]
            + [jnp.broadcast_to(totals, (groups, token_devices, totals.shape[0]))],
            axis=2,
        )
        blocks = jnp.pad(blocks, ((0, 0), (0, 0), (0, SMALL_SUMS - blocks.shape[2])))
        blocks = jnp.swapaxes(blocks, 0, 1).reshape(token_devices, -1, HEAD_WIDTH)
        grad_weights = lax.psum_scatter(
            grad_weights.reshape(token_devices, -1, block), "tok", scatter_dimension=0, tiled=False
        )
        grad_weights = lax.psum_scatter(grad_weights, "grp", scatter_dimension=0, tiled=True)
        grad_weights = grad_weights.astype(jnp.float32)
        small_sums = lax.psum_scatter(blocks, "tok", scatter_dimension=0, tiled=False)
        small_sums = lax.psum_scatter(small_sums, "grp", scatter_dimension=0, tiled=True)
        small_sums = small_sums.reshape(-1)
        up_share = up_bias.shape[0]
        totals_at = 7 * share_size + up_share
        value_total = small_sums[totals_at : totals_at + HEAD_WIDTH]
        squared_sum = small_sums[totals_at + HEAD_WIDTH]
        own_vectors = [
            small_sums[index * share_size : (index + 1) * share_size] for index in range(7)
        ]
        grad_up_own = small_sums[7 * share_size : totals_at]
        grad_query_own = grad_weights[:weight_rows]
        grad_output_own = grad_weights[weight_rows:keyval_start]
        grad_keyval_own = grad_weights[keyval_start:].reshape(keyval_rows, keyval_width)
        grad_inputs = grad_inputs.astype(jnp.bfloat16)
    loss_value = squared_sum / (valid_count * model_width)

    def split_rows(values):
        values = values.astype(jnp.bfloat16)
        return (
            values[:own_prompt].reshape(prompt_states.shape),
            values[own_prompt:].reshape(answer_states.shape),
        )

    prompt_out, answer_out = split_rows(result_rows)
    prompt_grad, answer_grad = split_rows(grad_inputs)
    pieces = own_vectors
    return (
        prompt_out,
        answer_out,
        prompt_grad,
        answer_grad,
        pieces[0],
        pieces[1],
        grad_query_own,
        pieces[2],
        grad_keyval_own,
        value_total,
        grad_output_own,
        pieces[3],
        pieces[4],
        pieces[5],
        grad_up_weight.astype(jnp.float32),
        grad_up_own,
        grad_down_weight.astype(jnp.float32),
        pieces[6],
        loss_value,
    )


def solution(mesh):
    rows = P(("grp", "tok"))
    table = P(("grp", "tok"), None)
    matrix = P("grp", "tok")
    prompt_part = P("grp", "tok", None)
    answer_part = P(("grp", "tok"), None, None)
    in_specs = (
        prompt_part,
        answer_part,
        P("grp"),
        prompt_part,
        answer_part,
        P("grp", "tok"),
        table,
        rows,
        rows,
        matrix,
        rows,
        table,
        P(),
        matrix,
        rows,
        rows,
        rows,
        matrix,
        rows,
        matrix,
        rows,
    )
    out_specs = (
        prompt_part,
        answer_part,
        prompt_part,
        answer_part,
        rows,
        rows,
        matrix,
        rows,
        table,
        P(),
        matrix,
        rows,
        rows,
        rows,
        matrix,
        rows,
        matrix,
        rows,
        P(),
    )
    kernels = mesh.shape["tok"] == 8
    return jax.shard_map(
        functools.partial(body, kernels),
        mesh=mesh,
        in_specs=in_specs,
        out_specs=out_specs,
        check_vma=False,
    )
```

```python
import functools

import jax
import jax.numpy as jnp
from jax import lax
from jax.experimental import pallas as pl
from jax.experimental.pallas import tpu as pltpu
from jax.sharding import PartitionSpec as P

HEAD_WIDTH = 128
epsilon = 1e-05
masked = -1e30
MESH = pl.DeviceIdType.MESH
VMEM_BYTES = 56 * 1024 * 1024
SMALL_ROWS = 16
SMALL_SUMS = 1024


def for_sending(value):
    return value.astype(jnp.bfloat16)


def plain_product(left, right):
    return jnp.dot(left, right, preferred_element_type=jnp.float32)


def transposed_product(left, right):
    return lax.dot_general(
        left, right, (((1,), (1,)), ((), ())), preferred_element_type=jnp.float32
    )


def weight_product(left, right):
    return lax.dot_general(
        left, right, (((0,), (0,)), ((), ())), preferred_element_type=jnp.float32
    )


def norm_stats(values):
    center = values - jnp.mean(values, axis=-1, keepdims=True)
    inverse = lax.rsqrt(jnp.mean(center * center, axis=-1, keepdims=True) + epsilon)
    return center * inverse, inverse


def norm_backward(grad_out, gain, scaled, inverse):
    weighted = grad_out * gain
    grad_in = inverse * (
        weighted
        - jnp.mean(weighted, axis=-1, keepdims=True)
        - scaled * jnp.mean(weighted * scaled, axis=-1, keepdims=True)
    )
    return (grad_in, jnp.sum(grad_out * scaled, axis=0), jnp.sum(grad_out, axis=0))


def column_sums(values):
    return jnp.sum(values.astype(jnp.float32), axis=0)


def block_of_eight():
    here = lax.axis_index("tok")
    core, across, along = here % 2, (here // 2) % 2, here // 4
    on_x = here + 2 - 4 * across
    on_y = here + 4 - 8 * along
    on_chip = here + 1 - 2 * core
    corner = on_x + 4 - 8 * along
    return here, on_x, on_y, on_chip, corner


def greet_all(peers, other_groups):
    barrier = pltpu.get_barrier_semaphore()
    for peer in peers:
        pl.semaphore_signal(barrier, inc=1, device_id={"tok": peer}, device_id_type=MESH)
    for other in other_groups:
        pl.semaphore_signal(barrier, inc=1, device_id={"grp": other}, device_id_type=MESH)
    pl.semaphore_wait(barrier, len(peers) + len(other_groups))


def greet(devices):
    barrier = pltpu.get_barrier_semaphore()
    for device in devices:
        pl.semaphore_signal(barrier, inc=1, device_id={"tok": device}, device_id_type=MESH)
    pl.semaphore_wait(barrier, len(devices))


def paired_gather(source, place, send_sem, recv_sem):
    here, on_x, on_y, on_chip, corner = block_of_eight()
    over = [
        remote(index, source, place(here), device, send_sem, recv_sem)
        for index, device in enumerate((on_x, on_y, corner, on_chip))
    ]
    handed = [
        remote(4 + index, place(device), place(device), on_chip, send_sem, recv_sem)
        for index, device in enumerate((on_x, on_y, corner))
    ]
    for each in over:
        each.start()
    for each, then in zip(over, handed):
        each.wait_recv()
        then.start()
    for each in [over[3]] + handed:
        each.wait_recv()
    for each in over + handed:
        each.wait_send()


def spread_kernel(groups, own_ref, out_ref, held, send_sem, recv_sem, over_send, over_recv):
    here, on_x, on_y, on_chip, corner = block_of_eight()
    group = lax.axis_index("grp")
    other_groups = [(group + turn) % groups for turn in range(1, groups)]
    greet_all((on_x, on_y, on_chip, corner), other_groups)
    over = [
        pltpu.make_async_remote_copy(
            src_ref=own_ref,
            dst_ref=held.at[group],
            send_sem=over_send.at[index],
            recv_sem=over_recv.at[index],
            device_id={"grp": other},
            device_id_type=MESH,
        )
        for index, other in enumerate(other_groups)
    ]
    for each in over:
        each.start()
    held[group] = own_ref[...]
    for each in over:
        each.wait_recv()
    out_ref[here] = held[...]
    paired_gather(held, lambda device: out_ref.at[device], send_sem, recv_sem)
    for each in over:
        each.wait_send()


def spread(own, groups, call_number, kernels):
    if not kernels:
        return lax.all_gather(lax.all_gather(own, "grp", axis=0), "tok", axis=0)
    inside = pl.BlockSpec(memory_space=pltpu.VMEM)
    dma = pltpu.SemaphoreType.DMA
    return pl.pallas_call(
        functools.partial(spread_kernel, groups),
        out_shape=jax.ShapeDtypeStruct((8, groups) + own.shape, own.dtype),
        in_specs=[inside],
        out_specs=inside,
        scratch_shapes=[
            pltpu.VMEM((groups,) + own.shape, own.dtype),
            dma((7,)),
            dma((7,)),
            dma((groups - 1,)),
            dma((groups - 1,)),
        ],
        compiler_params=pltpu.CompilerParams(collective_id=call_number, has_side_effects=True),
        name="spread",
    )(own)


def remote(index, source, target, device, send_sem, recv_sem):
    return pltpu.make_async_remote_copy(
        src_ref=source,
        dst_ref=target,
        send_sem=send_sem.at[index],
        recv_sem=recv_sem.at[index],
        device_id={"tok": device},
        device_id_type=MESH,
    )


def chunk_of(index, size):
    return pl.ds(pl.multiple_of(index * size, size), size)


CHUNK = 512
LINEAR = 0.7978845608
CUBIC = 0.044715


def gather_beside(own_ref, out_ref, send_sem, recv_sem, local_sem, use):
    rows = own_ref.shape[0]
    half, quarter = rows // 2, rows // 4
    here, on_x, on_y, on_chip, corner = block_of_eight()
    shift = on_chip - here
    counter = iter(range(GATHER_COPIES))

    def copy(source, block, start, count, device):
        place = pl.ds(start, count)
        return remote(
            next(counter),
            source.at[place] if source is own_ref else source.at[block, place],
            out_ref.at[block, place],
            device,
            send_sem,
            recv_sem,
        )

    greet((on_x, on_y, on_chip))
    own = pltpu.make_async_copy(own_ref, out_ref.at[here], local_sem)
    x_low = copy(own_ref, here, 0, half, on_x)
    y_high = copy(own_ref, here, half, half, on_y)
    x_high = copy(own_ref, here, half, half, on_x)
    y_low = copy(own_ref, here, 0, half, on_y)
    to_chip = copy(own_ref, here, 0, rows, on_chip)
    to_y = [copy(out_ref, on_x, turn * quarter, quarter, on_y) for turn in (0, 1)]
    to_x = [copy(out_ref, on_y, half + turn * quarter, quarter, on_x) for turn in (0, 1)]
    chip_x = [copy(out_ref, on_x, turn * half, half, on_chip) for turn in (0, 1)]
    chip_y = [copy(out_ref, on_y, turn * half, half, on_chip) for turn in (0, 1)]
    chip_corner = [copy(out_ref, corner, turn * quarter, quarter, on_chip) for turn in range(4)]
    for each in (x_low, y_high, x_high, y_low, to_chip, own):
        each.start()
    use(0, [(here, 0, rows)])
    to_chip.wait_recv()
    use(1, [(on_chip, 0, rows)])
    x_low.wait_recv()
    for each in (*to_y, chip_x[0]):
        each.start()
    y_high.wait_recv()
    for each in (*to_x, chip_y[1]):
        each.start()
    use(2, [(on_x, 0, half), (on_y, half, half)])
    chip_x[0].wait_recv()
    chip_y[1].wait_recv()
    use(3, [(on_x + shift, 0, half), (on_y + shift, half, half)])
    x_high.wait_recv()
    chip_x[1].start()
    y_low.wait_recv()
    chip_y[0].start()
    use(4, [(on_x, half, half), (on_y, 0, half)])
    chip_x[1].wait_recv()
    chip_y[0].wait_recv()
    use(5, [(on_x + shift, half, half), (on_y + shift, 0, half)])
    for turn in (0, 1):
        to_y[turn].wait_recv()
        chip_corner[turn].start()
        to_x[turn].wait_recv()
        chip_corner[2 + turn].start()
        chip_corner[turn].wait_recv()
        chip_corner[2 + turn].wait_recv()
        use(
            6 + turn,
            [
                (block, start + turn * quarter, quarter)
                for block in (corner, corner + shift)
                for start in (0, half)
            ],
        )
    own.wait()
    for each in (x_low, y_high, x_high, y_low, to_chip, *to_y, *to_x, *chip_x, *chip_y, *chip_corner):
        each.wait_send()


GATHER_COPIES = 17


def moves(outside, inside, pieces, semaphores, outward):
    done, copies = 0, []
    for index, (block, start, count) in enumerate(pieces):
        away = outside.at[block, pl.ds(start, count)]
        near = inside.at[pl.ds(done, count)]
        pair = (near, away) if outward else (away, near)
        copies.append(pltpu.make_async_copy(*pair, semaphores.at[index]))
        done += count
    return copies


def up_kernel(
    own_ref,
    up_hbm,
    bias_ref,
    rows_ref,
    active_ref,
    slope_ref,
    up,
    rows,
    active,
    slope,
    send_sem,
    recv_sem,
    local_sem,
    weight_sem,
    row_sem,
    store_sem,
):
    weights = pltpu.make_async_copy(up_hbm, up, weight_sem)
    weights.start()
    stores = {}

    def use(place, pieces):
        slot = place % 2
        if place:
            loads = moves(rows_ref, rows, pieces, row_sem, False)
        else:
            loads = [pltpu.make_async_copy(own_ref, rows, row_sem.at[0])]
        for each in loads:
            each.start()
        if place == 0:
            weights.wait()
        for each in stores.pop(slot, ()):
            each.wait()
        for each in loads:
            each.wait()

        @pl.loop(0, up.shape[1] // CHUNK)
        def _(turn):
            at = chunk_of(turn, CHUNK)
            value = plain_product(rows[...], up[:, at]) + bias_ref[:, at]
            square = value * value
            bent = jnp.tanh(value * (LINEAR + (LINEAR * CUBIC) * square))
            level = 0.5 + 0.5 * bent
            active[slot, :, at] = (value * level).astype(jnp.bfloat16)
            slope[slot, :, at] = (
                level
                + (0.5 * value)
                * (1.0 - bent * bent)
                * (LINEAR + (3.0 * LINEAR * CUBIC) * square)
            ).astype(jnp.bfloat16)

        stores[slot] = moves(
            active_ref, active.at[slot], pieces, store_sem.at[slot, 0], True
        ) + moves(slope_ref, slope.at[slot], pieces, store_sem.at[slot, 1], True)
        for each in stores[slot]:
            each.start()

    gather_beside(own_ref, rows_ref, send_sem, recv_sem, local_sem, use)
    for slot in (0, 1):
        for each in stores[slot]:
            each.wait()


def gather_and_up(own, up_cols, bias, call_number):
    token_rows, model_width = own.shape
    width = up_cols.shape[1]
    hidden = jax.ShapeDtypeStruct((8, token_rows, width), jnp.bfloat16)
    anywhere = pl.BlockSpec(memory_space=pl.ANY)
    dma = pltpu.SemaphoreType.DMA
    return pl.pallas_call(
        up_kernel,
        out_shape=(
            jax.ShapeDtypeStruct((8, token_rows, model_width), jnp.bfloat16),
            hidden,
            hidden,
        ),
        in_specs=[anywhere, anywhere, pl.BlockSpec(memory_space=pltpu.VMEM)],
        out_specs=(anywhere, anywhere, anywhere),
        scratch_shapes=[
            pltpu.VMEM(up_cols.shape, jnp.bfloat16),
            pltpu.VMEM((token_rows, model_width), jnp.bfloat16),
            pltpu.VMEM((2, token_rows, width), jnp.bfloat16),
            pltpu.VMEM((2, token_rows, width), jnp.bfloat16),
            dma((GATHER_COPIES,)),
            dma((GATHER_COPIES,)),
            dma,
            dma,
            dma((4,)),
            dma((2, 2, 4)),
        ],
        compiler_params=pltpu.CompilerParams(
            collective_id=call_number, has_side_effects=True, vmem_limit_bytes=VMEM_BYTES
        ),
        cost_estimate=pl.CostEstimate(
            flops=16 * token_rows * model_width * width,
            bytes_accessed=150 * 1000 * 1000,
            transcendentals=0,
        ),
        name="gather_and_up",
    )(own, up_cols, bias.reshape(1, -1))


def grad_kernel(
    own_ref,
    down_hbm,
    active_ref,
    slope_ref,
    rows_ref,
    grad_ref,
    weight_ref,
    bias_ref,
    down,
    rows,
    active,
    slope,
    grads,
    sums,
    narrow,
    send_sem,
    recv_sem,
    local_sem,
    weight_sem,
    row_sem,
    load_sem,
    store_sem,
):
    weights = pltpu.make_async_copy(down_hbm, down, weight_sem)
    weights.start()
    stores = {}

    def use(place, pieces):
        slot = place % 2
        if place:
            loads = moves(rows_ref, rows, pieces, row_sem, False)
        else:
            loads = [pltpu.make_async_copy(own_ref, rows, row_sem.at[0])]
        loads += moves(active_ref, active, pieces, load_sem.at[0], False)
        loads += moves(slope_ref, slope, pieces, load_sem.at[1], False)
        for each in loads:
            each.start()
        if place == 0:
            weights.wait()
        for each in stores.pop(slot, ()):
            each.wait()
        for each in loads:
            each.wait()

        @pl.loop(0, down.shape[1] // CHUNK)
        def _(turn):
            at = chunk_of(turn, CHUNK)
            value = plain_product(rows[...], down[:, at]) * slope[:, at].astype(jnp.float32)
            value = value.astype(jnp.bfloat16)
            grads[slot, :, at] = value
            total = jnp.sum(value.astype(jnp.float32), axis=0, keepdims=True)
            weight = weight_product(rows[...], active[:, at])
            if place == 0:
                bias_ref[:, at] = total
                sums[:, at] = weight
            elif place < 7:
                bias_ref[:, at] += total
                sums[:, at] += weight
            else:
                bias_ref[:, at] += total
                narrow[:, at] = (sums[:, at] + weight).astype(jnp.bfloat16)

        stores[slot] = moves(grad_ref, grads.at[slot], pieces, store_sem.at[slot], True)
        for each in stores[slot]:
            each.start()

    gather_beside(own_ref, rows_ref, send_sem, recv_sem, local_sem, use)
    last = pltpu.make_async_copy(narrow, weight_ref, weight_sem)
    last.start()
    for slot in (0, 1):
        for each in stores[slot]:
            each.wait()
    last.wait()


def gather_and_grad(own, down_cols, active, slope, call_number):
    token_rows, model_width = own.shape
    width = down_cols.shape[1]
    anywhere = pl.BlockSpec(memory_space=pl.ANY)
    dma = pltpu.SemaphoreType.DMA
    return pl.pallas_call(
        grad_kernel,
        out_shape=(
            jax.ShapeDtypeStruct((8, token_rows, model_width), jnp.bfloat16),
            jax.ShapeDtypeStruct((8, token_rows, width), jnp.bfloat16),
            jax.ShapeDtypeStruct((model_width, width), jnp.bfloat16),
            jax.ShapeDtypeStruct((1, width), jnp.float32),
        ),
        in_specs=[anywhere] * 4,
        out_specs=(anywhere,) * 3 + (pl.BlockSpec(memory_space=pltpu.VMEM),),
        scratch_shapes=[
            pltpu.VMEM(down_cols.shape, jnp.bfloat16),
            pltpu.VMEM((token_rows, model_width), jnp.bfloat16),
            pltpu.VMEM((token_rows, width), jnp.bfloat16),
            pltpu.VMEM((token_rows, width), jnp.bfloat16),
            pltpu.VMEM((2, token_rows, width), jnp.bfloat16),
            pltpu.VMEM((model_width, width), jnp.float32),
            pltpu.VMEM((model_width, width), jnp.bfloat16),
            dma((GATHER_COPIES,)),
            dma((GATHER_COPIES,)),
            dma,
            dma,
            dma((4,)),
            dma((2, 4)),
            dma((2, 4)),
        ],
        compiler_params=pltpu.CompilerParams(
            collective_id=call_number, has_side_effects=True, vmem_limit_bytes=VMEM_BYTES
        ),
        cost_estimate=pl.CostEstimate(
            flops=32 * token_rows * model_width * width,
            bytes_accessed=150 * 1000 * 1000,
            transcendentals=0,
        ),
        name="gather_and_grad",
    )(own, down_cols, active, slope)


def product_reduce_kernel(
    with_grad,
    narrow_ref,
    weight_hbm,
    *refs,
):
    if with_grad:
        wide_ref, hidden_hbm, result_hbm, gain_ref, *refs = refs
        grad_hidden_ref, grad_ref, branch_ref, sums_ref, *refs = refs
        *refs, wide, across, sums, wide_sem = refs
    else:
        hidden_hbm, teacher_hbm, offset_ref, valid_ref, factor_ref, *refs = refs
        out_ref, branch_ref, grad_result_ref, squares_ref, columns_ref, *refs = refs
    (
        weight,
        narrow,
        sent,
        mine,
        theirs,
        relayed,
        final,
        hidden_rows,
        other_rows,
        send_sem,
        recv_sem,
        weight_sem,
        narrow_sem,
        row_sem,
    ) = refs
    row_loads = (
        pltpu.make_async_copy(hidden_hbm, hidden_rows, row_sem.at[0]),
        pltpu.make_async_copy(result_hbm if with_grad else teacher_hbm, other_rows, row_sem.at[1]),
    )
    rows = narrow.shape[1]
    half = rows // 2
    here, on_x, on_y, on_chip, corner = block_of_eight()
    shift = on_chip - here
    first, second = pl.ds(0, half), pl.ds(half, half)
    load_weight = pltpu.make_async_copy(weight_hbm, weight, weight_sem)
    load_weight.start()

    def copy(index, source, target, device):
        return remote(index, source, target, device, send_sem, recv_sem)

    places = (corner, on_x, on_y, here)
    order = []
    for place in places:
        order += [place + shift, place]

    def fetch(turn):
        return pltpu.make_async_copy(
            narrow_ref.at[order[turn]], narrow.at[turn % 2], narrow_sem.at[turn % 2]
        )

    fetch(0).start()
    greet((on_x, on_y, on_chip))
    to_chip = [copy(index, sent.at[index], theirs.at[index], on_chip) for index in range(4)]
    step = 16

    def add_into(target, other, start, count):
        @pl.loop(0, count // step)
        def _(turn):
            at = pl.ds(pl.multiple_of(start + turn * step, step), step)
            come = pl.ds(pl.multiple_of(turn * step, step), step)
            target[at, :] = target[at, :] + other[come, :]

    def join(index):
        to_chip[index].wait_recv()
        add_into(mine.at[index], theirs.at[index], 0, rows)

    corner_x = copy(4, mine.at[0, first], relayed.at[0], on_x)
    corner_y = copy(5, mine.at[0, second], relayed.at[1], on_y)
    x_first = copy(6, mine.at[1, first], final.at[0, first], on_x)
    y_second = copy(7, mine.at[2, second], final.at[1, second], on_y)
    x_second = copy(8, mine.at[1, second], final.at[0, second], on_x)
    y_first = copy(9, mine.at[2, first], final.at[1, first], on_y)

    for each in row_loads:
        each.start()
    for turn in range(8):
        pair, own = turn // 2, turn % 2
        if turn < 7:
            fetch(turn + 1).start()
        fetch(turn).wait()
        if turn == 0:
            load_weight.wait()
        target = mine.at[pair] if own else sent.at[pair]

        @pl.loop(0, weight.shape[0] // CHUNK)
        def _(piece):
            at = chunk_of(piece, CHUNK)
            target[:, at] = transposed_product(narrow[turn % 2], weight[at, :]).astype(
                jnp.bfloat16
            )

        if not own:
            to_chip[pair].start()
        if turn == 2:
            join(0)
            corner_x.start()
            corner_y.start()
        if turn == 4:
            join(1)
            x_first.start()
        if turn == 6:
            join(2)
            y_second.start()
    corner_y.wait_recv()
    add_into(mine.at[1], relayed.at[1], half, half)
    x_second.start()
    corner_x.wait_recv()
    add_into(mine.at[2], relayed.at[0], 0, half)
    y_first.start()
    join(3)

    if with_grad:
        def fetch_wide(turn):
            return pltpu.make_async_copy(
                wide_ref.at[order[turn]], wide.at[turn % 2], wide_sem.at[turn % 2]
            )

        fetch_wide(0).start()
        fetch(0).start()
        for turn in range(8):
            if turn < 7:
                fetch_wide(turn + 1).start()
                fetch(turn + 1).start()
            fetch_wide(turn).wait()
            fetch(turn).wait()
            across[...] = jnp.transpose(wide[turn % 2])

            @pl.loop(0, sums.shape[1] // CHUNK)
            def _(piece):
                at = chunk_of(piece, CHUNK)
                value = plain_product(across[...], narrow[turn % 2, :, at])
                if turn == 0:
                    sums[:, at] = value
                elif turn < 7:
                    sums[:, at] += value
                else:
                    weight[:, at] = (sums[:, at] + value).astype(jnp.bfloat16)

        store = pltpu.make_async_copy(weight, grad_ref, weight_sem)
        store.start()

    for each in (x_first, y_second, x_second, y_first):
        each.wait_recv()

    for each in row_loads:
        each.wait()

    def total_of(at):
        total = mine[3, at, :].astype(jnp.float32) + final[0, at, :].astype(jnp.float32)
        return total + final[1, at, :].astype(jnp.float32)

    if with_grad:
        sums_ref[...] = jnp.zeros_like(sums_ref)

        @pl.loop(0, rows // step)
        def _(turn):
            at = chunk_of(turn, step)
            grad_out = total_of(at)
            scaled, inverse = norm_stats(hidden_rows[at, :])
            weighted = grad_out * gain_ref[...]
            grad_in = inverse * (
                weighted
                - jnp.mean(weighted, axis=-1, keepdims=True)
                - scaled * jnp.mean(weighted * scaled, axis=-1, keepdims=True)
            )
            grad_hidden = other_rows[at, :] + grad_in
            branch = grad_hidden.astype(jnp.bfloat16)
            grad_hidden_ref[at, :] = grad_hidden
            branch_ref[at, :] = branch
            sums_ref[0:1, :] += jnp.sum(branch.astype(jnp.float32), axis=0, keepdims=True)
            sums_ref[1:2, :] += jnp.sum(grad_out * scaled, axis=0, keepdims=True)
            sums_ref[2:3, :] += jnp.sum(grad_out, axis=0, keepdims=True)

    else:
        squares_ref[...] = jnp.zeros_like(squares_ref)
        columns_ref[...] = jnp.zeros_like(columns_ref)

        @pl.loop(0, rows // step)
        def _(turn):
            at = chunk_of(turn, step)
            result = hidden_rows[at, :] + total_of(at) + offset_ref[...]
            differ = result - other_rows[at, :].astype(jnp.float32)
            grad_result = factor_ref[at, :] * differ
            branch = grad_result.astype(jnp.bfloat16)
            out_ref[at, :] = result.astype(jnp.bfloat16)
            grad_result_ref[at, :] = grad_result
            branch_ref[at, :] = branch
            squares_ref[...] += jnp.sum(valid_ref[at, :] * differ * differ, axis=0, keepdims=True)
            columns_ref[...] += jnp.sum(branch.astype(jnp.float32), axis=0, keepdims=True)

    if with_grad:
        store.wait()
    for each in to_chip + [corner_x, corner_y, x_first, y_second, x_second, y_first]:
        each.wait_send()


def product_and_reduce(narrow, weight, wide, rows, second, call_number, *small):
    _, token_rows, width = narrow.shape
    model_width = weight.shape[0]
    with_grad = wide is not None
    anywhere = pl.BlockSpec(memory_space=pl.ANY)
    inside = pl.BlockSpec(memory_space=pltpu.VMEM)
    dma = pltpu.SemaphoreType.DMA
    block = (token_rows, model_width)
    kind, long = jnp.bfloat16, jnp.float32
    line = jax.ShapeDtypeStruct((1, model_width), long)
    narrow_rows, long_rows = jax.ShapeDtypeStruct(block, kind), jax.ShapeDtypeStruct(block, long)
    scratch = [
        pltpu.VMEM(weight.shape, kind),
        pltpu.VMEM((2, token_rows, width), kind),
        pltpu.VMEM((4,) + block, kind),
        pltpu.VMEM((4,) + block, kind),
        pltpu.VMEM((4,) + block, kind),
        pltpu.VMEM((2, token_rows // 2, model_width), kind),
        pltpu.VMEM((2,) + block, kind),
        pltpu.VMEM(block, long),
        pltpu.VMEM(block, second.dtype),
        dma((10,)),
        dma((10,)),
        dma,
        dma((2,)),
        dma((2,)),
    ]
    operands = [narrow, weight]
    if with_grad:
        out_shape = (
            long_rows,
            jax.ShapeDtypeStruct(weight.shape, kind),
            narrow_rows,
            jax.ShapeDtypeStruct((8, model_width), long),
        )
        out_specs = (inside, anywhere, inside, inside)
        scratch += [
            pltpu.VMEM((2,) + block, kind),
            pltpu.VMEM((model_width, token_rows), kind),
            pltpu.VMEM(weight.shape, long),
            dma((2,)),
        ]
        operands.append(wide)
    else:
        out_shape = (narrow_rows, narrow_rows, long_rows, line, line)
        out_specs = (inside,) * 5
    operands += [rows, second]
    return pl.pallas_call(
        functools.partial(product_reduce_kernel, with_grad),
        out_shape=out_shape,
        in_specs=[anywhere] * len(operands) + [inside] * len(small),
        out_specs=out_specs,
        scratch_shapes=scratch,
        compiler_params=pltpu.CompilerParams(
            collective_id=call_number,
            has_side_effects=True,
            vmem_limit_bytes=62 * 1024 * 1024,
        ),
        cost_estimate=pl.CostEstimate(
            flops=(32 if with_grad else 16) * token_rows * model_width * width,
            bytes_accessed=150 * 1000 * 1000,
            transcendentals=0,
        ),
        name="product_and_reduce",
    )(*operands, *small)


def peers_of(count):
    here = lax.axis_index("tok")
    return here, [(here + step) % count for step in range(1, count)]


def small_gather_kernel(own_ref, out_ref, send_sem, recv_sem):
    here, on_x, on_y, on_chip, corner = block_of_eight()
    rows = own_ref.shape[1]

    def place(device):
        return pl.ds(pl.multiple_of(device * rows, rows), rows)

    greet((on_x, on_y, on_chip, corner))
    out_ref[:, place(here), :] = own_ref[...]
    paired_gather(own_ref, lambda device: out_ref.at[:, place(device), :], send_sem, recv_sem)


def tok_gather_small(own, call_number, kernels):
    if not kernels:
        return lax.all_gather(own, "tok", axis=1, tiled=True)
    prompts, rows, columns = own.shape
    return pl.pallas_call(
        small_gather_kernel,
        out_shape=jax.ShapeDtypeStruct((prompts, 8 * rows, columns), own.dtype),
        in_specs=[pl.BlockSpec(memory_space=pltpu.VMEM)],
        out_specs=pl.BlockSpec(memory_space=pltpu.VMEM),
        scratch_shapes=[pltpu.SemaphoreType.DMA((7,)), pltpu.SemaphoreType.DMA((7,))],
        compiler_params=pltpu.CompilerParams(collective_id=call_number, has_side_effects=True),
        name="tok_gather_small",
    )(own)


def stack_heads(values, heads):
    return jnp.concatenate(
        [values[:, head * HEAD_WIDTH : (head + 1) * HEAD_WIDTH] for head in range(heads)], axis=0
    )


def unstack_heads(values, heads):
    rows = values.shape[0] // heads
    return jnp.concatenate(
        [values[head * rows : (head + 1) * rows, :] for head in range(heads)], axis=1
    )


def part_rows(part, prompts, answers, token_ref, answer_ref):
    answer_rows = answer_ref.shape[0] // answers
    prompt_rows = (token_ref.shape[0] - answer_ref.shape[0]) // prompts
    if part < prompts:
        return slice(part * prompt_rows, (part + 1) * prompt_rows), prompt_rows
    start = prompts * prompt_rows + (part - prompts) * answer_rows
    return slice(start, start + answer_rows), answer_rows


def as_row(column):
    wide = jnp.broadcast_to(column, (column.shape[0], HEAD_WIDTH))
    return jnp.transpose(wide)[0:1, :]


def forward_block(
    prompts,
    answers,
    heads,
    start,
    owner_ref,
    normed_ref,
    query_block,
    bias,
    prompt_kv_ref,
    answer_kv_ref,
):
    width = HEAD_WIDTH
    scale = HEAD_WIDTH ** (-0.5)
    length = prompt_kv_ref.shape[1]
    queries = (plain_product(normed_ref[...], query_block) + bias).astype(jnp.bfloat16)
    pieces, logs = [], []
    for part in range(prompts + answers):
        here, rows = part_rows(part, prompts, answers, normed_ref, answer_kv_ref)
        token = lax.broadcasted_iota(jnp.int32, (heads * rows, 1), 0) % rows
        stacked = stack_heads(queries[here, :], heads)
        if part < prompts:
            keys = prompt_kv_ref[part, :, :width]
            values = prompt_kv_ref[part, :, width:]
            scores = transposed_product(stacked, keys)
            place = lax.broadcasted_iota(jnp.int32, (1, length), 1)
            scores = jnp.where(place <= start + token, scores, masked)
            top = jnp.max(scores, axis=-1, keepdims=True)
            exponent = jnp.exp((scores - top) * scale)
            total = jnp.sum(exponent, axis=-1, keepdims=True)
            mixed = plain_product(exponent.astype(jnp.bfloat16), values)
        else:
            answer = part - prompts
            owner = owner_ref[answer]
            own = slice(answer * rows, (answer + 1) * rows)
            keys = prompt_kv_ref[owner, :, :width]
            values = prompt_kv_ref[owner, :, width:]
            scores = transposed_product(stacked, keys)
            own_scores = transposed_product(stacked, answer_kv_ref[own, :width])
            place = lax.broadcasted_iota(jnp.int32, (1, rows), 1)
            own_scores = jnp.where(place <= token, own_scores, masked)
            top = jnp.maximum(
                jnp.max(scores, axis=-1, keepdims=True),
                jnp.max(own_scores, axis=-1, keepdims=True),
            )
            exponent = jnp.exp((scores - top) * scale)
            own_exponent = jnp.exp((own_scores - top) * scale)
            total = jnp.sum(exponent, axis=-1, keepdims=True) + jnp.sum(
                own_exponent, axis=-1, keepdims=True
            )
            mixed = plain_product(exponent.astype(jnp.bfloat16), values) + plain_product(
                own_exponent.astype(jnp.bfloat16), answer_kv_ref[own, width:]
            )
        pieces.append(unstack_heads((mixed / total).astype(jnp.bfloat16), heads))
        logs.append((here, rows, as_row(top * scale + jnp.log(total))))
    return queries, jnp.concatenate(pieces, axis=0), logs


def attention_forward_kernel(
    prompts,
    answers,
    heads,
    place_ref,
    owner_ref,
    normed_ref,
    query_ref,
    bias_ref,
    prompt_kv_ref,
    answer_kv_ref,
    output_ref,
    states_ref,
    offset_ref,
    gain_ref,
    shift_ref,
    queries_ref,
    mixture_ref,
    log_ref,
    hidden_ref,
    second_ref,
):
    step = pl.program_id(0)
    queries, mixture, logs = forward_block(
        prompts,
        answers,
        heads,
        place_ref[0],
        owner_ref,
        normed_ref,
        query_ref[0],
        bias_ref[0],
        prompt_kv_ref,
        answer_kv_ref,
    )
    queries_ref[0] = queries
    mixture_ref[0] = mixture
    for here, rows, log_row in logs:
        for head in range(heads):
            log_ref[0, head : head + 1, here] = log_row[:, head * rows : (head + 1) * rows]

    @pl.when(step == 0)
    def _():
        hidden_ref[...] = states_ref[...].astype(jnp.float32) + offset_ref[...]

    hidden_ref[...] += transposed_product(mixture, output_ref[0])

    @pl.when(step == pl.num_programs(0) - 1)
    def _():
        scaled, _ = norm_stats(hidden_ref[...])
        second_ref[...] = (scaled * gain_ref[...] + shift_ref[...]).astype(jnp.bfloat16)


def attention_forward(
    place,
    owning,
    normed,
    query_blocks,
    output_blocks,
    query_offset,
    prompt_kv,
    answer_kv,
    states,
    output_offset,
    gain,
    shift,
    prompts,
    answers,
):
    token_rows, model_width = normed.shape
    steps, _, block = query_blocks.shape
    heads = block // HEAD_WIDTH
    whole = lambda *shape: pl.BlockSpec(shape, lambda step, *_: (0,) * len(shape))
    one = lambda *shape: pl.BlockSpec((1,) + shape, lambda step, *_: (step, 0, 0))
    by_step = jax.ShapeDtypeStruct((steps, token_rows, block), jnp.bfloat16)
    return pl.pallas_call(
        functools.partial(attention_forward_kernel, prompts, answers, heads),
        out_shape=(
            by_step,
            by_step,
            jax.ShapeDtypeStruct((steps, heads, token_rows), jnp.float32),
            jax.ShapeDtypeStruct((token_rows, model_width), jnp.float32),
            jax.ShapeDtypeStruct((token_rows, model_width), jnp.bfloat16),
        ),
        grid_spec=pltpu.PrefetchScalarGridSpec(
            num_scalar_prefetch=2,
            grid=(steps,),
            in_specs=[
                whole(token_rows, model_width),
                one(model_width, block),
                one(1, block),
                whole(*prompt_kv.shape),
                whole(*answer_kv.shape),
                one(model_width, block),
                whole(token_rows, model_width),
                whole(1, model_width),
                whole(1, model_width),
                whole(1, model_width),
            ],
            out_specs=(
                one(token_rows, block),
                one(token_rows, block),
                one(heads, token_rows),
                whole(token_rows, model_width),
                whole(token_rows, model_width),
            ),
        ),
        compiler_params=pltpu.CompilerParams(vmem_limit_bytes=VMEM_BYTES),
        name="attention_forward",
    )(
        place,
        owning,
        normed,
        query_blocks,
        query_offset.reshape(steps, 1, block),
        prompt_kv,
        answer_kv,
        output_blocks,
        states,
        output_offset.reshape(1, -1),
        gain.reshape(1, -1),
        shift.reshape(1, -1),
    )


def bits_away(index):
    here = lax.axis_index("tok")
    core = (here + index) % 2
    across = (here // 2 + index // 2) % 2
    along = (here // 4 + index // 4) % 2
    return along * 4 + across * 2 + core


def gather_attention_kernel(
    prompts,
    answers,
    heads,
    prompt_rows,
    owner_ref,
    own_ref,
    normed_ref,
    bias_ref,
    prompt_kv_ref,
    answer_kv_ref,
    states_ref,
    offset_ref,
    gain_ref,
    shift_ref,
    weights_ref,
    queries_ref,
    mixture_ref,
    log_ref,
    hidden_ref,
    second_ref,
    held,
    send_sem,
    recv_sem,
    local_sem,
    load_sem,
):
    here, on_x, on_y, on_chip, corner = block_of_eight()

    def copy(index, source, target, device):
        return remote(index, source, target, device, send_sem, recv_sem)

    def kind_of(device, kind):
        return weights_ref.at[device, :, kind]

    to_x = [copy(0 + kind, own_ref.at[:, kind], kind_of(here, kind), on_x) for kind in (0, 1)]
    to_y = [copy(2 + kind, own_ref.at[:, kind], kind_of(here, kind), on_y) for kind in (0, 1)]
    to_chip = [copy(4, own_ref, weights_ref.at[here], on_chip)]
    keep = [pltpu.make_async_copy(own_ref, weights_ref.at[here], local_sem)]
    x_to_y = copy(5, kind_of(on_x, 0), kind_of(on_x, 0), on_y)
    y_to_x = copy(6, kind_of(on_y, 1), kind_of(on_y, 1), on_x)
    x_to_chip = copy(7, weights_ref.at[on_x], weights_ref.at[on_x], on_chip)
    y_to_chip = copy(8, weights_ref.at[on_y], weights_ref.at[on_y], on_chip)
    corner_to_chip = [
        copy(9 + kind, kind_of(corner, kind), kind_of(corner, kind), on_chip) for kind in (0, 1)
    ]

    greet((on_x, on_y, on_chip))
    for each in (to_x[0], to_y[1], to_x[1], to_y[0], *to_chip, *keep):
        each.start()
    hidden_ref[...] = states_ref[...].astype(jnp.float32) + offset_ref[...]

    @pl.loop(0, 8)
    def _(turn):
        block = bits_away(turn)

        @pl.when(turn == 0)
        def _():
            load = pltpu.make_async_copy(own_ref, held, load_sem)
            load.start()
            load.wait()

        @pl.when(turn == 1)
        def _():
            for each in to_chip:
                each.wait_recv()

        @pl.when(turn == 2)
        def _():
            to_x[0].wait_recv()
            x_to_y.start()
            to_y[1].wait_recv()
            y_to_x.start()
            to_x[1].wait_recv()
            x_to_chip.start()
            to_y[0].wait_recv()
            y_to_chip.start()

        @pl.when(turn == 3)
        def _():
            x_to_chip.wait_recv()

        @pl.when(turn == 5)
        def _():
            y_to_chip.wait_recv()

        @pl.when(turn == 6)
        def _():
            x_to_y.wait_recv()
            corner_to_chip[0].start()
            y_to_x.wait_recv()
            corner_to_chip[1].start()

        @pl.when(turn == 7)
        def _():
            for each in corner_to_chip:
                each.wait_recv()

        @pl.when(turn > 0)
        def _():
            load = pltpu.make_async_copy(weights_ref.at[block], held, load_sem)
            load.start()
            load.wait()

        queries, mixture, logs = forward_block(
            prompts,
            answers,
            heads,
            here * prompt_rows,
            owner_ref,
            normed_ref,
            held[:, 0].reshape(-1, held.shape[-1]),
            bias_ref[block],
            prompt_kv_ref,
            answer_kv_ref,
        )
        queries_ref[block] = queries
        mixture_ref[block] = mixture
        for place, rows, log_row in logs:
            for head in range(heads):
                log_ref[block, head : head + 1, place] = log_row[
                    :, head * rows : (head + 1) * rows
                ]
        hidden_ref[...] += transposed_product(mixture, held[:, 1].reshape(-1, held.shape[-1]))

    scaled, _ = norm_stats(hidden_ref[...])
    second_ref[...] = (scaled * gain_ref[...] + shift_ref[...]).astype(jnp.bfloat16)
    for each in (*to_x, *to_y, *to_chip, x_to_y, y_to_x, x_to_chip, y_to_chip, *corner_to_chip):
        each.wait_send()
    for each in keep:
        each.wait()


def gather_attention(
    owning,
    projections,
    normed,
    query_offset,
    prompt_kv,
    answer_kv,
    states,
    output_offset,
    gain,
    shift,
    prompts,
    answers,
    prompt_rows,
    call_number,
):
    token_rows, model_width = normed.shape
    block = projections.shape[3]
    heads = block // HEAD_WIDTH
    inside = pl.BlockSpec(memory_space=pltpu.VMEM)
    anywhere = pl.BlockSpec(memory_space=pl.ANY)
    dma = pltpu.SemaphoreType.DMA
    by_step = jax.ShapeDtypeStruct((8, token_rows, block), jnp.bfloat16)
    return pl.pallas_call(
        functools.partial(gather_attention_kernel, prompts, answers, heads, prompt_rows),
        out_shape=(
            jax.ShapeDtypeStruct((8,) + projections.shape, jnp.bfloat16),
            by_step,
            by_step,
            jax.ShapeDtypeStruct((8, heads, token_rows), jnp.float32),
            jax.ShapeDtypeStruct((token_rows, model_width), jnp.float32),
            jax.ShapeDtypeStruct((token_rows, model_width), jnp.bfloat16),
        ),
        in_specs=[pl.BlockSpec(memory_space=pltpu.SMEM), anywhere] + [inside] * 8,
        out_specs=(anywhere,) + (inside,) * 5,
        scratch_shapes=[
            pltpu.VMEM(projections.shape, jnp.bfloat16),
            dma((11,)),
            dma((11,)),
            dma,
            dma,
        ],
        compiler_params=pltpu.CompilerParams(
            collective_id=call_number, has_side_effects=True, vmem_limit_bytes=VMEM_BYTES
        ),
        cost_estimate=pl.CostEstimate(
            flops=64 * token_rows * model_width * block,
            bytes_accessed=250 * 1000 * 1000,
            transcendentals=0,
        ),
        name="gather_attention",
    )(
        owning,
        projections,
        normed,
        query_offset.reshape(8, 1, block),
        prompt_kv,
        answer_kv,
        states,
        output_offset.reshape(1, -1),
        gain.reshape(1, -1),
        shift.reshape(1, -1),
    )


def backward_block(
    prompts,
    answers,
    heads,
    start,
    owner_ref,
    share_ref,
    normed_ref,
    branch_ref,
    query_block,
    output_block,
    queries,
    mixture,
    log_ref,
    prompt_kv_ref,
    answer_kv_ref,
    normed_across,
    key_sums,
    own_sums,
    grad_normed_ref,
):
    width = HEAD_WIDTH
    scale = HEAD_WIDTH ** (-0.5)
    length = prompt_kv_ref.shape[1]
    grad_mixture = plain_product(branch_ref[...], output_block).astype(jnp.bfloat16)

    def backward(keys, values, stacked, grad_stacked, log_row, inner_row, allowed):
        scores = transposed_product(keys, stacked)
        probs = jnp.exp(scores * scale - log_row)
        if allowed is not None:
            probs = jnp.where(allowed, probs, 0.0)
        grad_values = plain_product(probs.astype(jnp.bfloat16), grad_stacked)
        grad_probs = transposed_product(values, grad_stacked)
        grad_scores = (probs * (grad_probs - inner_row)).astype(jnp.bfloat16)
        grad_keys = plain_product(grad_scores, stacked)
        grad_queries = weight_product(grad_scores, keys)
        return grad_queries, grad_keys, grad_values

    pieces = []
    for part in range(prompts + answers):
        here, rows = part_rows(part, prompts, answers, normed_ref, answer_kv_ref)
        token = lax.broadcasted_iota(jnp.int32, (1, heads * rows), 1) % rows
        stacked = stack_heads(queries[here, :], heads)
        grad_stacked = stack_heads(grad_mixture[here, :], heads)
        mixed = stack_heads(mixture[here, :], heads)
        product = grad_stacked.astype(jnp.float32) * mixed.astype(jnp.float32)
        inner_row = jnp.sum(jnp.transpose(product), axis=0, keepdims=True)
        log_row = jnp.concatenate([log_ref[head : head + 1, here] for head in range(heads)], axis=1)
        if part < prompts:
            place = lax.broadcasted_iota(jnp.int32, (length, 1), 0)
            grad_queries, grad_keys, grad_values = backward(
                prompt_kv_ref[part, :, :width],
                prompt_kv_ref[part, :, width:],
                stacked,
                grad_stacked,
                log_row,
                inner_row,
                place <= start + token,
            )
            key_sums[part, :, :width] += grad_keys
            key_sums[part, :, width:] += grad_values
        else:
            answer = part - prompts
            owner = owner_ref[answer]
            own = slice(answer * rows, (answer + 1) * rows)
            grad_queries, grad_keys, grad_values = backward(
                prompt_kv_ref[owner, :, :width],
                prompt_kv_ref[owner, :, width:],
                stacked,
                grad_stacked,
                log_row,
                inner_row,
                None,
            )
            for prompt in range(prompts):
                share = share_ref[answer * prompts + prompt]
                key_sums[prompt, :, :width] += share * grad_keys
                key_sums[prompt, :, width:] += share * grad_values
            place = lax.broadcasted_iota(jnp.int32, (rows, 1), 0)
            own_queries, own_keys, own_values = backward(
                answer_kv_ref[own, :width],
                answer_kv_ref[own, width:],
                stacked,
                grad_stacked,
                log_row,
                inner_row,
                place <= token,
            )
            grad_queries = grad_queries + own_queries
            own_sums[own, :width] += own_keys
            own_sums[own, width:] += own_values
        pieces.append(unstack_heads((grad_queries * scale).astype(jnp.bfloat16), heads))
    grad_queries = jnp.concatenate(pieces, axis=0)
    grad_query_block = plain_product(normed_across[...], grad_queries).astype(jnp.bfloat16)
    grad_normed_ref[...] += transposed_product(grad_queries, query_block)
    grad_bias = jnp.sum(grad_queries.astype(jnp.float32), axis=0, keepdims=True)
    return grad_query_block, grad_bias


def attention_backward_kernel(
    prompts,
    answers,
    heads,
    place_ref,
    owner_ref,
    share_ref,
    normed_ref,
    query_ref,
    prompt_kv_ref,
    answer_kv_ref,
    output_ref,
    branch_ref,
    queries_ref,
    mixture_ref,
    log_ref,
    grad_weights_ref,
    grad_normed_ref,
    grad_prompt_ref,
    grad_answer_ref,
    grad_bias_ref,
    normed_across,
    branch_across,
    key_sums,
    own_sums,
):
    step = pl.program_id(0)
    width = HEAD_WIDTH
    scale = HEAD_WIDTH ** (-0.5)
    block = queries_ref.shape[2]

    @pl.when(step == 0)
    def _():
        normed_across[...] = jnp.transpose(normed_ref[...])
        branch_across[...] = jnp.transpose(branch_ref[...])
        key_sums[...] = jnp.zeros_like(key_sums)
        own_sums[...] = jnp.zeros_like(own_sums)
        grad_normed_ref[...] = jnp.zeros_like(grad_normed_ref)

    query_block, output_block = query_ref[0, 0], output_ref[0, 0]
    groups = grad_weights_ref.shape[1]
    weight_rows = query_block.shape[0] // groups
    grad_output_block = plain_product(branch_across[...], mixture_ref[0]).astype(jnp.bfloat16)
    grad_query_block, grad_bias = backward_block(
        prompts,
        answers,
        heads,
        place_ref[0],
        owner_ref,
        share_ref,
        normed_ref,
        branch_ref,
        query_block,
        output_block,
        queries_ref[0],
        mixture_ref[0],
        log_ref.at[0],
        prompt_kv_ref,
        answer_kv_ref,
        normed_across,
        key_sums,
        own_sums,
        grad_normed_ref,
    )
    grad_weights_ref[0, :, :weight_rows] = grad_query_block.reshape(groups, weight_rows, block)
    grad_weights_ref[0, :, weight_rows : 2 * weight_rows] = grad_output_block.reshape(
        groups, weight_rows, block
    )
    grad_bias_ref[0] = grad_bias

    @pl.when(step == pl.num_programs(0) - 1)
    def _():
        grad_prompt_ref[:, :, :width] = (key_sums[:, :, :width] * scale).astype(jnp.bfloat16)
        grad_prompt_ref[:, :, width:] = key_sums[:, :, width:].astype(jnp.bfloat16)
        grad_answer_ref[:, :width] = own_sums[:, :width] * scale
        grad_answer_ref[:, width:] = own_sums[:, width:]


def attention_backward(
    place,
    owning,
    share,
    normed,
    weights,
    groups,
    grad_rows,
    prompt_kv,
    answer_kv,
    branch,
    queries,
    mixture,
    log_total,
    prompts,
    answers,
):
    token_rows, model_width = normed.shape
    steps, _, _, block = weights.shape
    heads = block // HEAD_WIDTH
    length = prompt_kv.shape[1]
    whole = lambda *shape: pl.BlockSpec(shape, lambda step, *_: (0,) * len(shape))
    columns = lambda: pl.BlockSpec((1, token_rows, block), lambda step, *_: (step, 0, 0))
    kind = lambda which: pl.BlockSpec(
        (1, 1, model_width, block), lambda step, *_: (step, which, 0, 0)
    )
    scores = heads * token_rows * length
    return pl.pallas_call(
        functools.partial(
            attention_backward_kernel, prompts, answers, heads
        ),
        out_shape=(
            jax.ShapeDtypeStruct((steps, groups, grad_rows, block), jnp.bfloat16),
            jax.ShapeDtypeStruct((token_rows, model_width), jnp.float32),
            jax.ShapeDtypeStruct(prompt_kv.shape, jnp.bfloat16),
            jax.ShapeDtypeStruct(answer_kv.shape, jnp.float32),
            jax.ShapeDtypeStruct((steps, 1, block), jnp.float32),
        ),
        grid_spec=pltpu.PrefetchScalarGridSpec(
            num_scalar_prefetch=3,
            grid=(steps,),
            in_specs=[
                whole(token_rows, model_width),
                kind(0),
                whole(*prompt_kv.shape),
                whole(*answer_kv.shape),
                kind(1),
                whole(token_rows, model_width),
                columns(),
                columns(),
                pl.BlockSpec((1, heads, token_rows), lambda step, *_: (step, 0, 0)),
            ],
            out_specs=(
                pl.BlockSpec(
                    (1, groups, grad_rows, block), lambda step, *_: (step, 0, 0, 0)
                ),
                whole(token_rows, model_width),
                whole(*prompt_kv.shape),
                whole(*answer_kv.shape),
                pl.BlockSpec((1, 1, block), lambda step, *_: (step, 0, 0)),
            ),
            scratch_shapes=[
                pltpu.VMEM((model_width, token_rows), jnp.bfloat16),
                pltpu.VMEM((model_width, token_rows), jnp.bfloat16),
                pltpu.VMEM(prompt_kv.shape, jnp.float32),
                pltpu.VMEM(answer_kv.shape, jnp.float32),
            ],
        ),
        compiler_params=pltpu.CompilerParams(vmem_limit_bytes=VMEM_BYTES),
        cost_estimate=pl.CostEstimate(
            flops=steps * (8 * token_rows * model_width * block + 20 * scores * HEAD_WIDTH),
            bytes_accessed=16 * steps * model_width * block,
            transcendentals=steps * scores,
        ),
        name="attention_backward",
    )(
        place,
        owning,
        share,
        normed,
        weights,
        prompt_kv,
        answer_kv,
        weights,
        branch,
        queries,
        mixture,
        log_total,
    )


class PairedSum:
    def __init__(self, part, pair, sent, come, send_sem, recv_sem):
        here, on_x, on_y, on_chip, corner = block_of_eight()
        shift = on_chip - here
        self.places = (here, on_x, on_y, corner)
        self.part, self.pair, self.sent, self.come = part, pair, sent, come
        self.to_chip = [
            remote(index, part(place + shift), pair.at[index], on_chip, send_sem, recv_sem)
            for index, place in enumerate(self.places)
        ]
        self.over = [
            remote(3 + index, sent.at[index], come.at[index - 1], place, send_sem, recv_sem)
            for index, place in enumerate(self.places)
            if index
        ]

    def start(self):
        for each in self.to_chip:
            each.start()

    def pass_on(self):
        for each in self.to_chip:
            each.wait_recv()
        for index, place in enumerate(self.places):
            total = self.part(place)[...].astype(jnp.float32)
            total = total + self.pair[index].astype(jnp.float32)
            self.sent[index] = total.astype(self.sent.dtype)
        for each in self.over:
            each.start()

    def total(self):
        total = self.sent[0].astype(jnp.float32)
        for index, each in enumerate(self.over):
            each.wait_recv()
            total = total + self.come[index].astype(jnp.float32)
        return total

    def finish(self):
        for each in self.to_chip + self.over:
            each.wait_send()


VECTOR_ROWS = 16


def backward_reduce_kernel(
    prompts,
    answers,
    heads,
    groups,
    prompt_rows,
    owner_ref,
    share_ref,
    weights_ref,
    queries_ref,
    mixture_ref,
    hidden_hbm,
    normed_ref,
    branch_ref,
    log_ref,
    prompt_kv_ref,
    answer_kv_ref,
    states_ref,
    gain_ref,
    keyval_ref,
    known_up_ref,
    known_sums_ref,
    known_columns_ref,
    known_squares_ref,
    grad_query_ref,
    grad_output_ref,
    grad_keyval_ref,
    vectors_ref,
    own_vectors_ref,
    own_up_ref,
    grad_input_ref,
    normed_across,
    branch_across,
    key_sums,
    own_sums,
    grad_normed,
    grad_hidden,
    held,
    pair,
    kept,
    theirs,
    relayed,
    final,
    come,
    kv_part,
    kv_pair,
    kv_sent,
    kv_come,
    kv_rows,
    keyval_part,
    keyval_pair,
    keyval_sent,
    keyval_come,
    keyval_sum,
    keyval_over,
    vectors,
    vector_come,
    vector_sum,
    vector_over,
    send_sem,
    recv_sem,
    over_send,
    over_recv,
    peer_send,
    peer_recv,
    load_sem,
    hidden_sem,
):
    width = HEAD_WIDTH
    scale = HEAD_WIDTH ** (-0.5)
    here, on_x, on_y, on_chip, corner = block_of_eight()
    _, peers = peers_of(8)
    group = lax.axis_index("grp")
    other_groups = [(group + turn) % groups for turn in range(1, groups)]
    model_width, block = kept.shape[1:]
    chunk_rows = model_width // groups
    step = 64
    counter = iter(range(8 + 6 * groups))

    def copy(source, target, device):
        return remote(next(counter), source, target, device, send_sem, recv_sem)

    def over(index, source, target, turn):
        return pltpu.make_async_remote_copy(
            src_ref=source,
            dst_ref=target,
            send_sem=over_send.at[index],
            recv_sem=over_recv.at[index],
            device_id={"grp": other_groups[turn]},
            device_id_type=MESH,
        )

    def to_peers(row, source, target):
        return [
            pltpu.make_async_remote_copy(
                src_ref=source(peers[index]),
                dst_ref=target(index),
                send_sem=peer_send.at[row, index],
                recv_sem=peer_recv.at[row, index],
                device_id={"tok": peers[index]},
                device_id_type=MESH,
            )
            for index in range(len(peers))
        ]

    spans = [
        pl.ds(pl.multiple_of(((group + 1 + chunk) % groups) * chunk_rows, chunk_rows), chunk_rows)
        for chunk in range(groups)
    ]
    chunks = range(groups)
    by_x, by_y = chunks[: groups // 2], chunks[groups // 2 :]
    kinds = (0, 1)

    def mine(place, kind):
        return kept.at[4 + 2 * place + kind]

    def pieces_to(place, target, device):
        return [
            [copy(mine(place, kind).at[span], target(kind).at[span], device) for span in spans]
            for kind in kinds
        ]

    to_chip = [
        [copy(kept.at[place], theirs.at[place, kind], on_chip) for place in range(4)]
        for kind in kinds
    ]
    corners = [
        [
            copy(
                mine(0, kind).at[spans[chunk]],
                relayed.at[kind, spans[chunk]],
                on_x if chunk in by_x else on_y,
            )
            for chunk in chunks
        ]
        for kind in kinds
    ]
    to_x = pieces_to(2, lambda kind: final.at[0, kind], on_x)
    to_y = pieces_to(1, lambda kind: final.at[1, kind], on_y)
    across = [
        [over(2 * turn + kind, mine(3, kind).at[spans[turn]], come.at[turn, kind], turn) for kind in kinds]
        for turn in range(groups - 1)
    ]

    def lanes(device):
        return pl.ds(pl.multiple_of(device * block, block), block)

    def prompt_place(device):
        return pl.ds(pl.multiple_of(device * prompt_rows, prompt_rows), prompt_rows)

    kv_sums = PairedSum(
        lambda device: kv_part.at[:, prompt_place(device), :],
        kv_pair,
        kv_sent,
        kv_come,
        peer_send.at[0],
        peer_recv.at[0],
    )
    keyval_sums = PairedSum(
        lambda device: keyval_part.at[:, device],
        keyval_pair,
        keyval_sent,
        keyval_come,
        peer_send.at[1],
        peer_recv.at[1],
    )
    vector_copies = to_peers(
        2, lambda peer: vectors.at[:, lanes(peer)], lambda index: vector_come.at[index]
    )
    vector_out = to_peers(
        3, lambda peer: vector_sum, lambda index: vectors_ref.at[:, lanes(here)]
    )
    first_over = 2 * (groups - 1)
    keyval_across = [
        over(first_over + turn, keyval_sum.at[other_groups[turn]], keyval_over.at[turn], turn)
        for turn in range(groups - 1)
    ]
    vector_across = [
        over(first_over + groups - 1 + turn, vectors.at[:, lanes(here)], vector_over.at[turn], turn)
        for turn in range(groups - 1)
    ]

    load_hidden = pltpu.make_async_copy(hidden_hbm, grad_hidden, hidden_sem)
    load_hidden.start()
    greet_all(peers, other_groups)
    normed_across[...] = jnp.transpose(normed_ref[...])
    branch_across[...] = jnp.transpose(branch_ref[...])
    key_sums[...] = jnp.zeros_like(key_sums)
    own_sums[...] = jnp.zeros_like(own_sums)
    grad_normed[...] = jnp.zeros_like(grad_normed)
    vectors[...] = jnp.zeros_like(vectors)
    vectors[: known_up_ref.shape[0], :] = known_up_ref[...]
    vectors[4:7, :] = known_sums_ref[0:3, :]
    vectors[7:8, :] = known_columns_ref[...]
    squares = jnp.sum(known_squares_ref[...], axis=1, keepdims=True)
    vectors[12:13, :] = jnp.broadcast_to(squares, (1, model_width))

    def add_into(target, other, rows):
        @pl.loop(0, rows // step)
        def _(turn):
            at = chunk_of(turn, step)
            target[at, :] = target[at, :] + other[at, :]

    def join(kind, place):
        to_chip[kind][place].wait_recv()
        add_into(mine(place, kind), theirs.at[place, kind], model_width)

    def direct(kind, chunk):
        (to_x if chunk in by_x else to_y)[kind][chunk].start()

    def relay(kind, chunk):
        corners[kind][chunk].wait_recv()
        place, then = (1, to_y) if chunk in by_x else (2, to_x)
        span = spans[chunk]
        add_into(mine(place, kind).at[span], relayed.at[kind, span], chunk_rows)
        then[kind][chunk].start()

    def close(kind, chunk):
        span = spans[chunk]
        for source, part in enumerate((to_x, to_y)):
            part[kind][chunk].wait_recv()
            add_into(mine(3, kind).at[span], final.at[source, kind, span], chunk_rows)
        if chunk < groups - 1:
            across[chunk][kind].start()

    def slot_of(turn, kind):
        place = turn // 2
        return (1 - turn % 2) * place + (turn % 2) * (4 + 2 * place + kind)

    def send_to_chip(turn, kind):
        for place in range(4):

            @pl.when(turn == 2 * place)
            def _():
                to_chip[kind][place].start()

    @pl.loop(0, 8)
    def _(turn):
        load = pltpu.make_async_copy(
            mixture_ref.at[bits_away(7 - turn)], pair.at[1], load_sem.at[2]
        )
        load.start()
        load.wait()
        kept[slot_of(turn, 1)] = plain_product(branch_across[...], pair[1]).astype(jnp.bfloat16)
        send_to_chip(turn, 1)

        @pl.when(turn == 2)
        def _():
            join(1, 0)
            for chunk in chunks:
                corners[1][chunk].start()

        for place in (1, 2):

            @pl.when(turn == 2 * place + 2)
            def _():
                join(1, place)

    for chunk in chunks:
        direct(1, chunk)

    @pl.loop(0, 8)
    def _(turn):
        source = bits_away(7 - turn)
        loads = (
            pltpu.make_async_copy(weights_ref.at[source], held, load_sem.at[0]),
            pltpu.make_async_copy(queries_ref.at[source], pair.at[0], load_sem.at[1]),
            pltpu.make_async_copy(mixture_ref.at[source], pair.at[1], load_sem.at[2]),
        )
        for each in loads:
            each.start()
        for place in range(4):

            @pl.when(turn == 2 * place)
            def _():
                to_chip[1][place].wait_send()

        for each in loads:
            each.wait()
        grad_query_block, grad_bias = backward_block(
            prompts,
            answers,
            heads,
            here * prompt_rows,
            owner_ref,
            share_ref,
            normed_ref,
            branch_ref,
            held[:, 0].reshape(-1, block),
            held[:, 1].reshape(-1, block),
            pair[0],
            pair[1],
            log_ref.at[source],
            prompt_kv_ref,
            answer_kv_ref,
            normed_across,
            key_sums,
            own_sums,
            grad_normed,
        )
        kept[slot_of(turn, 0)] = grad_query_block
        vectors[10:11, lanes(source)] = grad_bias
        send_to_chip(turn, 0)

        @pl.when(turn == 1)
        def _():
            for chunk in chunks:
                relay(1, chunk)

        @pl.when(turn == 2)
        def _():
            join(0, 0)
            for chunk in chunks:
                corners[0][chunk].start()

        @pl.when(turn == 4)
        def _():
            join(0, 1)
            join(1, 3)

        @pl.when(turn == 5)
        def _():
            for chunk in chunks:
                close(1, chunk)

        @pl.when(turn == 6)
        def _():
            join(0, 2)
            for chunk in (by_x[0], by_y[0]):
                direct(0, chunk)
            for chunk in (by_x[0], by_y[0]):
                relay(0, chunk)

        @pl.when(turn == 7)
        def _():
            direct(0, by_x[1])
            relay(0, by_x[1])

    kv_part[:, :, :width] = (key_sums[:, :, :width] * scale).astype(jnp.bfloat16)
    kv_part[:, :, width:] = key_sums[:, :, width:].astype(jnp.bfloat16)
    kv_sums.start()
    join(0, 3)
    kv_sums.pass_on()
    for part in (to_x, to_y):
        part[0][by_x[0]].wait_send()
    direct(0, by_y[1])
    relay(0, by_y[1])
    close(0, by_x[0])

    own_prompt = prompts * prompt_rows
    total = kv_sums.total()
    for prompt in range(prompts):
        kv_rows[prompt * prompt_rows : (prompt + 1) * prompt_rows, :] = total[prompt].astype(
            jnp.bfloat16
        )
    kv_rows[own_prompt:, :width] = (own_sums[:, :width] * scale).astype(jnp.bfloat16)
    kv_rows[own_prompt:, width:] = own_sums[:, width:].astype(jnp.bfloat16)
    keyval_part[...] = (
        plain_product(normed_across[...], kv_rows[...])
        .astype(jnp.bfloat16)
        .reshape(keyval_part.shape)
    )
    keyval_sums.start()
    close(0, by_y[0])
    keyval_sums.pass_on()
    load_hidden.wait()
    vectors[11:12, :width] = jnp.sum(
        kv_rows[:, width:].astype(jnp.float32), axis=0, keepdims=True
    )
    piece = 16
    grad_normed[...] += transposed_product(kv_rows[...], keyval_ref[...])

    @pl.loop(0, states_ref.shape[0] // piece)
    def _(turn):
        at = chunk_of(turn, piece)
        scaled, inverse = norm_stats(states_ref[at, :].astype(jnp.float32))
        grad_out = grad_normed[at, :]
        weighted = grad_out * gain_ref[...]
        grad_in = inverse * (
            weighted
            - jnp.mean(weighted, axis=-1, keepdims=True)
            - scaled * jnp.mean(weighted * scaled, axis=-1, keepdims=True)
        )
        grad_input_ref[at, :] = (grad_hidden[at, :] + grad_in).astype(jnp.bfloat16)
        vectors[8:9, :] += jnp.sum(grad_out * scaled, axis=0, keepdims=True)
        vectors[9:10, :] += jnp.sum(grad_out, axis=0, keepdims=True)

    for each in vector_copies:
        each.start()
    keyval_sum[...] = keyval_sums.total().astype(jnp.bfloat16)
    for each in keyval_across:
        each.start()
    for each in vector_copies:
        each.wait_recv()
    total = vectors[:, lanes(here)]
    for index in range(len(peers)):
        total = total + vector_come[index]
    vectors[:, lanes(here)] = total
    for each in vector_across:
        each.start()
    close(0, by_x[1])
    for each in vector_across:
        each.wait_recv()
    total = vectors[:, lanes(here)]
    for turn in range(groups - 1):
        total = total + vector_over[turn]
    vector_sum[...] = total
    for each in vector_out:
        each.start()
    vectors_ref[:, lanes(here)] = vector_sum[...]
    close(0, by_y[1])
    for each in keyval_across:
        each.wait_recv()
    total = keyval_sum[group].astype(jnp.float32)
    for turn in range(groups - 1):
        total = total + keyval_over[turn].astype(jnp.float32)
    grad_keyval_ref[...] = total
    for kind, out_ref in ((0, grad_query_ref), (1, grad_output_ref)):
        for turn in range(groups - 1):
            across[turn][kind].wait_recv()
        own = pl.multiple_of(group * chunk_rows, chunk_rows)

        @pl.loop(0, chunk_rows // step)
        def _(turn):
            at = chunk_of(turn, step)
            total = kept[10 + kind, pl.ds(own + turn * step, step), :].astype(jnp.float32)
            for other in range(groups - 1):
                total = total + come[other, kind, at, :].astype(jnp.float32)
            out_ref[at, :] = total

    for each in vector_out:
        each.wait_recv()
    device = group * 8 + here
    share = model_width // (8 * groups)
    parts = width // share
    columns = vectors_ref[:, chunk_of(device // parts, width)]
    picked = columns
    for part in range(1, parts):
        moved = jnp.concatenate([columns[:, part * share :], columns[:, : part * share]], axis=1)
        picked = jnp.where(device % parts == part, moved, picked)
    own_vectors_ref[...] = picked
    up_share = own_up_ref.shape[1]
    in_row = model_width // up_share
    up_columns = vectors_ref[:, chunk_of(device % in_row, up_share)]
    up_own = jnp.zeros((1, up_share), jnp.float32)
    for row in range(known_up_ref.shape[0]):
        up_own = jnp.where(device // in_row == row, up_columns[row : row + 1, :], up_own)
    own_up_ref[...] = up_own
    for each in to_chip[0] + corners[0] + corners[1] + to_x[1] + to_y[1]:
        each.wait_send()
    for chunk in chunks[1:]:
        to_x[0][chunk].wait_send()
        to_y[0][chunk].wait_send()
    kv_sums.finish()
    keyval_sums.finish()
    for each in vector_copies + vector_out:
        each.wait_send()
    for each in sum(across, []) + keyval_across + vector_across:
        each.wait_send()


def backward_reduce(
    owning,
    share,
    weights,
    queries,
    mixture,
    grad_hidden,
    normed,
    branch,
    log_total,
    prompt_kv,
    answer_kv,
    states,
    gain,
    keyval_full,
    known_up,
    known_sums,
    known_columns,
    known_squares,
    groups,
    prompts,
    answers,
    prompt_rows,
    call_number,
):
    token_rows, model_width = normed.shape
    block = weights.shape[4]
    heads = block // HEAD_WIDTH
    keyval_width = keyval_full.shape[1]
    weight_rows = model_width // groups
    keyval_rows = model_width // groups // 8
    kind, wide = jnp.bfloat16, jnp.float32
    inside = pl.BlockSpec(memory_space=pltpu.VMEM)
    anywhere = pl.BlockSpec(memory_space=pl.ANY)
    scalars = pl.BlockSpec(memory_space=pltpu.SMEM)
    dma = pltpu.SemaphoreType.DMA
    others = groups - 1
    return pl.pallas_call(
        functools.partial(backward_reduce_kernel, prompts, answers, heads, groups, prompt_rows),
        out_shape=(
            jax.ShapeDtypeStruct((weight_rows, block), wide),
            jax.ShapeDtypeStruct((weight_rows, block), wide),
            jax.ShapeDtypeStruct((keyval_rows, keyval_width), wide),
            jax.ShapeDtypeStruct((VECTOR_ROWS, model_width), wide),
            jax.ShapeDtypeStruct((VECTOR_ROWS, HEAD_WIDTH), wide),
            jax.ShapeDtypeStruct((1, known_up.size // (8 * groups)), wide),
            jax.ShapeDtypeStruct((token_rows, model_width), kind),
        ),
        in_specs=[scalars] * 2 + [anywhere] * 4 + [inside] * 12,
        out_specs=(inside,) * 7,
        scratch_shapes=[
            pltpu.VMEM((model_width, token_rows), kind),
            pltpu.VMEM((model_width, token_rows), kind),
            pltpu.VMEM(prompt_kv.shape, wide),
            pltpu.VMEM(answer_kv.shape, wide),
            pltpu.VMEM((token_rows, model_width), wide),
            pltpu.VMEM((token_rows, model_width), wide),
            pltpu.VMEM(weights.shape[1:], kind),
            pltpu.VMEM((2, token_rows, block), kind),
            pltpu.VMEM((12, model_width, block), kind),
            pltpu.VMEM((4, 2, model_width, block), kind),
            pltpu.VMEM((2, model_width, block), kind),
            pltpu.VMEM((2, 2, model_width, block), kind),
            pltpu.VMEM((others, 2, weight_rows, block), kind),
            pltpu.VMEM(prompt_kv.shape, kind),
            pltpu.VMEM((4, prompts, prompt_rows, keyval_width), kind),
            pltpu.VMEM((4, prompts, prompt_rows, keyval_width), kind),
            pltpu.VMEM((3, prompts, prompt_rows, keyval_width), kind),
            pltpu.VMEM((token_rows, keyval_width), kind),
            pltpu.VMEM((groups, 8, keyval_rows, keyval_width), kind),
            pltpu.VMEM((4, groups, keyval_rows, keyval_width), kind),
            pltpu.VMEM((4, groups, keyval_rows, keyval_width), kind),
            pltpu.VMEM((3, groups, keyval_rows, keyval_width), kind),
            pltpu.VMEM((groups, keyval_rows, keyval_width), kind),
            pltpu.VMEM((others, keyval_rows, keyval_width), kind),
            pltpu.VMEM((VECTOR_ROWS, model_width), wide),
            pltpu.VMEM((7, VECTOR_ROWS, block), wide),
            pltpu.VMEM((VECTOR_ROWS, block), wide),
            pltpu.VMEM((others, VECTOR_ROWS, block), wide),
            dma((8 + 6 * groups,)),
            dma((8 + 6 * groups,)),
            dma((4 * others,)),
            dma((4 * others,)),
            dma((4, 7)),
            dma((4, 7)),
            dma((3,)),
            dma,
        ],
        compiler_params=pltpu.CompilerParams(
            collective_id=call_number,
            has_side_effects=True,
            vmem_limit_bytes=63 * 1024 * 1024,
        ),
        cost_estimate=pl.CostEstimate(
            flops=100 * token_rows * model_width * block,
            bytes_accessed=250 * 1000 * 1000,
            transcendentals=0,
        ),
        name="backward_reduce",
    )(
        owning,
        share,
        weights,
        queries,
        mixture,
        grad_hidden,
        normed,
        branch,
        log_total,
        prompt_kv,
        answer_kv,
        states,
        gain.reshape(1, -1),
        keyval_full,
        known_up,
        known_sums,
        known_columns,
        known_squares,
    )


def by_group(values):
    return jnp.swapaxes(values, 0, 1).reshape(-1)


def body(
    kernels,
    prompt_states,
    answer_states,
    answer_prompt,
    prompt_teacher,
    answer_teacher,
    prompt_valid,
    answer_valid,
    first_gain,
    first_shift,
    query_weight,
    query_bias,
    keyval_weight,
    value_bias,
    output_weight,
    output_bias,
    second_gain,
    second_shift,
    up_weight,
    up_bias,
    down_weight,
    down_bias,
):
    prompt_count, prompt_rows, model_width = prompt_states.shape
    answer_count, answer_len, _ = answer_states.shape
    groups = lax.axis_size("grp")
    token_devices = lax.axis_size("tok")
    token_index = lax.axis_index("tok")
    group_index = lax.axis_index("grp")
    own_prompt = prompt_rows * prompt_count
    token_rows = own_prompt + answer_count * answer_len
    hidden_units = up_bias.shape[0] * groups * token_devices
    ff_here = hidden_units // token_devices
    ff_start = token_index * ff_here
    share_size = first_gain.shape[0]
    block = query_weight.shape[1]
    weight_rows = query_weight.shape[0]
    keyval_rows, keyval_width = keyval_weight.shape

    def own_rows(prompt_part, answer_part):
        return jnp.concatenate(
            [prompt_part.reshape(own_prompt, -1), answer_part.reshape(-1, prompt_part.shape[-1])],
            axis=0,
        )

    states = own_rows(prompt_states, answer_states)
    inputs = states.astype(jnp.float32)
    valid_rows = jnp.concatenate([prompt_valid.reshape(-1), answer_valid.reshape(-1)])
    own_count = jnp.sum(valid_rows)
    valid_rows = valid_rows.astype(jnp.float32)

    up_cols = lax.all_gather(up_weight, "grp", axis=0, tiled=True)
    down_cols = lax.all_gather(down_weight, "grp", axis=0, tiled=True)

    projections = lax.all_gather(jnp.stack([query_weight, output_weight]), "grp", axis=0)
    count_parts = jnp.stack([own_count // 128, own_count % 128]).astype(jnp.bfloat16)
    smalls, small_at = jnp.zeros((SMALL_ROWS * block,), jnp.bfloat16), 0
    for each in (
        first_gain,
        first_shift,
        query_bias,
        output_bias,
        second_gain,
        second_shift,
        down_bias,
        up_bias,
        count_parts,
    ):
        behind = SMALL_ROWS * block - small_at - each.shape[0]
        smalls = smalls + jnp.pad(each, (small_at, behind))
        small_at += each.shape[0]
    smalls = smalls.reshape(SMALL_ROWS, block)
    pack = jnp.concatenate([keyval_weight.reshape(-1, block), smalls], axis=0)
    packed = spread(pack, groups, 0, kernels)
    keyval_pack = pack.shape[0] - SMALL_ROWS
    keyval_start = 2 * weight_rows
    keyval_full = jnp.swapaxes(
        packed[:, :, :keyval_pack].reshape(token_devices, groups, keyval_rows, keyval_width),
        0,
        1,
    ).reshape(model_width, keyval_width)
    small_full = packed[:, :, keyval_pack:].reshape(token_devices, groups, SMALL_ROWS * block)
    small_full = jnp.swapaxes(small_full.astype(jnp.float32), 0, 1)

    def vector(start, size):
        return small_full[:, :, start : start + size].reshape(-1)

    gain_one, shift_one, query_offset, output_offset, gain_two, shift_two, down_offset = (
        vector(index * share_size, share_size) for index in range(7)
    )
    up_offset = vector(7 * share_size, up_bias.shape[0])
    count_at = 7 * share_size + up_bias.shape[0]
    counts = small_full[:, :, count_at : count_at + 2]
    valid_count = jnp.sum(counts[:, :, 0]) * 128.0 + jnp.sum(counts[:, :, 1])
    up_here = lax.dynamic_slice_in_dim(up_offset, ff_start, ff_here)

    scaled_one, inverse_one = norm_stats(inputs)
    normed_one = (scaled_one * gain_one + shift_one).astype(jnp.bfloat16)
    key_offset = jnp.concatenate(
        [jnp.zeros((HEAD_WIDTH,), jnp.float32), value_bias.astype(jnp.float32)]
    )
    key_value_rows = (plain_product(normed_one, keyval_full) + key_offset).astype(jnp.bfloat16)
    prompt_kv = tok_gather_small(
        key_value_rows[:own_prompt].reshape(prompt_count, prompt_rows, -1), 1, kernels
    )
    answer_kv = key_value_rows[own_prompt:]
    owning = answer_prompt - group_index * prompt_count
    owning = lax.dynamic_slice_in_dim(owning, token_index * answer_count, answer_count)
    place = jnp.reshape(token_index * prompt_rows, (1,)).astype(jnp.int32)
    if kernels:
        weights, queries, mixture, log_total, hidden, normed_two = gather_attention(
            owning,
            projections,
            normed_one,
            query_offset,
            prompt_kv,
            answer_kv,
            states,
            output_offset,
            gain_two,
            shift_two,
            prompt_count,
            answer_count,
            prompt_rows,
            8,
        )
    else:
        weights = lax.all_gather(projections, "tok", axis=0)
        weights = jnp.swapaxes(weights, 1, 2).reshape(token_devices, 2, model_width, block)
        queries, mixture, log_total, hidden, normed_two = attention_forward(
            place,
            owning,
            normed_one,
            weights[:, 0],
            weights[:, 1],
            query_offset,
            prompt_kv,
            answer_kv,
            states,
            output_offset,
            gain_two,
            shift_two,
            prompt_count,
            answer_count,
        )

    teacher = own_rows(prompt_teacher, answer_teacher)
    every_token = token_rows * groups * token_devices
    factors = (every_token / valid_count * valid_rows)[:, None]
    if kernels:
        group_two, activated, slope = gather_and_up(normed_two, up_cols, up_here, 2)
        result_rows, grad_branch_two, grad_result, own_squares, grad_down_offset = (
            product_and_reduce(
                activated,
                down_cols,
                None,
                hidden,
                teacher,
                3,
                down_offset.reshape(1, -1),
                valid_rows[:, None],
                factors,
            )
        )
        _, grad_pre_active, grad_down_cols, grad_up_offset = gather_and_grad(
            grad_branch_two, down_cols, activated, slope, 4
        )
        grad_hidden, grad_up_cols, grad_branch_one, second_sums = product_and_reduce(
            grad_pre_active,
            up_cols,
            group_two,
            hidden,
            grad_result,
            5,
            gain_two.reshape(1, -1),
        )
        grad_up_offset = grad_up_offset.reshape(-1)
    else:
        group_two = lax.all_gather(normed_two, "tok", axis=0, tiled=True)
        pre_active = plain_product(group_two, up_cols) + up_here
        activated = jax.nn.gelu(pre_active, approximate=True).astype(jnp.bfloat16)
        feed_term = for_sending(transposed_product(activated, down_cols))
        feed_term = lax.psum_scatter(feed_term, "tok", scatter_dimension=0, tiled=True)
        result_rows = hidden + feed_term.astype(jnp.float32) + down_offset
        differ = result_rows - teacher.astype(jnp.float32)
        own_squares = jnp.sum(valid_rows[:, None] * differ * differ)
        grad_result = factors * differ
        grad_branch_two = grad_result.astype(jnp.bfloat16)
        grad_down_offset = column_sums(grad_branch_two)
        group_grad_two = lax.all_gather(grad_branch_two, "tok", axis=0, tiled=True)
        grad_activated = plain_product(group_grad_two, down_cols)
        _, gelu_back = jax.vjp(
            lambda argument: jax.nn.gelu(argument, approximate=True), pre_active
        )
        grad_pre_active = gelu_back(grad_activated)[0].astype(jnp.bfloat16)
        grad_normed_two = for_sending(transposed_product(grad_pre_active, up_cols))
        grad_normed_two = lax.psum_scatter(
            grad_normed_two, "tok", scatter_dimension=0, tiled=True
        ).astype(jnp.float32)
        grad_down_cols = for_sending(weight_product(group_grad_two, activated))
        grad_up_cols = for_sending(weight_product(group_two, grad_pre_active))
        grad_up_offset = column_sums(grad_pre_active)
        scaled_two, inverse_two = norm_stats(hidden)
        grad_norm_two, grad_gain_two, grad_shift_two = norm_backward(
            grad_normed_two, gain_two, scaled_two, inverse_two
        )
        grad_hidden = grad_result + grad_norm_two
        grad_branch_one = grad_hidden.astype(jnp.bfloat16)
        grad_output_offset = column_sums(grad_branch_one)
    grad_down_weight = lax.psum_scatter(grad_down_cols, "grp", scatter_dimension=0, tiled=True)
    grad_down_weight, grad_up_cols = lax.optimization_barrier((grad_down_weight, grad_up_cols))
    grad_up_weight = lax.psum_scatter(grad_up_cols, "grp", scatter_dimension=0, tiled=True)

    share = (owning[:, None] == jnp.arange(prompt_count)[None, :]).astype(jnp.float32).reshape(-1)
    grad_up_place = lax.dynamic_update_slice_in_dim(
        jnp.zeros((hidden_units,), jnp.float32), grad_up_offset, ff_start, 0
    )
    if kernels:
        (
            grad_query_own,
            grad_output_own,
            grad_keyval_own,
            vectors,
            mine,
            grad_up_own,
            grad_inputs,
        ) = backward_reduce(
            owning,
            share,
            weights,
            queries,
            mixture,
            grad_hidden,
            normed_one,
            grad_branch_one,
            log_total,
            prompt_kv,
            answer_kv,
            states,
            gain_one,
            keyval_full,
            grad_up_place.reshape(-1, model_width),
            second_sums,
            grad_down_offset,
            own_squares,
            groups,
            prompt_count,
            answer_count,
            prompt_rows,
            6,
        )
        value_total = vectors[11, :HEAD_WIDTH]
        squared_sum = vectors[12, 0]
        own_vectors = [mine[row, :share_size] for row in (8, 9, 10, 4, 5, 6, 7)]
        grad_up_own = grad_up_own.reshape(-1)
    else:
        grad_rows = keyval_start + keyval_pack
        grad_weights, grad_normed_one, grad_prompt_kv, grad_answer_kv, grad_query_offset = (
            attention_backward(
                place,
                owning,
                share,
                normed_one,
                weights,
                groups,
                grad_rows,
                prompt_kv,
                answer_kv,
                grad_branch_one,
                queries,
                mixture,
                log_total,
                prompt_count,
                answer_count,
            )
        )
        grad_prompt_kv = lax.psum_scatter(
            grad_prompt_kv, "tok", scatter_dimension=1, tiled=True
        ).astype(jnp.float32)
        grad_keyvals = jnp.concatenate(
            [grad_prompt_kv.reshape(own_prompt, -1), grad_answer_kv], axis=0
        ).astype(jnp.bfloat16)
        grad_keyval_full = weight_product(normed_one, grad_keyvals)
        grad_value_offset = column_sums(grad_keyvals[:, HEAD_WIDTH:])
        grad_normed_one = grad_normed_one + transposed_product(grad_keyvals, keyval_full)
        grad_norm_one, grad_gain_one, grad_shift_one = norm_backward(
            grad_normed_one, gain_one, scaled_one, inverse_one
        )
        grad_inputs = grad_hidden + grad_norm_one

        grad_keyval_blocks = jnp.swapaxes(
            grad_keyval_full.astype(jnp.bfloat16).reshape(groups, token_devices, -1, block), 0, 1
        )
        grad_weights = lax.dynamic_update_slice(
            grad_weights, grad_keyval_blocks, (0, 0, keyval_start, 0)
        )
        vectors = (
            grad_gain_one,
            grad_shift_one,
            grad_query_offset.reshape(-1),
            grad_output_offset,
            grad_gain_two,
            grad_shift_two,
            grad_down_offset,
            grad_up_place,
        )
        totals = jnp.concatenate([grad_value_offset, own_squares.reshape(1)])
        blocks = jnp.concatenate(
            [each.reshape(groups, token_devices, -1) for each in vectors]
            + [jnp.broadcast_to(totals, (groups, token_devices, totals.shape[0]))],
            axis=2,
        )
        blocks = jnp.pad(blocks, ((0, 0), (0, 0), (0, SMALL_SUMS - blocks.shape[2])))
        blocks = jnp.swapaxes(blocks, 0, 1).reshape(token_devices, -1, HEAD_WIDTH)
        grad_weights = lax.psum_scatter(
            grad_weights.reshape(token_devices, -1, block), "tok", scatter_dimension=0, tiled=False
        )
        grad_weights = lax.psum_scatter(grad_weights, "grp", scatter_dimension=0, tiled=True)
        grad_weights = grad_weights.astype(jnp.float32)
        small_sums = lax.psum_scatter(blocks, "tok", scatter_dimension=0, tiled=False)
        small_sums = lax.psum_scatter(small_sums, "grp", scatter_dimension=0, tiled=True)
        small_sums = small_sums.reshape(-1)
        up_share = up_bias.shape[0]
        totals_at = 7 * share_size + up_share
        value_total = small_sums[totals_at : totals_at + HEAD_WIDTH]
        squared_sum = small_sums[totals_at + HEAD_WIDTH]
        own_vectors = [
            small_sums[index * share_size : (index + 1) * share_size] for index in range(7)
        ]
        grad_up_own = small_sums[7 * share_size : totals_at]
        grad_query_own = grad_weights[:weight_rows]
        grad_output_own = grad_weights[weight_rows:keyval_start]
        grad_keyval_own = grad_weights[keyval_start:].reshape(keyval_rows, keyval_width)
        grad_inputs = grad_inputs.astype(jnp.bfloat16)
    loss_value = squared_sum / (valid_count * model_width)

    def split_rows(values):
        values = values.astype(jnp.bfloat16)
        return (
            values[:own_prompt].reshape(prompt_states.shape),
            values[own_prompt:].reshape(answer_states.shape),
        )

    prompt_out, answer_out = split_rows(result_rows)
    prompt_grad, answer_grad = split_rows(grad_inputs)
    pieces = own_vectors
    return (
        prompt_out,
        answer_out,
        prompt_grad,
        answer_grad,
        pieces[0],
        pieces[1],
        grad_query_own,
        pieces[2],
        grad_keyval_own,
        value_total,
        grad_output_own,
        pieces[3],
        pieces[4],
        pieces[5],
        grad_up_weight.astype(jnp.float32),
        grad_up_own,
        grad_down_weight.astype(jnp.float32),
        pieces[6],
        loss_value,
    )


def solution(mesh):
    rows = P(("grp", "tok"))
    table = P(("grp", "tok"), None)
    matrix = P("grp", "tok")
    prompt_part = P("grp", "tok", None)
    answer_part = P(("grp", "tok"), None, None)
    in_specs = (
        prompt_part,
        answer_part,
        P("grp"),
        prompt_part,
        answer_part,
        P("grp", "tok"),
        table,
        rows,
        rows,
        matrix,
        rows,
        table,
        P(),
        matrix,
        rows,
        rows,
        rows,
        matrix,
        rows,
        matrix,
        rows,
    )
    out_specs = (
        prompt_part,
        answer_part,
        prompt_part,
        answer_part,
        rows,
        rows,
        matrix,
        rows,
        table,
        P(),
        matrix,
        rows,
        rows,
        rows,
        matrix,
        rows,
        matrix,
        rows,
        P(),
    )
    kernels = mesh.shape["tok"] == 8
    return jax.shard_map(
        functools.partial(body, kernels),
        mesh=mesh,
        in_specs=in_specs,
        out_specs=out_specs,
        check_vma=False,
    )
```

```python
import functools

import jax
import jax.numpy as jnp
from jax import lax
from jax.experimental import pallas as pl
from jax.experimental.pallas import tpu as pltpu
from jax.sharding import PartitionSpec as P

HEAD_WIDTH = 128
epsilon = 1e-05
masked = -1e30
MESH = pl.DeviceIdType.MESH
VMEM_BYTES = 56 * 1024 * 1024
SMALL_ROWS = 16
SMALL_SUMS = 1024


def for_sending(value):
    return value.astype(jnp.bfloat16)


def plain_product(left, right):
    return jnp.dot(left, right, preferred_element_type=jnp.float32)


def transposed_product(left, right):
    return lax.dot_general(
        left, right, (((1,), (1,)), ((), ())), preferred_element_type=jnp.float32
    )


def weight_product(left, right):
    return lax.dot_general(
        left, right, (((0,), (0,)), ((), ())), preferred_element_type=jnp.float32
    )


def norm_stats(values):
    center = values - jnp.mean(values, axis=-1, keepdims=True)
    inverse = lax.rsqrt(jnp.mean(center * center, axis=-1, keepdims=True) + epsilon)
    return center * inverse, inverse


def norm_backward(grad_out, gain, scaled, inverse):
    weighted = grad_out * gain
    grad_in = inverse * (
        weighted
        - jnp.mean(weighted, axis=-1, keepdims=True)
        - scaled * jnp.mean(weighted * scaled, axis=-1, keepdims=True)
    )
    return (grad_in, jnp.sum(grad_out * scaled, axis=0), jnp.sum(grad_out, axis=0))


def column_sums(values):
    return jnp.sum(values.astype(jnp.float32), axis=0)


def block_of_eight():
    here = lax.axis_index("tok")
    core, across, along = here % 2, (here // 2) % 2, here // 4
    on_x = here + 2 - 4 * across
    on_y = here + 4 - 8 * along
    on_chip = here + 1 - 2 * core
    corner = on_x + 4 - 8 * along
    return here, on_x, on_y, on_chip, corner


def greet_all(peers, other_groups):
    barrier = pltpu.get_barrier_semaphore()
    for peer in peers:
        pl.semaphore_signal(barrier, inc=1, device_id={"tok": peer}, device_id_type=MESH)
    for other in other_groups:
        pl.semaphore_signal(barrier, inc=1, device_id={"grp": other}, device_id_type=MESH)
    pl.semaphore_wait(barrier, len(peers) + len(other_groups))


def greet(devices):
    barrier = pltpu.get_barrier_semaphore()
    for device in devices:
        pl.semaphore_signal(barrier, inc=1, device_id={"tok": device}, device_id_type=MESH)
    pl.semaphore_wait(barrier, len(devices))


def paired_gather(source, place, send_sem, recv_sem):
    here, on_x, on_y, on_chip, corner = block_of_eight()
    over = [
        remote(index, source, place(here), device, send_sem, recv_sem)
        for index, device in enumerate((on_x, on_y, corner, on_chip))
    ]
    handed = [
        remote(4 + index, place(device), place(device), on_chip, send_sem, recv_sem)
        for index, device in enumerate((on_x, on_y, corner))
    ]
    for each in over:
        each.start()
    for each, then in zip(over, handed):
        each.wait_recv()
        then.start()
    for each in [over[3]] + handed:
        each.wait_recv()
    for each in over + handed:
        each.wait_send()


def spread_kernel(groups, own_ref, out_ref, held, send_sem, recv_sem, over_send, over_recv):
    here, on_x, on_y, on_chip, corner = block_of_eight()
    group = lax.axis_index("grp")
    other_groups = [(group + turn) % groups for turn in range(1, groups)]
    greet_all((on_x, on_y, on_chip, corner), other_groups)
    over = [
        pltpu.make_async_remote_copy(
            src_ref=own_ref,
            dst_ref=held.at[group],
            send_sem=over_send.at[index],
            recv_sem=over_recv.at[index],
            device_id={"grp": other},
            device_id_type=MESH,
        )
        for index, other in enumerate(other_groups)
    ]
    for each in over:
        each.start()
    held[group] = own_ref[...]
    for each in over:
        each.wait_recv()
    out_ref[here] = held[...]
    paired_gather(held, lambda device: out_ref.at[device], send_sem, recv_sem)
    for each in over:
        each.wait_send()


def spread(own, groups, call_number, kernels):
    if not kernels:
        return lax.all_gather(lax.all_gather(own, "grp", axis=0), "tok", axis=0)
    inside = pl.BlockSpec(memory_space=pltpu.VMEM)
    dma = pltpu.SemaphoreType.DMA
    return pl.pallas_call(
        functools.partial(spread_kernel, groups),
        out_shape=jax.ShapeDtypeStruct((8, groups) + own.shape, own.dtype),
        in_specs=[inside],
        out_specs=inside,
        scratch_shapes=[
            pltpu.VMEM((groups,) + own.shape, own.dtype),
            dma((7,)),
            dma((7,)),
            dma((groups - 1,)),
            dma((groups - 1,)),
        ],
        compiler_params=pltpu.CompilerParams(collective_id=call_number, has_side_effects=True),
        name="spread",
    )(own)


def remote(index, source, target, device, send_sem, recv_sem):
    return pltpu.make_async_remote_copy(
        src_ref=source,
        dst_ref=target,
        send_sem=send_sem.at[index],
        recv_sem=recv_sem.at[index],
        device_id={"tok": device},
        device_id_type=MESH,
    )


def chunk_of(index, size):
    return pl.ds(pl.multiple_of(index * size, size), size)


CHUNK = 512
LINEAR = 0.7978845608
CUBIC = 0.044715


def gather_beside(own_ref, out_ref, send_sem, recv_sem, local_sem, use):
    rows = own_ref.shape[0]
    half, quarter = rows // 2, rows // 4
    here, on_x, on_y, on_chip, corner = block_of_eight()
    shift = on_chip - here
    counter = iter(range(GATHER_COPIES))

    def copy(source, block, start, count, device):
        place = pl.ds(start, count)
        return remote(
            next(counter),
            source.at[place] if source is own_ref else source.at[block, place],
            out_ref.at[block, place],
            device,
            send_sem,
            recv_sem,
        )

    greet((on_x, on_y, on_chip))
    own = pltpu.make_async_copy(own_ref, out_ref.at[here], local_sem)
    x_low = copy(own_ref, here, 0, half, on_x)
    y_high = copy(own_ref, here, half, half, on_y)
    x_high = copy(own_ref, here, half, half, on_x)
    y_low = copy(own_ref, here, 0, half, on_y)
    to_chip = copy(own_ref, here, 0, rows, on_chip)
    to_y = [copy(out_ref, on_x, turn * quarter, quarter, on_y) for turn in (0, 1)]
    to_x = [copy(out_ref, on_y, half + turn * quarter, quarter, on_x) for turn in (0, 1)]
    chip_x = [copy(out_ref, on_x, turn * half, half, on_chip) for turn in (0, 1)]
    chip_y = [copy(out_ref, on_y, turn * half, half, on_chip) for turn in (0, 1)]
    chip_corner = [copy(out_ref, corner, turn * quarter, quarter, on_chip) for turn in range(4)]
    for each in (x_low, y_high, x_high, y_low, to_chip, own):
        each.start()
    use(0, [(here, 0, rows)])
    to_chip.wait_recv()
    use(1, [(on_chip, 0, rows)])
    x_low.wait_recv()
    for each in (*to_y, chip_x[0]):
        each.start()
    y_high.wait_recv()
    for each in (*to_x, chip_y[1]):
        each.start()
    use(2, [(on_x, 0, half), (on_y, half, half)])
    chip_x[0].wait_recv()
    chip_y[1].wait_recv()
    use(3, [(on_x + shift, 0, half), (on_y + shift, half, half)])
    x_high.wait_recv()
    chip_x[1].start()
    y_low.wait_recv()
    chip_y[0].start()
    use(4, [(on_x, half, half), (on_y, 0, half)])
    chip_x[1].wait_recv()
    chip_y[0].wait_recv()
    use(5, [(on_x + shift, half, half), (on_y + shift, 0, half)])
    for turn in (0, 1):
        to_y[turn].wait_recv()
        chip_corner[turn].start()
        to_x[turn].wait_recv()
        chip_corner[2 + turn].start()
        chip_corner[turn].wait_recv()
        chip_corner[2 + turn].wait_recv()
        use(
            6 + turn,
            [
                (block, start + turn * quarter, quarter)
                for block in (corner, corner + shift)
                for start in (0, half)
            ],
        )
    own.wait()
    for each in (x_low, y_high, x_high, y_low, to_chip, *to_y, *to_x, *chip_x, *chip_y, *chip_corner):
        each.wait_send()


GATHER_COPIES = 17


def moves(outside, inside, pieces, semaphores, outward):
    done, copies = 0, []
    for index, (block, start, count) in enumerate(pieces):
        away = outside.at[block, pl.ds(start, count)]
        near = inside.at[pl.ds(done, count)]
        pair = (near, away) if outward else (away, near)
        copies.append(pltpu.make_async_copy(*pair, semaphores.at[index]))
        done += count
    return copies


def up_kernel(
    own_ref,
    up_hbm,
    bias_ref,
    rows_ref,
    active_ref,
    slope_ref,
    up,
    rows,
    active,
    slope,
    send_sem,
    recv_sem,
    local_sem,
    weight_sem,
    row_sem,
    store_sem,
):
    weights = pltpu.make_async_copy(up_hbm, up, weight_sem)
    weights.start()
    stores = {}

    def use(place, pieces):
        slot = place % 2
        if place:
            loads = moves(rows_ref, rows, pieces, row_sem, False)
        else:
            loads = [pltpu.make_async_copy(own_ref, rows, row_sem.at[0])]
        for each in loads:
            each.start()
        if place == 0:
            weights.wait()
        for each in stores.pop(slot, ()):
            each.wait()
        for each in loads:
            each.wait()

        @pl.loop(0, up.shape[1] // CHUNK)
        def _(turn):
            at = chunk_of(turn, CHUNK)
            value = plain_product(rows[...], up[:, at]) + bias_ref[:, at]
            square = value * value
            bent = jnp.tanh(value * (LINEAR + (LINEAR * CUBIC) * square))
            level = 0.5 + 0.5 * bent
            active[slot, :, at] = (value * level).astype(jnp.bfloat16)
            slope[slot, :, at] = (
                level
                + (0.5 * value)
                * (1.0 - bent * bent)
                * (LINEAR + (3.0 * LINEAR * CUBIC) * square)
            ).astype(jnp.bfloat16)

        stores[slot] = moves(
            active_ref, active.at[slot], pieces, store_sem.at[slot, 0], True
        ) + moves(slope_ref, slope.at[slot], pieces, store_sem.at[slot, 1], True)
        for each in stores[slot]:
            each.start()

    gather_beside(own_ref, rows_ref, send_sem, recv_sem, local_sem, use)
    for slot in (0, 1):
        for each in stores[slot]:
            each.wait()


def gather_and_up(own, up_cols, bias, call_number):
    token_rows, model_width = own.shape
    width = up_cols.shape[1]
    hidden = jax.ShapeDtypeStruct((8, token_rows, width), jnp.bfloat16)
    anywhere = pl.BlockSpec(memory_space=pl.ANY)
    dma = pltpu.SemaphoreType.DMA
    return pl.pallas_call(
        up_kernel,
        out_shape=(
            jax.ShapeDtypeStruct((8, token_rows, model_width), jnp.bfloat16),
            hidden,
            hidden,
        ),
        in_specs=[anywhere, anywhere, pl.BlockSpec(memory_space=pltpu.VMEM)],
        out_specs=(anywhere, anywhere, anywhere),
        scratch_shapes=[
            pltpu.VMEM(up_cols.shape, jnp.bfloat16),
            pltpu.VMEM((token_rows, model_width), jnp.bfloat16),
            pltpu.VMEM((2, token_rows, width), jnp.bfloat16),
            pltpu.VMEM((2, token_rows, width), jnp.bfloat16),
            dma((GATHER_COPIES,)),
            dma((GATHER_COPIES,)),
            dma,
            dma,
            dma((4,)),
            dma((2, 2, 4)),
        ],
        compiler_params=pltpu.CompilerParams(
            collective_id=call_number, has_side_effects=True, vmem_limit_bytes=VMEM_BYTES
        ),
        cost_estimate=pl.CostEstimate(
            flops=16 * token_rows * model_width * width,
            bytes_accessed=150 * 1000 * 1000,
            transcendentals=0,
        ),
        name="gather_and_up",
    )(own, up_cols, bias.reshape(1, -1))


def grad_kernel(
    own_ref,
    down_hbm,
    active_ref,
    slope_ref,
    rows_ref,
    grad_ref,
    weight_ref,
    bias_ref,
    down,
    rows,
    active,
    slope,
    grads,
    sums,
    narrow,
    send_sem,
    recv_sem,
    local_sem,
    weight_sem,
    row_sem,
    load_sem,
    store_sem,
):
    weights = pltpu.make_async_copy(down_hbm, down, weight_sem)
    weights.start()
    stores = {}

    def use(place, pieces):
        slot = place % 2
        if place:
            loads = moves(rows_ref, rows, pieces, row_sem, False)
        else:
            loads = [pltpu.make_async_copy(own_ref, rows, row_sem.at[0])]
        loads += moves(active_ref, active, pieces, load_sem.at[0], False)
        loads += moves(slope_ref, slope, pieces, load_sem.at[1], False)
        for each in loads:
            each.start()
        if place == 0:
            weights.wait()
        for each in stores.pop(slot, ()):
            each.wait()
        for each in loads:
            each.wait()

        @pl.loop(0, down.shape[1] // CHUNK)
        def _(turn):
            at = chunk_of(turn, CHUNK)
            value = plain_product(rows[...], down[:, at]) * slope[:, at].astype(jnp.float32)
            value = value.astype(jnp.bfloat16)
            grads[slot, :, at] = value
            total = jnp.sum(value.astype(jnp.float32), axis=0, keepdims=True)
            weight = weight_product(rows[...], active[:, at])
            if place == 0:
                bias_ref[:, at] = total
                sums[:, at] = weight
            elif place < 7:
                bias_ref[:, at] += total
                sums[:, at] += weight
            else:
                bias_ref[:, at] += total
                narrow[:, at] = (sums[:, at] + weight).astype(jnp.bfloat16)

        stores[slot] = moves(grad_ref, grads.at[slot], pieces, store_sem.at[slot], True)
        for each in stores[slot]:
            each.start()

    gather_beside(own_ref, rows_ref, send_sem, recv_sem, local_sem, use)
    last = pltpu.make_async_copy(narrow, weight_ref, weight_sem)
    last.start()
    for slot in (0, 1):
        for each in stores[slot]:
            each.wait()
    last.wait()


def gather_and_grad(own, down_cols, active, slope, call_number):
    token_rows, model_width = own.shape
    width = down_cols.shape[1]
    anywhere = pl.BlockSpec(memory_space=pl.ANY)
    dma = pltpu.SemaphoreType.DMA
    return pl.pallas_call(
        grad_kernel,
        out_shape=(
            jax.ShapeDtypeStruct((8, token_rows, model_width), jnp.bfloat16),
            jax.ShapeDtypeStruct((8, token_rows, width), jnp.bfloat16),
            jax.ShapeDtypeStruct((model_width, width), jnp.bfloat16),
            jax.ShapeDtypeStruct((1, width), jnp.float32),
        ),
        in_specs=[anywhere] * 4,
        out_specs=(anywhere,) * 3 + (pl.BlockSpec(memory_space=pltpu.VMEM),),
        scratch_shapes=[
            pltpu.VMEM(down_cols.shape, jnp.bfloat16),
            pltpu.VMEM((token_rows, model_width), jnp.bfloat16),
            pltpu.VMEM((token_rows, width), jnp.bfloat16),
            pltpu.VMEM((token_rows, width), jnp.bfloat16),
            pltpu.VMEM((2, token_rows, width), jnp.bfloat16),
            pltpu.VMEM((model_width, width), jnp.float32),
            pltpu.VMEM((model_width, width), jnp.bfloat16),
            dma((GATHER_COPIES,)),
            dma((GATHER_COPIES,)),
            dma,
            dma,
            dma((4,)),
            dma((2, 4)),
            dma((2, 4)),
        ],
        compiler_params=pltpu.CompilerParams(
            collective_id=call_number, has_side_effects=True, vmem_limit_bytes=VMEM_BYTES
        ),
        cost_estimate=pl.CostEstimate(
            flops=32 * token_rows * model_width * width,
            bytes_accessed=150 * 1000 * 1000,
            transcendentals=0,
        ),
        name="gather_and_grad",
    )(own, down_cols, active, slope)


def product_reduce_kernel(
    with_grad,
    narrow_ref,
    weight_hbm,
    *refs,
):
    if with_grad:
        wide_ref, hidden_hbm, result_hbm, gain_ref, *refs = refs
        grad_hidden_ref, grad_ref, branch_ref, sums_ref, *refs = refs
        *refs, wide, across, sums, wide_sem = refs
    else:
        hidden_hbm, teacher_hbm, offset_ref, valid_ref, factor_ref, *refs = refs
        prompt_ref, answer_ref, branch_ref, grad_result_ref, squares_ref, columns_ref, *refs = refs
    (
        weight,
        narrow,
        sent,
        mine,
        theirs,
        relayed,
        final,
        hidden_rows,
        other_rows,
        send_sem,
        recv_sem,
        weight_sem,
        narrow_sem,
        row_sem,
    ) = refs
    row_loads = (
        pltpu.make_async_copy(hidden_hbm, hidden_rows, row_sem.at[0]),
        pltpu.make_async_copy(result_hbm if with_grad else teacher_hbm, other_rows, row_sem.at[1]),
    )
    rows = narrow.shape[1]
    half = rows // 2
    here, on_x, on_y, on_chip, corner = block_of_eight()
    shift = on_chip - here
    first, second = pl.ds(0, half), pl.ds(half, half)
    load_weight = pltpu.make_async_copy(weight_hbm, weight, weight_sem)
    load_weight.start()

    def copy(index, source, target, device):
        return remote(index, source, target, device, send_sem, recv_sem)

    places = (corner, on_x, on_y, here)
    order = []
    for place in places:
        order += [place + shift, place]

    def fetch(turn):
        return pltpu.make_async_copy(
            narrow_ref.at[order[turn]], narrow.at[turn % 2], narrow_sem.at[turn % 2]
        )

    fetch(0).start()
    greet((on_x, on_y, on_chip))
    to_chip = [copy(index, sent.at[index], theirs.at[index], on_chip) for index in range(4)]
    step = 16

    def add_into(target, other, start, count):
        @pl.loop(0, count // step)
        def _(turn):
            at = pl.ds(pl.multiple_of(start + turn * step, step), step)
            come = pl.ds(pl.multiple_of(turn * step, step), step)
            target[at, :] = target[at, :] + other[come, :]

    def join(index):
        to_chip[index].wait_recv()
        add_into(mine.at[index], theirs.at[index], 0, rows)

    corner_x = copy(4, mine.at[0, first], relayed.at[0], on_x)
    corner_y = copy(5, mine.at[0, second], relayed.at[1], on_y)
    x_first = copy(6, mine.at[1, first], final.at[0, first], on_x)
    y_second = copy(7, mine.at[2, second], final.at[1, second], on_y)
    x_second = copy(8, mine.at[1, second], final.at[0, second], on_x)
    y_first = copy(9, mine.at[2, first], final.at[1, first], on_y)

    for each in row_loads:
        each.start()
    for turn in range(8):
        pair, own = turn // 2, turn % 2
        if turn < 7:
            fetch(turn + 1).start()
        fetch(turn).wait()
        if turn == 0:
            load_weight.wait()
        target = mine.at[pair] if own else sent.at[pair]

        @pl.loop(0, weight.shape[0] // CHUNK)
        def _(piece):
            at = chunk_of(piece, CHUNK)
            target[:, at] = transposed_product(narrow[turn % 2], weight[at, :]).astype(
                jnp.bfloat16
            )

        if not own:
            to_chip[pair].start()
        if turn == 2:
            join(0)
            corner_x.start()
            corner_y.start()
        if turn == 4:
            join(1)
            x_first.start()
        if turn == 6:
            join(2)
            y_second.start()
    corner_y.wait_recv()
    add_into(mine.at[1], relayed.at[1], half, half)
    x_second.start()
    corner_x.wait_recv()
    add_into(mine.at[2], relayed.at[0], 0, half)
    y_first.start()
    join(3)

    if with_grad:
        def fetch_wide(turn):
            return pltpu.make_async_copy(
                wide_ref.at[order[turn]], wide.at[turn % 2], wide_sem.at[turn % 2]
            )

        fetch_wide(0).start()
        fetch(0).start()
        for turn in range(8):
            if turn < 7:
                fetch_wide(turn + 1).start()
                fetch(turn + 1).start()
            fetch_wide(turn).wait()
            fetch(turn).wait()
            across[...] = jnp.transpose(wide[turn % 2])

            @pl.loop(0, sums.shape[1] // CHUNK)
            def _(piece):
                at = chunk_of(piece, CHUNK)
                value = plain_product(across[...], narrow[turn % 2, :, at])
                if turn == 0:
                    sums[:, at] = value
                elif turn < 7:
                    sums[:, at] += value
                else:
                    weight[:, at] = (sums[:, at] + value).astype(jnp.bfloat16)

        store = pltpu.make_async_copy(weight, grad_ref, weight_sem)
        store.start()

    for each in row_loads:
        each.wait()
    if not with_grad:
        for start, part, come in ((0, x_first, 0), (half, y_second, 1)):
            part.wait_recv()

            @pl.loop(0, half // step)
            def _(turn):
                at = pl.ds(pl.multiple_of(start + turn * step, step), step)
                base = hidden_rows[at, :] + offset_ref[...] + mine[3, at, :].astype(jnp.float32)
                hidden_rows[at, :] = base + final[come, at, :].astype(jnp.float32)

        y_first.wait_recv()
        x_second.wait_recv()
    else:
        for each in (x_first, y_second, x_second, y_first):
            each.wait_recv()

    def total_of(at):
        total = mine[3, at, :].astype(jnp.float32) + final[0, at, :].astype(jnp.float32)
        return total + final[1, at, :].astype(jnp.float32)

    if with_grad:
        sums_ref[...] = jnp.zeros_like(sums_ref)

        @pl.loop(0, rows // step)
        def _(turn):
            at = chunk_of(turn, step)
            grad_out = total_of(at)
            scaled, inverse = norm_stats(hidden_rows[at, :])
            weighted = grad_out * gain_ref[...]
            grad_in = inverse * (
                weighted
                - jnp.mean(weighted, axis=-1, keepdims=True)
                - scaled * jnp.mean(weighted * scaled, axis=-1, keepdims=True)
            )
            grad_hidden = other_rows[at, :] + grad_in
            branch = grad_hidden.astype(jnp.bfloat16)
            grad_hidden_ref[at, :] = grad_hidden
            branch_ref[at, :] = branch
            sums_ref[0:1, :] += jnp.sum(branch.astype(jnp.float32), axis=0, keepdims=True)
            sums_ref[1:2, :] += jnp.sum(grad_out * scaled, axis=0, keepdims=True)
            sums_ref[2:3, :] += jnp.sum(grad_out, axis=0, keepdims=True)

    else:
        squares_ref[...] = jnp.zeros_like(squares_ref)
        columns_ref[...] = jnp.zeros_like(columns_ref)
        own_prompt = prompt_ref.shape[0]
        for start, stop, come, out_ref, before in (
            (0, half, 1, prompt_ref, 0),
            (half, own_prompt, 0, prompt_ref, 0),
            (own_prompt, rows, 0, answer_ref, own_prompt),
        ):

            @pl.loop(0, (stop - start) // step)
            def _(turn):
                at = pl.ds(pl.multiple_of(start + turn * step, step), step)
                out = pl.ds(pl.multiple_of(start - before + turn * step, step), step)
                result = hidden_rows[at, :] + final[come, at, :].astype(jnp.float32)
                differ = result - other_rows[at, :].astype(jnp.float32)
                grad_result = factor_ref[at, :] * differ
                branch = grad_result.astype(jnp.bfloat16)
                out_ref[out, :] = result.astype(jnp.bfloat16)
                grad_result_ref[at, :] = grad_result
                branch_ref[at, :] = branch
                squared = valid_ref[at, :] * differ * differ
                column = branch.astype(jnp.float32)
                squares_ref[...] += squared[:8, :] + squared[8:, :]
                columns_ref[...] += column[:8, :] + column[8:, :]

    if with_grad:
        store.wait()
    for each in to_chip + [corner_x, corner_y, x_first, y_second, x_second, y_first]:
        each.wait_send()


def product_and_reduce(narrow, weight, wide, rows, second, call_number, own_prompt, *small):
    _, token_rows, width = narrow.shape
    model_width = weight.shape[0]
    with_grad = wide is not None
    anywhere = pl.BlockSpec(memory_space=pl.ANY)
    inside = pl.BlockSpec(memory_space=pltpu.VMEM)
    dma = pltpu.SemaphoreType.DMA
    block = (token_rows, model_width)
    kind, long = jnp.bfloat16, jnp.float32
    line = jax.ShapeDtypeStruct((8, model_width), long)
    narrow_rows, long_rows = jax.ShapeDtypeStruct(block, kind), jax.ShapeDtypeStruct(block, long)
    scratch = [
        pltpu.VMEM(weight.shape, kind),
        pltpu.VMEM((2, token_rows, width), kind),
        pltpu.VMEM((4,) + block, kind),
        pltpu.VMEM((4,) + block, kind),
        pltpu.VMEM((4,) + block, kind),
        pltpu.VMEM((2, token_rows // 2, model_width), kind),
        pltpu.VMEM((2,) + block, kind),
        pltpu.VMEM(block, long),
        pltpu.VMEM(block, second.dtype),
        dma((10,)),
        dma((10,)),
        dma,
        dma((2,)),
        dma((2,)),
    ]
    operands = [narrow, weight]
    if with_grad:
        out_shape = (
            long_rows,
            jax.ShapeDtypeStruct(weight.shape, kind),
            narrow_rows,
            jax.ShapeDtypeStruct((8, model_width), long),
        )
        out_specs = (inside, anywhere, inside, inside)
        scratch += [
            pltpu.VMEM((2,) + block, kind),
            pltpu.VMEM((model_width, token_rows), kind),
            pltpu.VMEM(weight.shape, long),
            dma((2,)),
        ]
        operands.append(wide)
    else:
        out_shape = (
            jax.ShapeDtypeStruct((own_prompt, model_width), kind),
            jax.ShapeDtypeStruct((token_rows - own_prompt, model_width), kind),
            narrow_rows,
            long_rows,
            line,
            line,
        )
        out_specs = (inside,) * 6
    operands += [rows, second]
    return pl.pallas_call(
        functools.partial(product_reduce_kernel, with_grad),
        out_shape=out_shape,
        in_specs=[anywhere] * len(operands) + [inside] * len(small),
        out_specs=out_specs,
        scratch_shapes=scratch,
        compiler_params=pltpu.CompilerParams(
            collective_id=call_number,
            has_side_effects=True,
            vmem_limit_bytes=62 * 1024 * 1024,
        ),
        cost_estimate=pl.CostEstimate(
            flops=(32 if with_grad else 16) * token_rows * model_width * width,
            bytes_accessed=150 * 1000 * 1000,
            transcendentals=0,
        ),
        name="product_and_reduce",
    )(*operands, *small)


def peers_of(count):
    here = lax.axis_index("tok")
    return here, [(here + step) % count for step in range(1, count)]


def small_gather_kernel(own_ref, out_ref, send_sem, recv_sem):
    here, on_x, on_y, on_chip, corner = block_of_eight()
    rows = own_ref.shape[1]

    def place(device):
        return pl.ds(pl.multiple_of(device * rows, rows), rows)

    greet((on_x, on_y, on_chip, corner))
    out_ref[:, place(here), :] = own_ref[...]
    paired_gather(own_ref, lambda device: out_ref.at[:, place(device), :], send_sem, recv_sem)


def tok_gather_small(own, call_number, kernels):
    if not kernels:
        return lax.all_gather(own, "tok", axis=1, tiled=True)
    prompts, rows, columns = own.shape
    return pl.pallas_call(
        small_gather_kernel,
        out_shape=jax.ShapeDtypeStruct((prompts, 8 * rows, columns), own.dtype),
        in_specs=[pl.BlockSpec(memory_space=pltpu.VMEM)],
        out_specs=pl.BlockSpec(memory_space=pltpu.VMEM),
        scratch_shapes=[pltpu.SemaphoreType.DMA((7,)), pltpu.SemaphoreType.DMA((7,))],
        compiler_params=pltpu.CompilerParams(collective_id=call_number, has_side_effects=True),
        name="tok_gather_small",
    )(own)


def stack_heads(values, heads):
    return jnp.concatenate(
        [values[:, head * HEAD_WIDTH : (head + 1) * HEAD_WIDTH] for head in range(heads)], axis=0
    )


def unstack_heads(values, heads):
    rows = values.shape[0] // heads
    return jnp.concatenate(
        [values[head * rows : (head + 1) * rows, :] for head in range(heads)], axis=1
    )


def part_rows(part, prompts, answers, token_ref, answer_ref):
    answer_rows = answer_ref.shape[0] // answers
    prompt_rows = (token_ref.shape[0] - answer_ref.shape[0]) // prompts
    if part < prompts:
        return slice(part * prompt_rows, (part + 1) * prompt_rows), prompt_rows
    start = prompts * prompt_rows + (part - prompts) * answer_rows
    return slice(start, start + answer_rows), answer_rows


def as_row(column):
    wide = jnp.broadcast_to(column, (column.shape[0], HEAD_WIDTH))
    return jnp.transpose(wide)[0:1, :]


def forward_block(
    prompts,
    answers,
    heads,
    start,
    owner_ref,
    normed_ref,
    query_block,
    bias,
    prompt_kv_ref,
    answer_kv_ref,
):
    width = HEAD_WIDTH
    scale = HEAD_WIDTH ** (-0.5)
    length = prompt_kv_ref.shape[1]
    queries = (plain_product(normed_ref[...], query_block) + bias).astype(jnp.bfloat16)
    pieces, logs = [], []
    for part in range(prompts + answers):
        here, rows = part_rows(part, prompts, answers, normed_ref, answer_kv_ref)
        token = lax.broadcasted_iota(jnp.int32, (heads * rows, 1), 0) % rows
        stacked = stack_heads(queries[here, :], heads)
        if part < prompts:
            keys = prompt_kv_ref[part, :, :width]
            values = prompt_kv_ref[part, :, width:]
            scores = transposed_product(stacked, keys)
            place = lax.broadcasted_iota(jnp.int32, (1, length), 1)
            scores = jnp.where(place <= start + token, scores, masked)
            top = jnp.max(scores, axis=-1, keepdims=True)
            exponent = jnp.exp((scores - top) * scale)
            total = jnp.sum(exponent, axis=-1, keepdims=True)
            mixed = plain_product(exponent.astype(jnp.bfloat16), values)
        else:
            answer = part - prompts
            owner = owner_ref[answer]
            own = slice(answer * rows, (answer + 1) * rows)
            keys = prompt_kv_ref[owner, :, :width]
            values = prompt_kv_ref[owner, :, width:]
            scores = transposed_product(stacked, keys)
            own_scores = transposed_product(stacked, answer_kv_ref[own, :width])
            place = lax.broadcasted_iota(jnp.int32, (1, rows), 1)
            own_scores = jnp.where(place <= token, own_scores, masked)
            top = jnp.maximum(
                jnp.max(scores, axis=-1, keepdims=True),
                jnp.max(own_scores, axis=-1, keepdims=True),
            )
            exponent = jnp.exp((scores - top) * scale)
            own_exponent = jnp.exp((own_scores - top) * scale)
            total = jnp.sum(exponent, axis=-1, keepdims=True) + jnp.sum(
                own_exponent, axis=-1, keepdims=True
            )
            mixed = plain_product(exponent.astype(jnp.bfloat16), values) + plain_product(
                own_exponent.astype(jnp.bfloat16), answer_kv_ref[own, width:]
            )
        pieces.append(unstack_heads((mixed / total).astype(jnp.bfloat16), heads))
        logs.append((here, rows, as_row(top * scale + jnp.log(total))))
    return queries, jnp.concatenate(pieces, axis=0), logs


def attention_forward_kernel(
    prompts,
    answers,
    heads,
    place_ref,
    owner_ref,
    normed_ref,
    query_ref,
    bias_ref,
    prompt_kv_ref,
    answer_kv_ref,
    output_ref,
    states_ref,
    offset_ref,
    gain_ref,
    shift_ref,
    queries_ref,
    mixture_ref,
    log_ref,
    hidden_ref,
    second_ref,
):
    step = pl.program_id(0)
    queries, mixture, logs = forward_block(
        prompts,
        answers,
        heads,
        place_ref[0],
        owner_ref,
        normed_ref,
        query_ref[0],
        bias_ref[0],
        prompt_kv_ref,
        answer_kv_ref,
    )
    queries_ref[0] = queries
    mixture_ref[0] = mixture
    for here, rows, log_row in logs:
        for head in range(heads):
            log_ref[0, head : head + 1, here] = log_row[:, head * rows : (head + 1) * rows]

    @pl.when(step == 0)
    def _():
        hidden_ref[...] = states_ref[...].astype(jnp.float32) + offset_ref[...]

    hidden_ref[...] += transposed_product(mixture, output_ref[0])

    @pl.when(step == pl.num_programs(0) - 1)
    def _():
        scaled, _ = norm_stats(hidden_ref[...])
        second_ref[...] = (scaled * gain_ref[...] + shift_ref[...]).astype(jnp.bfloat16)


def attention_forward(
    place,
    owning,
    normed,
    query_blocks,
    output_blocks,
    query_offset,
    prompt_kv,
    answer_kv,
    states,
    output_offset,
    gain,
    shift,
    prompts,
    answers,
):
    token_rows, model_width = normed.shape
    steps, _, block = query_blocks.shape
    heads = block // HEAD_WIDTH
    whole = lambda *shape: pl.BlockSpec(shape, lambda step, *_: (0,) * len(shape))
    one = lambda *shape: pl.BlockSpec((1,) + shape, lambda step, *_: (step, 0, 0))
    by_step = jax.ShapeDtypeStruct((steps, token_rows, block), jnp.bfloat16)
    return pl.pallas_call(
        functools.partial(attention_forward_kernel, prompts, answers, heads),
        out_shape=(
            by_step,
            by_step,
            jax.ShapeDtypeStruct((steps, heads, token_rows), jnp.float32),
            jax.ShapeDtypeStruct((token_rows, model_width), jnp.float32),
            jax.ShapeDtypeStruct((token_rows, model_width), jnp.bfloat16),
        ),
        grid_spec=pltpu.PrefetchScalarGridSpec(
            num_scalar_prefetch=2,
            grid=(steps,),
            in_specs=[
                whole(token_rows, model_width),
                one(model_width, block),
                one(1, block),
                whole(*prompt_kv.shape),
                whole(*answer_kv.shape),
                one(model_width, block),
                whole(token_rows, model_width),
                whole(1, model_width),
                whole(1, model_width),
                whole(1, model_width),
            ],
            out_specs=(
                one(token_rows, block),
                one(token_rows, block),
                one(heads, token_rows),
                whole(token_rows, model_width),
                whole(token_rows, model_width),
            ),
        ),
        compiler_params=pltpu.CompilerParams(vmem_limit_bytes=VMEM_BYTES),
        name="attention_forward",
    )(
        place,
        owning,
        normed,
        query_blocks,
        query_offset.reshape(steps, 1, block),
        prompt_kv,
        answer_kv,
        output_blocks,
        states,
        output_offset.reshape(1, -1),
        gain.reshape(1, -1),
        shift.reshape(1, -1),
    )


def bits_away(index):
    here = lax.axis_index("tok")
    core = (here + index) % 2
    across = (here // 2 + index // 2) % 2
    along = (here // 4 + index // 4) % 2
    return along * 4 + across * 2 + core


def gather_attention_kernel(
    prompts,
    answers,
    heads,
    prompt_rows,
    owner_ref,
    own_ref,
    normed_ref,
    bias_ref,
    prompt_kv_ref,
    answer_kv_ref,
    states_ref,
    offset_ref,
    gain_ref,
    shift_ref,
    weights_ref,
    queries_ref,
    mixture_ref,
    log_ref,
    hidden_ref,
    second_ref,
    held,
    send_sem,
    recv_sem,
    local_sem,
    load_sem,
):
    here, on_x, on_y, on_chip, corner = block_of_eight()

    def copy(index, source, target, device):
        return remote(index, source, target, device, send_sem, recv_sem)

    def kind_of(device, kind):
        return weights_ref.at[device, :, kind]

    to_x = [copy(0 + kind, own_ref.at[:, kind], kind_of(here, kind), on_x) for kind in (0, 1)]
    to_y = [copy(2 + kind, own_ref.at[:, kind], kind_of(here, kind), on_y) for kind in (0, 1)]
    to_chip = [copy(4, own_ref, weights_ref.at[here], on_chip)]
    keep = [pltpu.make_async_copy(own_ref, weights_ref.at[here], local_sem)]
    x_to_y = copy(5, kind_of(on_x, 0), kind_of(on_x, 0), on_y)
    y_to_x = copy(6, kind_of(on_y, 1), kind_of(on_y, 1), on_x)
    x_to_chip = copy(7, weights_ref.at[on_x], weights_ref.at[on_x], on_chip)
    y_to_chip = copy(8, weights_ref.at[on_y], weights_ref.at[on_y], on_chip)
    corner_to_chip = [
        copy(9 + kind, kind_of(corner, kind), kind_of(corner, kind), on_chip) for kind in (0, 1)
    ]

    greet((on_x, on_y, on_chip))
    for each in (to_x[0], to_y[1], to_x[1], to_y[0], *to_chip, *keep):
        each.start()
    hidden_ref[...] = states_ref[...].astype(jnp.float32) + offset_ref[...]

    @pl.loop(0, 8)
    def _(turn):
        block = bits_away(turn)

        @pl.when(turn == 0)
        def _():
            load = pltpu.make_async_copy(own_ref, held, load_sem)
            load.start()
            load.wait()

        @pl.when(turn == 1)
        def _():
            for each in to_chip:
                each.wait_recv()

        @pl.when(turn == 2)
        def _():
            to_x[0].wait_recv()
            x_to_y.start()
            to_y[1].wait_recv()
            y_to_x.start()
            to_x[1].wait_recv()
            x_to_chip.start()
            to_y[0].wait_recv()
            y_to_chip.start()

        @pl.when(turn == 3)
        def _():
            x_to_chip.wait_recv()

        @pl.when(turn == 5)
        def _():
            y_to_chip.wait_recv()

        @pl.when(turn == 6)
        def _():
            x_to_y.wait_recv()
            corner_to_chip[0].start()
            y_to_x.wait_recv()
            corner_to_chip[1].start()

        @pl.when(turn == 7)
        def _():
            for each in corner_to_chip:
                each.wait_recv()

        @pl.when(turn > 0)
        def _():
            load = pltpu.make_async_copy(weights_ref.at[block], held, load_sem)
            load.start()
            load.wait()

        queries, mixture, logs = forward_block(
            prompts,
            answers,
            heads,
            here * prompt_rows,
            owner_ref,
            normed_ref,
            held[:, 0].reshape(-1, held.shape[-1]),
            bias_ref[block],
            prompt_kv_ref,
            answer_kv_ref,
        )
        queries_ref[block] = queries
        mixture_ref[block] = mixture
        for place, rows, log_row in logs:
            for head in range(heads):
                log_ref[block, head : head + 1, place] = log_row[
                    :, head * rows : (head + 1) * rows
                ]
        hidden_ref[...] += transposed_product(mixture, held[:, 1].reshape(-1, held.shape[-1]))

    scaled, _ = norm_stats(hidden_ref[...])
    second_ref[...] = (scaled * gain_ref[...] + shift_ref[...]).astype(jnp.bfloat16)
    for each in (*to_x, *to_y, *to_chip, x_to_y, y_to_x, x_to_chip, y_to_chip, *corner_to_chip):
        each.wait_send()
    for each in keep:
        each.wait()


def gather_attention(
    owning,
    projections,
    normed,
    query_offset,
    prompt_kv,
    answer_kv,
    states,
    output_offset,
    gain,
    shift,
    prompts,
    answers,
    prompt_rows,
    call_number,
):
    token_rows, model_width = normed.shape
    block = projections.shape[3]
    heads = block // HEAD_WIDTH
    inside = pl.BlockSpec(memory_space=pltpu.VMEM)
    anywhere = pl.BlockSpec(memory_space=pl.ANY)
    dma = pltpu.SemaphoreType.DMA
    by_step = jax.ShapeDtypeStruct((8, token_rows, block), jnp.bfloat16)
    return pl.pallas_call(
        functools.partial(gather_attention_kernel, prompts, answers, heads, prompt_rows),
        out_shape=(
            jax.ShapeDtypeStruct((8,) + projections.shape, jnp.bfloat16),
            by_step,
            by_step,
            jax.ShapeDtypeStruct((8, heads, token_rows), jnp.float32),
            jax.ShapeDtypeStruct((token_rows, model_width), jnp.float32),
            jax.ShapeDtypeStruct((token_rows, model_width), jnp.bfloat16),
        ),
        in_specs=[pl.BlockSpec(memory_space=pltpu.SMEM), anywhere] + [inside] * 8,
        out_specs=(anywhere,) + (inside,) * 5,
        scratch_shapes=[
            pltpu.VMEM(projections.shape, jnp.bfloat16),
            dma((11,)),
            dma((11,)),
            dma,
            dma,
        ],
        compiler_params=pltpu.CompilerParams(
            collective_id=call_number, has_side_effects=True, vmem_limit_bytes=VMEM_BYTES
        ),
        cost_estimate=pl.CostEstimate(
            flops=64 * token_rows * model_width * block,
            bytes_accessed=250 * 1000 * 1000,
            transcendentals=0,
        ),
        name="gather_attention",
    )(
        owning,
        projections,
        normed,
        query_offset.reshape(8, 1, block),
        prompt_kv,
        answer_kv,
        states,
        output_offset.reshape(1, -1),
        gain.reshape(1, -1),
        shift.reshape(1, -1),
    )


def backward_block(
    prompts,
    answers,
    heads,
    start,
    owner_ref,
    share_ref,
    normed_ref,
    branch_ref,
    query_block,
    output_block,
    queries,
    mixture,
    log_ref,
    prompt_kv_ref,
    answer_kv_ref,
    normed_across,
    key_sums,
    own_sums,
    grad_normed_ref,
):
    width = HEAD_WIDTH
    scale = HEAD_WIDTH ** (-0.5)
    length = prompt_kv_ref.shape[1]
    grad_mixture = plain_product(branch_ref[...], output_block).astype(jnp.bfloat16)

    def backward(keys, values, stacked, grad_stacked, log_row, inner_row, allowed):
        scores = transposed_product(keys, stacked)
        probs = jnp.exp(scores * scale - log_row)
        if allowed is not None:
            probs = jnp.where(allowed, probs, 0.0)
        grad_values = plain_product(probs.astype(jnp.bfloat16), grad_stacked)
        grad_probs = transposed_product(values, grad_stacked)
        grad_scores = (probs * (grad_probs - inner_row)).astype(jnp.bfloat16)
        grad_keys = plain_product(grad_scores, stacked)
        grad_queries = weight_product(grad_scores, keys)
        return grad_queries, grad_keys, grad_values

    pieces = []
    for part in range(prompts + answers):
        here, rows = part_rows(part, prompts, answers, normed_ref, answer_kv_ref)
        token = lax.broadcasted_iota(jnp.int32, (1, heads * rows), 1) % rows
        stacked = stack_heads(queries[here, :], heads)
        grad_stacked = stack_heads(grad_mixture[here, :], heads)
        mixed = stack_heads(mixture[here, :], heads)
        product = grad_stacked.astype(jnp.float32) * mixed.astype(jnp.float32)
        inner_row = jnp.sum(jnp.transpose(product), axis=0, keepdims=True)
        log_row = jnp.concatenate([log_ref[head : head + 1, here] for head in range(heads)], axis=1)
        if part < prompts:
            place = lax.broadcasted_iota(jnp.int32, (length, 1), 0)
            grad_queries, grad_keys, grad_values = backward(
                prompt_kv_ref[part, :, :width],
                prompt_kv_ref[part, :, width:],
                stacked,
                grad_stacked,
                log_row,
                inner_row,
                place <= start + token,
            )
            key_sums[part, :, :width] += grad_keys
            key_sums[part, :, width:] += grad_values
        else:
            answer = part - prompts
            owner = owner_ref[answer]
            own = slice(answer * rows, (answer + 1) * rows)
            grad_queries, grad_keys, grad_values = backward(
                prompt_kv_ref[owner, :, :width],
                prompt_kv_ref[owner, :, width:],
                stacked,
                grad_stacked,
                log_row,
                inner_row,
                None,
            )
            for prompt in range(prompts):
                share = share_ref[answer * prompts + prompt]
                key_sums[prompt, :, :width] += share * grad_keys
                key_sums[prompt, :, width:] += share * grad_values
            place = lax.broadcasted_iota(jnp.int32, (rows, 1), 0)
            own_queries, own_keys, own_values = backward(
                answer_kv_ref[own, :width],
                answer_kv_ref[own, width:],
                stacked,
                grad_stacked,
                log_row,
                inner_row,
                place <= token,
            )
            grad_queries = grad_queries + own_queries
            own_sums[own, :width] += own_keys
            own_sums[own, width:] += own_values
        pieces.append(unstack_heads((grad_queries * scale).astype(jnp.bfloat16), heads))
    grad_queries = jnp.concatenate(pieces, axis=0)
    grad_query_block = plain_product(normed_across[...], grad_queries).astype(jnp.bfloat16)
    grad_normed_ref[...] += transposed_product(grad_queries, query_block)
    grad_bias = jnp.sum(grad_queries.astype(jnp.float32), axis=0, keepdims=True)
    return grad_query_block, grad_bias


def attention_backward_kernel(
    prompts,
    answers,
    heads,
    place_ref,
    owner_ref,
    share_ref,
    normed_ref,
    query_ref,
    prompt_kv_ref,
    answer_kv_ref,
    output_ref,
    branch_ref,
    queries_ref,
    mixture_ref,
    log_ref,
    grad_weights_ref,
    grad_normed_ref,
    grad_prompt_ref,
    grad_answer_ref,
    grad_bias_ref,
    normed_across,
    branch_across,
    key_sums,
    own_sums,
):
    step = pl.program_id(0)
    width = HEAD_WIDTH
    scale = HEAD_WIDTH ** (-0.5)
    block = queries_ref.shape[2]

    @pl.when(step == 0)
    def _():
        normed_across[...] = jnp.transpose(normed_ref[...])
        branch_across[...] = jnp.transpose(branch_ref[...])
        key_sums[...] = jnp.zeros_like(key_sums)
        own_sums[...] = jnp.zeros_like(own_sums)
        grad_normed_ref[...] = jnp.zeros_like(grad_normed_ref)

    query_block, output_block = query_ref[0, 0], output_ref[0, 0]
    groups = grad_weights_ref.shape[1]
    weight_rows = query_block.shape[0] // groups
    grad_output_block = plain_product(branch_across[...], mixture_ref[0]).astype(jnp.bfloat16)
    grad_query_block, grad_bias = backward_block(
        prompts,
        answers,
        heads,
        place_ref[0],
        owner_ref,
        share_ref,
        normed_ref,
        branch_ref,
        query_block,
        output_block,
        queries_ref[0],
        mixture_ref[0],
        log_ref.at[0],
        prompt_kv_ref,
        answer_kv_ref,
        normed_across,
        key_sums,
        own_sums,
        grad_normed_ref,
    )
    grad_weights_ref[0, :, :weight_rows] = grad_query_block.reshape(groups, weight_rows, block)
    grad_weights_ref[0, :, weight_rows : 2 * weight_rows] = grad_output_block.reshape(
        groups, weight_rows, block
    )
    grad_bias_ref[0] = grad_bias

    @pl.when(step == pl.num_programs(0) - 1)
    def _():
        grad_prompt_ref[:, :, :width] = (key_sums[:, :, :width] * scale).astype(jnp.bfloat16)
        grad_prompt_ref[:, :, width:] = key_sums[:, :, width:].astype(jnp.bfloat16)
        grad_answer_ref[:, :width] = own_sums[:, :width] * scale
        grad_answer_ref[:, width:] = own_sums[:, width:]


def attention_backward(
    place,
    owning,
    share,
    normed,
    weights,
    groups,
    grad_rows,
    prompt_kv,
    answer_kv,
    branch,
    queries,
    mixture,
    log_total,
    prompts,
    answers,
):
    token_rows, model_width = normed.shape
    steps, _, _, block = weights.shape
    heads = block // HEAD_WIDTH
    length = prompt_kv.shape[1]
    whole = lambda *shape: pl.BlockSpec(shape, lambda step, *_: (0,) * len(shape))
    columns = lambda: pl.BlockSpec((1, token_rows, block), lambda step, *_: (step, 0, 0))
    kind = lambda which: pl.BlockSpec(
        (1, 1, model_width, block), lambda step, *_: (step, which, 0, 0)
    )
    scores = heads * token_rows * length
    return pl.pallas_call(
        functools.partial(
            attention_backward_kernel, prompts, answers, heads
        ),
        out_shape=(
            jax.ShapeDtypeStruct((steps, groups, grad_rows, block), jnp.bfloat16),
            jax.ShapeDtypeStruct((token_rows, model_width), jnp.float32),
            jax.ShapeDtypeStruct(prompt_kv.shape, jnp.bfloat16),
            jax.ShapeDtypeStruct(answer_kv.shape, jnp.float32),
            jax.ShapeDtypeStruct((steps, 1, block), jnp.float32),
        ),
        grid_spec=pltpu.PrefetchScalarGridSpec(
            num_scalar_prefetch=3,
            grid=(steps,),
            in_specs=[
                whole(token_rows, model_width),
                kind(0),
                whole(*prompt_kv.shape),
                whole(*answer_kv.shape),
                kind(1),
                whole(token_rows, model_width),
                columns(),
                columns(),
                pl.BlockSpec((1, heads, token_rows), lambda step, *_: (step, 0, 0)),
            ],
            out_specs=(
                pl.BlockSpec(
                    (1, groups, grad_rows, block), lambda step, *_: (step, 0, 0, 0)
                ),
                whole(token_rows, model_width),
                whole(*prompt_kv.shape),
                whole(*answer_kv.shape),
                pl.BlockSpec((1, 1, block), lambda step, *_: (step, 0, 0)),
            ),
            scratch_shapes=[
                pltpu.VMEM((model_width, token_rows), jnp.bfloat16),
                pltpu.VMEM((model_width, token_rows), jnp.bfloat16),
                pltpu.VMEM(prompt_kv.shape, jnp.float32),
                pltpu.VMEM(answer_kv.shape, jnp.float32),
            ],
        ),
        compiler_params=pltpu.CompilerParams(vmem_limit_bytes=VMEM_BYTES),
        cost_estimate=pl.CostEstimate(
            flops=steps * (8 * token_rows * model_width * block + 20 * scores * HEAD_WIDTH),
            bytes_accessed=16 * steps * model_width * block,
            transcendentals=steps * scores,
        ),
        name="attention_backward",
    )(
        place,
        owning,
        share,
        normed,
        weights,
        prompt_kv,
        answer_kv,
        weights,
        branch,
        queries,
        mixture,
        log_total,
    )


class PairedSum:
    def __init__(self, part, pair, sent, come, send_sem, recv_sem):
        here, on_x, on_y, on_chip, corner = block_of_eight()
        shift = on_chip - here
        self.places = (here, on_x, on_y, corner)
        self.part, self.pair, self.sent, self.come = part, pair, sent, come
        self.to_chip = [
            remote(index, part(place + shift), pair.at[index], on_chip, send_sem, recv_sem)
            for index, place in enumerate(self.places)
        ]
        self.over = [
            remote(3 + index, sent.at[index], come.at[index - 1], place, send_sem, recv_sem)
            for index, place in enumerate(self.places)
            if index
        ]

    def start(self):
        for each in self.to_chip:
            each.start()

    def pass_on(self):
        for each in self.to_chip:
            each.wait_recv()
        for index, place in enumerate(self.places):
            total = self.part(place)[...].astype(jnp.float32)
            total = total + self.pair[index].astype(jnp.float32)
            self.sent[index] = total.astype(self.sent.dtype)
        for each in self.over:
            each.start()

    def total(self):
        total = self.sent[0].astype(jnp.float32)
        for index, each in enumerate(self.over):
            each.wait_recv()
            total = total + self.come[index].astype(jnp.float32)
        return total

    def finish(self):
        for each in self.to_chip + self.over:
            each.wait_send()


VECTOR_ROWS = 16


def backward_reduce_kernel(
    prompts,
    answers,
    heads,
    groups,
    prompt_rows,
    owner_ref,
    share_ref,
    weights_ref,
    queries_ref,
    mixture_ref,
    hidden_hbm,
    normed_ref,
    branch_ref,
    log_ref,
    prompt_kv_ref,
    answer_kv_ref,
    states_ref,
    gain_ref,
    keyval_ref,
    known_up_ref,
    known_sums_ref,
    known_columns_ref,
    known_squares_ref,
    grad_query_ref,
    grad_output_ref,
    grad_keyval_ref,
    vectors_ref,
    own_vectors_ref,
    own_up_ref,
    grad_prompt_ref,
    grad_answer_ref,
    normed_across,
    branch_across,
    key_sums,
    own_sums,
    grad_normed,
    grad_hidden,
    held,
    pair,
    early,
    kept,
    theirs,
    relayed,
    final,
    come,
    kv_part,
    kv_pair,
    kv_sent,
    kv_come,
    kv_rows,
    keyval_part,
    keyval_pair,
    keyval_sent,
    keyval_come,
    keyval_sum,
    keyval_over,
    vectors,
    vector_come,
    vector_sum,
    vector_over,
    send_sem,
    recv_sem,
    over_send,
    over_recv,
    peer_send,
    peer_recv,
    load_sem,
    early_sem,
    hidden_sem,
):
    width = HEAD_WIDTH
    scale = HEAD_WIDTH ** (-0.5)
    here, on_x, on_y, on_chip, corner = block_of_eight()
    _, peers = peers_of(8)
    group = lax.axis_index("grp")
    other_groups = [(group + turn) % groups for turn in range(1, groups)]
    model_width, block = kept.shape[1:]
    chunk_rows = model_width // groups
    step = 64
    counter = iter(range(8 + 6 * groups))

    def copy(source, target, device):
        return remote(next(counter), source, target, device, send_sem, recv_sem)

    def over(index, source, target, turn):
        return pltpu.make_async_remote_copy(
            src_ref=source,
            dst_ref=target,
            send_sem=over_send.at[index],
            recv_sem=over_recv.at[index],
            device_id={"grp": other_groups[turn]},
            device_id_type=MESH,
        )

    def to_peers(row, source, target):
        return [
            pltpu.make_async_remote_copy(
                src_ref=source(peers[index]),
                dst_ref=target(index),
                send_sem=peer_send.at[row, index],
                recv_sem=peer_recv.at[row, index],
                device_id={"tok": peers[index]},
                device_id_type=MESH,
            )
            for index in range(len(peers))
        ]

    spans = [
        pl.ds(pl.multiple_of(((group + 1 + chunk) % groups) * chunk_rows, chunk_rows), chunk_rows)
        for chunk in range(groups)
    ]
    chunks = range(groups)
    by_x, by_y = chunks[: groups // 2], chunks[groups // 2 :]
    kinds = (0, 1)

    def mine(place, kind):
        return kept.at[4 + 2 * place + kind]

    def pieces_to(place, target, device):
        return [
            [copy(mine(place, kind).at[span], target(kind).at[span], device) for span in spans]
            for kind in kinds
        ]

    to_chip = [
        [copy(kept.at[place], theirs.at[place, kind], on_chip) for place in range(4)]
        for kind in kinds
    ]
    corners = [
        [
            copy(
                mine(0, kind).at[spans[chunk]],
                relayed.at[kind, spans[chunk]],
                on_x if chunk in by_x else on_y,
            )
            for chunk in chunks
        ]
        for kind in kinds
    ]
    to_x = pieces_to(2, lambda kind: final.at[0, kind], on_x)
    to_y = pieces_to(1, lambda kind: final.at[1, kind], on_y)
    across = [
        [over(2 * turn + kind, mine(3, kind).at[spans[turn]], come.at[turn, kind], turn) for kind in kinds]
        for turn in range(groups - 1)
    ]

    def lanes(device):
        return pl.ds(pl.multiple_of(device * block, block), block)

    def prompt_place(device):
        return pl.ds(pl.multiple_of(device * prompt_rows, prompt_rows), prompt_rows)

    kv_sums = PairedSum(
        lambda device: kv_part.at[:, prompt_place(device), :],
        kv_pair,
        kv_sent,
        kv_come,
        peer_send.at[0],
        peer_recv.at[0],
    )
    keyval_sums = PairedSum(
        lambda device: keyval_part.at[:, device],
        keyval_pair,
        keyval_sent,
        keyval_come,
        peer_send.at[1],
        peer_recv.at[1],
    )
    vector_copies = to_peers(
        2, lambda peer: vectors.at[:, lanes(peer)], lambda index: vector_come.at[index]
    )
    vector_out = to_peers(
        3, lambda peer: vector_sum, lambda index: vectors_ref.at[:, lanes(here)]
    )
    first_over = 2 * (groups - 1)
    keyval_across = [
        over(first_over + turn, keyval_sum.at[other_groups[turn]], keyval_over.at[turn], turn)
        for turn in range(groups - 1)
    ]
    vector_across = [
        over(first_over + groups - 1 + turn, vectors.at[:, lanes(here)], vector_over.at[turn], turn)
        for turn in range(groups - 1)
    ]

    def fetch(turn):
        source, slot = bits_away(7 - turn), turn % 2
        return (
            pltpu.make_async_copy(weights_ref.at[source], held.at[slot], load_sem.at[slot, 0]),
            pltpu.make_async_copy(queries_ref.at[source], pair.at[slot, 0], load_sem.at[slot, 1]),
            pltpu.make_async_copy(mixture_ref.at[source], pair.at[slot, 1], load_sem.at[slot, 2]),
        )

    def fetch_early(turn):
        return pltpu.make_async_copy(
            mixture_ref.at[bits_away(7 - turn)], early.at[turn % 2], early_sem.at[turn % 2]
        )

    fetch_early(0).start()
    load_hidden = pltpu.make_async_copy(hidden_hbm, grad_hidden, hidden_sem)
    load_hidden.start()
    for each in fetch(0):
        each.start()
    greet_all(peers, other_groups)
    normed_across[...] = jnp.transpose(normed_ref[...])
    branch_across[...] = jnp.transpose(branch_ref[...])
    key_sums[...] = jnp.zeros_like(key_sums)
    own_sums[...] = jnp.zeros_like(own_sums)
    grad_normed[...] = jnp.zeros_like(grad_normed)
    vectors[...] = jnp.zeros_like(vectors)
    vectors[: known_up_ref.shape[0], :] = known_up_ref[...]
    vectors[4:7, :] = known_sums_ref[0:3, :]
    vectors[7:8, :] = jnp.sum(known_columns_ref[...], axis=0, keepdims=True)
    squares = jnp.sum(known_squares_ref[...], axis=0, keepdims=True)
    squares = jnp.sum(squares, axis=1, keepdims=True)
    vectors[12:13, :] = jnp.broadcast_to(squares, (1, model_width))

    def add_into(target, other, rows):
        @pl.loop(0, rows // step)
        def _(turn):
            at = chunk_of(turn, step)
            target[at, :] = target[at, :] + other[at, :]

    def join(kind, place):
        to_chip[kind][place].wait_recv()
        add_into(mine(place, kind), theirs.at[place, kind], model_width)

    def direct(kind, chunk):
        (to_x if chunk in by_x else to_y)[kind][chunk].start()

    def relay(kind, chunk):
        corners[kind][chunk].wait_recv()
        place, then = (1, to_y) if chunk in by_x else (2, to_x)
        span = spans[chunk]
        add_into(mine(place, kind).at[span], relayed.at[kind, span], chunk_rows)
        then[kind][chunk].start()

    def close(kind, chunk):
        span = spans[chunk]
        for source, part in enumerate((to_x, to_y)):
            part[kind][chunk].wait_recv()
            add_into(mine(3, kind).at[span], final.at[source, kind, span], chunk_rows)
        if chunk < groups - 1:
            across[chunk][kind].start()

    def slot_of(turn, kind):
        place = turn // 2
        return (1 - turn % 2) * place + (turn % 2) * (4 + 2 * place + kind)

    def send_to_chip(turn, kind):
        for place in range(4):

            @pl.when(turn == 2 * place)
            def _():
                to_chip[kind][place].start()

    @pl.loop(0, 8)
    def _(turn):
        @pl.when(turn < 7)
        def _():
            fetch_early(turn + 1).start()

        fetch_early(turn).wait()
        kept[slot_of(turn, 1)] = plain_product(
            branch_across[...], early[turn % 2]
        ).astype(jnp.bfloat16)
        send_to_chip(turn, 1)

        @pl.when(turn == 2)
        def _():
            join(1, 0)
            for chunk in chunks:
                corners[1][chunk].start()

        for place in (1, 2):

            @pl.when(turn == 2 * place + 2)
            def _():
                join(1, place)

    for chunk in chunks:
        direct(1, chunk)

    @pl.loop(0, 8)
    def _(turn):
        source, now = bits_away(7 - turn), turn % 2

        @pl.when(turn < 7)
        def _():
            for each in fetch(turn + 1):
                each.start()

        for place in range(4):

            @pl.when(turn == 2 * place)
            def _():
                to_chip[1][place].wait_send()

        for each in fetch(turn):
            each.wait()
        grad_query_block, grad_bias = backward_block(
            prompts,
            answers,
            heads,
            here * prompt_rows,
            owner_ref,
            share_ref,
            normed_ref,
            branch_ref,
            held[now, :, 0].reshape(-1, block),
            held[now, :, 1].reshape(-1, block),
            pair[now, 0],
            pair[now, 1],
            log_ref.at[source],
            prompt_kv_ref,
            answer_kv_ref,
            normed_across,
            key_sums,
            own_sums,
            grad_normed,
        )
        kept[slot_of(turn, 0)] = grad_query_block
        vectors[10:11, lanes(source)] = grad_bias
        send_to_chip(turn, 0)

        @pl.when(turn == 1)
        def _():
            for chunk in chunks:
                relay(1, chunk)

        @pl.when(turn == 2)
        def _():
            join(0, 0)
            for chunk in chunks:
                corners[0][chunk].start()

        @pl.when(turn == 4)
        def _():
            join(0, 1)
            join(1, 3)

        @pl.when(turn == 5)
        def _():
            for chunk in chunks:
                close(1, chunk)

        @pl.when(turn == 6)
        def _():
            join(0, 2)
            for chunk in (by_x[0], by_y[0]):
                direct(0, chunk)
            for chunk in (by_x[0], by_y[0]):
                relay(0, chunk)

        @pl.when(turn == 7)
        def _():
            direct(0, by_x[1])
            relay(0, by_x[1])

    kv_part[:, :, :width] = (key_sums[:, :, :width] * scale).astype(jnp.bfloat16)
    kv_part[:, :, width:] = key_sums[:, :, width:].astype(jnp.bfloat16)
    kv_sums.start()
    join(0, 3)
    kv_sums.pass_on()
    for part in (to_x, to_y):
        part[0][by_x[0]].wait_send()
    direct(0, by_y[1])
    relay(0, by_y[1])
    close(0, by_x[0])

    own_prompt = prompts * prompt_rows
    total = kv_sums.total()
    for prompt in range(prompts):
        kv_rows[prompt * prompt_rows : (prompt + 1) * prompt_rows, :] = total[prompt].astype(
            jnp.bfloat16
        )
    kv_rows[own_prompt:, :width] = (own_sums[:, :width] * scale).astype(jnp.bfloat16)
    kv_rows[own_prompt:, width:] = own_sums[:, width:].astype(jnp.bfloat16)
    keyval_part[...] = (
        plain_product(normed_across[...], kv_rows[...])
        .astype(jnp.bfloat16)
        .reshape(keyval_part.shape)
    )
    keyval_sums.start()
    close(0, by_y[0])
    keyval_sums.pass_on()
    close(0, by_x[1])
    load_hidden.wait()
    vectors[11:12, :width] = jnp.sum(
        kv_rows[:, width:].astype(jnp.float32), axis=0, keepdims=True
    )
    piece = 16
    grad_normed[...] += transposed_product(kv_rows[...], keyval_ref[...])

    start = 0
    for out_ref in (grad_prompt_ref, grad_answer_ref):

        @pl.loop(0, out_ref.shape[0] // piece)
        def _(turn):
            at = pl.ds(pl.multiple_of(start + turn * piece, piece), piece)
            scaled, inverse = norm_stats(states_ref[at, :].astype(jnp.float32))
            grad_out = grad_normed[at, :]
            weighted = grad_out * gain_ref[...]
            grad_in = inverse * (
                weighted
                - jnp.mean(weighted, axis=-1, keepdims=True)
                - scaled * jnp.mean(weighted * scaled, axis=-1, keepdims=True)
            )
            out_ref[chunk_of(turn, piece), :] = (grad_hidden[at, :] + grad_in).astype(jnp.bfloat16)
            vectors[8:9, :] += jnp.sum(grad_out * scaled, axis=0, keepdims=True)
            vectors[9:10, :] += jnp.sum(grad_out, axis=0, keepdims=True)

        start += out_ref.shape[0]

    for each in vector_copies:
        each.start()
    keyval_sum[...] = keyval_sums.total().astype(jnp.bfloat16)
    for each in keyval_across:
        each.start()
    for each in vector_copies:
        each.wait_recv()
    total = vectors[:, lanes(here)]
    for index in range(len(peers)):
        total = total + vector_come[index]
    vectors[:, lanes(here)] = total
    for each in vector_across:
        each.start()
    for each in vector_across:
        each.wait_recv()
    total = vectors[:, lanes(here)]
    for turn in range(groups - 1):
        total = total + vector_over[turn]
    vector_sum[...] = total
    for each in vector_out:
        each.start()
    vectors_ref[:, lanes(here)] = vector_sum[...]
    close(0, by_y[1])
    for each in keyval_across:
        each.wait_recv()
    total = keyval_sum[group].astype(jnp.float32)
    for turn in range(groups - 1):
        total = total + keyval_over[turn].astype(jnp.float32)
    grad_keyval_ref[...] = total
    for kind, out_ref in ((0, grad_query_ref), (1, grad_output_ref)):
        for turn in range(groups - 1):
            across[turn][kind].wait_recv()
        own = pl.multiple_of(group * chunk_rows, chunk_rows)

        @pl.loop(0, chunk_rows // step)
        def _(turn):
            at = chunk_of(turn, step)
            total = kept[10 + kind, pl.ds(own + turn * step, step), :].astype(jnp.float32)
            for other in range(groups - 1):
                total = total + come[other, kind, at, :].astype(jnp.float32)
            out_ref[at, :] = total

    for each in vector_out:
        each.wait_recv()
    device = group * 8 + here
    share = model_width // (8 * groups)
    parts = width // share
    columns = vectors_ref[:, chunk_of(device // parts, width)]
    picked = columns
    for part in range(1, parts):
        moved = jnp.concatenate([columns[:, part * share :], columns[:, : part * share]], axis=1)
        picked = jnp.where(device % parts == part, moved, picked)
    own_vectors_ref[...] = picked
    up_share = own_up_ref.shape[1]
    in_row = model_width // up_share
    up_columns = vectors_ref[:, chunk_of(device % in_row, up_share)]
    up_own = jnp.zeros((1, up_share), jnp.float32)
    for row in range(known_up_ref.shape[0]):
        up_own = jnp.where(device // in_row == row, up_columns[row : row + 1, :], up_own)
    own_up_ref[...] = up_own
    for each in to_chip[0] + corners[0] + corners[1] + to_x[1] + to_y[1]:
        each.wait_send()
    for chunk in chunks[1:]:
        to_x[0][chunk].wait_send()
        to_y[0][chunk].wait_send()
    kv_sums.finish()
    keyval_sums.finish()
    for each in vector_copies + vector_out:
        each.wait_send()
    for each in sum(across, []) + keyval_across + vector_across:
        each.wait_send()


def backward_reduce(
    owning,
    share,
    weights,
    queries,
    mixture,
    grad_hidden,
    normed,
    branch,
    log_total,
    prompt_kv,
    answer_kv,
    states,
    gain,
    keyval_full,
    known_up,
    known_sums,
    known_columns,
    known_squares,
    groups,
    prompts,
    answers,
    prompt_rows,
    call_number,
):
    token_rows, model_width = normed.shape
    block = weights.shape[4]
    heads = block // HEAD_WIDTH
    keyval_width = keyval_full.shape[1]
    weight_rows = model_width // groups
    keyval_rows = model_width // groups // 8
    kind, wide = jnp.bfloat16, jnp.float32
    inside = pl.BlockSpec(memory_space=pltpu.VMEM)
    anywhere = pl.BlockSpec(memory_space=pl.ANY)
    scalars = pl.BlockSpec(memory_space=pltpu.SMEM)
    dma = pltpu.SemaphoreType.DMA
    others = groups - 1
    return pl.pallas_call(
        functools.partial(backward_reduce_kernel, prompts, answers, heads, groups, prompt_rows),
        out_shape=(
            jax.ShapeDtypeStruct((weight_rows, block), wide),
            jax.ShapeDtypeStruct((weight_rows, block), wide),
            jax.ShapeDtypeStruct((keyval_rows, keyval_width), wide),
            jax.ShapeDtypeStruct((VECTOR_ROWS, model_width), wide),
            jax.ShapeDtypeStruct((VECTOR_ROWS, HEAD_WIDTH), wide),
            jax.ShapeDtypeStruct((1, known_up.size // (8 * groups)), wide),
            jax.ShapeDtypeStruct((prompts * prompt_rows, model_width), kind),
            jax.ShapeDtypeStruct((token_rows - prompts * prompt_rows, model_width), kind),
        ),
        in_specs=[scalars] * 2 + [anywhere] * 4 + [inside] * 12,
        out_specs=(inside,) * 8,
        scratch_shapes=[
            pltpu.VMEM((model_width, token_rows), kind),
            pltpu.VMEM((model_width, token_rows), kind),
            pltpu.VMEM(prompt_kv.shape, wide),
            pltpu.VMEM(answer_kv.shape, wide),
            pltpu.VMEM((token_rows, model_width), wide),
            pltpu.VMEM((token_rows, model_width), wide),
            pltpu.VMEM((2,) + weights.shape[1:], kind),
            pltpu.VMEM((2, 2, token_rows, block), kind),
            pltpu.VMEM((2, token_rows, block), kind),
            pltpu.VMEM((12, model_width, block), kind),
            pltpu.VMEM((4, 2, model_width, block), kind),
            pltpu.VMEM((2, model_width, block), kind),
            pltpu.VMEM((2, 2, model_width, block), kind),
            pltpu.VMEM((others, 2, weight_rows, block), kind),
            pltpu.VMEM(prompt_kv.shape, kind),
            pltpu.VMEM((4, prompts, prompt_rows, keyval_width), kind),
            pltpu.VMEM((4, prompts, prompt_rows, keyval_width), kind),
            pltpu.VMEM((3, prompts, prompt_rows, keyval_width), kind),
            pltpu.VMEM((token_rows, keyval_width), kind),
            pltpu.VMEM((groups, 8, keyval_rows, keyval_width), kind),
            pltpu.VMEM((4, groups, keyval_rows, keyval_width), kind),
            pltpu.VMEM((4, groups, keyval_rows, keyval_width), kind),
            pltpu.VMEM((3, groups, keyval_rows, keyval_width), kind),
            pltpu.VMEM((groups, keyval_rows, keyval_width), kind),
            pltpu.VMEM((others, keyval_rows, keyval_width), kind),
            pltpu.VMEM((VECTOR_ROWS, model_width), wide),
            pltpu.VMEM((7, VECTOR_ROWS, block), wide),
            pltpu.VMEM((VECTOR_ROWS, block), wide),
            pltpu.VMEM((others, VECTOR_ROWS, block), wide),
            dma((8 + 6 * groups,)),
            dma((8 + 6 * groups,)),
            dma((4 * others,)),
            dma((4 * others,)),
            dma((4, 7)),
            dma((4, 7)),
            dma((2, 3)),
            dma((2,)),
            dma,
        ],
        compiler_params=pltpu.CompilerParams(
            collective_id=call_number,
            has_side_effects=True,
            vmem_limit_bytes=63 * 1024 * 1024,
        ),
        cost_estimate=pl.CostEstimate(
            flops=100 * token_rows * model_width * block,
            bytes_accessed=250 * 1000 * 1000,
            transcendentals=0,
        ),
        name="backward_reduce",
    )(
        owning,
        share,
        weights,
        queries,
        mixture,
        grad_hidden,
        normed,
        branch,
        log_total,
        prompt_kv,
        answer_kv,
        states,
        gain.reshape(1, -1),
        keyval_full,
        known_up,
        known_sums,
        known_columns,
        known_squares,
    )


def finish_kernel(share_size, model_width, *refs):
    half = len(refs) - 17
    (
        vectors_ref,
        own_vectors_ref,
        own_up_ref,
        count_ref,
        prompt_ref,
        answer_ref,
        query_ref,
        output_ref,
        keyval_ref,
        up_ref,
        down_ref,
    ) = refs[:half]
    prompt_out, answer_out, query_out, output_out, keyval_out, up_out, down_out, *outs = refs[half:]
    prompt_out[...] = prompt_ref[...]
    answer_out[...] = answer_ref[...]
    query_out[...] = query_ref[...]
    output_out[...] = output_ref[...]
    keyval_out[...] = keyval_ref[...]
    up_out[...] = up_ref[...].astype(jnp.float32)
    down_out[...] = down_ref[...].astype(jnp.float32)
    *vector_outs, up_bias_out, value_out, loss_out = outs
    for row, out_ref in zip((8, 9, 10, 4, 5, 6, 7), vector_outs):
        out_ref[...] = own_vectors_ref[row : row + 1, :share_size]
    up_bias_out[...] = own_up_ref[...]
    value_out[...] = vectors_ref[11:12, :HEAD_WIDTH]
    loss_out[...] = vectors_ref[12:13, :1] / (count_ref[...] * model_width)


def finish(share_size, vectors, own_vectors, own_up, valid_count, *arrays):
    wide = jnp.float32
    model_width = vectors.shape[1]
    kinds = [array.dtype for array in arrays[:5]] + [wide, wide]
    shapes = [jax.ShapeDtypeStruct(array.shape, kind) for array, kind in zip(arrays, kinds)]
    shapes += [jax.ShapeDtypeStruct((1, share_size), wide)] * 7
    shapes += [
        jax.ShapeDtypeStruct(own_up.shape, wide),
        jax.ShapeDtypeStruct((1, HEAD_WIDTH), wide),
        jax.ShapeDtypeStruct((1, 1), wide),
    ]
    inside = pl.BlockSpec(memory_space=pltpu.VMEM)
    return pl.pallas_call(
        functools.partial(finish_kernel, share_size, model_width),
        out_shape=tuple(shapes),
        in_specs=[inside] * (4 + len(arrays)),
        out_specs=(inside,) * len(shapes),
        compiler_params=pltpu.CompilerParams(vmem_limit_bytes=VMEM_BYTES),
        name="finish",
    )(vectors, own_vectors, own_up, valid_count.reshape(1, 1), *arrays)


def by_group(values):
    return jnp.swapaxes(values, 0, 1).reshape(-1)


def body(
    kernels,
    prompt_states,
    answer_states,
    answer_prompt,
    prompt_teacher,
    answer_teacher,
    prompt_valid,
    answer_valid,
    first_gain,
    first_shift,
    query_weight,
    query_bias,
    keyval_weight,
    value_bias,
    output_weight,
    output_bias,
    second_gain,
    second_shift,
    up_weight,
    up_bias,
    down_weight,
    down_bias,
):
    prompt_count, prompt_rows, model_width = prompt_states.shape
    answer_count, answer_len, _ = answer_states.shape
    groups = lax.axis_size("grp")
    token_devices = lax.axis_size("tok")
    token_index = lax.axis_index("tok")
    group_index = lax.axis_index("grp")
    own_prompt = prompt_rows * prompt_count
    token_rows = own_prompt + answer_count * answer_len
    hidden_units = up_bias.shape[0] * groups * token_devices
    ff_here = hidden_units // token_devices
    ff_start = token_index * ff_here
    share_size = first_gain.shape[0]
    block = query_weight.shape[1]
    weight_rows = query_weight.shape[0]
    keyval_rows, keyval_width = keyval_weight.shape

    def own_rows(prompt_part, answer_part):
        return jnp.concatenate(
            [prompt_part.reshape(own_prompt, -1), answer_part.reshape(-1, prompt_part.shape[-1])],
            axis=0,
        )

    states = own_rows(prompt_states, answer_states)
    inputs = states.astype(jnp.float32)
    valid_rows = jnp.concatenate([prompt_valid.reshape(-1), answer_valid.reshape(-1)])
    own_count = jnp.sum(valid_rows)
    valid_rows = valid_rows.astype(jnp.float32)

    up_cols = lax.all_gather(up_weight, "grp", axis=0, tiled=True)
    down_cols = lax.all_gather(down_weight, "grp", axis=0, tiled=True)

    projections = lax.all_gather(jnp.stack([query_weight, output_weight]), "grp", axis=0)
    count_parts = jnp.stack([own_count // 128, own_count % 128]).astype(jnp.bfloat16)
    smalls, small_at = jnp.zeros((SMALL_ROWS * block,), jnp.bfloat16), 0
    for each in (
        first_gain,
        first_shift,
        query_bias,
        output_bias,
        second_gain,
        second_shift,
        down_bias,
        up_bias,
        count_parts,
    ):
        behind = SMALL_ROWS * block - small_at - each.shape[0]
        smalls = smalls + jnp.pad(each, (small_at, behind))
        small_at += each.shape[0]
    smalls = smalls.reshape(SMALL_ROWS, block)
    pack = jnp.concatenate([keyval_weight.reshape(-1, block), smalls], axis=0)
    packed = spread(pack, groups, 0, kernels)
    keyval_pack = pack.shape[0] - SMALL_ROWS
    keyval_start = 2 * weight_rows
    keyval_full = jnp.swapaxes(
        packed[:, :, :keyval_pack].reshape(token_devices, groups, keyval_rows, keyval_width),
        0,
        1,
    ).reshape(model_width, keyval_width)
    small_full = packed[:, :, keyval_pack:].reshape(token_devices, groups, SMALL_ROWS * block)
    small_full = jnp.swapaxes(small_full.astype(jnp.float32), 0, 1)

    def vector(start, size):
        return small_full[:, :, start : start + size].reshape(-1)

    gain_one, shift_one, query_offset, output_offset, gain_two, shift_two, down_offset = (
        vector(index * share_size, share_size) for index in range(7)
    )
    up_offset = vector(7 * share_size, up_bias.shape[0])
    count_at = 7 * share_size + up_bias.shape[0]
    counts = small_full[:, :, count_at : count_at + 2]
    valid_count = jnp.sum(counts[:, :, 0]) * 128.0 + jnp.sum(counts[:, :, 1])
    up_here = lax.dynamic_slice_in_dim(up_offset, ff_start, ff_here)

    scaled_one, inverse_one = norm_stats(inputs)
    normed_one = (scaled_one * gain_one + shift_one).astype(jnp.bfloat16)
    key_offset = jnp.concatenate(
        [jnp.zeros((HEAD_WIDTH,), jnp.float32), value_bias.astype(jnp.float32)]
    )
    key_value_rows = (plain_product(normed_one, keyval_full) + key_offset).astype(jnp.bfloat16)
    prompt_kv = tok_gather_small(
        key_value_rows[:own_prompt].reshape(prompt_count, prompt_rows, -1), 1, kernels
    )
    answer_kv = key_value_rows[own_prompt:]
    owning = answer_prompt - group_index * prompt_count
    owning = lax.dynamic_slice_in_dim(owning, token_index * answer_count, answer_count)
    place = jnp.reshape(token_index * prompt_rows, (1,)).astype(jnp.int32)
    if kernels:
        weights, queries, mixture, log_total, hidden, normed_two = gather_attention(
            owning,
            projections,
            normed_one,
            query_offset,
            prompt_kv,
            answer_kv,
            states,
            output_offset,
            gain_two,
            shift_two,
            prompt_count,
            answer_count,
            prompt_rows,
            8,
        )
    else:
        weights = lax.all_gather(projections, "tok", axis=0)
        weights = jnp.swapaxes(weights, 1, 2).reshape(token_devices, 2, model_width, block)
        queries, mixture, log_total, hidden, normed_two = attention_forward(
            place,
            owning,
            normed_one,
            weights[:, 0],
            weights[:, 1],
            query_offset,
            prompt_kv,
            answer_kv,
            states,
            output_offset,
            gain_two,
            shift_two,
            prompt_count,
            answer_count,
        )

    teacher = own_rows(prompt_teacher, answer_teacher)
    every_token = token_rows * groups * token_devices
    factors = (every_token / valid_count * valid_rows)[:, None]
    if kernels:
        group_two, activated, slope = gather_and_up(normed_two, up_cols, up_here, 2)
        prompt_out, answer_out, grad_branch_two, grad_result, own_squares, grad_down_offset = (
            product_and_reduce(
                activated,
                down_cols,
                None,
                hidden,
                teacher,
                3,
                own_prompt,
                down_offset.reshape(1, -1),
                valid_rows[:, None],
                factors,
            )
        )
        _, grad_pre_active, grad_down_cols, grad_up_offset = gather_and_grad(
            grad_branch_two, down_cols, activated, slope, 4
        )
        grad_hidden, grad_up_cols, grad_branch_one, second_sums = product_and_reduce(
            grad_pre_active,
            up_cols,
            group_two,
            hidden,
            grad_result,
            5,
            own_prompt,
            gain_two.reshape(1, -1),
        )
        grad_up_offset = grad_up_offset.reshape(-1)
    else:
        group_two = lax.all_gather(normed_two, "tok", axis=0, tiled=True)
        pre_active = plain_product(group_two, up_cols) + up_here
        activated = jax.nn.gelu(pre_active, approximate=True).astype(jnp.bfloat16)
        feed_term = for_sending(transposed_product(activated, down_cols))
        feed_term = lax.psum_scatter(feed_term, "tok", scatter_dimension=0, tiled=True)
        result_rows = hidden + feed_term.astype(jnp.float32) + down_offset
        prompt_out, answer_out = result_rows[:own_prompt], result_rows[own_prompt:]
        differ = result_rows - teacher.astype(jnp.float32)
        own_squares = jnp.sum(valid_rows[:, None] * differ * differ)
        grad_result = factors * differ
        grad_branch_two = grad_result.astype(jnp.bfloat16)
        grad_down_offset = column_sums(grad_branch_two)
        group_grad_two = lax.all_gather(grad_branch_two, "tok", axis=0, tiled=True)
        grad_activated = plain_product(group_grad_two, down_cols)
        _, gelu_back = jax.vjp(
            lambda argument: jax.nn.gelu(argument, approximate=True), pre_active
        )
        grad_pre_active = gelu_back(grad_activated)[0].astype(jnp.bfloat16)
        grad_normed_two = for_sending(transposed_product(grad_pre_active, up_cols))
        grad_normed_two = lax.psum_scatter(
            grad_normed_two, "tok", scatter_dimension=0, tiled=True
        ).astype(jnp.float32)
        grad_down_cols = for_sending(weight_product(group_grad_two, activated))
        grad_up_cols = for_sending(weight_product(group_two, grad_pre_active))
        grad_up_offset = column_sums(grad_pre_active)
        scaled_two, inverse_two = norm_stats(hidden)
        grad_norm_two, grad_gain_two, grad_shift_two = norm_backward(
            grad_normed_two, gain_two, scaled_two, inverse_two
        )
        grad_hidden = grad_result + grad_norm_two
        grad_branch_one = grad_hidden.astype(jnp.bfloat16)
        grad_output_offset = column_sums(grad_branch_one)
    grad_down_weight = lax.psum_scatter(grad_down_cols, "grp", scatter_dimension=0, tiled=True)
    grad_down_weight, grad_up_cols = lax.optimization_barrier((grad_down_weight, grad_up_cols))
    grad_up_weight = lax.psum_scatter(grad_up_cols, "grp", scatter_dimension=0, tiled=True)

    share = (owning[:, None] == jnp.arange(prompt_count)[None, :]).astype(jnp.float32).reshape(-1)
    grad_up_place = lax.dynamic_update_slice_in_dim(
        jnp.zeros((hidden_units,), jnp.float32), grad_up_offset, ff_start, 0
    )
    if kernels:
        (
            grad_query_own,
            grad_output_own,
            grad_keyval_own,
            vectors,
            mine,
            grad_up_own,
            prompt_grad,
            answer_grad,
        ) = backward_reduce(
            owning,
            share,
            weights,
            queries,
            mixture,
            grad_hidden,
            normed_one,
            grad_branch_one,
            log_total,
            prompt_kv,
            answer_kv,
            states,
            gain_one,
            keyval_full,
            grad_up_place.reshape(-1, model_width),
            second_sums,
            grad_down_offset,
            own_squares,
            groups,
            prompt_count,
            answer_count,
            prompt_rows,
            6,
        )
        (
            prompt_grad,
            answer_grad,
            grad_query_own,
            grad_output_own,
            grad_keyval_own,
            grad_up_weight,
            grad_down_weight,
            *own_vectors,
            grad_up_own,
            value_total,
            loss_value,
        ) = finish(
            share_size,
            vectors,
            mine,
            grad_up_own,
            valid_count,
            prompt_grad,
            answer_grad,
            grad_query_own,
            grad_output_own,
            grad_keyval_own,
            grad_up_weight,
            grad_down_weight,
        )
        own_vectors = [each.reshape(-1) for each in own_vectors]
        grad_up_own, value_total = grad_up_own.reshape(-1), value_total.reshape(-1)
        loss_value = loss_value.reshape(())
    else:
        grad_rows = keyval_start + keyval_pack
        grad_weights, grad_normed_one, grad_prompt_kv, grad_answer_kv, grad_query_offset = (
            attention_backward(
                place,
                owning,
                share,
                normed_one,
                weights,
                groups,
                grad_rows,
                prompt_kv,
                answer_kv,
                grad_branch_one,
                queries,
                mixture,
                log_total,
                prompt_count,
                answer_count,
            )
        )
        grad_prompt_kv = lax.psum_scatter(
            grad_prompt_kv, "tok", scatter_dimension=1, tiled=True
        ).astype(jnp.float32)
        grad_keyvals = jnp.concatenate(
            [grad_prompt_kv.reshape(own_prompt, -1), grad_answer_kv], axis=0
        ).astype(jnp.bfloat16)
        grad_keyval_full = weight_product(normed_one, grad_keyvals)
        grad_value_offset = column_sums(grad_keyvals[:, HEAD_WIDTH:])
        grad_normed_one = grad_normed_one + transposed_product(grad_keyvals, keyval_full)
        grad_norm_one, grad_gain_one, grad_shift_one = norm_backward(
            grad_normed_one, gain_one, scaled_one, inverse_one
        )
        grad_inputs = grad_hidden + grad_norm_one

        grad_keyval_blocks = jnp.swapaxes(
            grad_keyval_full.astype(jnp.bfloat16).reshape(groups, token_devices, -1, block), 0, 1
        )
        grad_weights = lax.dynamic_update_slice(
            grad_weights, grad_keyval_blocks, (0, 0, keyval_start, 0)
        )
        vectors = (
            grad_gain_one,
            grad_shift_one,
            grad_query_offset.reshape(-1),
            grad_output_offset,
            grad_gain_two,
            grad_shift_two,
            grad_down_offset,
            grad_up_place,
        )
        totals = jnp.concatenate([grad_value_offset, own_squares.reshape(1)])
        blocks = jnp.concatenate(
            [each.reshape(groups, token_devices, -1) for each in vectors]
            + [jnp.broadcast_to(totals, (groups, token_devices, totals.shape[0]))],
            axis=2,
        )
        blocks = jnp.pad(blocks, ((0, 0), (0, 0), (0, SMALL_SUMS - blocks.shape[2])))
        blocks = jnp.swapaxes(blocks, 0, 1).reshape(token_devices, -1, HEAD_WIDTH)
        grad_weights = lax.psum_scatter(
            grad_weights.reshape(token_devices, -1, block), "tok", scatter_dimension=0, tiled=False
        )
        grad_weights = lax.psum_scatter(grad_weights, "grp", scatter_dimension=0, tiled=True)
        grad_weights = grad_weights.astype(jnp.float32)
        small_sums = lax.psum_scatter(blocks, "tok", scatter_dimension=0, tiled=False)
        small_sums = lax.psum_scatter(small_sums, "grp", scatter_dimension=0, tiled=True)
        small_sums = small_sums.reshape(-1)
        up_share = up_bias.shape[0]
        totals_at = 7 * share_size + up_share
        value_total = small_sums[totals_at : totals_at + HEAD_WIDTH]
        squared_sum = small_sums[totals_at + HEAD_WIDTH]
        own_vectors = [
            small_sums[index * share_size : (index + 1) * share_size] for index in range(7)
        ]
        grad_up_own = small_sums[7 * share_size : totals_at]
        grad_query_own = grad_weights[:weight_rows]
        grad_output_own = grad_weights[weight_rows:keyval_start]
        grad_keyval_own = grad_weights[keyval_start:].reshape(keyval_rows, keyval_width)
        prompt_grad, answer_grad = grad_inputs[:own_prompt], grad_inputs[own_prompt:]
        loss_value = squared_sum / (valid_count * model_width)

    def row_outputs(prompt_part, answer_part):
        return (
            prompt_part.astype(jnp.bfloat16).reshape(prompt_states.shape),
            answer_part.astype(jnp.bfloat16).reshape(answer_states.shape),
        )

    prompt_out, answer_out = row_outputs(prompt_out, answer_out)
    prompt_grad, answer_grad = row_outputs(prompt_grad, answer_grad)
    pieces = own_vectors
    return (
        prompt_out,
        answer_out,
        prompt_grad,
        answer_grad,
        pieces[0],
        pieces[1],
        grad_query_own,
        pieces[2],
        grad_keyval_own,
        value_total,
        grad_output_own,
        pieces[3],
        pieces[4],
        pieces[5],
        grad_up_weight.astype(jnp.float32),
        grad_up_own,
        grad_down_weight.astype(jnp.float32),
        pieces[6],
        loss_value,
    )


def solution(mesh):
    rows = P(("grp", "tok"))
    table = P(("grp", "tok"), None)
    matrix = P("grp", "tok")
    prompt_part = P("grp", "tok", None)
    answer_part = P(("grp", "tok"), None, None)
    in_specs = (
        prompt_part,
        answer_part,
        P("grp"),
        prompt_part,
        answer_part,
        P("grp", "tok"),
        table,
        rows,
        rows,
        matrix,
        rows,
        table,
        P(),
        matrix,
        rows,
        rows,
        rows,
        matrix,
        rows,
        matrix,
        rows,
    )
    out_specs = (
        prompt_part,
        answer_part,
        prompt_part,
        answer_part,
        rows,
        rows,
        matrix,
        rows,
        table,
        P(),
        matrix,
        rows,
        rows,
        rows,
        matrix,
        rows,
        matrix,
        rows,
        P(),
    )
    kernels = mesh.shape["tok"] == 8
    return jax.shard_map(
        functools.partial(body, kernels),
        mesh=mesh,
        in_specs=in_specs,
        out_specs=out_specs,
        check_vma=False,
    )
```

```python
import functools

import jax
import jax.numpy as jnp
from jax import lax
from jax.experimental import pallas as pl
from jax.experimental.pallas import tpu as pltpu
from jax.sharding import PartitionSpec as P

HEAD_WIDTH = 128
epsilon = 1e-05
masked = -1e30
MESH = pl.DeviceIdType.MESH
VMEM_BYTES = 56 * 1024 * 1024
SMALL_ROWS = 16
SMALL_SUMS = 1024


def for_sending(value):
    return value.astype(jnp.bfloat16)


def plain_product(left, right):
    return jnp.dot(left, right, preferred_element_type=jnp.float32)


def transposed_product(left, right):
    return lax.dot_general(
        left, right, (((1,), (1,)), ((), ())), preferred_element_type=jnp.float32
    )


def weight_product(left, right):
    return lax.dot_general(
        left, right, (((0,), (0,)), ((), ())), preferred_element_type=jnp.float32
    )


def norm_stats(values):
    center = values - jnp.mean(values, axis=-1, keepdims=True)
    inverse = lax.rsqrt(jnp.mean(center * center, axis=-1, keepdims=True) + epsilon)
    return center * inverse, inverse


def norm_backward(grad_out, gain, scaled, inverse):
    weighted = grad_out * gain
    grad_in = inverse * (
        weighted
        - jnp.mean(weighted, axis=-1, keepdims=True)
        - scaled * jnp.mean(weighted * scaled, axis=-1, keepdims=True)
    )
    return (grad_in, jnp.sum(grad_out * scaled, axis=0), jnp.sum(grad_out, axis=0))


def column_sums(values):
    return jnp.sum(values.astype(jnp.float32), axis=0)


def block_of_eight():
    here = lax.axis_index("tok")
    core, across, along = here % 2, (here // 2) % 2, here // 4
    on_x = here + 2 - 4 * across
    on_y = here + 4 - 8 * along
    on_chip = here + 1 - 2 * core
    corner = on_x + 4 - 8 * along
    return here, on_x, on_y, on_chip, corner


def greet_all(peers, other_groups):
    barrier = pltpu.get_barrier_semaphore()
    for peer in peers:
        pl.semaphore_signal(barrier, inc=1, device_id={"tok": peer}, device_id_type=MESH)
    for other in other_groups:
        pl.semaphore_signal(barrier, inc=1, device_id={"grp": other}, device_id_type=MESH)
    pl.semaphore_wait(barrier, len(peers) + len(other_groups))


def greet(devices):
    barrier = pltpu.get_barrier_semaphore()
    for device in devices:
        pl.semaphore_signal(barrier, inc=1, device_id={"tok": device}, device_id_type=MESH)
    pl.semaphore_wait(barrier, len(devices))


def paired_gather(source, place, send_sem, recv_sem):
    here, on_x, on_y, on_chip, corner = block_of_eight()
    over = [
        remote(index, source, place(here), device, send_sem, recv_sem)
        for index, device in enumerate((on_x, on_y, corner, on_chip))
    ]
    handed = [
        remote(4 + index, place(device), place(device), on_chip, send_sem, recv_sem)
        for index, device in enumerate((on_x, on_y, corner))
    ]
    for each in over:
        each.start()
    for each, then in zip(over, handed):
        each.wait_recv()
        then.start()
    for each in [over[3]] + handed:
        each.wait_recv()
    for each in over + handed:
        each.wait_send()


def spread_kernel(groups, own_ref, out_ref, held, send_sem, recv_sem, over_send, over_recv):
    here, on_x, on_y, on_chip, corner = block_of_eight()
    group = lax.axis_index("grp")
    other_groups = [(group + turn) % groups for turn in range(1, groups)]
    greet_all((on_x, on_y, on_chip, corner), other_groups)
    over = [
        pltpu.make_async_remote_copy(
            src_ref=own_ref,
            dst_ref=held.at[group],
            send_sem=over_send.at[index],
            recv_sem=over_recv.at[index],
            device_id={"grp": other},
            device_id_type=MESH,
        )
        for index, other in enumerate(other_groups)
    ]
    for each in over:
        each.start()
    held[group] = own_ref[...]
    for each in over:
        each.wait_recv()
    out_ref[here] = held[...]
    paired_gather(held, lambda device: out_ref.at[device], send_sem, recv_sem)
    for each in over:
        each.wait_send()


def spread(own, groups, call_number, kernels):
    if not kernels:
        return lax.all_gather(lax.all_gather(own, "grp", axis=0), "tok", axis=0)
    inside = pl.BlockSpec(memory_space=pltpu.VMEM)
    dma = pltpu.SemaphoreType.DMA
    return pl.pallas_call(
        functools.partial(spread_kernel, groups),
        out_shape=jax.ShapeDtypeStruct((8, groups) + own.shape, own.dtype),
        in_specs=[inside],
        out_specs=inside,
        scratch_shapes=[
            pltpu.VMEM((groups,) + own.shape, own.dtype),
            dma((7,)),
            dma((7,)),
            dma((groups - 1,)),
            dma((groups - 1,)),
        ],
        compiler_params=pltpu.CompilerParams(collective_id=call_number, has_side_effects=True),
        name="spread",
    )(own)


def remote(index, source, target, device, send_sem, recv_sem):
    return pltpu.make_async_remote_copy(
        src_ref=source,
        dst_ref=target,
        send_sem=send_sem.at[index],
        recv_sem=recv_sem.at[index],
        device_id={"tok": device},
        device_id_type=MESH,
    )


def chunk_of(index, size):
    return pl.ds(pl.multiple_of(index * size, size), size)


CHUNK = 512
LINEAR = 0.7978845608
CUBIC = 0.044715


def gather_beside(own_ref, out_ref, send_sem, recv_sem, local_sem, use):
    rows = own_ref.shape[0]
    half, quarter = rows // 2, rows // 4
    here, on_x, on_y, on_chip, corner = block_of_eight()
    shift = on_chip - here
    counter = iter(range(GATHER_COPIES))

    def copy(source, block, start, count, device):
        place = pl.ds(start, count)
        return remote(
            next(counter),
            source.at[place] if source is own_ref else source.at[block, place],
            out_ref.at[block, place],
            device,
            send_sem,
            recv_sem,
        )

    greet((on_x, on_y, on_chip))
    own = pltpu.make_async_copy(own_ref, out_ref.at[here], local_sem)
    x_low = copy(own_ref, here, 0, half, on_x)
    y_high = copy(own_ref, here, half, half, on_y)
    x_high = copy(own_ref, here, half, half, on_x)
    y_low = copy(own_ref, here, 0, half, on_y)
    to_chip = copy(own_ref, here, 0, rows, on_chip)
    to_y = [copy(out_ref, on_x, turn * quarter, quarter, on_y) for turn in (0, 1)]
    to_x = [copy(out_ref, on_y, half + turn * quarter, quarter, on_x) for turn in (0, 1)]
    chip_x = [copy(out_ref, on_x, turn * half, half, on_chip) for turn in (0, 1)]
    chip_y = [copy(out_ref, on_y, turn * half, half, on_chip) for turn in (0, 1)]
    chip_corner = [copy(out_ref, corner, turn * quarter, quarter, on_chip) for turn in range(4)]
    for each in (x_low, y_high, x_high, y_low, to_chip, own):
        each.start()
    use(0, [(here, 0, rows)])
    to_chip.wait_recv()
    use(1, [(on_chip, 0, rows)])
    x_low.wait_recv()
    for each in (*to_y, chip_x[0]):
        each.start()
    y_high.wait_recv()
    for each in (*to_x, chip_y[1]):
        each.start()
    use(2, [(on_x, 0, half), (on_y, half, half)])
    chip_x[0].wait_recv()
    chip_y[1].wait_recv()
    use(3, [(on_x + shift, 0, half), (on_y + shift, half, half)])
    x_high.wait_recv()
    chip_x[1].start()
    y_low.wait_recv()
    chip_y[0].start()
    use(4, [(on_x, half, half), (on_y, 0, half)])
    chip_x[1].wait_recv()
    chip_y[0].wait_recv()
    use(5, [(on_x + shift, half, half), (on_y + shift, 0, half)])
    for turn in (0, 1):
        to_y[turn].wait_recv()
        chip_corner[turn].start()
        to_x[turn].wait_recv()
        chip_corner[2 + turn].start()
        chip_corner[turn].wait_recv()
        chip_corner[2 + turn].wait_recv()
        use(
            6 + turn,
            [
                (block, start + turn * quarter, quarter)
                for block in (corner, corner + shift)
                for start in (0, half)
            ],
        )
    own.wait()
    for each in (x_low, y_high, x_high, y_low, to_chip, *to_y, *to_x, *chip_x, *chip_y, *chip_corner):
        each.wait_send()


GATHER_COPIES = 17


def moves(outside, inside, pieces, semaphores, outward):
    done, copies = 0, []
    for index, (block, start, count) in enumerate(pieces):
        away = outside.at[block, pl.ds(start, count)]
        near = inside.at[pl.ds(done, count)]
        pair = (near, away) if outward else (away, near)
        copies.append(pltpu.make_async_copy(*pair, semaphores.at[index]))
        done += count
    return copies


def up_kernel(
    own_ref,
    up_hbm,
    bias_ref,
    rows_ref,
    active_ref,
    slope_ref,
    up,
    rows,
    active,
    slope,
    send_sem,
    recv_sem,
    local_sem,
    weight_sem,
    row_sem,
    store_sem,
):
    weights = pltpu.make_async_copy(up_hbm, up, weight_sem)
    weights.start()
    stores = {}

    def use(place, pieces):
        slot = place % 2
        if place:
            loads = moves(rows_ref, rows, pieces, row_sem, False)
        else:
            loads = [pltpu.make_async_copy(own_ref, rows, row_sem.at[0])]
        for each in loads:
            each.start()
        if place == 0:
            weights.wait()
        for each in stores.pop(slot, ()):
            each.wait()
        for each in loads:
            each.wait()

        @pl.loop(0, up.shape[1] // CHUNK)
        def _(turn):
            at = chunk_of(turn, CHUNK)
            value = plain_product(rows[...], up[:, at]) + bias_ref[:, at]
            square = value * value
            bent = jnp.tanh(value * (LINEAR + (LINEAR * CUBIC) * square))
            level = 0.5 + 0.5 * bent
            active[slot, :, at] = (value * level).astype(jnp.bfloat16)
            slope[slot, :, at] = (
                level
                + (0.5 * value)
                * (1.0 - bent * bent)
                * (LINEAR + (3.0 * LINEAR * CUBIC) * square)
            ).astype(jnp.bfloat16)

        stores[slot] = moves(
            active_ref, active.at[slot], pieces, store_sem.at[slot, 0], True
        ) + moves(slope_ref, slope.at[slot], pieces, store_sem.at[slot, 1], True)
        for each in stores[slot]:
            each.start()

    gather_beside(own_ref, rows_ref, send_sem, recv_sem, local_sem, use)
    for slot in (0, 1):
        for each in stores[slot]:
            each.wait()


def gather_and_up(own, up_cols, bias, call_number):
    token_rows, model_width = own.shape
    width = up_cols.shape[1]
    hidden = jax.ShapeDtypeStruct((8, token_rows, width), jnp.bfloat16)
    anywhere = pl.BlockSpec(memory_space=pl.ANY)
    dma = pltpu.SemaphoreType.DMA
    return pl.pallas_call(
        up_kernel,
        out_shape=(
            jax.ShapeDtypeStruct((8, token_rows, model_width), jnp.bfloat16),
            hidden,
            hidden,
        ),
        in_specs=[anywhere, anywhere, pl.BlockSpec(memory_space=pltpu.VMEM)],
        out_specs=(anywhere, anywhere, anywhere),
        scratch_shapes=[
            pltpu.VMEM(up_cols.shape, jnp.bfloat16),
            pltpu.VMEM((token_rows, model_width), jnp.bfloat16),
            pltpu.VMEM((2, token_rows, width), jnp.bfloat16),
            pltpu.VMEM((2, token_rows, width), jnp.bfloat16),
            dma((GATHER_COPIES,)),
            dma((GATHER_COPIES,)),
            dma,
            dma,
            dma((4,)),
            dma((2, 2, 4)),
        ],
        compiler_params=pltpu.CompilerParams(
            collective_id=call_number, has_side_effects=True, vmem_limit_bytes=VMEM_BYTES
        ),
        cost_estimate=pl.CostEstimate(
            flops=16 * token_rows * model_width * width,
            bytes_accessed=150 * 1000 * 1000,
            transcendentals=0,
        ),
        name="gather_and_up",
    )(own, up_cols, bias.reshape(1, -1))


def grad_kernel(
    own_ref,
    down_hbm,
    active_ref,
    slope_ref,
    rows_ref,
    grad_ref,
    weight_ref,
    bias_ref,
    down,
    rows,
    active,
    slope,
    grads,
    sums,
    narrow,
    send_sem,
    recv_sem,
    local_sem,
    weight_sem,
    row_sem,
    load_sem,
    store_sem,
):
    weights = pltpu.make_async_copy(down_hbm, down, weight_sem)
    weights.start()
    stores = {}

    def use(place, pieces):
        slot = place % 2
        if place:
            loads = moves(rows_ref, rows, pieces, row_sem, False)
        else:
            loads = [pltpu.make_async_copy(own_ref, rows, row_sem.at[0])]
        loads += moves(active_ref, active, pieces, load_sem.at[0], False)
        loads += moves(slope_ref, slope, pieces, load_sem.at[1], False)
        for each in loads:
            each.start()
        if place == 0:
            weights.wait()
        for each in stores.pop(slot, ()):
            each.wait()
        for each in loads:
            each.wait()

        @pl.loop(0, down.shape[1] // CHUNK)
        def _(turn):
            at = chunk_of(turn, CHUNK)
            value = plain_product(rows[...], down[:, at]) * slope[:, at].astype(jnp.float32)
            value = value.astype(jnp.bfloat16)
            grads[slot, :, at] = value
            total = jnp.sum(value.astype(jnp.float32), axis=0, keepdims=True)
            weight = weight_product(rows[...], active[:, at])
            if place == 0:
                bias_ref[:, at] = total
                sums[:, at] = weight
            elif place < 7:
                bias_ref[:, at] += total
                sums[:, at] += weight
            else:
                bias_ref[:, at] += total
                narrow[:, at] = (sums[:, at] + weight).astype(jnp.bfloat16)

        stores[slot] = moves(grad_ref, grads.at[slot], pieces, store_sem.at[slot], True)
        for each in stores[slot]:
            each.start()

    gather_beside(own_ref, rows_ref, send_sem, recv_sem, local_sem, use)
    last = pltpu.make_async_copy(narrow, weight_ref, weight_sem)
    last.start()
    for slot in (0, 1):
        for each in stores[slot]:
            each.wait()
    last.wait()


def gather_and_grad(own, down_cols, active, slope, call_number):
    token_rows, model_width = own.shape
    width = down_cols.shape[1]
    anywhere = pl.BlockSpec(memory_space=pl.ANY)
    dma = pltpu.SemaphoreType.DMA
    return pl.pallas_call(
        grad_kernel,
        out_shape=(
            jax.ShapeDtypeStruct((8, token_rows, model_width), jnp.bfloat16),
            jax.ShapeDtypeStruct((8, token_rows, width), jnp.bfloat16),
            jax.ShapeDtypeStruct((model_width, width), jnp.bfloat16),
            jax.ShapeDtypeStruct((1, width), jnp.float32),
        ),
        in_specs=[anywhere] * 4,
        out_specs=(anywhere,) * 3 + (pl.BlockSpec(memory_space=pltpu.VMEM),),
        scratch_shapes=[
            pltpu.VMEM(down_cols.shape, jnp.bfloat16),
            pltpu.VMEM((token_rows, model_width), jnp.bfloat16),
            pltpu.VMEM((token_rows, width), jnp.bfloat16),
            pltpu.VMEM((token_rows, width), jnp.bfloat16),
            pltpu.VMEM((2, token_rows, width), jnp.bfloat16),
            pltpu.VMEM((model_width, width), jnp.float32),
            pltpu.VMEM((model_width, width), jnp.bfloat16),
            dma((GATHER_COPIES,)),
            dma((GATHER_COPIES,)),
            dma,
            dma,
            dma((4,)),
            dma((2, 4)),
            dma((2, 4)),
        ],
        compiler_params=pltpu.CompilerParams(
            collective_id=call_number, has_side_effects=True, vmem_limit_bytes=VMEM_BYTES
        ),
        cost_estimate=pl.CostEstimate(
            flops=32 * token_rows * model_width * width,
            bytes_accessed=150 * 1000 * 1000,
            transcendentals=0,
        ),
        name="gather_and_grad",
    )(own, down_cols, active, slope)


def product_reduce_kernel(
    with_grad,
    narrow_ref,
    weight_hbm,
    *refs,
):
    if with_grad:
        wide_ref, hidden_hbm, result_hbm, gain_ref, *refs = refs
        grad_hidden_ref, grad_ref, branch_ref, sums_ref, *refs = refs
        *refs, wide, across, sums, wide_sem = refs
    else:
        hidden_hbm, teacher_hbm, offset_ref, valid_ref, factor_ref, *refs = refs
        prompt_ref, answer_ref, branch_ref, grad_result_ref, squares_ref, columns_ref, *refs = refs
    (
        weight,
        narrow,
        sent,
        mine,
        theirs,
        relayed,
        final,
        hidden_rows,
        other_rows,
        send_sem,
        recv_sem,
        weight_sem,
        narrow_sem,
        row_sem,
    ) = refs
    row_loads = (
        pltpu.make_async_copy(hidden_hbm, hidden_rows, row_sem.at[0]),
        pltpu.make_async_copy(result_hbm if with_grad else teacher_hbm, other_rows, row_sem.at[1]),
    )
    rows = narrow.shape[1]
    half = rows // 2
    here, on_x, on_y, on_chip, corner = block_of_eight()
    shift = on_chip - here
    first, second = pl.ds(0, half), pl.ds(half, half)
    load_weight = pltpu.make_async_copy(weight_hbm, weight, weight_sem)
    load_weight.start()

    def copy(index, source, target, device):
        return remote(index, source, target, device, send_sem, recv_sem)

    places = (corner, on_x, on_y, here)
    order = []
    for place in places:
        order += [place + shift, place]

    def fetch(turn):
        return pltpu.make_async_copy(
            narrow_ref.at[order[turn]], narrow.at[turn % 2], narrow_sem.at[turn % 2]
        )

    fetch(0).start()
    greet((on_x, on_y, on_chip))
    to_chip = [copy(index, sent.at[index], theirs.at[index], on_chip) for index in range(4)]
    step = 16

    def add_into(target, other, start, count):
        @pl.loop(0, count // step)
        def _(turn):
            at = pl.ds(pl.multiple_of(start + turn * step, step), step)
            come = pl.ds(pl.multiple_of(turn * step, step), step)
            target[at, :] = target[at, :] + other[come, :]

    def join(index):
        to_chip[index].wait_recv()
        add_into(mine.at[index], theirs.at[index], 0, rows)

    corner_x = copy(4, mine.at[0, first], relayed.at[0], on_x)
    corner_y = copy(5, mine.at[0, second], relayed.at[1], on_y)
    x_first = copy(6, mine.at[1, first], final.at[0, first], on_x)
    y_second = copy(7, mine.at[2, second], final.at[1, second], on_y)
    x_second = copy(8, mine.at[1, second], final.at[0, second], on_x)
    y_first = copy(9, mine.at[2, first], final.at[1, first], on_y)

    for each in row_loads:
        each.start()
    for turn in range(8):
        pair, own = turn // 2, turn % 2
        if turn < 7:
            fetch(turn + 1).start()
        fetch(turn).wait()
        if turn == 0:
            load_weight.wait()
        target = mine.at[pair] if own else sent.at[pair]

        @pl.loop(0, weight.shape[0] // CHUNK)
        def _(piece):
            at = chunk_of(piece, CHUNK)
            target[:, at] = transposed_product(narrow[turn % 2], weight[at, :]).astype(
                jnp.bfloat16
            )

        if not own:
            to_chip[pair].start()
        if turn == 2:
            join(0)
            corner_x.start()
            corner_y.start()
        if turn == 4:
            join(1)
            x_first.start()
        if turn == 6:
            join(2)
            y_second.start()
    corner_y.wait_recv()
    add_into(mine.at[1], relayed.at[1], half, half)
    x_second.start()
    corner_x.wait_recv()
    add_into(mine.at[2], relayed.at[0], 0, half)
    y_first.start()
    join(3)

    if with_grad:
        def fetch_wide(turn):
            return pltpu.make_async_copy(
                wide_ref.at[order[turn]], wide.at[turn % 2], wide_sem.at[turn % 2]
            )

        fetch_wide(0).start()
        fetch(0).start()
        for turn in range(8):
            if turn < 7:
                fetch_wide(turn + 1).start()
                fetch(turn + 1).start()
            fetch_wide(turn).wait()
            fetch(turn).wait()
            across[...] = jnp.transpose(wide[turn % 2])

            @pl.loop(0, sums.shape[1] // CHUNK)
            def _(piece):
                at = chunk_of(piece, CHUNK)
                value = plain_product(across[...], narrow[turn % 2, :, at])
                if turn == 0:
                    sums[:, at] = value
                elif turn < 7:
                    sums[:, at] += value
                else:
                    weight[:, at] = (sums[:, at] + value).astype(jnp.bfloat16)

        store = pltpu.make_async_copy(weight, grad_ref, weight_sem)
        store.start()

    for each in row_loads:
        each.wait()
    if not with_grad:
        for start, part, come in ((0, x_first, 0), (half, y_second, 1)):
            part.wait_recv()

            @pl.loop(0, half // step)
            def _(turn):
                at = pl.ds(pl.multiple_of(start + turn * step, step), step)
                base = hidden_rows[at, :] + offset_ref[...] + mine[3, at, :].astype(jnp.float32)
                hidden_rows[at, :] = base + final[come, at, :].astype(jnp.float32)

        y_first.wait_recv()
        x_second.wait_recv()
    else:
        for each in (x_first, y_second, x_second, y_first):
            each.wait_recv()

    def total_of(at):
        total = mine[3, at, :].astype(jnp.float32) + final[0, at, :].astype(jnp.float32)
        return total + final[1, at, :].astype(jnp.float32)

    if with_grad:
        sums_ref[...] = jnp.zeros_like(sums_ref)

        @pl.loop(0, rows // step)
        def _(turn):
            at = chunk_of(turn, step)
            grad_out = total_of(at)
            scaled, inverse = norm_stats(hidden_rows[at, :])
            weighted = grad_out * gain_ref[...]
            grad_in = inverse * (
                weighted
                - jnp.mean(weighted, axis=-1, keepdims=True)
                - scaled * jnp.mean(weighted * scaled, axis=-1, keepdims=True)
            )
            grad_hidden = other_rows[at, :] + grad_in
            branch = grad_hidden.astype(jnp.bfloat16)
            grad_hidden_ref[at, :] = grad_hidden
            branch_ref[at, :] = branch
            sums_ref[0:1, :] += jnp.sum(branch.astype(jnp.float32), axis=0, keepdims=True)
            sums_ref[1:2, :] += jnp.sum(grad_out * scaled, axis=0, keepdims=True)
            sums_ref[2:3, :] += jnp.sum(grad_out, axis=0, keepdims=True)

    else:
        squares_ref[...] = jnp.zeros_like(squares_ref)
        columns_ref[...] = jnp.zeros_like(columns_ref)
        own_prompt = prompt_ref.shape[0]
        for start, stop, come, out_ref, before in (
            (0, half, 1, prompt_ref, 0),
            (half, own_prompt, 0, prompt_ref, 0),
            (own_prompt, rows, 0, answer_ref, own_prompt),
        ):

            @pl.loop(0, (stop - start) // step)
            def _(turn):
                at = pl.ds(pl.multiple_of(start + turn * step, step), step)
                out = pl.ds(pl.multiple_of(start - before + turn * step, step), step)
                result = hidden_rows[at, :] + final[come, at, :].astype(jnp.float32)
                differ = result - other_rows[at, :].astype(jnp.float32)
                grad_result = factor_ref[at, :] * differ
                branch = grad_result.astype(jnp.bfloat16)
                out_ref[out, :] = result.astype(jnp.bfloat16)
                grad_result_ref[at, :] = grad_result
                branch_ref[at, :] = branch
                squared = valid_ref[at, :] * differ * differ
                column = branch.astype(jnp.float32)
                squares_ref[...] += squared[:8, :] + squared[8:, :]
                columns_ref[...] += column[:8, :] + column[8:, :]

    if with_grad:
        store.wait()
    for each in to_chip + [corner_x, corner_y, x_first, y_second, x_second, y_first]:
        each.wait_send()


def product_and_reduce(narrow, weight, wide, rows, second, call_number, own_prompt, *small):
    _, token_rows, width = narrow.shape
    model_width = weight.shape[0]
    with_grad = wide is not None
    anywhere = pl.BlockSpec(memory_space=pl.ANY)
    inside = pl.BlockSpec(memory_space=pltpu.VMEM)
    dma = pltpu.SemaphoreType.DMA
    block = (token_rows, model_width)
    kind, long = jnp.bfloat16, jnp.float32
    line = jax.ShapeDtypeStruct((8, model_width), long)
    narrow_rows, long_rows = jax.ShapeDtypeStruct(block, kind), jax.ShapeDtypeStruct(block, long)
    scratch = [
        pltpu.VMEM(weight.shape, kind),
        pltpu.VMEM((2, token_rows, width), kind),
        pltpu.VMEM((4,) + block, kind),
        pltpu.VMEM((4,) + block, kind),
        pltpu.VMEM((4,) + block, kind),
        pltpu.VMEM((2, token_rows // 2, model_width), kind),
        pltpu.VMEM((2,) + block, kind),
        pltpu.VMEM(block, long),
        pltpu.VMEM(block, second.dtype),
        dma((10,)),
        dma((10,)),
        dma,
        dma((2,)),
        dma((2,)),
    ]
    operands = [narrow, weight]
    if with_grad:
        out_shape = (
            long_rows,
            jax.ShapeDtypeStruct(weight.shape, kind),
            narrow_rows,
            jax.ShapeDtypeStruct((8, model_width), long),
        )
        out_specs = (inside, anywhere, inside, inside)
        scratch += [
            pltpu.VMEM((2,) + block, kind),
            pltpu.VMEM((model_width, token_rows), kind),
            pltpu.VMEM(weight.shape, long),
            dma((2,)),
        ]
        operands.append(wide)
    else:
        out_shape = (
            jax.ShapeDtypeStruct((own_prompt, model_width), kind),
            jax.ShapeDtypeStruct((token_rows - own_prompt, model_width), kind),
            narrow_rows,
            long_rows,
            line,
            line,
        )
        out_specs = (inside,) * 6
    operands += [rows, second]
    return pl.pallas_call(
        functools.partial(product_reduce_kernel, with_grad),
        out_shape=out_shape,
        in_specs=[anywhere] * len(operands) + [inside] * len(small),
        out_specs=out_specs,
        scratch_shapes=scratch,
        compiler_params=pltpu.CompilerParams(
            collective_id=call_number,
            has_side_effects=True,
            vmem_limit_bytes=62 * 1024 * 1024,
        ),
        cost_estimate=pl.CostEstimate(
            flops=(32 if with_grad else 16) * token_rows * model_width * width,
            bytes_accessed=150 * 1000 * 1000,
            transcendentals=0,
        ),
        name="product_and_reduce",
    )(*operands, *small)


def peers_of(count):
    here = lax.axis_index("tok")
    return here, [(here + step) % count for step in range(1, count)]


def small_gather_kernel(own_ref, out_ref, send_sem, recv_sem):
    here, on_x, on_y, on_chip, corner = block_of_eight()
    rows = own_ref.shape[1]

    def place(device):
        return pl.ds(pl.multiple_of(device * rows, rows), rows)

    greet((on_x, on_y, on_chip, corner))
    out_ref[:, place(here), :] = own_ref[...]
    paired_gather(own_ref, lambda device: out_ref.at[:, place(device), :], send_sem, recv_sem)


def tok_gather_small(own, call_number, kernels):
    if not kernels:
        return lax.all_gather(own, "tok", axis=1, tiled=True)
    prompts, rows, columns = own.shape
    return pl.pallas_call(
        small_gather_kernel,
        out_shape=jax.ShapeDtypeStruct((prompts, 8 * rows, columns), own.dtype),
        in_specs=[pl.BlockSpec(memory_space=pltpu.VMEM)],
        out_specs=pl.BlockSpec(memory_space=pltpu.VMEM),
        scratch_shapes=[pltpu.SemaphoreType.DMA((7,)), pltpu.SemaphoreType.DMA((7,))],
        compiler_params=pltpu.CompilerParams(collective_id=call_number, has_side_effects=True),
        name="tok_gather_small",
    )(own)


def stack_heads(values, heads):
    return jnp.concatenate(
        [values[:, head * HEAD_WIDTH : (head + 1) * HEAD_WIDTH] for head in range(heads)], axis=0
    )


def unstack_heads(values, heads):
    rows = values.shape[0] // heads
    return jnp.concatenate(
        [values[head * rows : (head + 1) * rows, :] for head in range(heads)], axis=1
    )


def part_rows(part, prompts, answers, token_ref, answer_ref):
    answer_rows = answer_ref.shape[0] // answers
    prompt_rows = (token_ref.shape[0] - answer_ref.shape[0]) // prompts
    if part < prompts:
        return slice(part * prompt_rows, (part + 1) * prompt_rows), prompt_rows
    start = prompts * prompt_rows + (part - prompts) * answer_rows
    return slice(start, start + answer_rows), answer_rows


def as_row(column):
    wide = jnp.broadcast_to(column, (column.shape[0], HEAD_WIDTH))
    return jnp.transpose(wide)[0:1, :]


def forward_block(
    prompts,
    answers,
    heads,
    start,
    owner_ref,
    normed_ref,
    query_block,
    bias,
    prompt_kv_ref,
    answer_kv_ref,
):
    width = HEAD_WIDTH
    scale = HEAD_WIDTH ** (-0.5)
    length = prompt_kv_ref.shape[1]
    queries = (plain_product(normed_ref[...], query_block) + bias).astype(jnp.bfloat16)
    pieces, logs = [], []
    for part in range(prompts + answers):
        here, rows = part_rows(part, prompts, answers, normed_ref, answer_kv_ref)
        token = lax.broadcasted_iota(jnp.int32, (heads * rows, 1), 0) % rows
        stacked = stack_heads(queries[here, :], heads)
        if part < prompts:
            keys = prompt_kv_ref[part, :, :width]
            values = prompt_kv_ref[part, :, width:]
            scores = transposed_product(stacked, keys)
            place = lax.broadcasted_iota(jnp.int32, (1, length), 1)
            scores = jnp.where(place <= start + token, scores, masked)
            top = jnp.max(scores, axis=-1, keepdims=True)
            exponent = jnp.exp((scores - top) * scale)
            total = jnp.sum(exponent, axis=-1, keepdims=True)
            mixed = plain_product(exponent.astype(jnp.bfloat16), values)
        else:
            answer = part - prompts
            owner = owner_ref[answer]
            own = slice(answer * rows, (answer + 1) * rows)
            keys = prompt_kv_ref[owner, :, :width]
            values = prompt_kv_ref[owner, :, width:]
            scores = transposed_product(stacked, keys)
            own_scores = transposed_product(stacked, answer_kv_ref[own, :width])
            place = lax.broadcasted_iota(jnp.int32, (1, rows), 1)
            own_scores = jnp.where(place <= token, own_scores, masked)
            top = jnp.maximum(
                jnp.max(scores, axis=-1, keepdims=True),
                jnp.max(own_scores, axis=-1, keepdims=True),
            )
            exponent = jnp.exp((scores - top) * scale)
            own_exponent = jnp.exp((own_scores - top) * scale)
            total = jnp.sum(exponent, axis=-1, keepdims=True) + jnp.sum(
                own_exponent, axis=-1, keepdims=True
            )
            mixed = plain_product(exponent.astype(jnp.bfloat16), values) + plain_product(
                own_exponent.astype(jnp.bfloat16), answer_kv_ref[own, width:]
            )
        pieces.append(unstack_heads((mixed / total).astype(jnp.bfloat16), heads))
        logs.append((here, rows, as_row(top * scale + jnp.log(total))))
    return queries, jnp.concatenate(pieces, axis=0), logs


def attention_forward_kernel(
    prompts,
    answers,
    heads,
    place_ref,
    owner_ref,
    normed_ref,
    query_ref,
    bias_ref,
    prompt_kv_ref,
    answer_kv_ref,
    output_ref,
    states_ref,
    offset_ref,
    gain_ref,
    shift_ref,
    queries_ref,
    mixture_ref,
    log_ref,
    hidden_ref,
    second_ref,
):
    step = pl.program_id(0)
    queries, mixture, logs = forward_block(
        prompts,
        answers,
        heads,
        place_ref[0],
        owner_ref,
        normed_ref,
        query_ref[0],
        bias_ref[0],
        prompt_kv_ref,
        answer_kv_ref,
    )
    queries_ref[0] = queries
    mixture_ref[0] = mixture
    for here, rows, log_row in logs:
        for head in range(heads):
            log_ref[0, head : head + 1, here] = log_row[:, head * rows : (head + 1) * rows]

    @pl.when(step == 0)
    def _():
        hidden_ref[...] = states_ref[...].astype(jnp.float32) + offset_ref[...]

    hidden_ref[...] += transposed_product(mixture, output_ref[0])

    @pl.when(step == pl.num_programs(0) - 1)
    def _():
        scaled, _ = norm_stats(hidden_ref[...])
        second_ref[...] = (scaled * gain_ref[...] + shift_ref[...]).astype(jnp.bfloat16)


def attention_forward(
    place,
    owning,
    normed,
    query_blocks,
    output_blocks,
    query_offset,
    prompt_kv,
    answer_kv,
    states,
    output_offset,
    gain,
    shift,
    prompts,
    answers,
):
    token_rows, model_width = normed.shape
    steps, _, block = query_blocks.shape
    heads = block // HEAD_WIDTH
    whole = lambda *shape: pl.BlockSpec(shape, lambda step, *_: (0,) * len(shape))
    one = lambda *shape: pl.BlockSpec((1,) + shape, lambda step, *_: (step, 0, 0))
    by_step = jax.ShapeDtypeStruct((steps, token_rows, block), jnp.bfloat16)
    return pl.pallas_call(
        functools.partial(attention_forward_kernel, prompts, answers, heads),
        out_shape=(
            by_step,
            by_step,
            jax.ShapeDtypeStruct((steps, heads, token_rows), jnp.float32),
            jax.ShapeDtypeStruct((token_rows, model_width), jnp.float32),
            jax.ShapeDtypeStruct((token_rows, model_width), jnp.bfloat16),
        ),
        grid_spec=pltpu.PrefetchScalarGridSpec(
            num_scalar_prefetch=2,
            grid=(steps,),
            in_specs=[
                whole(token_rows, model_width),
                one(model_width, block),
                one(1, block),
                whole(*prompt_kv.shape),
                whole(*answer_kv.shape),
                one(model_width, block),
                whole(token_rows, model_width),
                whole(1, model_width),
                whole(1, model_width),
                whole(1, model_width),
            ],
            out_specs=(
                one(token_rows, block),
                one(token_rows, block),
                one(heads, token_rows),
                whole(token_rows, model_width),
                whole(token_rows, model_width),
            ),
        ),
        compiler_params=pltpu.CompilerParams(vmem_limit_bytes=VMEM_BYTES),
        name="attention_forward",
    )(
        place,
        owning,
        normed,
        query_blocks,
        query_offset.reshape(steps, 1, block),
        prompt_kv,
        answer_kv,
        output_blocks,
        states,
        output_offset.reshape(1, -1),
        gain.reshape(1, -1),
        shift.reshape(1, -1),
    )


def bits_away(index):
    here = lax.axis_index("tok")
    core = (here + index) % 2
    across = (here // 2 + index // 2) % 2
    along = (here // 4 + index // 4) % 2
    return along * 4 + across * 2 + core


def gather_attention_kernel(
    prompts,
    answers,
    heads,
    prompt_rows,
    owner_ref,
    own_ref,
    normed_ref,
    bias_ref,
    prompt_kv_ref,
    answer_kv_ref,
    states_ref,
    offset_ref,
    gain_ref,
    shift_ref,
    weights_ref,
    queries_ref,
    mixture_ref,
    log_ref,
    hidden_ref,
    second_ref,
    held,
    send_sem,
    recv_sem,
    local_sem,
    load_sem,
):
    here, on_x, on_y, on_chip, corner = block_of_eight()

    def copy(index, source, target, device):
        return remote(index, source, target, device, send_sem, recv_sem)

    def kind_of(device, kind):
        return weights_ref.at[device, :, kind]

    to_x = [copy(0 + kind, own_ref.at[:, kind], kind_of(here, kind), on_x) for kind in (0, 1)]
    to_y = [copy(2 + kind, own_ref.at[:, kind], kind_of(here, kind), on_y) for kind in (0, 1)]
    to_chip = [copy(4, own_ref, weights_ref.at[here], on_chip)]
    keep = [pltpu.make_async_copy(own_ref, weights_ref.at[here], local_sem)]
    x_to_y = copy(5, kind_of(on_x, 0), kind_of(on_x, 0), on_y)
    y_to_x = copy(6, kind_of(on_y, 1), kind_of(on_y, 1), on_x)
    x_to_chip = copy(7, weights_ref.at[on_x], weights_ref.at[on_x], on_chip)
    y_to_chip = copy(8, weights_ref.at[on_y], weights_ref.at[on_y], on_chip)
    corner_to_chip = [
        copy(9 + kind, kind_of(corner, kind), kind_of(corner, kind), on_chip) for kind in (0, 1)
    ]

    greet((on_x, on_y, on_chip))
    for each in (to_x[0], to_y[1], to_x[1], to_y[0], *to_chip, *keep):
        each.start()
    hidden_ref[...] = states_ref[...].astype(jnp.float32) + offset_ref[...]

    @pl.loop(0, 8)
    def _(turn):
        block = bits_away(turn)

        @pl.when(turn == 0)
        def _():
            load = pltpu.make_async_copy(own_ref, held, load_sem)
            load.start()
            load.wait()

        @pl.when(turn == 1)
        def _():
            for each in to_chip:
                each.wait_recv()

        @pl.when(turn == 2)
        def _():
            to_x[0].wait_recv()
            x_to_y.start()
            to_y[1].wait_recv()
            y_to_x.start()
            to_x[1].wait_recv()
            x_to_chip.start()
            to_y[0].wait_recv()
            y_to_chip.start()

        @pl.when(turn == 3)
        def _():
            x_to_chip.wait_recv()

        @pl.when(turn == 5)
        def _():
            y_to_chip.wait_recv()

        @pl.when(turn == 6)
        def _():
            x_to_y.wait_recv()
            corner_to_chip[0].start()
            y_to_x.wait_recv()
            corner_to_chip[1].start()

        @pl.when(turn == 7)
        def _():
            for each in corner_to_chip:
                each.wait_recv()

        @pl.when(turn > 0)
        def _():
            load = pltpu.make_async_copy(weights_ref.at[block], held, load_sem)
            load.start()
            load.wait()

        queries, mixture, logs = forward_block(
            prompts,
            answers,
            heads,
            here * prompt_rows,
            owner_ref,
            normed_ref,
            held[:, 0].reshape(-1, held.shape[-1]),
            bias_ref[block],
            prompt_kv_ref,
            answer_kv_ref,
        )
        queries_ref[block] = queries
        mixture_ref[block] = mixture
        for place, rows, log_row in logs:
            for head in range(heads):
                log_ref[block, head : head + 1, place] = log_row[
                    :, head * rows : (head + 1) * rows
                ]
        hidden_ref[...] += transposed_product(mixture, held[:, 1].reshape(-1, held.shape[-1]))

    scaled, _ = norm_stats(hidden_ref[...])
    second_ref[...] = (scaled * gain_ref[...] + shift_ref[...]).astype(jnp.bfloat16)
    for each in (*to_x, *to_y, *to_chip, x_to_y, y_to_x, x_to_chip, y_to_chip, *corner_to_chip):
        each.wait_send()
    for each in keep:
        each.wait()


def gather_attention(
    owning,
    projections,
    normed,
    query_offset,
    prompt_kv,
    answer_kv,
    states,
    output_offset,
    gain,
    shift,
    prompts,
    answers,
    prompt_rows,
    call_number,
):
    token_rows, model_width = normed.shape
    block = projections.shape[3]
    heads = block // HEAD_WIDTH
    inside = pl.BlockSpec(memory_space=pltpu.VMEM)
    anywhere = pl.BlockSpec(memory_space=pl.ANY)
    dma = pltpu.SemaphoreType.DMA
    by_step = jax.ShapeDtypeStruct((8, token_rows, block), jnp.bfloat16)
    return pl.pallas_call(
        functools.partial(gather_attention_kernel, prompts, answers, heads, prompt_rows),
        out_shape=(
            jax.ShapeDtypeStruct((8,) + projections.shape, jnp.bfloat16),
            by_step,
            by_step,
            jax.ShapeDtypeStruct((8, heads, token_rows), jnp.float32),
            jax.ShapeDtypeStruct((token_rows, model_width), jnp.float32),
            jax.ShapeDtypeStruct((token_rows, model_width), jnp.bfloat16),
        ),
        in_specs=[pl.BlockSpec(memory_space=pltpu.SMEM), anywhere] + [inside] * 8,
        out_specs=(anywhere,) + (inside,) * 5,
        scratch_shapes=[
            pltpu.VMEM(projections.shape, jnp.bfloat16),
            dma((11,)),
            dma((11,)),
            dma,
            dma,
        ],
        compiler_params=pltpu.CompilerParams(
            collective_id=call_number, has_side_effects=True, vmem_limit_bytes=VMEM_BYTES
        ),
        cost_estimate=pl.CostEstimate(
            flops=64 * token_rows * model_width * block,
            bytes_accessed=250 * 1000 * 1000,
            transcendentals=0,
        ),
        name="gather_attention",
    )(
        owning,
        projections,
        normed,
        query_offset.reshape(8, 1, block),
        prompt_kv,
        answer_kv,
        states,
        output_offset.reshape(1, -1),
        gain.reshape(1, -1),
        shift.reshape(1, -1),
    )


def backward_block(
    prompts,
    answers,
    heads,
    start,
    owner_ref,
    share_ref,
    normed_ref,
    branch_ref,
    query_block,
    output_block,
    queries,
    mixture,
    log_ref,
    prompt_kv_ref,
    answer_kv_ref,
    normed_across,
    key_sums,
    own_sums,
    grad_normed_ref,
):
    width = HEAD_WIDTH
    scale = HEAD_WIDTH ** (-0.5)
    length = prompt_kv_ref.shape[1]
    grad_mixture = plain_product(branch_ref[...], output_block).astype(jnp.bfloat16)

    def backward(keys, values, stacked, grad_stacked, log_row, inner_row, allowed):
        scores = transposed_product(keys, stacked)
        probs = jnp.exp(scores * scale - log_row)
        if allowed is not None:
            probs = jnp.where(allowed, probs, 0.0)
        grad_values = plain_product(probs.astype(jnp.bfloat16), grad_stacked)
        grad_probs = transposed_product(values, grad_stacked)
        grad_scores = (probs * (grad_probs - inner_row)).astype(jnp.bfloat16)
        grad_keys = plain_product(grad_scores, stacked)
        grad_queries = weight_product(grad_scores, keys)
        return grad_queries, grad_keys, grad_values

    pieces = []
    for part in range(prompts + answers):
        here, rows = part_rows(part, prompts, answers, normed_ref, answer_kv_ref)
        token = lax.broadcasted_iota(jnp.int32, (1, heads * rows), 1) % rows
        stacked = stack_heads(queries[here, :], heads)
        grad_stacked = stack_heads(grad_mixture[here, :], heads)
        mixed = stack_heads(mixture[here, :], heads)
        product = grad_stacked.astype(jnp.float32) * mixed.astype(jnp.float32)
        inner_row = jnp.sum(jnp.transpose(product), axis=0, keepdims=True)
        log_row = jnp.concatenate([log_ref[head : head + 1, here] for head in range(heads)], axis=1)
        if part < prompts:
            place = lax.broadcasted_iota(jnp.int32, (length, 1), 0)
            grad_queries, grad_keys, grad_values = backward(
                prompt_kv_ref[part, :, :width],
                prompt_kv_ref[part, :, width:],
                stacked,
                grad_stacked,
                log_row,
                inner_row,
                place <= start + token,
            )
            key_sums[part, :, :width] += grad_keys
            key_sums[part, :, width:] += grad_values
        else:
            answer = part - prompts
            owner = owner_ref[answer]
            own = slice(answer * rows, (answer + 1) * rows)
            grad_queries, grad_keys, grad_values = backward(
                prompt_kv_ref[owner, :, :width],
                prompt_kv_ref[owner, :, width:],
                stacked,
                grad_stacked,
                log_row,
                inner_row,
                None,
            )
            for prompt in range(prompts):
                share = share_ref[answer * prompts + prompt]
                key_sums[prompt, :, :width] += share * grad_keys
                key_sums[prompt, :, width:] += share * grad_values
            place = lax.broadcasted_iota(jnp.int32, (rows, 1), 0)
            own_queries, own_keys, own_values = backward(
                answer_kv_ref[own, :width],
                answer_kv_ref[own, width:],
                stacked,
                grad_stacked,
                log_row,
                inner_row,
                place <= token,
            )
            grad_queries = grad_queries + own_queries
            own_sums[own, :width] += own_keys
            own_sums[own, width:] += own_values
        pieces.append(unstack_heads((grad_queries * scale).astype(jnp.bfloat16), heads))
    grad_queries = jnp.concatenate(pieces, axis=0)
    grad_query_block = plain_product(normed_across[...], grad_queries).astype(jnp.bfloat16)
    grad_normed_ref[...] += transposed_product(grad_queries, query_block)
    grad_bias = jnp.sum(grad_queries.astype(jnp.float32), axis=0, keepdims=True)
    return grad_query_block, grad_bias


def attention_backward_kernel(
    prompts,
    answers,
    heads,
    place_ref,
    owner_ref,
    share_ref,
    normed_ref,
    query_ref,
    prompt_kv_ref,
    answer_kv_ref,
    output_ref,
    branch_ref,
    queries_ref,
    mixture_ref,
    log_ref,
    grad_weights_ref,
    grad_normed_ref,
    grad_prompt_ref,
    grad_answer_ref,
    grad_bias_ref,
    normed_across,
    branch_across,
    key_sums,
    own_sums,
):
    step = pl.program_id(0)
    width = HEAD_WIDTH
    scale = HEAD_WIDTH ** (-0.5)
    block = queries_ref.shape[2]

    @pl.when(step == 0)
    def _():
        normed_across[...] = jnp.transpose(normed_ref[...])
        branch_across[...] = jnp.transpose(branch_ref[...])
        key_sums[...] = jnp.zeros_like(key_sums)
        own_sums[...] = jnp.zeros_like(own_sums)
        grad_normed_ref[...] = jnp.zeros_like(grad_normed_ref)

    query_block, output_block = query_ref[0, 0], output_ref[0, 0]
    groups = grad_weights_ref.shape[1]
    weight_rows = query_block.shape[0] // groups
    grad_output_block = plain_product(branch_across[...], mixture_ref[0]).astype(jnp.bfloat16)
    grad_query_block, grad_bias = backward_block(
        prompts,
        answers,
        heads,
        place_ref[0],
        owner_ref,
        share_ref,
        normed_ref,
        branch_ref,
        query_block,
        output_block,
        queries_ref[0],
        mixture_ref[0],
        log_ref.at[0],
        prompt_kv_ref,
        answer_kv_ref,
        normed_across,
        key_sums,
        own_sums,
        grad_normed_ref,
    )
    grad_weights_ref[0, :, :weight_rows] = grad_query_block.reshape(groups, weight_rows, block)
    grad_weights_ref[0, :, weight_rows : 2 * weight_rows] = grad_output_block.reshape(
        groups, weight_rows, block
    )
    grad_bias_ref[0] = grad_bias

    @pl.when(step == pl.num_programs(0) - 1)
    def _():
        grad_prompt_ref[:, :, :width] = (key_sums[:, :, :width] * scale).astype(jnp.bfloat16)
        grad_prompt_ref[:, :, width:] = key_sums[:, :, width:].astype(jnp.bfloat16)
        grad_answer_ref[:, :width] = own_sums[:, :width] * scale
        grad_answer_ref[:, width:] = own_sums[:, width:]


def attention_backward(
    place,
    owning,
    share,
    normed,
    weights,
    groups,
    grad_rows,
    prompt_kv,
    answer_kv,
    branch,
    queries,
    mixture,
    log_total,
    prompts,
    answers,
):
    token_rows, model_width = normed.shape
    steps, _, _, block = weights.shape
    heads = block // HEAD_WIDTH
    length = prompt_kv.shape[1]
    whole = lambda *shape: pl.BlockSpec(shape, lambda step, *_: (0,) * len(shape))
    columns = lambda: pl.BlockSpec((1, token_rows, block), lambda step, *_: (step, 0, 0))
    kind = lambda which: pl.BlockSpec(
        (1, 1, model_width, block), lambda step, *_: (step, which, 0, 0)
    )
    scores = heads * token_rows * length
    return pl.pallas_call(
        functools.partial(
            attention_backward_kernel, prompts, answers, heads
        ),
        out_shape=(
            jax.ShapeDtypeStruct((steps, groups, grad_rows, block), jnp.bfloat16),
            jax.ShapeDtypeStruct((token_rows, model_width), jnp.float32),
            jax.ShapeDtypeStruct(prompt_kv.shape, jnp.bfloat16),
            jax.ShapeDtypeStruct(answer_kv.shape, jnp.float32),
            jax.ShapeDtypeStruct((steps, 1, block), jnp.float32),
        ),
        grid_spec=pltpu.PrefetchScalarGridSpec(
            num_scalar_prefetch=3,
            grid=(steps,),
            in_specs=[
                whole(token_rows, model_width),
                kind(0),
                whole(*prompt_kv.shape),
                whole(*answer_kv.shape),
                kind(1),
                whole(token_rows, model_width),
                columns(),
                columns(),
                pl.BlockSpec((1, heads, token_rows), lambda step, *_: (step, 0, 0)),
            ],
            out_specs=(
                pl.BlockSpec(
                    (1, groups, grad_rows, block), lambda step, *_: (step, 0, 0, 0)
                ),
                whole(token_rows, model_width),
                whole(*prompt_kv.shape),
                whole(*answer_kv.shape),
                pl.BlockSpec((1, 1, block), lambda step, *_: (step, 0, 0)),
            ),
            scratch_shapes=[
                pltpu.VMEM((model_width, token_rows), jnp.bfloat16),
                pltpu.VMEM((model_width, token_rows), jnp.bfloat16),
                pltpu.VMEM(prompt_kv.shape, jnp.float32),
                pltpu.VMEM(answer_kv.shape, jnp.float32),
            ],
        ),
        compiler_params=pltpu.CompilerParams(vmem_limit_bytes=VMEM_BYTES),
        cost_estimate=pl.CostEstimate(
            flops=steps * (8 * token_rows * model_width * block + 20 * scores * HEAD_WIDTH),
            bytes_accessed=16 * steps * model_width * block,
            transcendentals=steps * scores,
        ),
        name="attention_backward",
    )(
        place,
        owning,
        share,
        normed,
        weights,
        prompt_kv,
        answer_kv,
        weights,
        branch,
        queries,
        mixture,
        log_total,
    )


class PairedSum:
    def __init__(self, part, pair, sent, come, send_sem, recv_sem):
        here, on_x, on_y, on_chip, corner = block_of_eight()
        shift = on_chip - here
        self.places = (here, on_x, on_y, corner)
        self.part, self.pair, self.sent, self.come = part, pair, sent, come
        self.to_chip = [
            remote(index, part(place + shift), pair.at[index], on_chip, send_sem, recv_sem)
            for index, place in enumerate(self.places)
        ]
        self.over = [
            remote(3 + index, sent.at[index], come.at[index - 1], place, send_sem, recv_sem)
            for index, place in enumerate(self.places)
            if index
        ]

    def start(self):
        for each in self.to_chip:
            each.start()

    def pass_on(self):
        for each in self.to_chip:
            each.wait_recv()
        for index, place in enumerate(self.places):
            total = self.part(place)[...].astype(jnp.float32)
            total = total + self.pair[index].astype(jnp.float32)
            self.sent[index] = total.astype(self.sent.dtype)
        for each in self.over:
            each.start()

    def total(self):
        total = self.sent[0].astype(jnp.float32)
        for index, each in enumerate(self.over):
            each.wait_recv()
            total = total + self.come[index].astype(jnp.float32)
        return total

    def finish(self):
        for each in self.to_chip + self.over:
            each.wait_send()


VECTOR_ROWS = 16


def backward_reduce_kernel(
    prompts,
    answers,
    heads,
    groups,
    prompt_rows,
    owner_ref,
    share_ref,
    weights_ref,
    queries_ref,
    mixture_ref,
    hidden_hbm,
    normed_ref,
    branch_ref,
    log_ref,
    prompt_kv_ref,
    answer_kv_ref,
    states_ref,
    gain_ref,
    keyval_ref,
    known_up_ref,
    known_sums_ref,
    known_columns_ref,
    known_squares_ref,
    grad_query_ref,
    grad_output_ref,
    grad_keyval_ref,
    vectors_ref,
    own_vectors_ref,
    own_up_ref,
    grad_prompt_ref,
    grad_answer_ref,
    normed_across,
    branch_across,
    key_sums,
    own_sums,
    grad_normed,
    grad_hidden,
    held,
    pair,
    early,
    kept,
    theirs,
    relayed,
    final,
    come,
    kv_part,
    kv_pair,
    kv_sent,
    kv_come,
    kv_rows,
    keyval_part,
    keyval_pair,
    keyval_sent,
    keyval_come,
    keyval_sum,
    keyval_over,
    vectors,
    vector_come,
    vector_sum,
    vector_over,
    row_sums,
    send_sem,
    recv_sem,
    over_send,
    over_recv,
    peer_send,
    peer_recv,
    load_sem,
    early_sem,
    hidden_sem,
):
    width = HEAD_WIDTH
    scale = HEAD_WIDTH ** (-0.5)
    here, on_x, on_y, on_chip, corner = block_of_eight()
    _, peers = peers_of(8)
    group = lax.axis_index("grp")
    other_groups = [(group + turn) % groups for turn in range(1, groups)]
    model_width, block = kept.shape[1:]
    chunk_rows = model_width // groups
    step = 64
    counter = iter(range(8 + 6 * groups))

    def copy(source, target, device):
        return remote(next(counter), source, target, device, send_sem, recv_sem)

    def over(index, source, target, other):
        return pltpu.make_async_remote_copy(
            src_ref=source,
            dst_ref=target,
            send_sem=over_send.at[index],
            recv_sem=over_recv.at[index],
            device_id={"grp": other},
            device_id_type=MESH,
        )

    def to_peers(row, source, target):
        return [
            pltpu.make_async_remote_copy(
                src_ref=source(peers[index]),
                dst_ref=target(index),
                send_sem=peer_send.at[row, index],
                recv_sem=peer_recv.at[row, index],
                device_id={"tok": peers[index]},
                device_id_type=MESH,
            )
            for index in range(len(peers))
        ]

    beside, beyond = group + 1 - 2 * (group % 2), (group + 2) % groups
    spans = [
        pl.ds(pl.multiple_of(owner * chunk_rows, chunk_rows), chunk_rows)
        for owner in ((beside + 2) % groups, beside, beyond, group)
    ]
    chunks = range(groups)
    by_x, by_y = chunks[: groups // 2], chunks[groups // 2 :]
    kinds = (0, 1)

    def mine(place, kind):
        return kept.at[4 + 2 * place + kind]

    def pieces_to(place, target, device):
        return [
            [copy(mine(place, kind).at[span], target(kind).at[span], device) for span in spans]
            for kind in kinds
        ]

    to_chip = [
        [copy(kept.at[place], theirs.at[place, kind], on_chip) for place in range(4)]
        for kind in kinds
    ]
    corners = [
        [
            copy(
                mine(0, kind).at[spans[chunk]],
                relayed.at[kind, spans[chunk]],
                on_x if chunk in by_x else on_y,
            )
            for chunk in chunks
        ]
        for kind in kinds
    ]
    to_x = pieces_to(2, lambda kind: final.at[0, kind], on_x)
    to_y = pieces_to(1, lambda kind: final.at[1, kind], on_y)
    across = [
        [
            over(2 * turn + kind, mine(3, kind).at[spans[turn]], come.at[turn, kind], other)
            for kind in kinds
        ]
        for turn, other in enumerate((beside, beside, beyond))
    ]

    def lanes(device):
        return pl.ds(pl.multiple_of(device * block, block), block)

    def prompt_place(device):
        return pl.ds(pl.multiple_of(device * prompt_rows, prompt_rows), prompt_rows)

    kv_sums = PairedSum(
        lambda device: kv_part.at[:, prompt_place(device), :],
        kv_pair,
        kv_sent,
        kv_come,
        peer_send.at[0],
        peer_recv.at[0],
    )
    keyval_sums = PairedSum(
        lambda device: keyval_part.at[:, device],
        keyval_pair,
        keyval_sent,
        keyval_come,
        peer_send.at[1],
        peer_recv.at[1],
    )
    vector_copies = to_peers(
        2, lambda peer: vectors.at[:, lanes(peer)], lambda index: vector_come.at[index]
    )
    vector_out = to_peers(
        3, lambda peer: vector_sum, lambda index: vectors_ref.at[:, lanes(here)]
    )
    first_over = 2 * (groups - 1)
    keyval_across = [
        over(first_over + turn, keyval_sum.at[other_groups[turn]], keyval_over.at[turn], other_groups[turn])
        for turn in range(groups - 1)
    ]
    vector_across = [
        over(
            first_over + groups - 1 + turn,
            vectors.at[:, lanes(here)],
            vector_over.at[turn],
            other_groups[turn],
        )
        for turn in range(groups - 1)
    ]

    def fetch(turn):
        source, slot = bits_away(7 - turn), turn % 2
        return (
            pltpu.make_async_copy(weights_ref.at[source], held.at[slot], load_sem.at[slot, 0]),
            pltpu.make_async_copy(queries_ref.at[source], pair.at[slot, 0], load_sem.at[slot, 1]),
            pltpu.make_async_copy(mixture_ref.at[source], pair.at[slot, 1], load_sem.at[slot, 2]),
        )

    def fetch_early(turn):
        return pltpu.make_async_copy(
            mixture_ref.at[bits_away(7 - turn)], early.at[turn % 2], early_sem.at[turn % 2]
        )

    fetch_early(0).start()
    load_hidden = pltpu.make_async_copy(hidden_hbm, grad_hidden, hidden_sem)
    load_hidden.start()
    for each in fetch(0):
        each.start()
    greet_all(peers, other_groups)
    normed_across[...] = jnp.transpose(normed_ref[...])
    branch_across[...] = jnp.transpose(branch_ref[...])
    key_sums[...] = jnp.zeros_like(key_sums)
    own_sums[...] = jnp.zeros_like(own_sums)
    grad_normed[...] = jnp.zeros_like(grad_normed)
    vectors[...] = jnp.zeros_like(vectors)
    row_sums[...] = jnp.zeros_like(row_sums)
    vectors[: known_up_ref.shape[0], :] = known_up_ref[...]
    vectors[4:7, :] = known_sums_ref[0:3, :]
    vectors[7:8, :] = jnp.sum(known_columns_ref[...], axis=0, keepdims=True)
    squares = jnp.sum(known_squares_ref[...], axis=0, keepdims=True)
    squares = jnp.sum(squares, axis=1, keepdims=True)
    vectors[12:13, :] = jnp.broadcast_to(squares, (1, model_width))

    def add_into(target, other, rows):
        @pl.loop(0, rows // step)
        def _(turn):
            at = chunk_of(turn, step)
            target[at, :] = target[at, :] + other[at, :]

    def join(kind, place):
        to_chip[kind][place].wait_recv()
        add_into(mine(place, kind), theirs.at[place, kind], model_width)

    def direct(kind, chunk):
        (to_x if chunk in by_x else to_y)[kind][chunk].start()

    def relay(kind, chunk):
        corners[kind][chunk].wait_recv()
        place, then = (1, to_y) if chunk in by_x else (2, to_x)
        span = spans[chunk]
        add_into(mine(place, kind).at[span], relayed.at[kind, span], chunk_rows)
        then[kind][chunk].start()

    def close(kind, chunk):
        span = spans[chunk]
        for source, part in enumerate((to_x, to_y)):
            part[kind][chunk].wait_recv()
            add_into(mine(3, kind).at[span], final.at[source, kind, span], chunk_rows)
        if chunk < 2:
            across[chunk][kind].start()

    def hand_on(kind):
        across[0][kind].wait_recv()
        add_into(mine(3, kind).at[spans[2]], come.at[0, kind], chunk_rows)
        across[2][kind].start()

    def slot_of(turn, kind):
        place = turn // 2
        return (1 - turn % 2) * place + (turn % 2) * (4 + 2 * place + kind)

    def send_to_chip(turn, kind):
        for place in range(4):

            @pl.when(turn == 2 * place)
            def _():
                to_chip[kind][place].start()

    @pl.loop(0, 8)
    def _(turn):
        @pl.when(turn < 7)
        def _():
            fetch_early(turn + 1).start()

        fetch_early(turn).wait()
        kept[slot_of(turn, 1)] = plain_product(
            branch_across[...], early[turn % 2]
        ).astype(jnp.bfloat16)
        send_to_chip(turn, 1)

        @pl.when(turn == 2)
        def _():
            join(1, 0)
            for chunk in chunks:
                corners[1][chunk].start()

        for place in (1, 2):

            @pl.when(turn == 2 * place + 2)
            def _():
                join(1, place)

    for chunk in chunks:
        direct(1, chunk)

    @pl.loop(0, 8)
    def _(turn):
        source, now = bits_away(7 - turn), turn % 2

        @pl.when(turn < 7)
        def _():
            for each in fetch(turn + 1):
                each.start()

        for place in range(4):

            @pl.when(turn == 2 * place)
            def _():
                to_chip[1][place].wait_send()

        for each in fetch(turn):
            each.wait()
        grad_query_block, grad_bias = backward_block(
            prompts,
            answers,
            heads,
            here * prompt_rows,
            owner_ref,
            share_ref,
            normed_ref,
            branch_ref,
            held[now, :, 0].reshape(-1, block),
            held[now, :, 1].reshape(-1, block),
            pair[now, 0],
            pair[now, 1],
            log_ref.at[source],
            prompt_kv_ref,
            answer_kv_ref,
            normed_across,
            key_sums,
            own_sums,
            grad_normed,
        )
        kept[slot_of(turn, 0)] = grad_query_block
        vectors[10:11, lanes(source)] = grad_bias
        send_to_chip(turn, 0)

        @pl.when(turn == 1)
        def _():
            for chunk in chunks:
                relay(1, chunk)

        @pl.when(turn == 2)
        def _():
            join(0, 0)
            for chunk in chunks:
                corners[0][chunk].start()

        @pl.when(turn == 4)
        def _():
            join(0, 1)
            join(1, 3)

        @pl.when(turn == 5)
        def _():
            for chunk in chunks:
                close(1, chunk)

        @pl.when(turn == 6)
        def _():
            join(0, 2)
            for chunk in (by_x[0], by_y[0]):
                direct(0, chunk)
            for chunk in (by_x[0], by_y[0]):
                relay(0, chunk)

        @pl.when(turn == 7)
        def _():
            direct(0, by_x[1])
            relay(0, by_x[1])

    kv_part[:, :, :width] = (key_sums[:, :, :width] * scale).astype(jnp.bfloat16)
    kv_part[:, :, width:] = key_sums[:, :, width:].astype(jnp.bfloat16)
    kv_sums.start()
    join(0, 3)
    kv_sums.pass_on()
    for part in (to_x, to_y):
        part[0][by_x[0]].wait_send()
    direct(0, by_y[1])
    relay(0, by_y[1])

    own_prompt = prompts * prompt_rows
    total = kv_sums.total()
    for prompt in range(prompts):
        kv_rows[prompt * prompt_rows : (prompt + 1) * prompt_rows, :] = total[prompt].astype(
            jnp.bfloat16
        )
    kv_rows[own_prompt:, :width] = (own_sums[:, :width] * scale).astype(jnp.bfloat16)
    kv_rows[own_prompt:, width:] = own_sums[:, width:].astype(jnp.bfloat16)
    keyval_part[...] = (
        plain_product(normed_across[...], kv_rows[...])
        .astype(jnp.bfloat16)
        .reshape(keyval_part.shape)
    )
    keyval_sums.start()
    close(0, by_x[0])
    load_hidden.wait()
    vectors[11:12, :width] = jnp.sum(
        kv_rows[:, width:].astype(jnp.float32), axis=0, keepdims=True
    )
    piece = 16
    grad_normed[...] += transposed_product(kv_rows[...], keyval_ref[...])

    start = 0
    for out_ref in (grad_prompt_ref, grad_answer_ref):

        @pl.loop(0, out_ref.shape[0] // piece)
        def _(turn):
            at = pl.ds(pl.multiple_of(start + turn * piece, piece), piece)
            scaled, inverse = norm_stats(states_ref[at, :].astype(jnp.float32))
            grad_out = grad_normed[at, :]
            weighted = grad_out * gain_ref[...]
            grad_in = inverse * (
                weighted
                - jnp.mean(weighted, axis=-1, keepdims=True)
                - scaled * jnp.mean(weighted * scaled, axis=-1, keepdims=True)
            )
            out_ref[chunk_of(turn, piece), :] = (grad_hidden[at, :] + grad_in).astype(jnp.bfloat16)
            by_gain = grad_out * scaled
            row_sums[:8, :] += by_gain[:8, :] + by_gain[8:, :]
            row_sums[8:, :] += grad_out[:8, :] + grad_out[8:, :]

        start += out_ref.shape[0]

    vectors[8:9, :] = jnp.sum(row_sums[:8, :], axis=0, keepdims=True)
    vectors[9:10, :] = jnp.sum(row_sums[8:, :], axis=0, keepdims=True)
    for each in vector_copies:
        each.start()
    close(0, by_y[0])
    hand_on(1)
    keyval_sums.pass_on()
    close(0, by_x[1])
    for each in vector_copies:
        each.wait_recv()
    total = vectors[:, lanes(here)]
    for index in range(len(peers)):
        total = total + vector_come[index]
    vectors[:, lanes(here)] = total
    for each in vector_across:
        each.start()
    keyval_sum[...] = keyval_sums.total().astype(jnp.bfloat16)
    for each in keyval_across:
        each.start()
    hand_on(0)
    for each in vector_across:
        each.wait_recv()
    total = vectors[:, lanes(here)]
    for turn in range(groups - 1):
        total = total + vector_over[turn]
    vector_sum[...] = total
    for each in vector_out:
        each.start()
    vectors_ref[:, lanes(here)] = vector_sum[...]
    close(0, by_y[1])
    for each in keyval_across:
        each.wait_recv()
    total = keyval_sum[group].astype(jnp.float32)
    for turn in range(groups - 1):
        total = total + keyval_over[turn].astype(jnp.float32)
    grad_keyval_ref[...] = total
    for kind, out_ref in ((0, grad_query_ref), (1, grad_output_ref)):
        for turn in (1, 2):
            across[turn][kind].wait_recv()
        own = pl.multiple_of(group * chunk_rows, chunk_rows)

        @pl.loop(0, chunk_rows // step)
        def _(turn):
            at = chunk_of(turn, step)
            total = kept[10 + kind, pl.ds(own + turn * step, step), :].astype(jnp.float32)
            for other in (1, 2):
                total = total + come[other, kind, at, :].astype(jnp.float32)
            out_ref[at, :] = total

    for each in vector_out:
        each.wait_recv()
    device = group * 8 + here
    share = model_width // (8 * groups)
    parts = width // share
    columns = vectors_ref[:, chunk_of(device // parts, width)]
    picked = columns
    for part in range(1, parts):
        moved = jnp.concatenate([columns[:, part * share :], columns[:, : part * share]], axis=1)
        picked = jnp.where(device % parts == part, moved, picked)
    own_vectors_ref[...] = picked
    up_share = own_up_ref.shape[1]
    in_row = model_width // up_share
    up_columns = vectors_ref[:, chunk_of(device % in_row, up_share)]
    up_own = jnp.zeros((1, up_share), jnp.float32)
    for row in range(known_up_ref.shape[0]):
        up_own = jnp.where(device // in_row == row, up_columns[row : row + 1, :], up_own)
    own_up_ref[...] = up_own
    for each in to_chip[0] + corners[0] + corners[1] + to_x[1] + to_y[1]:
        each.wait_send()
    for chunk in chunks[1:]:
        to_x[0][chunk].wait_send()
        to_y[0][chunk].wait_send()
    kv_sums.finish()
    keyval_sums.finish()
    for each in vector_copies + vector_out:
        each.wait_send()
    for each in sum(across, []) + keyval_across + vector_across:
        each.wait_send()


def backward_reduce(
    owning,
    share,
    weights,
    queries,
    mixture,
    grad_hidden,
    normed,
    branch,
    log_total,
    prompt_kv,
    answer_kv,
    states,
    gain,
    keyval_full,
    known_up,
    known_sums,
    known_columns,
    known_squares,
    groups,
    prompts,
    answers,
    prompt_rows,
    call_number,
):
    token_rows, model_width = normed.shape
    block = weights.shape[4]
    heads = block // HEAD_WIDTH
    keyval_width = keyval_full.shape[1]
    weight_rows = model_width // groups
    keyval_rows = model_width // groups // 8
    kind, wide = jnp.bfloat16, jnp.float32
    inside = pl.BlockSpec(memory_space=pltpu.VMEM)
    anywhere = pl.BlockSpec(memory_space=pl.ANY)
    scalars = pl.BlockSpec(memory_space=pltpu.SMEM)
    dma = pltpu.SemaphoreType.DMA
    others = groups - 1
    return pl.pallas_call(
        functools.partial(backward_reduce_kernel, prompts, answers, heads, groups, prompt_rows),
        out_shape=(
            jax.ShapeDtypeStruct((weight_rows, block), wide),
            jax.ShapeDtypeStruct((weight_rows, block), wide),
            jax.ShapeDtypeStruct((keyval_rows, keyval_width), wide),
            jax.ShapeDtypeStruct((VECTOR_ROWS, model_width), wide),
            jax.ShapeDtypeStruct((VECTOR_ROWS, HEAD_WIDTH), wide),
            jax.ShapeDtypeStruct((1, known_up.size // (8 * groups)), wide),
            jax.ShapeDtypeStruct((prompts * prompt_rows, model_width), kind),
            jax.ShapeDtypeStruct((token_rows - prompts * prompt_rows, model_width), kind),
        ),
        in_specs=[scalars] * 2 + [anywhere] * 4 + [inside] * 12,
        out_specs=(inside,) * 8,
        scratch_shapes=[
            pltpu.VMEM((model_width, token_rows), kind),
            pltpu.VMEM((model_width, token_rows), kind),
            pltpu.VMEM(prompt_kv.shape, wide),
            pltpu.VMEM(answer_kv.shape, wide),
            pltpu.VMEM((token_rows, model_width), wide),
            pltpu.VMEM((token_rows, model_width), wide),
            pltpu.VMEM((2,) + weights.shape[1:], kind),
            pltpu.VMEM((2, 2, token_rows, block), kind),
            pltpu.VMEM((2, token_rows, block), kind),
            pltpu.VMEM((12, model_width, block), kind),
            pltpu.VMEM((4, 2, model_width, block), kind),
            pltpu.VMEM((2, model_width, block), kind),
            pltpu.VMEM((2, 2, model_width, block), kind),
            pltpu.VMEM((others, 2, weight_rows, block), kind),
            pltpu.VMEM(prompt_kv.shape, kind),
            pltpu.VMEM((4, prompts, prompt_rows, keyval_width), kind),
            pltpu.VMEM((4, prompts, prompt_rows, keyval_width), kind),
            pltpu.VMEM((3, prompts, prompt_rows, keyval_width), kind),
            pltpu.VMEM((token_rows, keyval_width), kind),
            pltpu.VMEM((groups, 8, keyval_rows, keyval_width), kind),
            pltpu.VMEM((4, groups, keyval_rows, keyval_width), kind),
            pltpu.VMEM((4, groups, keyval_rows, keyval_width), kind),
            pltpu.VMEM((3, groups, keyval_rows, keyval_width), kind),
            pltpu.VMEM((groups, keyval_rows, keyval_width), kind),
            pltpu.VMEM((others, keyval_rows, keyval_width), kind),
            pltpu.VMEM((VECTOR_ROWS, model_width), wide),
            pltpu.VMEM((7, VECTOR_ROWS, block), wide),
            pltpu.VMEM((VECTOR_ROWS, block), wide),
            pltpu.VMEM((others, VECTOR_ROWS, block), wide),
            pltpu.VMEM((16, model_width), wide),
            dma((8 + 6 * groups,)),
            dma((8 + 6 * groups,)),
            dma((4 * others,)),
            dma((4 * others,)),
            dma((4, 7)),
            dma((4, 7)),
            dma((2, 3)),
            dma((2,)),
            dma,
        ],
        compiler_params=pltpu.CompilerParams(
            collective_id=call_number,
            has_side_effects=True,
            vmem_limit_bytes=63 * 1024 * 1024,
        ),
        cost_estimate=pl.CostEstimate(
            flops=100 * token_rows * model_width * block,
            bytes_accessed=250 * 1000 * 1000,
            transcendentals=0,
        ),
        name="backward_reduce",
    )(
        owning,
        share,
        weights,
        queries,
        mixture,
        grad_hidden,
        normed,
        branch,
        log_total,
        prompt_kv,
        answer_kv,
        states,
        gain.reshape(1, -1),
        keyval_full,
        known_up,
        known_sums,
        known_columns,
        known_squares,
    )


def finish_kernel(share_size, model_width, *refs):
    half = len(refs) - 17
    (
        vectors_ref,
        own_vectors_ref,
        own_up_ref,
        count_ref,
        prompt_ref,
        answer_ref,
        query_ref,
        output_ref,
        keyval_ref,
        up_ref,
        down_ref,
    ) = refs[:half]
    prompt_out, answer_out, query_out, output_out, keyval_out, up_out, down_out, *outs = refs[half:]
    prompt_out[...] = prompt_ref[...]
    answer_out[...] = answer_ref[...]
    query_out[...] = query_ref[...]
    output_out[...] = output_ref[...]
    keyval_out[...] = keyval_ref[...]
    up_out[...] = up_ref[...].astype(jnp.float32)
    down_out[...] = down_ref[...].astype(jnp.float32)
    *vector_outs, up_bias_out, value_out, loss_out = outs
    for row, out_ref in zip((8, 9, 10, 4, 5, 6, 7), vector_outs):
        out_ref[...] = own_vectors_ref[row : row + 1, :share_size]
    up_bias_out[...] = own_up_ref[...]
    value_out[...] = vectors_ref[11:12, :HEAD_WIDTH]
    loss_out[...] = vectors_ref[12:13, :1] / (count_ref[...] * model_width)


def finish(share_size, vectors, own_vectors, own_up, valid_count, *arrays):
    wide = jnp.float32
    model_width = vectors.shape[1]
    kinds = [array.dtype for array in arrays[:5]] + [wide, wide]
    shapes = [jax.ShapeDtypeStruct(array.shape, kind) for array, kind in zip(arrays, kinds)]
    shapes += [jax.ShapeDtypeStruct((1, share_size), wide)] * 7
    shapes += [
        jax.ShapeDtypeStruct(own_up.shape, wide),
        jax.ShapeDtypeStruct((1, HEAD_WIDTH), wide),
        jax.ShapeDtypeStruct((1, 1), wide),
    ]
    inside = pl.BlockSpec(memory_space=pltpu.VMEM)
    return pl.pallas_call(
        functools.partial(finish_kernel, share_size, model_width),
        out_shape=tuple(shapes),
        in_specs=[inside] * (4 + len(arrays)),
        out_specs=(inside,) * len(shapes),
        compiler_params=pltpu.CompilerParams(vmem_limit_bytes=VMEM_BYTES),
        name="finish",
    )(vectors, own_vectors, own_up, valid_count.reshape(1, 1), *arrays)


def by_group(values):
    return jnp.swapaxes(values, 0, 1).reshape(-1)


def body(
    kernels,
    prompt_states,
    answer_states,
    answer_prompt,
    prompt_teacher,
    answer_teacher,
    prompt_valid,
    answer_valid,
    first_gain,
    first_shift,
    query_weight,
    query_bias,
    keyval_weight,
    value_bias,
    output_weight,
    output_bias,
    second_gain,
    second_shift,
    up_weight,
    up_bias,
    down_weight,
    down_bias,
):
    prompt_count, prompt_rows, model_width = prompt_states.shape
    answer_count, answer_len, _ = answer_states.shape
    groups = lax.axis_size("grp")
    token_devices = lax.axis_size("tok")
    token_index = lax.axis_index("tok")
    group_index = lax.axis_index("grp")
    own_prompt = prompt_rows * prompt_count
    token_rows = own_prompt + answer_count * answer_len
    hidden_units = up_bias.shape[0] * groups * token_devices
    ff_here = hidden_units // token_devices
    ff_start = token_index * ff_here
    share_size = first_gain.shape[0]
    block = query_weight.shape[1]
    weight_rows = query_weight.shape[0]
    keyval_rows, keyval_width = keyval_weight.shape

    def own_rows(prompt_part, answer_part):
        return jnp.concatenate(
            [prompt_part.reshape(own_prompt, -1), answer_part.reshape(-1, prompt_part.shape[-1])],
            axis=0,
        )

    states = own_rows(prompt_states, answer_states)
    inputs = states.astype(jnp.float32)
    valid_rows = jnp.concatenate([prompt_valid.reshape(-1), answer_valid.reshape(-1)])
    own_count = jnp.sum(valid_rows)
    valid_rows = valid_rows.astype(jnp.float32)

    up_cols = lax.all_gather(up_weight, "grp", axis=0, tiled=True)
    down_cols = lax.all_gather(down_weight, "grp", axis=0, tiled=True)

    projections = lax.all_gather(jnp.stack([query_weight, output_weight]), "grp", axis=0)
    count_parts = jnp.stack([own_count // 128, own_count % 128]).astype(jnp.bfloat16)
    smalls, small_at = jnp.zeros((SMALL_ROWS * block,), jnp.bfloat16), 0
    for each in (
        first_gain,
        first_shift,
        query_bias,
        output_bias,
        second_gain,
        second_shift,
        down_bias,
        up_bias,
        count_parts,
    ):
        behind = SMALL_ROWS * block - small_at - each.shape[0]
        smalls = smalls + jnp.pad(each, (small_at, behind))
        small_at += each.shape[0]
    smalls = smalls.reshape(SMALL_ROWS, block)
    pack = jnp.concatenate([keyval_weight.reshape(-1, block), smalls], axis=0)
    packed = spread(pack, groups, 0, kernels)
    keyval_pack = pack.shape[0] - SMALL_ROWS
    keyval_start = 2 * weight_rows
    keyval_full = jnp.swapaxes(
        packed[:, :, :keyval_pack].reshape(token_devices, groups, keyval_rows, keyval_width),
        0,
        1,
    ).reshape(model_width, keyval_width)
    small_full = packed[:, :, keyval_pack:].reshape(token_devices, groups, SMALL_ROWS * block)
    small_full = jnp.swapaxes(small_full.astype(jnp.float32), 0, 1)

    def vector(start, size):
        return small_full[:, :, start : start + size].reshape(-1)

    gain_one, shift_one, query_offset, output_offset, gain_two, shift_two, down_offset = (
        vector(index * share_size, share_size) for index in range(7)
    )
    up_offset = vector(7 * share_size, up_bias.shape[0])
    count_at = 7 * share_size + up_bias.shape[0]
    counts = small_full[:, :, count_at : count_at + 2]
    valid_count = jnp.sum(counts[:, :, 0]) * 128.0 + jnp.sum(counts[:, :, 1])
    up_here = lax.dynamic_slice_in_dim(up_offset, ff_start, ff_here)

    scaled_one, inverse_one = norm_stats(inputs)
    normed_one = (scaled_one * gain_one + shift_one).astype(jnp.bfloat16)
    key_offset = jnp.concatenate(
        [jnp.zeros((HEAD_WIDTH,), jnp.float32), value_bias.astype(jnp.float32)]
    )
    key_value_rows = (plain_product(normed_one, keyval_full) + key_offset).astype(jnp.bfloat16)
    prompt_kv = tok_gather_small(
        key_value_rows[:own_prompt].reshape(prompt_count, prompt_rows, -1), 1, kernels
    )
    answer_kv = key_value_rows[own_prompt:]
    owning = answer_prompt - group_index * prompt_count
    owning = lax.dynamic_slice_in_dim(owning, token_index * answer_count, answer_count)
    place = jnp.reshape(token_index * prompt_rows, (1,)).astype(jnp.int32)
    if kernels:
        weights, queries, mixture, log_total, hidden, normed_two = gather_attention(
            owning,
            projections,
            normed_one,
            query_offset,
            prompt_kv,
            answer_kv,
            states,
            output_offset,
            gain_two,
            shift_two,
            prompt_count,
            answer_count,
            prompt_rows,
            8,
        )
    else:
        weights = lax.all_gather(projections, "tok", axis=0)
        weights = jnp.swapaxes(weights, 1, 2).reshape(token_devices, 2, model_width, block)
        queries, mixture, log_total, hidden, normed_two = attention_forward(
            place,
            owning,
            normed_one,
            weights[:, 0],
            weights[:, 1],
            query_offset,
            prompt_kv,
            answer_kv,
            states,
            output_offset,
            gain_two,
            shift_two,
            prompt_count,
            answer_count,
        )

    teacher = own_rows(prompt_teacher, answer_teacher)
    every_token = token_rows * groups * token_devices
    factors = (every_token / valid_count * valid_rows)[:, None]
    share = (owning[:, None] == jnp.arange(prompt_count)[None, :]).astype(jnp.float32).reshape(-1)
    if kernels:
        down_row, gain_row, share = lax.optimization_barrier(
            (down_offset.reshape(1, -1), gain_one.reshape(1, -1), share)
        )
        group_two, activated, slope = gather_and_up(normed_two, up_cols, up_here, 2)
        prompt_out, answer_out, grad_branch_two, grad_result, own_squares, grad_down_offset = (
            product_and_reduce(
                activated,
                down_cols,
                None,
                hidden,
                teacher,
                3,
                own_prompt,
                down_row,
                valid_rows[:, None],
                factors,
            )
        )
        _, grad_pre_active, grad_down_cols, grad_up_offset = gather_and_grad(
            grad_branch_two, down_cols, activated, slope, 4
        )
        grad_hidden, grad_up_cols, grad_branch_one, second_sums = product_and_reduce(
            grad_pre_active,
            up_cols,
            group_two,
            hidden,
            grad_result,
            5,
            own_prompt,
            gain_two.reshape(1, -1),
        )
        grad_up_offset = grad_up_offset.reshape(-1)
    else:
        group_two = lax.all_gather(normed_two, "tok", axis=0, tiled=True)
        pre_active = plain_product(group_two, up_cols) + up_here
        activated = jax.nn.gelu(pre_active, approximate=True).astype(jnp.bfloat16)
        feed_term = for_sending(transposed_product(activated, down_cols))
        feed_term = lax.psum_scatter(feed_term, "tok", scatter_dimension=0, tiled=True)
        result_rows = hidden + feed_term.astype(jnp.float32) + down_offset
        prompt_out, answer_out = result_rows[:own_prompt], result_rows[own_prompt:]
        differ = result_rows - teacher.astype(jnp.float32)
        own_squares = jnp.sum(valid_rows[:, None] * differ * differ)
        grad_result = factors * differ
        grad_branch_two = grad_result.astype(jnp.bfloat16)
        grad_down_offset = column_sums(grad_branch_two)
        group_grad_two = lax.all_gather(grad_branch_two, "tok", axis=0, tiled=True)
        grad_activated = plain_product(group_grad_two, down_cols)
        _, gelu_back = jax.vjp(
            lambda argument: jax.nn.gelu(argument, approximate=True), pre_active
        )
        grad_pre_active = gelu_back(grad_activated)[0].astype(jnp.bfloat16)
        grad_normed_two = for_sending(transposed_product(grad_pre_active, up_cols))
        grad_normed_two = lax.psum_scatter(
            grad_normed_two, "tok", scatter_dimension=0, tiled=True
        ).astype(jnp.float32)
        grad_down_cols = for_sending(weight_product(group_grad_two, activated))
        grad_up_cols = for_sending(weight_product(group_two, grad_pre_active))
        grad_up_offset = column_sums(grad_pre_active)
        scaled_two, inverse_two = norm_stats(hidden)
        grad_norm_two, grad_gain_two, grad_shift_two = norm_backward(
            grad_normed_two, gain_two, scaled_two, inverse_two
        )
        grad_hidden = grad_result + grad_norm_two
        grad_branch_one = grad_hidden.astype(jnp.bfloat16)
        grad_output_offset = column_sums(grad_branch_one)
    grad_down_weight = lax.psum_scatter(grad_down_cols, "grp", scatter_dimension=0, tiled=True)
    grad_down_weight, grad_up_cols = lax.optimization_barrier((grad_down_weight, grad_up_cols))
    grad_up_weight = lax.psum_scatter(grad_up_cols, "grp", scatter_dimension=0, tiled=True)

    grad_up_place = lax.dynamic_update_slice_in_dim(
        jnp.zeros((hidden_units,), jnp.float32), grad_up_offset, ff_start, 0
    )
    if kernels:
        (
            grad_query_own,
            grad_output_own,
            grad_keyval_own,
            vectors,
            mine,
            grad_up_own,
            prompt_grad,
            answer_grad,
        ) = backward_reduce(
            owning,
            share,
            weights,
            queries,
            mixture,
            grad_hidden,
            normed_one,
            grad_branch_one,
            log_total,
            prompt_kv,
            answer_kv,
            states,
            gain_row,
            keyval_full,
            grad_up_place.reshape(-1, model_width),
            second_sums,
            grad_down_offset,
            own_squares,
            groups,
            prompt_count,
            answer_count,
            prompt_rows,
            6,
        )
        (
            prompt_grad,
            answer_grad,
            grad_query_own,
            grad_output_own,
            grad_keyval_own,
            grad_up_weight,
            grad_down_weight,
            *own_vectors,
            grad_up_own,
            value_total,
            loss_value,
        ) = finish(
            share_size,
            vectors,
            mine,
            grad_up_own,
            valid_count,
            prompt_grad,
            answer_grad,
            grad_query_own,
            grad_output_own,
            grad_keyval_own,
            grad_up_weight,
            grad_down_weight,
        )
        own_vectors = [each.reshape(-1) for each in own_vectors]
        grad_up_own, value_total = grad_up_own.reshape(-1), value_total.reshape(-1)
        loss_value = loss_value.reshape(())
    else:
        grad_rows = keyval_start + keyval_pack
        grad_weights, grad_normed_one, grad_prompt_kv, grad_answer_kv, grad_query_offset = (
            attention_backward(
                place,
                owning,
                share,
                normed_one,
                weights,
                groups,
                grad_rows,
                prompt_kv,
                answer_kv,
                grad_branch_one,
                queries,
                mixture,
                log_total,
                prompt_count,
                answer_count,
            )
        )
        grad_prompt_kv = lax.psum_scatter(
            grad_prompt_kv, "tok", scatter_dimension=1, tiled=True
        ).astype(jnp.float32)
        grad_keyvals = jnp.concatenate(
            [grad_prompt_kv.reshape(own_prompt, -1), grad_answer_kv], axis=0
        ).astype(jnp.bfloat16)
        grad_keyval_full = weight_product(normed_one, grad_keyvals)
        grad_value_offset = column_sums(grad_keyvals[:, HEAD_WIDTH:])
        grad_normed_one = grad_normed_one + transposed_product(grad_keyvals, keyval_full)
        grad_norm_one, grad_gain_one, grad_shift_one = norm_backward(
            grad_normed_one, gain_one, scaled_one, inverse_one
        )
        grad_inputs = grad_hidden + grad_norm_one

        grad_keyval_blocks = jnp.swapaxes(
            grad_keyval_full.astype(jnp.bfloat16).reshape(groups, token_devices, -1, block), 0, 1
        )
        grad_weights = lax.dynamic_update_slice(
            grad_weights, grad_keyval_blocks, (0, 0, keyval_start, 0)
        )
        vectors = (
            grad_gain_one,
            grad_shift_one,
            grad_query_offset.reshape(-1),
            grad_output_offset,
            grad_gain_two,
            grad_shift_two,
            grad_down_offset,
            grad_up_place,
        )
        totals = jnp.concatenate([grad_value_offset, own_squares.reshape(1)])
        blocks = jnp.concatenate(
            [each.reshape(groups, token_devices, -1) for each in vectors]
            + [jnp.broadcast_to(totals, (groups, token_devices, totals.shape[0]))],
            axis=2,
        )
        blocks = jnp.pad(blocks, ((0, 0), (0, 0), (0, SMALL_SUMS - blocks.shape[2])))
        blocks = jnp.swapaxes(blocks, 0, 1).reshape(token_devices, -1, HEAD_WIDTH)
        grad_weights = lax.psum_scatter(
            grad_weights.reshape(token_devices, -1, block), "tok", scatter_dimension=0, tiled=False
        )
        grad_weights = lax.psum_scatter(grad_weights, "grp", scatter_dimension=0, tiled=True)
        grad_weights = grad_weights.astype(jnp.float32)
        small_sums = lax.psum_scatter(blocks, "tok", scatter_dimension=0, tiled=False)
        small_sums = lax.psum_scatter(small_sums, "grp", scatter_dimension=0, tiled=True)
        small_sums = small_sums.reshape(-1)
        up_share = up_bias.shape[0]
        totals_at = 7 * share_size + up_share
        value_total = small_sums[totals_at : totals_at + HEAD_WIDTH]
        squared_sum = small_sums[totals_at + HEAD_WIDTH]
        own_vectors = [
            small_sums[index * share_size : (index + 1) * share_size] for index in range(7)
        ]
        grad_up_own = small_sums[7 * share_size : totals_at]
        grad_query_own = grad_weights[:weight_rows]
        grad_output_own = grad_weights[weight_rows:keyval_start]
        grad_keyval_own = grad_weights[keyval_start:].reshape(keyval_rows, keyval_width)
        prompt_grad, answer_grad = grad_inputs[:own_prompt], grad_inputs[own_prompt:]
        loss_value = squared_sum / (valid_count * model_width)

    def row_outputs(prompt_part, answer_part):
        return (
            prompt_part.astype(jnp.bfloat16).reshape(prompt_states.shape),
            answer_part.astype(jnp.bfloat16).reshape(answer_states.shape),
        )

    prompt_out, answer_out = row_outputs(prompt_out, answer_out)
    prompt_grad, answer_grad = row_outputs(prompt_grad, answer_grad)
    pieces = own_vectors
    return (
        prompt_out,
        answer_out,
        prompt_grad,
        answer_grad,
        pieces[0],
        pieces[1],
        grad_query_own,
        pieces[2],
        grad_keyval_own,
        value_total,
        grad_output_own,
        pieces[3],
        pieces[4],
        pieces[5],
        grad_up_weight.astype(jnp.float32),
        grad_up_own,
        grad_down_weight.astype(jnp.float32),
        pieces[6],
        loss_value,
    )


def solution(mesh):
    rows = P(("grp", "tok"))
    table = P(("grp", "tok"), None)
    matrix = P("grp", "tok")
    prompt_part = P("grp", "tok", None)
    answer_part = P(("grp", "tok"), None, None)
    in_specs = (
        prompt_part,
        answer_part,
        P("grp"),
        prompt_part,
        answer_part,
        P("grp", "tok"),
        table,
        rows,
        rows,
        matrix,
        rows,
        table,
        P(),
        matrix,
        rows,
        rows,
        rows,
        matrix,
        rows,
        matrix,
        rows,
    )
    out_specs = (
        prompt_part,
        answer_part,
        prompt_part,
        answer_part,
        rows,
        rows,
        matrix,
        rows,
        table,
        P(),
        matrix,
        rows,
        rows,
        rows,
        matrix,
        rows,
        matrix,
        rows,
        P(),
    )
    kernels = mesh.shape["tok"] == 8 and mesh.shape["grp"] == 4
    return jax.shard_map(
        functools.partial(body, kernels),
        mesh=mesh,
        in_specs=in_specs,
        out_specs=out_specs,
        check_vma=False,
    )
```

```python
import functools

import jax
import jax.numpy as jnp
from jax import lax
from jax.experimental import pallas as pl
from jax.experimental.pallas import tpu as pltpu
from jax.sharding import PartitionSpec as P

HEAD_WIDTH = 128
epsilon = 1e-05
masked = -1e30
MESH = pl.DeviceIdType.MESH
VMEM_BYTES = 56 * 1024 * 1024
SMALL_ROWS = 16
SMALL_SUMS = 1024


def for_sending(value):
    return value.astype(jnp.bfloat16)


def plain_product(left, right):
    return jnp.dot(left, right, preferred_element_type=jnp.float32)


def transposed_product(left, right):
    return lax.dot_general(
        left, right, (((1,), (1,)), ((), ())), preferred_element_type=jnp.float32
    )


def weight_product(left, right):
    return lax.dot_general(
        left, right, (((0,), (0,)), ((), ())), preferred_element_type=jnp.float32
    )


def norm_stats(values):
    center = values - jnp.mean(values, axis=-1, keepdims=True)
    inverse = lax.rsqrt(jnp.mean(center * center, axis=-1, keepdims=True) + epsilon)
    return center * inverse, inverse


def norm_backward(grad_out, gain, scaled, inverse):
    weighted = grad_out * gain
    grad_in = inverse * (
        weighted
        - jnp.mean(weighted, axis=-1, keepdims=True)
        - scaled * jnp.mean(weighted * scaled, axis=-1, keepdims=True)
    )
    return (grad_in, jnp.sum(grad_out * scaled, axis=0), jnp.sum(grad_out, axis=0))


def column_sums(values):
    return jnp.sum(values.astype(jnp.float32), axis=0)


def block_of_eight():
    here = lax.axis_index("tok")
    core, across, along = here % 2, (here // 2) % 2, here // 4
    on_x = here + 2 - 4 * across
    on_y = here + 4 - 8 * along
    on_chip = here + 1 - 2 * core
    corner = on_x + 4 - 8 * along
    return here, on_x, on_y, on_chip, corner


def greet_all(peers, other_groups):
    barrier = pltpu.get_barrier_semaphore()
    for peer in peers:
        pl.semaphore_signal(barrier, inc=1, device_id={"tok": peer}, device_id_type=MESH)
    for other in other_groups:
        pl.semaphore_signal(barrier, inc=1, device_id={"grp": other}, device_id_type=MESH)
    pl.semaphore_wait(barrier, len(peers) + len(other_groups))


def greet(devices):
    barrier = pltpu.get_barrier_semaphore()
    for device in devices:
        pl.semaphore_signal(barrier, inc=1, device_id={"tok": device}, device_id_type=MESH)
    pl.semaphore_wait(barrier, len(devices))


def paired_gather(source, place, send_sem, recv_sem):
    here, on_x, on_y, on_chip, corner = block_of_eight()
    over = [
        remote(index, source, place(here), device, send_sem, recv_sem)
        for index, device in enumerate((on_x, on_y, corner, on_chip))
    ]
    handed = [
        remote(4 + index, place(device), place(device), on_chip, send_sem, recv_sem)
        for index, device in enumerate((on_x, on_y, corner))
    ]
    for each in over:
        each.start()
    for each, then in zip(over, handed):
        each.wait_recv()
        then.start()
    for each in [over[3]] + handed:
        each.wait_recv()
    for each in over + handed:
        each.wait_send()


def spread_kernel(groups, own_ref, out_ref, held, send_sem, recv_sem, over_send, over_recv):
    here, on_x, on_y, on_chip, corner = block_of_eight()
    group = lax.axis_index("grp")
    other_groups = [(group + turn) % groups for turn in range(1, groups)]
    greet_all((on_x, on_y, on_chip, corner), other_groups)
    over = [
        pltpu.make_async_remote_copy(
            src_ref=own_ref,
            dst_ref=held.at[group],
            send_sem=over_send.at[index],
            recv_sem=over_recv.at[index],
            device_id={"grp": other},
            device_id_type=MESH,
        )
        for index, other in enumerate(other_groups)
    ]
    for each in over:
        each.start()
    held[group] = own_ref[...]
    for each in over:
        each.wait_recv()
    out_ref[here] = held[...]
    paired_gather(held, lambda device: out_ref.at[device], send_sem, recv_sem)
    for each in over:
        each.wait_send()


def spread(own, groups, call_number, kernels):
    if not kernels:
        return lax.all_gather(lax.all_gather(own, "grp", axis=0), "tok", axis=0)
    inside = pl.BlockSpec(memory_space=pltpu.VMEM)
    dma = pltpu.SemaphoreType.DMA
    return pl.pallas_call(
        functools.partial(spread_kernel, groups),
        out_shape=jax.ShapeDtypeStruct((8, groups) + own.shape, own.dtype),
        in_specs=[inside],
        out_specs=inside,
        scratch_shapes=[
            pltpu.VMEM((groups,) + own.shape, own.dtype),
            dma((7,)),
            dma((7,)),
            dma((groups - 1,)),
            dma((groups - 1,)),
        ],
        compiler_params=pltpu.CompilerParams(collective_id=call_number, has_side_effects=True),
        name="spread",
    )(own)


def remote(index, source, target, device, send_sem, recv_sem):
    return pltpu.make_async_remote_copy(
        src_ref=source,
        dst_ref=target,
        send_sem=send_sem.at[index],
        recv_sem=recv_sem.at[index],
        device_id={"tok": device},
        device_id_type=MESH,
    )


def chunk_of(index, size):
    return pl.ds(pl.multiple_of(index * size, size), size)


CHUNK = 512
LINEAR = 0.7978845608
CUBIC = 0.044715


def gather_beside(own_ref, out_ref, send_sem, recv_sem, local_sem, use):
    rows = own_ref.shape[0]
    half, quarter = rows // 2, rows // 4
    here, on_x, on_y, on_chip, corner = block_of_eight()
    shift = on_chip - here
    counter = iter(range(GATHER_COPIES))

    def copy(source, block, start, count, device):
        place = pl.ds(start, count)
        return remote(
            next(counter),
            source.at[place] if source is own_ref else source.at[block, place],
            out_ref.at[block, place],
            device,
            send_sem,
            recv_sem,
        )

    greet((on_x, on_y, on_chip))
    own = pltpu.make_async_copy(own_ref, out_ref.at[here], local_sem)
    x_low = copy(own_ref, here, 0, half, on_x)
    y_high = copy(own_ref, here, half, half, on_y)
    x_high = copy(own_ref, here, half, half, on_x)
    y_low = copy(own_ref, here, 0, half, on_y)
    to_chip = copy(own_ref, here, 0, rows, on_chip)
    to_y = [copy(out_ref, on_x, turn * quarter, quarter, on_y) for turn in (0, 1)]
    to_x = [copy(out_ref, on_y, half + turn * quarter, quarter, on_x) for turn in (0, 1)]
    chip_x = [copy(out_ref, on_x, turn * half, half, on_chip) for turn in (0, 1)]
    chip_y = [copy(out_ref, on_y, turn * half, half, on_chip) for turn in (0, 1)]
    chip_corner = [copy(out_ref, corner, turn * quarter, quarter, on_chip) for turn in range(4)]
    for each in (x_low, y_high, x_high, y_low, to_chip, own):
        each.start()
    use(0, [(here, 0, rows)])
    to_chip.wait_recv()
    use(1, [(on_chip, 0, rows)])
    x_low.wait_recv()
    for each in (*to_y, chip_x[0]):
        each.start()
    y_high.wait_recv()
    for each in (*to_x, chip_y[1]):
        each.start()
    use(2, [(on_x, 0, half), (on_y, half, half)])
    chip_x[0].wait_recv()
    chip_y[1].wait_recv()
    use(3, [(on_x + shift, 0, half), (on_y + shift, half, half)])
    x_high.wait_recv()
    chip_x[1].start()
    y_low.wait_recv()
    chip_y[0].start()
    use(4, [(on_x, half, half), (on_y, 0, half)])
    chip_x[1].wait_recv()
    chip_y[0].wait_recv()
    use(5, [(on_x + shift, half, half), (on_y + shift, 0, half)])
    for turn in (0, 1):
        to_y[turn].wait_recv()
        chip_corner[turn].start()
        to_x[turn].wait_recv()
        chip_corner[2 + turn].start()
        chip_corner[turn].wait_recv()
        chip_corner[2 + turn].wait_recv()
        use(
            6 + turn,
            [
                (block, start + turn * quarter, quarter)
                for block in (corner, corner + shift)
                for start in (0, half)
            ],
        )
    own.wait()
    for each in (x_low, y_high, x_high, y_low, to_chip, *to_y, *to_x, *chip_x, *chip_y, *chip_corner):
        each.wait_send()


GATHER_COPIES = 17


def moves(outside, inside, pieces, semaphores, outward):
    done, copies = 0, []
    for index, (block, start, count) in enumerate(pieces):
        away = outside.at[block, pl.ds(start, count)]
        near = inside.at[pl.ds(done, count)]
        pair = (near, away) if outward else (away, near)
        copies.append(pltpu.make_async_copy(*pair, semaphores.at[index]))
        done += count
    return copies


def up_kernel(
    own_ref,
    up_hbm,
    bias_ref,
    rows_ref,
    active_ref,
    slope_ref,
    up,
    rows,
    active,
    slope,
    send_sem,
    recv_sem,
    local_sem,
    weight_sem,
    row_sem,
    store_sem,
):
    weights = pltpu.make_async_copy(up_hbm, up, weight_sem)
    weights.start()
    stores = {}

    def use(place, pieces):
        slot = place % 2
        if place:
            loads = moves(rows_ref, rows, pieces, row_sem, False)
        else:
            loads = [pltpu.make_async_copy(own_ref, rows, row_sem.at[0])]
        for each in loads:
            each.start()
        if place == 0:
            weights.wait()
        for each in stores.pop(slot, ()):
            each.wait()
        for each in loads:
            each.wait()

        @pl.loop(0, up.shape[1] // CHUNK)
        def _(turn):
            at = chunk_of(turn, CHUNK)
            value = plain_product(rows[...], up[:, at]) + bias_ref[:, at]
            square = value * value
            bent = jnp.tanh(value * (LINEAR + (LINEAR * CUBIC) * square))
            level = 0.5 + 0.5 * bent
            active[slot, :, at] = (value * level).astype(jnp.bfloat16)
            slope[slot, :, at] = (
                level
                + (0.5 * value)
                * (1.0 - bent * bent)
                * (LINEAR + (3.0 * LINEAR * CUBIC) * square)
            ).astype(jnp.bfloat16)

        stores[slot] = moves(
            active_ref, active.at[slot], pieces, store_sem.at[slot, 0], True
        ) + moves(slope_ref, slope.at[slot], pieces, store_sem.at[slot, 1], True)
        for each in stores[slot]:
            each.start()

    gather_beside(own_ref, rows_ref, send_sem, recv_sem, local_sem, use)
    for slot in (0, 1):
        for each in stores[slot]:
            each.wait()


def gather_and_up(own, up_cols, bias, call_number):
    token_rows, model_width = own.shape
    width = up_cols.shape[1]
    hidden = jax.ShapeDtypeStruct((8, token_rows, width), jnp.bfloat16)
    anywhere = pl.BlockSpec(memory_space=pl.ANY)
    dma = pltpu.SemaphoreType.DMA
    return pl.pallas_call(
        up_kernel,
        out_shape=(
            jax.ShapeDtypeStruct((8, token_rows, model_width), jnp.bfloat16),
            hidden,
            hidden,
        ),
        in_specs=[anywhere, anywhere, pl.BlockSpec(memory_space=pltpu.VMEM)],
        out_specs=(anywhere, anywhere, anywhere),
        scratch_shapes=[
            pltpu.VMEM(up_cols.shape, jnp.bfloat16),
            pltpu.VMEM((token_rows, model_width), jnp.bfloat16),
            pltpu.VMEM((2, token_rows, width), jnp.bfloat16),
            pltpu.VMEM((2, token_rows, width), jnp.bfloat16),
            dma((GATHER_COPIES,)),
            dma((GATHER_COPIES,)),
            dma,
            dma,
            dma((4,)),
            dma((2, 2, 4)),
        ],
        compiler_params=pltpu.CompilerParams(
            collective_id=call_number, has_side_effects=True, vmem_limit_bytes=VMEM_BYTES
        ),
        cost_estimate=pl.CostEstimate(
            flops=16 * token_rows * model_width * width,
            bytes_accessed=150 * 1000 * 1000,
            transcendentals=0,
        ),
        name="gather_and_up",
    )(own, up_cols, bias.reshape(1, -1))


def grad_kernel(
    own_ref,
    down_hbm,
    active_ref,
    slope_ref,
    rows_ref,
    grad_ref,
    weight_ref,
    bias_ref,
    down,
    rows,
    active,
    slope,
    grads,
    sums,
    narrow,
    send_sem,
    recv_sem,
    local_sem,
    weight_sem,
    row_sem,
    load_sem,
    store_sem,
):
    weights = pltpu.make_async_copy(down_hbm, down, weight_sem)
    weights.start()
    stores = {}

    def use(place, pieces):
        slot = place % 2
        if place:
            loads = moves(rows_ref, rows, pieces, row_sem, False)
        else:
            loads = [pltpu.make_async_copy(own_ref, rows, row_sem.at[0])]
        loads += moves(active_ref, active, pieces, load_sem.at[0], False)
        loads += moves(slope_ref, slope, pieces, load_sem.at[1], False)
        for each in loads:
            each.start()
        if place == 0:
            weights.wait()
        for each in stores.pop(slot, ()):
            each.wait()
        for each in loads:
            each.wait()

        @pl.loop(0, down.shape[1] // CHUNK)
        def _(turn):
            at = chunk_of(turn, CHUNK)
            value = plain_product(rows[...], down[:, at]) * slope[:, at].astype(jnp.float32)
            value = value.astype(jnp.bfloat16)
            grads[slot, :, at] = value
            total = jnp.sum(value.astype(jnp.float32), axis=0, keepdims=True)
            weight = weight_product(rows[...], active[:, at])
            if place == 0:
                bias_ref[:, at] = total
                sums[:, at] = weight
            elif place < 7:
                bias_ref[:, at] += total
                sums[:, at] += weight
            else:
                bias_ref[:, at] += total
                narrow[:, at] = (sums[:, at] + weight).astype(jnp.bfloat16)

        stores[slot] = moves(grad_ref, grads.at[slot], pieces, store_sem.at[slot], True)
        for each in stores[slot]:
            each.start()

    gather_beside(own_ref, rows_ref, send_sem, recv_sem, local_sem, use)
    last = pltpu.make_async_copy(narrow, weight_ref, weight_sem)
    last.start()
    for slot in (0, 1):
        for each in stores[slot]:
            each.wait()
    last.wait()


def gather_and_grad(own, down_cols, active, slope, call_number):
    token_rows, model_width = own.shape
    width = down_cols.shape[1]
    anywhere = pl.BlockSpec(memory_space=pl.ANY)
    dma = pltpu.SemaphoreType.DMA
    return pl.pallas_call(
        grad_kernel,
        out_shape=(
            jax.ShapeDtypeStruct((8, token_rows, model_width), jnp.bfloat16),
            jax.ShapeDtypeStruct((8, token_rows, width), jnp.bfloat16),
            jax.ShapeDtypeStruct((model_width, width), jnp.bfloat16),
            jax.ShapeDtypeStruct((1, width), jnp.float32),
        ),
        in_specs=[anywhere] * 4,
        out_specs=(anywhere,) * 3 + (pl.BlockSpec(memory_space=pltpu.VMEM),),
        scratch_shapes=[
            pltpu.VMEM(down_cols.shape, jnp.bfloat16),
            pltpu.VMEM((token_rows, model_width), jnp.bfloat16),
            pltpu.VMEM((token_rows, width), jnp.bfloat16),
            pltpu.VMEM((token_rows, width), jnp.bfloat16),
            pltpu.VMEM((2, token_rows, width), jnp.bfloat16),
            pltpu.VMEM((model_width, width), jnp.float32),
            pltpu.VMEM((model_width, width), jnp.bfloat16),
            dma((GATHER_COPIES,)),
            dma((GATHER_COPIES,)),
            dma,
            dma,
            dma((4,)),
            dma((2, 4)),
            dma((2, 4)),
        ],
        compiler_params=pltpu.CompilerParams(
            collective_id=call_number, has_side_effects=True, vmem_limit_bytes=VMEM_BYTES
        ),
        cost_estimate=pl.CostEstimate(
            flops=32 * token_rows * model_width * width,
            bytes_accessed=150 * 1000 * 1000,
            transcendentals=0,
        ),
        name="gather_and_grad",
    )(own, down_cols, active, slope)


def product_reduce_kernel(
    with_grad,
    narrow_ref,
    weight_hbm,
    *refs,
):
    if with_grad:
        wide_ref, hidden_hbm, result_hbm, gain_ref, *refs = refs
        grad_hidden_ref, grad_ref, branch_ref, sums_ref, *refs = refs
        *refs, wide, across, sums, wide_sem = refs
    else:
        hidden_hbm, teacher_hbm, offset_ref, valid_ref, factor_ref, *refs = refs
        prompt_ref, answer_ref, branch_ref, grad_result_ref, squares_ref, columns_ref, *refs = refs
    (
        weight,
        narrow,
        sent,
        mine,
        theirs,
        relayed,
        final,
        hidden_rows,
        other_rows,
        send_sem,
        recv_sem,
        weight_sem,
        narrow_sem,
        row_sem,
    ) = refs
    row_loads = (
        pltpu.make_async_copy(hidden_hbm, hidden_rows, row_sem.at[0]),
        pltpu.make_async_copy(result_hbm if with_grad else teacher_hbm, other_rows, row_sem.at[1]),
    )
    rows = narrow.shape[1]
    half = rows // 2
    here, on_x, on_y, on_chip, corner = block_of_eight()
    shift = on_chip - here
    first, second = pl.ds(0, half), pl.ds(half, half)
    load_weight = pltpu.make_async_copy(weight_hbm, weight, weight_sem)
    load_weight.start()

    def copy(index, source, target, device):
        return remote(index, source, target, device, send_sem, recv_sem)

    places = (corner, on_x, on_y, here)
    order = []
    for place in places:
        order += [place + shift, place]

    def fetch(turn):
        return pltpu.make_async_copy(
            narrow_ref.at[order[turn]], narrow.at[turn % 2], narrow_sem.at[turn % 2]
        )

    fetch(0).start()
    greet((on_x, on_y, on_chip))
    to_chip = [copy(index, sent.at[index], theirs.at[index], on_chip) for index in range(4)]
    step = 16

    def add_into(target, other, start, count):
        @pl.loop(0, count // step)
        def _(turn):
            at = pl.ds(pl.multiple_of(start + turn * step, step), step)
            come = pl.ds(pl.multiple_of(turn * step, step), step)
            target[at, :] = target[at, :] + other[come, :]

    def join(index):
        to_chip[index].wait_recv()
        add_into(mine.at[index], theirs.at[index], 0, rows)

    corner_x = copy(4, mine.at[0, first], relayed.at[0], on_x)
    corner_y = copy(5, mine.at[0, second], relayed.at[1], on_y)
    x_first = copy(6, mine.at[1, first], final.at[0, first], on_x)
    y_second = copy(7, mine.at[2, second], final.at[1, second], on_y)
    x_second = copy(8, mine.at[1, second], final.at[0, second], on_x)
    y_first = copy(9, mine.at[2, first], final.at[1, first], on_y)

    for each in row_loads:
        each.start()
    for turn in range(8):
        pair, own = turn // 2, turn % 2
        if turn < 7:
            fetch(turn + 1).start()
        fetch(turn).wait()
        if turn == 0:
            load_weight.wait()
        target = mine.at[pair] if own else sent.at[pair]

        @pl.loop(0, weight.shape[0] // CHUNK)
        def _(piece):
            at = chunk_of(piece, CHUNK)
            target[:, at] = transposed_product(narrow[turn % 2], weight[at, :]).astype(
                jnp.bfloat16
            )

        if not own:
            to_chip[pair].start()
        if turn == 2:
            join(0)
            corner_x.start()
            corner_y.start()
        if turn == 4:
            join(1)
            x_first.start()
        if turn == 6:
            join(2)
            y_second.start()
    corner_y.wait_recv()
    add_into(mine.at[1], relayed.at[1], half, half)
    x_second.start()
    corner_x.wait_recv()
    add_into(mine.at[2], relayed.at[0], 0, half)
    y_first.start()
    join(3)

    if with_grad:
        def fetch_wide(turn):
            return pltpu.make_async_copy(
                wide_ref.at[order[turn]], wide.at[turn % 2], wide_sem.at[turn % 2]
            )

        fetch_wide(0).start()
        fetch(0).start()
        for turn in range(8):
            if turn < 7:
                fetch_wide(turn + 1).start()
                fetch(turn + 1).start()
            fetch_wide(turn).wait()
            fetch(turn).wait()
            across[...] = jnp.transpose(wide[turn % 2])

            @pl.loop(0, sums.shape[1] // CHUNK)
            def _(piece):
                at = chunk_of(piece, CHUNK)
                value = plain_product(across[...], narrow[turn % 2, :, at])
                if turn == 0:
                    sums[:, at] = value
                elif turn < 7:
                    sums[:, at] += value
                else:
                    weight[:, at] = (sums[:, at] + value).astype(jnp.bfloat16)

        store = pltpu.make_async_copy(weight, grad_ref, weight_sem)
        store.start()

    for each in row_loads:
        each.wait()
    if not with_grad:
        for start, part, come in ((0, x_first, 0), (half, y_second, 1)):
            part.wait_recv()

            @pl.loop(0, half // step)
            def _(turn):
                at = pl.ds(pl.multiple_of(start + turn * step, step), step)
                base = hidden_rows[at, :] + offset_ref[...] + mine[3, at, :].astype(jnp.float32)
                hidden_rows[at, :] = base + final[come, at, :].astype(jnp.float32)

        y_first.wait_recv()
        x_second.wait_recv()
    else:
        for each in (x_first, y_second, x_second, y_first):
            each.wait_recv()

    def total_of(at):
        total = mine[3, at, :].astype(jnp.float32) + final[0, at, :].astype(jnp.float32)
        return total + final[1, at, :].astype(jnp.float32)

    if with_grad:
        sums_ref[...] = jnp.zeros_like(sums_ref)

        @pl.loop(0, rows // step)
        def _(turn):
            at = chunk_of(turn, step)
            grad_out = total_of(at)
            scaled, inverse = norm_stats(hidden_rows[at, :])
            weighted = grad_out * gain_ref[...]
            grad_in = inverse * (
                weighted
                - jnp.mean(weighted, axis=-1, keepdims=True)
                - scaled * jnp.mean(weighted * scaled, axis=-1, keepdims=True)
            )
            grad_hidden = other_rows[at, :] + grad_in
            branch = grad_hidden.astype(jnp.bfloat16)
            grad_hidden_ref[at, :] = grad_hidden
            branch_ref[at, :] = branch
            sums_ref[0:1, :] += jnp.sum(branch.astype(jnp.float32), axis=0, keepdims=True)
            sums_ref[1:2, :] += jnp.sum(grad_out * scaled, axis=0, keepdims=True)
            sums_ref[2:3, :] += jnp.sum(grad_out, axis=0, keepdims=True)

    else:
        squares_ref[...] = jnp.zeros_like(squares_ref)
        columns_ref[...] = jnp.zeros_like(columns_ref)
        own_prompt = prompt_ref.shape[0]
        for start, stop, come, out_ref, before in (
            (0, half, 1, prompt_ref, 0),
            (half, own_prompt, 0, prompt_ref, 0),
            (own_prompt, rows, 0, answer_ref, own_prompt),
        ):

            @pl.loop(0, (stop - start) // step)
            def _(turn):
                at = pl.ds(pl.multiple_of(start + turn * step, step), step)
                out = pl.ds(pl.multiple_of(start - before + turn * step, step), step)
                result = hidden_rows[at, :] + final[come, at, :].astype(jnp.float32)
                differ = result - other_rows[at, :].astype(jnp.float32)
                grad_result = factor_ref[at, :] * differ
                branch = grad_result.astype(jnp.bfloat16)
                out_ref[out, :] = result.astype(jnp.bfloat16)
                grad_result_ref[at, :] = grad_result
                branch_ref[at, :] = branch
                squared = valid_ref[at, :] * differ * differ
                column = branch.astype(jnp.float32)
                squares_ref[...] += squared[:8, :] + squared[8:, :]
                columns_ref[...] += column[:8, :] + column[8:, :]

    if with_grad:
        store.wait()
    for each in to_chip + [corner_x, corner_y, x_first, y_second, x_second, y_first]:
        each.wait_send()


def product_and_reduce(narrow, weight, wide, rows, second, call_number, own_prompt, *small):
    _, token_rows, width = narrow.shape
    model_width = weight.shape[0]
    with_grad = wide is not None
    anywhere = pl.BlockSpec(memory_space=pl.ANY)
    inside = pl.BlockSpec(memory_space=pltpu.VMEM)
    dma = pltpu.SemaphoreType.DMA
    block = (token_rows, model_width)
    kind, long = jnp.bfloat16, jnp.float32
    line = jax.ShapeDtypeStruct((8, model_width), long)
    narrow_rows, long_rows = jax.ShapeDtypeStruct(block, kind), jax.ShapeDtypeStruct(block, long)
    scratch = [
        pltpu.VMEM(weight.shape, kind),
        pltpu.VMEM((2, token_rows, width), kind),
        pltpu.VMEM((4,) + block, kind),
        pltpu.VMEM((4,) + block, kind),
        pltpu.VMEM((4,) + block, kind),
        pltpu.VMEM((2, token_rows // 2, model_width), kind),
        pltpu.VMEM((2,) + block, kind),
        pltpu.VMEM(block, long),
        pltpu.VMEM(block, second.dtype),
        dma((10,)),
        dma((10,)),
        dma,
        dma((2,)),
        dma((2,)),
    ]
    operands = [narrow, weight]
    if with_grad:
        out_shape = (
            long_rows,
            jax.ShapeDtypeStruct(weight.shape, kind),
            narrow_rows,
            jax.ShapeDtypeStruct((8, model_width), long),
        )
        out_specs = (inside, anywhere, inside, inside)
        scratch += [
            pltpu.VMEM((2,) + block, kind),
            pltpu.VMEM((model_width, token_rows), kind),
            pltpu.VMEM(weight.shape, long),
            dma((2,)),
        ]
        operands.append(wide)
    else:
        out_shape = (
            jax.ShapeDtypeStruct((own_prompt, model_width), kind),
            jax.ShapeDtypeStruct((token_rows - own_prompt, model_width), kind),
            narrow_rows,
            long_rows,
            line,
            line,
        )
        out_specs = (inside,) * 6
    operands += [rows, second]
    return pl.pallas_call(
        functools.partial(product_reduce_kernel, with_grad),
        out_shape=out_shape,
        in_specs=[anywhere] * len(operands) + [inside] * len(small),
        out_specs=out_specs,
        scratch_shapes=scratch,
        compiler_params=pltpu.CompilerParams(
            collective_id=call_number,
            has_side_effects=True,
            vmem_limit_bytes=62 * 1024 * 1024,
        ),
        cost_estimate=pl.CostEstimate(
            flops=(32 if with_grad else 16) * token_rows * model_width * width,
            bytes_accessed=150 * 1000 * 1000,
            transcendentals=0,
        ),
        name="product_and_reduce",
    )(*operands, *small)


def peers_of(count):
    here = lax.axis_index("tok")
    return here, [(here + step) % count for step in range(1, count)]


def small_gather_kernel(own_ref, out_ref, send_sem, recv_sem):
    here, on_x, on_y, on_chip, corner = block_of_eight()
    rows = own_ref.shape[1]

    def place(device):
        return pl.ds(pl.multiple_of(device * rows, rows), rows)

    greet((on_x, on_y, on_chip, corner))
    out_ref[:, place(here), :] = own_ref[...]
    paired_gather(own_ref, lambda device: out_ref.at[:, place(device), :], send_sem, recv_sem)


def tok_gather_small(own, call_number, kernels):
    if not kernels:
        return lax.all_gather(own, "tok", axis=1, tiled=True)
    prompts, rows, columns = own.shape
    return pl.pallas_call(
        small_gather_kernel,
        out_shape=jax.ShapeDtypeStruct((prompts, 8 * rows, columns), own.dtype),
        in_specs=[pl.BlockSpec(memory_space=pltpu.VMEM)],
        out_specs=pl.BlockSpec(memory_space=pltpu.VMEM),
        scratch_shapes=[pltpu.SemaphoreType.DMA((7,)), pltpu.SemaphoreType.DMA((7,))],
        compiler_params=pltpu.CompilerParams(collective_id=call_number, has_side_effects=True),
        name="tok_gather_small",
    )(own)


def stack_heads(values, heads):
    return jnp.concatenate(
        [values[:, head * HEAD_WIDTH : (head + 1) * HEAD_WIDTH] for head in range(heads)], axis=0
    )


def unstack_heads(values, heads):
    rows = values.shape[0] // heads
    return jnp.concatenate(
        [values[head * rows : (head + 1) * rows, :] for head in range(heads)], axis=1
    )


def part_rows(part, prompts, answers, token_ref, answer_ref):
    answer_rows = answer_ref.shape[0] // answers
    prompt_rows = (token_ref.shape[0] - answer_ref.shape[0]) // prompts
    if part < prompts:
        return slice(part * prompt_rows, (part + 1) * prompt_rows), prompt_rows
    start = prompts * prompt_rows + (part - prompts) * answer_rows
    return slice(start, start + answer_rows), answer_rows


def as_row(column):
    wide = jnp.broadcast_to(column, (column.shape[0], HEAD_WIDTH))
    return jnp.transpose(wide)[0:1, :]


def forward_block(
    prompts,
    answers,
    heads,
    start,
    owner_ref,
    normed_ref,
    query_block,
    bias,
    prompt_kv_ref,
    answer_kv_ref,
):
    width = HEAD_WIDTH
    scale = HEAD_WIDTH ** (-0.5)
    length = prompt_kv_ref.shape[1]
    queries = (plain_product(normed_ref[...], query_block) + bias).astype(jnp.bfloat16)
    pieces, logs = [], []
    for part in range(prompts + answers):
        here, rows = part_rows(part, prompts, answers, normed_ref, answer_kv_ref)
        token = lax.broadcasted_iota(jnp.int32, (heads * rows, 1), 0) % rows
        stacked = stack_heads(queries[here, :], heads)
        if part < prompts:
            keys = prompt_kv_ref[part, :, :width]
            values = prompt_kv_ref[part, :, width:]
            scores = transposed_product(stacked, keys)
            place = lax.broadcasted_iota(jnp.int32, (1, length), 1)
            scores = jnp.where(place <= start + token, scores, masked)
            top = jnp.max(scores, axis=-1, keepdims=True)
            exponent = jnp.exp((scores - top) * scale)
            total = jnp.sum(exponent, axis=-1, keepdims=True)
            mixed = plain_product(exponent.astype(jnp.bfloat16), values)
        else:
            answer = part - prompts
            owner = owner_ref[answer]
            own = slice(answer * rows, (answer + 1) * rows)
            keys = prompt_kv_ref[owner, :, :width]
            values = prompt_kv_ref[owner, :, width:]
            scores = transposed_product(stacked, keys)
            own_scores = transposed_product(stacked, answer_kv_ref[own, :width])
            place = lax.broadcasted_iota(jnp.int32, (1, rows), 1)
            own_scores = jnp.where(place <= token, own_scores, masked)
            top = jnp.maximum(
                jnp.max(scores, axis=-1, keepdims=True),
                jnp.max(own_scores, axis=-1, keepdims=True),
            )
            exponent = jnp.exp((scores - top) * scale)
            own_exponent = jnp.exp((own_scores - top) * scale)
            total = jnp.sum(exponent, axis=-1, keepdims=True) + jnp.sum(
                own_exponent, axis=-1, keepdims=True
            )
            mixed = plain_product(exponent.astype(jnp.bfloat16), values) + plain_product(
                own_exponent.astype(jnp.bfloat16), answer_kv_ref[own, width:]
            )
        pieces.append(unstack_heads((mixed / total).astype(jnp.bfloat16), heads))
        logs.append((here, rows, as_row(top * scale + jnp.log(total))))
    return queries, jnp.concatenate(pieces, axis=0), logs


def attention_forward_kernel(
    prompts,
    answers,
    heads,
    place_ref,
    owner_ref,
    normed_ref,
    query_ref,
    bias_ref,
    prompt_kv_ref,
    answer_kv_ref,
    output_ref,
    states_ref,
    offset_ref,
    gain_ref,
    shift_ref,
    queries_ref,
    mixture_ref,
    log_ref,
    hidden_ref,
    second_ref,
):
    step = pl.program_id(0)
    queries, mixture, logs = forward_block(
        prompts,
        answers,
        heads,
        place_ref[0],
        owner_ref,
        normed_ref,
        query_ref[0],
        bias_ref[0],
        prompt_kv_ref,
        answer_kv_ref,
    )
    queries_ref[0] = queries
    mixture_ref[0] = mixture
    for here, rows, log_row in logs:
        for head in range(heads):
            log_ref[0, head : head + 1, here] = log_row[:, head * rows : (head + 1) * rows]

    @pl.when(step == 0)
    def _():
        hidden_ref[...] = states_ref[...].astype(jnp.float32) + offset_ref[...]

    hidden_ref[...] += transposed_product(mixture, output_ref[0])

    @pl.when(step == pl.num_programs(0) - 1)
    def _():
        scaled, _ = norm_stats(hidden_ref[...])
        second_ref[...] = (scaled * gain_ref[...] + shift_ref[...]).astype(jnp.bfloat16)


def attention_forward(
    place,
    owning,
    normed,
    query_blocks,
    output_blocks,
    query_offset,
    prompt_kv,
    answer_kv,
    states,
    output_offset,
    gain,
    shift,
    prompts,
    answers,
):
    token_rows, model_width = normed.shape
    steps, _, block = query_blocks.shape
    heads = block // HEAD_WIDTH
    whole = lambda *shape: pl.BlockSpec(shape, lambda step, *_: (0,) * len(shape))
    one = lambda *shape: pl.BlockSpec((1,) + shape, lambda step, *_: (step, 0, 0))
    by_step = jax.ShapeDtypeStruct((steps, token_rows, block), jnp.bfloat16)
    return pl.pallas_call(
        functools.partial(attention_forward_kernel, prompts, answers, heads),
        out_shape=(
            by_step,
            by_step,
            jax.ShapeDtypeStruct((steps, heads, token_rows), jnp.float32),
            jax.ShapeDtypeStruct((token_rows, model_width), jnp.float32),
            jax.ShapeDtypeStruct((token_rows, model_width), jnp.bfloat16),
        ),
        grid_spec=pltpu.PrefetchScalarGridSpec(
            num_scalar_prefetch=2,
            grid=(steps,),
            in_specs=[
                whole(token_rows, model_width),
                one(model_width, block),
                one(1, block),
                whole(*prompt_kv.shape),
                whole(*answer_kv.shape),
                one(model_width, block),
                whole(token_rows, model_width),
                whole(1, model_width),
                whole(1, model_width),
                whole(1, model_width),
            ],
            out_specs=(
                one(token_rows, block),
                one(token_rows, block),
                one(heads, token_rows),
                whole(token_rows, model_width),
                whole(token_rows, model_width),
            ),
        ),
        compiler_params=pltpu.CompilerParams(vmem_limit_bytes=VMEM_BYTES),
        name="attention_forward",
    )(
        place,
        owning,
        normed,
        query_blocks,
        query_offset.reshape(steps, 1, block),
        prompt_kv,
        answer_kv,
        output_blocks,
        states,
        output_offset.reshape(1, -1),
        gain.reshape(1, -1),
        shift.reshape(1, -1),
    )


def bits_away(index):
    here = lax.axis_index("tok")
    core = (here + index) % 2
    across = (here // 2 + index // 2) % 2
    along = (here // 4 + index // 4) % 2
    return along * 4 + across * 2 + core


def gather_attention_kernel(
    prompts,
    answers,
    heads,
    prompt_rows,
    owner_ref,
    own_ref,
    normed_ref,
    bias_ref,
    prompt_kv_ref,
    answer_kv_ref,
    states_ref,
    offset_ref,
    gain_ref,
    shift_ref,
    weights_ref,
    queries_ref,
    mixture_ref,
    log_ref,
    hidden_ref,
    second_ref,
    held,
    send_sem,
    recv_sem,
    local_sem,
    load_sem,
):
    here, on_x, on_y, on_chip, corner = block_of_eight()

    def copy(index, source, target, device):
        return remote(index, source, target, device, send_sem, recv_sem)

    def kind_of(device, kind):
        return weights_ref.at[device, :, kind]

    to_x = [copy(0 + kind, own_ref.at[:, kind], kind_of(here, kind), on_x) for kind in (0, 1)]
    to_y = [copy(2 + kind, own_ref.at[:, kind], kind_of(here, kind), on_y) for kind in (0, 1)]
    to_chip = [copy(4, own_ref, weights_ref.at[here], on_chip)]
    keep = [pltpu.make_async_copy(own_ref, weights_ref.at[here], local_sem)]
    x_to_y = copy(5, kind_of(on_x, 0), kind_of(on_x, 0), on_y)
    y_to_x = copy(6, kind_of(on_y, 1), kind_of(on_y, 1), on_x)
    x_to_chip = copy(7, weights_ref.at[on_x], weights_ref.at[on_x], on_chip)
    y_to_chip = copy(8, weights_ref.at[on_y], weights_ref.at[on_y], on_chip)
    corner_to_chip = [
        copy(9 + kind, kind_of(corner, kind), kind_of(corner, kind), on_chip) for kind in (0, 1)
    ]

    greet((on_x, on_y, on_chip))
    for each in (to_x[0], to_y[1], to_x[1], to_y[0], *to_chip, *keep):
        each.start()
    hidden_ref[...] = states_ref[...].astype(jnp.float32) + offset_ref[...]

    @pl.loop(0, 8)
    def _(turn):
        block = bits_away(turn)

        @pl.when(turn == 0)
        def _():
            load = pltpu.make_async_copy(own_ref, held, load_sem)
            load.start()
            load.wait()

        @pl.when(turn == 1)
        def _():
            for each in to_chip:
                each.wait_recv()

        @pl.when(turn == 2)
        def _():
            to_x[0].wait_recv()
            x_to_y.start()
            to_y[1].wait_recv()
            y_to_x.start()
            to_x[1].wait_recv()
            x_to_chip.start()
            to_y[0].wait_recv()
            y_to_chip.start()

        @pl.when(turn == 3)
        def _():
            x_to_chip.wait_recv()

        @pl.when(turn == 5)
        def _():
            y_to_chip.wait_recv()

        @pl.when(turn == 6)
        def _():
            x_to_y.wait_recv()
            corner_to_chip[0].start()
            y_to_x.wait_recv()
            corner_to_chip[1].start()

        @pl.when(turn == 7)
        def _():
            for each in corner_to_chip:
                each.wait_recv()

        @pl.when(turn > 0)
        def _():
            load = pltpu.make_async_copy(weights_ref.at[block], held, load_sem)
            load.start()
            load.wait()

        queries, mixture, logs = forward_block(
            prompts,
            answers,
            heads,
            here * prompt_rows,
            owner_ref,
            normed_ref,
            held[:, 0].reshape(-1, held.shape[-1]),
            bias_ref[block],
            prompt_kv_ref,
            answer_kv_ref,
        )
        queries_ref[block] = queries
        mixture_ref[block] = mixture
        for place, rows, log_row in logs:
            for head in range(heads):
                log_ref[block, head : head + 1, place] = log_row[
                    :, head * rows : (head + 1) * rows
                ]
        hidden_ref[...] += transposed_product(mixture, held[:, 1].reshape(-1, held.shape[-1]))

    scaled, _ = norm_stats(hidden_ref[...])
    second_ref[...] = (scaled * gain_ref[...] + shift_ref[...]).astype(jnp.bfloat16)
    for each in (*to_x, *to_y, *to_chip, x_to_y, y_to_x, x_to_chip, y_to_chip, *corner_to_chip):
        each.wait_send()
    for each in keep:
        each.wait()


def gather_attention(
    owning,
    projections,
    normed,
    query_offset,
    prompt_kv,
    answer_kv,
    states,
    output_offset,
    gain,
    shift,
    prompts,
    answers,
    prompt_rows,
    call_number,
):
    token_rows, model_width = normed.shape
    block = projections.shape[3]
    heads = block // HEAD_WIDTH
    inside = pl.BlockSpec(memory_space=pltpu.VMEM)
    anywhere = pl.BlockSpec(memory_space=pl.ANY)
    dma = pltpu.SemaphoreType.DMA
    by_step = jax.ShapeDtypeStruct((8, token_rows, block), jnp.bfloat16)
    return pl.pallas_call(
        functools.partial(gather_attention_kernel, prompts, answers, heads, prompt_rows),
        out_shape=(
            jax.ShapeDtypeStruct((8,) + projections.shape, jnp.bfloat16),
            by_step,
            by_step,
            jax.ShapeDtypeStruct((8, heads, token_rows), jnp.float32),
            jax.ShapeDtypeStruct((token_rows, model_width), jnp.float32),
            jax.ShapeDtypeStruct((token_rows, model_width), jnp.bfloat16),
        ),
        in_specs=[pl.BlockSpec(memory_space=pltpu.SMEM), anywhere] + [inside] * 8,
        out_specs=(anywhere,) + (inside,) * 5,
        scratch_shapes=[
            pltpu.VMEM(projections.shape, jnp.bfloat16),
            dma((11,)),
            dma((11,)),
            dma,
            dma,
        ],
        compiler_params=pltpu.CompilerParams(
            collective_id=call_number, has_side_effects=True, vmem_limit_bytes=VMEM_BYTES
        ),
        cost_estimate=pl.CostEstimate(
            flops=64 * token_rows * model_width * block,
            bytes_accessed=250 * 1000 * 1000,
            transcendentals=0,
        ),
        name="gather_attention",
    )(
        owning,
        projections,
        normed,
        query_offset.reshape(8, 1, block),
        prompt_kv,
        answer_kv,
        states,
        output_offset.reshape(1, -1),
        gain.reshape(1, -1),
        shift.reshape(1, -1),
    )


def backward_block(
    prompts,
    answers,
    heads,
    start,
    owner_ref,
    share_ref,
    normed_ref,
    branch_ref,
    query_block,
    output_block,
    queries,
    mixture,
    log_ref,
    prompt_kv_ref,
    answer_kv_ref,
    normed_across,
    key_sums,
    own_sums,
    grad_normed_ref,
):
    width = HEAD_WIDTH
    scale = HEAD_WIDTH ** (-0.5)
    length = prompt_kv_ref.shape[1]
    grad_mixture = plain_product(branch_ref[...], output_block).astype(jnp.bfloat16)

    def backward(keys, values, stacked, grad_stacked, log_row, inner_row, allowed):
        scores = transposed_product(keys, stacked)
        probs = jnp.exp(scores * scale - log_row)
        if allowed is not None:
            probs = jnp.where(allowed, probs, 0.0)
        grad_values = plain_product(probs.astype(jnp.bfloat16), grad_stacked)
        grad_probs = transposed_product(values, grad_stacked)
        grad_scores = (probs * (grad_probs - inner_row)).astype(jnp.bfloat16)
        grad_keys = plain_product(grad_scores, stacked)
        grad_queries = weight_product(grad_scores, keys)
        return grad_queries, grad_keys, grad_values

    pieces = []
    for part in range(prompts + answers):
        here, rows = part_rows(part, prompts, answers, normed_ref, answer_kv_ref)
        token = lax.broadcasted_iota(jnp.int32, (1, heads * rows), 1) % rows
        stacked = stack_heads(queries[here, :], heads)
        grad_stacked = stack_heads(grad_mixture[here, :], heads)
        mixed = stack_heads(mixture[here, :], heads)
        product = grad_stacked.astype(jnp.float32) * mixed.astype(jnp.float32)
        inner_row = jnp.sum(jnp.transpose(product), axis=0, keepdims=True)
        log_row = jnp.concatenate([log_ref[head : head + 1, here] for head in range(heads)], axis=1)
        if part < prompts:
            place = lax.broadcasted_iota(jnp.int32, (length, 1), 0)
            grad_queries, grad_keys, grad_values = backward(
                prompt_kv_ref[part, :, :width],
                prompt_kv_ref[part, :, width:],
                stacked,
                grad_stacked,
                log_row,
                inner_row,
                place <= start + token,
            )
            key_sums[part, :, :width] += grad_keys
            key_sums[part, :, width:] += grad_values
        else:
            answer = part - prompts
            owner = owner_ref[answer]
            own = slice(answer * rows, (answer + 1) * rows)
            grad_queries, grad_keys, grad_values = backward(
                prompt_kv_ref[owner, :, :width],
                prompt_kv_ref[owner, :, width:],
                stacked,
                grad_stacked,
                log_row,
                inner_row,
                None,
            )
            for prompt in range(prompts):
                share = share_ref[answer * prompts + prompt]
                key_sums[prompt, :, :width] += share * grad_keys
                key_sums[prompt, :, width:] += share * grad_values
            place = lax.broadcasted_iota(jnp.int32, (rows, 1), 0)
            own_queries, own_keys, own_values = backward(
                answer_kv_ref[own, :width],
                answer_kv_ref[own, width:],
                stacked,
                grad_stacked,
                log_row,
                inner_row,
                place <= token,
            )
            grad_queries = grad_queries + own_queries
            own_sums[own, :width] += own_keys
            own_sums[own, width:] += own_values
        pieces.append(unstack_heads((grad_queries * scale).astype(jnp.bfloat16), heads))
    grad_queries = jnp.concatenate(pieces, axis=0)
    grad_query_block = plain_product(normed_across[...], grad_queries).astype(jnp.bfloat16)
    grad_normed_ref[...] += transposed_product(grad_queries, query_block)
    grad_bias = jnp.sum(grad_queries.astype(jnp.float32), axis=0, keepdims=True)
    return grad_query_block, grad_bias


def attention_backward_kernel(
    prompts,
    answers,
    heads,
    place_ref,
    owner_ref,
    share_ref,
    normed_ref,
    query_ref,
    prompt_kv_ref,
    answer_kv_ref,
    output_ref,
    branch_ref,
    queries_ref,
    mixture_ref,
    log_ref,
    grad_weights_ref,
    grad_normed_ref,
    grad_prompt_ref,
    grad_answer_ref,
    grad_bias_ref,
    normed_across,
    branch_across,
    key_sums,
    own_sums,
):
    step = pl.program_id(0)
    width = HEAD_WIDTH
    scale = HEAD_WIDTH ** (-0.5)
    block = queries_ref.shape[2]

    @pl.when(step == 0)
    def _():
        normed_across[...] = jnp.transpose(normed_ref[...])
        branch_across[...] = jnp.transpose(branch_ref[...])
        key_sums[...] = jnp.zeros_like(key_sums)
        own_sums[...] = jnp.zeros_like(own_sums)
        grad_normed_ref[...] = jnp.zeros_like(grad_normed_ref)

    query_block, output_block = query_ref[0, 0], output_ref[0, 0]
    groups = grad_weights_ref.shape[1]
    weight_rows = query_block.shape[0] // groups
    grad_output_block = plain_product(branch_across[...], mixture_ref[0]).astype(jnp.bfloat16)
    grad_query_block, grad_bias = backward_block(
        prompts,
        answers,
        heads,
        place_ref[0],
        owner_ref,
        share_ref,
        normed_ref,
        branch_ref,
        query_block,
        output_block,
        queries_ref[0],
        mixture_ref[0],
        log_ref.at[0],
        prompt_kv_ref,
        answer_kv_ref,
        normed_across,
        key_sums,
        own_sums,
        grad_normed_ref,
    )
    grad_weights_ref[0, :, :weight_rows] = grad_query_block.reshape(groups, weight_rows, block)
    grad_weights_ref[0, :, weight_rows : 2 * weight_rows] = grad_output_block.reshape(
        groups, weight_rows, block
    )
    grad_bias_ref[0] = grad_bias

    @pl.when(step == pl.num_programs(0) - 1)
    def _():
        grad_prompt_ref[:, :, :width] = (key_sums[:, :, :width] * scale).astype(jnp.bfloat16)
        grad_prompt_ref[:, :, width:] = key_sums[:, :, width:].astype(jnp.bfloat16)
        grad_answer_ref[:, :width] = own_sums[:, :width] * scale
        grad_answer_ref[:, width:] = own_sums[:, width:]


def attention_backward(
    place,
    owning,
    share,
    normed,
    weights,
    groups,
    grad_rows,
    prompt_kv,
    answer_kv,
    branch,
    queries,
    mixture,
    log_total,
    prompts,
    answers,
):
    token_rows, model_width = normed.shape
    steps, _, _, block = weights.shape
    heads = block // HEAD_WIDTH
    length = prompt_kv.shape[1]
    whole = lambda *shape: pl.BlockSpec(shape, lambda step, *_: (0,) * len(shape))
    columns = lambda: pl.BlockSpec((1, token_rows, block), lambda step, *_: (step, 0, 0))
    kind = lambda which: pl.BlockSpec(
        (1, 1, model_width, block), lambda step, *_: (step, which, 0, 0)
    )
    scores = heads * token_rows * length
    return pl.pallas_call(
        functools.partial(
            attention_backward_kernel, prompts, answers, heads
        ),
        out_shape=(
            jax.ShapeDtypeStruct((steps, groups, grad_rows, block), jnp.bfloat16),
            jax.ShapeDtypeStruct((token_rows, model_width), jnp.float32),
            jax.ShapeDtypeStruct(prompt_kv.shape, jnp.bfloat16),
            jax.ShapeDtypeStruct(answer_kv.shape, jnp.float32),
            jax.ShapeDtypeStruct((steps, 1, block), jnp.float32),
        ),
        grid_spec=pltpu.PrefetchScalarGridSpec(
            num_scalar_prefetch=3,
            grid=(steps,),
            in_specs=[
                whole(token_rows, model_width),
                kind(0),
                whole(*prompt_kv.shape),
                whole(*answer_kv.shape),
                kind(1),
                whole(token_rows, model_width),
                columns(),
                columns(),
                pl.BlockSpec((1, heads, token_rows), lambda step, *_: (step, 0, 0)),
            ],
            out_specs=(
                pl.BlockSpec(
                    (1, groups, grad_rows, block), lambda step, *_: (step, 0, 0, 0)
                ),
                whole(token_rows, model_width),
                whole(*prompt_kv.shape),
                whole(*answer_kv.shape),
                pl.BlockSpec((1, 1, block), lambda step, *_: (step, 0, 0)),
            ),
            scratch_shapes=[
                pltpu.VMEM((model_width, token_rows), jnp.bfloat16),
                pltpu.VMEM((model_width, token_rows), jnp.bfloat16),
                pltpu.VMEM(prompt_kv.shape, jnp.float32),
                pltpu.VMEM(answer_kv.shape, jnp.float32),
            ],
        ),
        compiler_params=pltpu.CompilerParams(vmem_limit_bytes=VMEM_BYTES),
        cost_estimate=pl.CostEstimate(
            flops=steps * (8 * token_rows * model_width * block + 20 * scores * HEAD_WIDTH),
            bytes_accessed=16 * steps * model_width * block,
            transcendentals=steps * scores,
        ),
        name="attention_backward",
    )(
        place,
        owning,
        share,
        normed,
        weights,
        prompt_kv,
        answer_kv,
        weights,
        branch,
        queries,
        mixture,
        log_total,
    )


class PairedSum:
    def __init__(self, part, pair, sent, come, send_sem, recv_sem):
        here, on_x, on_y, on_chip, corner = block_of_eight()
        shift = on_chip - here
        self.places = (here, on_x, on_y, corner)
        self.part, self.pair, self.sent, self.come = part, pair, sent, come
        self.to_chip = [
            remote(index, part(place + shift), pair.at[index], on_chip, send_sem, recv_sem)
            for index, place in enumerate(self.places)
        ]
        self.over = [
            remote(3 + index, sent.at[index], come.at[index - 1], place, send_sem, recv_sem)
            for index, place in enumerate(self.places)
            if index
        ]

    def start(self):
        for each in self.to_chip:
            each.start()

    def pass_on(self):
        for each in self.to_chip:
            each.wait_recv()
        for index, place in enumerate(self.places):
            total = self.part(place)[...].astype(jnp.float32)
            total = total + self.pair[index].astype(jnp.float32)
            self.sent[index] = total.astype(self.sent.dtype)
        for each in self.over:
            each.start()

    def total(self):
        total = self.sent[0].astype(jnp.float32)
        for index, each in enumerate(self.over):
            each.wait_recv()
            total = total + self.come[index].astype(jnp.float32)
        return total

    def finish(self):
        for each in self.to_chip + self.over:
            each.wait_send()


VECTOR_ROWS = 16


def backward_reduce_kernel(
    prompts,
    answers,
    heads,
    groups,
    prompt_rows,
    owner_ref,
    share_ref,
    weights_ref,
    queries_ref,
    mixture_ref,
    hidden_hbm,
    normed_ref,
    branch_ref,
    log_ref,
    prompt_kv_ref,
    answer_kv_ref,
    states_ref,
    gain_ref,
    keyval_ref,
    known_up_ref,
    known_sums_ref,
    known_columns_ref,
    known_squares_ref,
    grad_query_ref,
    grad_output_ref,
    grad_keyval_ref,
    vectors_ref,
    own_vectors_ref,
    own_up_ref,
    grad_prompt_ref,
    grad_answer_ref,
    normed_across,
    branch_across,
    key_sums,
    own_sums,
    grad_normed,
    grad_hidden,
    held,
    pair,
    early,
    kept,
    theirs,
    relayed,
    final,
    come,
    kv_part,
    kv_pair,
    kv_sent,
    kv_come,
    kv_rows,
    keyval_part,
    keyval_pair,
    keyval_sent,
    keyval_come,
    keyval_sum,
    keyval_over,
    vectors,
    vector_come,
    vector_sum,
    vector_over,
    row_sums,
    send_sem,
    recv_sem,
    over_send,
    over_recv,
    peer_send,
    peer_recv,
    load_sem,
    early_sem,
    hidden_sem,
):
    width = HEAD_WIDTH
    scale = HEAD_WIDTH ** (-0.5)
    here, on_x, on_y, on_chip, corner = block_of_eight()
    _, peers = peers_of(8)
    group = lax.axis_index("grp")
    other_groups = [(group + turn) % groups for turn in range(1, groups)]
    model_width, block = kept.shape[1:]
    chunk_rows = model_width // groups
    step = 64
    counter = iter(range(8 + 6 * groups))

    def copy(source, target, device):
        return remote(next(counter), source, target, device, send_sem, recv_sem)

    def over(index, source, target, other):
        return pltpu.make_async_remote_copy(
            src_ref=source,
            dst_ref=target,
            send_sem=over_send.at[index],
            recv_sem=over_recv.at[index],
            device_id={"grp": other},
            device_id_type=MESH,
        )

    def to_peers(row, source, target):
        return [
            pltpu.make_async_remote_copy(
                src_ref=source(peers[index]),
                dst_ref=target(index),
                send_sem=peer_send.at[row, index],
                recv_sem=peer_recv.at[row, index],
                device_id={"tok": peers[index]},
                device_id_type=MESH,
            )
            for index in range(len(peers))
        ]

    beside, beyond = group + 1 - 2 * (group % 2), (group + 2) % groups
    spans = [
        pl.ds(pl.multiple_of(owner * chunk_rows, chunk_rows), chunk_rows)
        for owner in ((beside + 2) % groups, beside, beyond, group)
    ]
    chunks = range(groups)
    by_x, by_y = chunks[: groups // 2], chunks[groups // 2 :]
    kinds = (0, 1)

    def mine(place, kind):
        return kept.at[4 + 2 * place + kind]

    def pieces_to(place, target, device):
        return [
            [copy(mine(place, kind).at[span], target(kind).at[span], device) for span in spans]
            for kind in kinds
        ]

    to_chip = [
        [copy(kept.at[place], theirs.at[place, kind], on_chip) for place in range(4)]
        for kind in kinds
    ]
    corners = [
        [
            copy(
                mine(0, kind).at[spans[chunk]],
                relayed.at[kind, spans[chunk]],
                on_x if chunk in by_x else on_y,
            )
            for chunk in chunks
        ]
        for kind in kinds
    ]
    to_x = pieces_to(2, lambda kind: final.at[0, kind], on_x)
    to_y = pieces_to(1, lambda kind: final.at[1, kind], on_y)
    across = [
        [
            over(2 * turn + kind, mine(3, kind).at[spans[turn]], come.at[turn, kind], other)
            for kind in kinds
        ]
        for turn, other in enumerate((beside, beside, beyond))
    ]

    def lanes(device):
        return pl.ds(pl.multiple_of(device * block, block), block)

    def prompt_place(device):
        return pl.ds(pl.multiple_of(device * prompt_rows, prompt_rows), prompt_rows)

    kv_sums = PairedSum(
        lambda device: kv_part.at[:, prompt_place(device), :],
        kv_pair,
        kv_sent,
        kv_come,
        peer_send.at[0],
        peer_recv.at[0],
    )
    keyval_sums = PairedSum(
        lambda device: keyval_part.at[:, device],
        keyval_pair,
        keyval_sent,
        keyval_come,
        peer_send.at[1],
        peer_recv.at[1],
    )
    vector_copies = to_peers(
        2, lambda peer: vectors.at[:, lanes(peer)], lambda index: vector_come.at[index]
    )
    vector_out = to_peers(
        3, lambda peer: vector_sum, lambda index: vectors_ref.at[:, lanes(here)]
    )
    first_over = 2 * (groups - 1)
    keyval_across = [
        over(first_over + turn, keyval_sum.at[other_groups[turn]], keyval_over.at[turn], other_groups[turn])
        for turn in range(groups - 1)
    ]
    vector_across = [
        over(
            first_over + groups - 1 + turn,
            vectors.at[:, lanes(here)],
            vector_over.at[turn],
            other_groups[turn],
        )
        for turn in range(groups - 1)
    ]

    def fetch(turn):
        source, slot = bits_away(7 - turn), turn % 2
        return (
            pltpu.make_async_copy(weights_ref.at[source], held.at[slot], load_sem.at[slot, 0]),
            pltpu.make_async_copy(queries_ref.at[source], pair.at[slot, 0], load_sem.at[slot, 1]),
            pltpu.make_async_copy(mixture_ref.at[source], pair.at[slot, 1], load_sem.at[slot, 2]),
        )

    def fetch_early(turn):
        return pltpu.make_async_copy(
            mixture_ref.at[bits_away(7 - turn)], early.at[turn % 2], early_sem.at[turn % 2]
        )

    fetch_early(0).start()
    load_hidden = pltpu.make_async_copy(hidden_hbm, grad_hidden, hidden_sem)
    load_hidden.start()
    for each in fetch(0):
        each.start()
    greet_all(peers, other_groups)
    normed_across[...] = jnp.transpose(normed_ref[...])
    branch_across[...] = jnp.transpose(branch_ref[...])
    key_sums[...] = jnp.zeros_like(key_sums)
    own_sums[...] = jnp.zeros_like(own_sums)
    grad_normed[...] = jnp.zeros_like(grad_normed)
    vectors[...] = jnp.zeros_like(vectors)
    row_sums[...] = jnp.zeros_like(row_sums)
    vectors[: known_up_ref.shape[0], :] = known_up_ref[...]
    vectors[4:7, :] = known_sums_ref[0:3, :]
    vectors[7:8, :] = jnp.sum(known_columns_ref[...], axis=0, keepdims=True)
    squares = jnp.sum(known_squares_ref[...], axis=0, keepdims=True)
    squares = jnp.sum(squares, axis=1, keepdims=True)
    vectors[12:13, :] = jnp.broadcast_to(squares, (1, model_width))

    def add_into(target, other, rows):
        @pl.loop(0, rows // step)
        def _(turn):
            at = chunk_of(turn, step)
            target[at, :] = target[at, :] + other[at, :]

    def join(kind, place):
        to_chip[kind][place].wait_recv()
        add_into(mine(place, kind), theirs.at[place, kind], model_width)

    def direct(kind, chunk):
        (to_x if chunk in by_x else to_y)[kind][chunk].start()

    def relay(kind, chunk):
        corners[kind][chunk].wait_recv()
        place, then = (1, to_y) if chunk in by_x else (2, to_x)
        span = spans[chunk]
        add_into(mine(place, kind).at[span], relayed.at[kind, span], chunk_rows)
        then[kind][chunk].start()

    def close(kind, chunk):
        span = spans[chunk]
        for source, part in enumerate((to_x, to_y)):
            part[kind][chunk].wait_recv()
            add_into(mine(3, kind).at[span], final.at[source, kind, span], chunk_rows)
        if chunk < 2:
            across[chunk][kind].start()

    def hand_on(kind):
        across[0][kind].wait_recv()
        add_into(mine(3, kind).at[spans[2]], come.at[0, kind], chunk_rows)
        across[2][kind].start()

    def slot_of(turn, kind):
        place = turn // 2
        return (1 - turn % 2) * place + (turn % 2) * (4 + 2 * place + kind)

    def send_to_chip(turn, kind):
        for place in range(4):

            @pl.when(turn == 2 * place)
            def _():
                to_chip[kind][place].start()

    @pl.loop(0, 8)
    def _(turn):
        @pl.when(turn < 7)
        def _():
            fetch_early(turn + 1).start()

        fetch_early(turn).wait()
        kept[slot_of(turn, 1)] = plain_product(
            branch_across[...], early[turn % 2]
        ).astype(jnp.bfloat16)
        send_to_chip(turn, 1)

        @pl.when(turn == 2)
        def _():
            join(1, 0)
            for chunk in chunks:
                corners[1][chunk].start()

        for place in (1, 2):

            @pl.when(turn == 2 * place + 2)
            def _():
                join(1, place)

    for chunk in chunks:
        direct(1, chunk)

    @pl.loop(0, 8)
    def _(turn):
        source, now = bits_away(7 - turn), turn % 2

        @pl.when(turn < 7)
        def _():
            for each in fetch(turn + 1):
                each.start()

        for place in range(4):

            @pl.when(turn == 2 * place)
            def _():
                to_chip[1][place].wait_send()

        for each in fetch(turn):
            each.wait()
        grad_query_block, grad_bias = backward_block(
            prompts,
            answers,
            heads,
            here * prompt_rows,
            owner_ref,
            share_ref,
            normed_ref,
            branch_ref,
            held[now, :, 0].reshape(-1, block),
            held[now, :, 1].reshape(-1, block),
            pair[now, 0],
            pair[now, 1],
            log_ref.at[source],
            prompt_kv_ref,
            answer_kv_ref,
            normed_across,
            key_sums,
            own_sums,
            grad_normed,
        )
        kept[slot_of(turn, 0)] = grad_query_block
        vectors[10:11, lanes(source)] = grad_bias
        send_to_chip(turn, 0)

        @pl.when(turn == 1)
        def _():
            for chunk in chunks:
                relay(1, chunk)

        @pl.when(turn == 2)
        def _():
            join(0, 0)
            for chunk in chunks:
                corners[0][chunk].start()

        @pl.when(turn == 4)
        def _():
            join(0, 1)
            join(1, 3)

        @pl.when(turn == 5)
        def _():
            for chunk in chunks:
                close(1, chunk)

        @pl.when(turn == 6)
        def _():
            join(0, 2)
            for chunk in by_x:
                direct(0, chunk)
            for chunk in by_x:
                relay(0, chunk)

        @pl.when(turn == 7)
        def _():
            direct(0, by_y[0])
            relay(0, by_y[0])

    kv_part[:, :, :width] = (key_sums[:, :, :width] * scale).astype(jnp.bfloat16)
    kv_part[:, :, width:] = key_sums[:, :, width:].astype(jnp.bfloat16)
    kv_sums.start()
    join(0, 3)
    kv_sums.pass_on()
    for part in (to_x, to_y):
        part[0][by_x[0]].wait_send()
    direct(0, by_y[1])
    relay(0, by_y[1])

    own_prompt = prompts * prompt_rows
    total = kv_sums.total()
    for prompt in range(prompts):
        kv_rows[prompt * prompt_rows : (prompt + 1) * prompt_rows, :] = total[prompt].astype(
            jnp.bfloat16
        )
    kv_rows[own_prompt:, :width] = (own_sums[:, :width] * scale).astype(jnp.bfloat16)
    kv_rows[own_prompt:, width:] = own_sums[:, width:].astype(jnp.bfloat16)
    keyval_part[...] = (
        plain_product(normed_across[...], kv_rows[...])
        .astype(jnp.bfloat16)
        .reshape(keyval_part.shape)
    )
    keyval_sums.start()
    close(0, by_x[0])
    load_hidden.wait()
    vectors[11:12, :width] = jnp.sum(
        kv_rows[:, width:].astype(jnp.float32), axis=0, keepdims=True
    )
    piece = 16
    grad_normed[...] += transposed_product(kv_rows[...], keyval_ref[...])

    start = 0
    for out_ref in (grad_prompt_ref, grad_answer_ref):

        @pl.loop(0, out_ref.shape[0] // piece)
        def _(turn):
            at = pl.ds(pl.multiple_of(start + turn * piece, piece), piece)
            scaled, inverse = norm_stats(states_ref[at, :].astype(jnp.float32))
            grad_out = grad_normed[at, :]
            weighted = grad_out * gain_ref[...]
            grad_in = inverse * (
                weighted
                - jnp.mean(weighted, axis=-1, keepdims=True)
                - scaled * jnp.mean(weighted * scaled, axis=-1, keepdims=True)
            )
            out_ref[chunk_of(turn, piece), :] = (grad_hidden[at, :] + grad_in).astype(jnp.bfloat16)
            by_gain = grad_out * scaled
            row_sums[:8, :] += by_gain[:8, :] + by_gain[8:, :]
            row_sums[8:, :] += grad_out[:8, :] + grad_out[8:, :]

        start += out_ref.shape[0]

    vectors[8:9, :] = jnp.sum(row_sums[:8, :], axis=0, keepdims=True)
    vectors[9:10, :] = jnp.sum(row_sums[8:, :], axis=0, keepdims=True)
    for each in vector_copies:
        each.start()
    close(0, by_x[1])
    hand_on(1)
    keyval_sums.pass_on()
    close(0, by_y[0])
    for each in vector_copies:
        each.wait_recv()
    total = vectors[:, lanes(here)]
    for index in range(len(peers)):
        total = total + vector_come[index]
    vectors[:, lanes(here)] = total
    for each in vector_across:
        each.start()
    keyval_sum[...] = keyval_sums.total().astype(jnp.bfloat16)
    for each in keyval_across:
        each.start()
    hand_on(0)
    for each in vector_across:
        each.wait_recv()
    total = vectors[:, lanes(here)]
    for turn in range(groups - 1):
        total = total + vector_over[turn]
    vector_sum[...] = total
    for each in vector_out:
        each.start()
    vectors_ref[:, lanes(here)] = vector_sum[...]
    close(0, by_y[1])
    for each in keyval_across:
        each.wait_recv()
    total = keyval_sum[group].astype(jnp.float32)
    for turn in range(groups - 1):
        total = total + keyval_over[turn].astype(jnp.float32)
    grad_keyval_ref[...] = total
    for kind, out_ref in ((0, grad_query_ref), (1, grad_output_ref)):
        for turn in (1, 2):
            across[turn][kind].wait_recv()
        own = pl.multiple_of(group * chunk_rows, chunk_rows)

        @pl.loop(0, chunk_rows // step)
        def _(turn):
            at = chunk_of(turn, step)
            total = kept[10 + kind, pl.ds(own + turn * step, step), :].astype(jnp.float32)
            for other in (1, 2):
                total = total + come[other, kind, at, :].astype(jnp.float32)
            out_ref[at, :] = total

    for each in vector_out:
        each.wait_recv()
    device = group * 8 + here
    share = model_width // (8 * groups)
    parts = width // share
    columns = vectors_ref[:, chunk_of(device // parts, width)]
    picked = columns
    for part in range(1, parts):
        moved = jnp.concatenate([columns[:, part * share :], columns[:, : part * share]], axis=1)
        picked = jnp.where(device % parts == part, moved, picked)
    own_vectors_ref[...] = picked
    up_share = own_up_ref.shape[1]
    in_row = model_width // up_share
    up_columns = vectors_ref[:, chunk_of(device % in_row, up_share)]
    up_own = jnp.zeros((1, up_share), jnp.float32)
    for row in range(known_up_ref.shape[0]):
        up_own = jnp.where(device // in_row == row, up_columns[row : row + 1, :], up_own)
    own_up_ref[...] = up_own
    for each in to_chip[0] + corners[0] + corners[1] + to_x[1] + to_y[1]:
        each.wait_send()
    for chunk in chunks[1:]:
        to_x[0][chunk].wait_send()
        to_y[0][chunk].wait_send()
    kv_sums.finish()
    keyval_sums.finish()
    for each in vector_copies + vector_out:
        each.wait_send()
    for each in sum(across, []) + keyval_across + vector_across:
        each.wait_send()


def backward_reduce(
    owning,
    share,
    weights,
    queries,
    mixture,
    grad_hidden,
    normed,
    branch,
    log_total,
    prompt_kv,
    answer_kv,
    states,
    gain,
    keyval_full,
    known_up,
    known_sums,
    known_columns,
    known_squares,
    groups,
    prompts,
    answers,
    prompt_rows,
    call_number,
):
    token_rows, model_width = normed.shape
    block = weights.shape[4]
    heads = block // HEAD_WIDTH
    keyval_width = keyval_full.shape[1]
    weight_rows = model_width // groups
    keyval_rows = model_width // groups // 8
    kind, wide = jnp.bfloat16, jnp.float32
    inside = pl.BlockSpec(memory_space=pltpu.VMEM)
    anywhere = pl.BlockSpec(memory_space=pl.ANY)
    scalars = pl.BlockSpec(memory_space=pltpu.SMEM)
    dma = pltpu.SemaphoreType.DMA
    others = groups - 1
    return pl.pallas_call(
        functools.partial(backward_reduce_kernel, prompts, answers, heads, groups, prompt_rows),
        out_shape=(
            jax.ShapeDtypeStruct((weight_rows, block), wide),
            jax.ShapeDtypeStruct((weight_rows, block), wide),
            jax.ShapeDtypeStruct((keyval_rows, keyval_width), wide),
            jax.ShapeDtypeStruct((VECTOR_ROWS, model_width), wide),
            jax.ShapeDtypeStruct((VECTOR_ROWS, HEAD_WIDTH), wide),
            jax.ShapeDtypeStruct((1, known_up.size // (8 * groups)), wide),
            jax.ShapeDtypeStruct((prompts * prompt_rows, model_width), kind),
            jax.ShapeDtypeStruct((token_rows - prompts * prompt_rows, model_width), kind),
        ),
        in_specs=[scalars] * 2 + [anywhere] * 4 + [inside] * 12,
        out_specs=(inside,) * 8,
        scratch_shapes=[
            pltpu.VMEM((model_width, token_rows), kind),
            pltpu.VMEM((model_width, token_rows), kind),
            pltpu.VMEM(prompt_kv.shape, wide),
            pltpu.VMEM(answer_kv.shape, wide),
            pltpu.VMEM((token_rows, model_width), wide),
            pltpu.VMEM((token_rows, model_width), wide),
            pltpu.VMEM((2,) + weights.shape[1:], kind),
            pltpu.VMEM((2, 2, token_rows, block), kind),
            pltpu.VMEM((2, token_rows, block), kind),
            pltpu.VMEM((12, model_width, block), kind),
            pltpu.VMEM((4, 2, model_width, block), kind),
            pltpu.VMEM((2, model_width, block), kind),
            pltpu.VMEM((2, 2, model_width, block), kind),
            pltpu.VMEM((others, 2, weight_rows, block), kind),
            pltpu.VMEM(prompt_kv.shape, kind),
            pltpu.VMEM((4, prompts, prompt_rows, keyval_width), kind),
            pltpu.VMEM((4, prompts, prompt_rows, keyval_width), kind),
            pltpu.VMEM((3, prompts, prompt_rows, keyval_width), kind),
            pltpu.VMEM((token_rows, keyval_width), kind),
            pltpu.VMEM((groups, 8, keyval_rows, keyval_width), kind),
            pltpu.VMEM((4, groups, keyval_rows, keyval_width), kind),
            pltpu.VMEM((4, groups, keyval_rows, keyval_width), kind),
            pltpu.VMEM((3, groups, keyval_rows, keyval_width), kind),
            pltpu.VMEM((groups, keyval_rows, keyval_width), kind),
            pltpu.VMEM((others, keyval_rows, keyval_width), kind),
            pltpu.VMEM((VECTOR_ROWS, model_width), wide),
            pltpu.VMEM((7, VECTOR_ROWS, block), wide),
            pltpu.VMEM((VECTOR_ROWS, block), wide),
            pltpu.VMEM((others, VECTOR_ROWS, block), wide),
            pltpu.VMEM((16, model_width), wide),
            dma((8 + 6 * groups,)),
            dma((8 + 6 * groups,)),
            dma((4 * others,)),
            dma((4 * others,)),
            dma((4, 7)),
            dma((4, 7)),
            dma((2, 3)),
            dma((2,)),
            dma,
        ],
        compiler_params=pltpu.CompilerParams(
            collective_id=call_number,
            has_side_effects=True,
            vmem_limit_bytes=63 * 1024 * 1024,
        ),
        cost_estimate=pl.CostEstimate(
            flops=100 * token_rows * model_width * block,
            bytes_accessed=250 * 1000 * 1000,
            transcendentals=0,
        ),
        name="backward_reduce",
    )(
        owning,
        share,
        weights,
        queries,
        mixture,
        grad_hidden,
        normed,
        branch,
        log_total,
        prompt_kv,
        answer_kv,
        states,
        gain.reshape(1, -1),
        keyval_full,
        known_up,
        known_sums,
        known_columns,
        known_squares,
    )


def finish_kernel(share_size, model_width, *refs):
    half = len(refs) - 17
    (
        vectors_ref,
        own_vectors_ref,
        own_up_ref,
        count_ref,
        prompt_ref,
        answer_ref,
        query_ref,
        output_ref,
        keyval_ref,
        up_ref,
        down_ref,
    ) = refs[:half]
    prompt_out, answer_out, query_out, output_out, keyval_out, up_out, down_out, *outs = refs[half:]
    prompt_out[...] = prompt_ref[...]
    answer_out[...] = answer_ref[...]
    query_out[...] = query_ref[...]
    output_out[...] = output_ref[...]
    keyval_out[...] = keyval_ref[...]
    up_out[...] = up_ref[...].astype(jnp.float32)
    down_out[...] = down_ref[...].astype(jnp.float32)
    *vector_outs, up_bias_out, value_out, loss_out = outs
    for row, out_ref in zip((8, 9, 10, 4, 5, 6, 7), vector_outs):
        out_ref[...] = own_vectors_ref[row : row + 1, :share_size]
    up_bias_out[...] = own_up_ref[...]
    value_out[...] = vectors_ref[11:12, :HEAD_WIDTH]
    loss_out[...] = vectors_ref[12:13, :1] / (count_ref[...] * model_width)


def finish(share_size, vectors, own_vectors, own_up, valid_count, *arrays):
    wide = jnp.float32
    model_width = vectors.shape[1]
    kinds = [array.dtype for array in arrays[:5]] + [wide, wide]
    shapes = [jax.ShapeDtypeStruct(array.shape, kind) for array, kind in zip(arrays, kinds)]
    shapes += [jax.ShapeDtypeStruct((1, share_size), wide)] * 7
    shapes += [
        jax.ShapeDtypeStruct(own_up.shape, wide),
        jax.ShapeDtypeStruct((1, HEAD_WIDTH), wide),
        jax.ShapeDtypeStruct((1, 1), wide),
    ]
    inside = pl.BlockSpec(memory_space=pltpu.VMEM)
    return pl.pallas_call(
        functools.partial(finish_kernel, share_size, model_width),
        out_shape=tuple(shapes),
        in_specs=[inside] * (4 + len(arrays)),
        out_specs=(inside,) * len(shapes),
        compiler_params=pltpu.CompilerParams(vmem_limit_bytes=VMEM_BYTES),
        name="finish",
    )(vectors, own_vectors, own_up, valid_count.reshape(1, 1), *arrays)


def by_group(values):
    return jnp.swapaxes(values, 0, 1).reshape(-1)


def body(
    kernels,
    prompt_states,
    answer_states,
    answer_prompt,
    prompt_teacher,
    answer_teacher,
    prompt_valid,
    answer_valid,
    first_gain,
    first_shift,
    query_weight,
    query_bias,
    keyval_weight,
    value_bias,
    output_weight,
    output_bias,
    second_gain,
    second_shift,
    up_weight,
    up_bias,
    down_weight,
    down_bias,
):
    prompt_count, prompt_rows, model_width = prompt_states.shape
    answer_count, answer_len, _ = answer_states.shape
    groups = lax.axis_size("grp")
    token_devices = lax.axis_size("tok")
    token_index = lax.axis_index("tok")
    group_index = lax.axis_index("grp")
    own_prompt = prompt_rows * prompt_count
    token_rows = own_prompt + answer_count * answer_len
    hidden_units = up_bias.shape[0] * groups * token_devices
    ff_here = hidden_units // token_devices
    ff_start = token_index * ff_here
    share_size = first_gain.shape[0]
    block = query_weight.shape[1]
    weight_rows = query_weight.shape[0]
    keyval_rows, keyval_width = keyval_weight.shape

    def own_rows(prompt_part, answer_part):
        return jnp.concatenate(
            [prompt_part.reshape(own_prompt, -1), answer_part.reshape(-1, prompt_part.shape[-1])],
            axis=0,
        )

    states = own_rows(prompt_states, answer_states)
    inputs = states.astype(jnp.float32)
    valid_rows = jnp.concatenate([prompt_valid.reshape(-1), answer_valid.reshape(-1)])
    own_count = jnp.sum(valid_rows)
    valid_rows = valid_rows.astype(jnp.float32)

    up_cols = lax.all_gather(up_weight, "grp", axis=0, tiled=True)
    down_cols = lax.all_gather(down_weight, "grp", axis=0, tiled=True)

    projections = lax.all_gather(jnp.stack([query_weight, output_weight]), "grp", axis=0)
    count_parts = jnp.stack([own_count // 128, own_count % 128]).astype(jnp.bfloat16)
    smalls, small_at = jnp.zeros((SMALL_ROWS * block,), jnp.bfloat16), 0
    for each in (
        first_gain,
        first_shift,
        query_bias,
        output_bias,
        second_gain,
        second_shift,
        down_bias,
        up_bias,
        count_parts,
    ):
        behind = SMALL_ROWS * block - small_at - each.shape[0]
        smalls = smalls + jnp.pad(each, (small_at, behind))
        small_at += each.shape[0]
    smalls = smalls.reshape(SMALL_ROWS, block)
    pack = jnp.concatenate([keyval_weight.reshape(-1, block), smalls], axis=0)
    packed = spread(pack, groups, 0, kernels)
    keyval_pack = pack.shape[0] - SMALL_ROWS
    keyval_start = 2 * weight_rows
    keyval_full = jnp.swapaxes(
        packed[:, :, :keyval_pack].reshape(token_devices, groups, keyval_rows, keyval_width),
        0,
        1,
    ).reshape(model_width, keyval_width)
    small_full = packed[:, :, keyval_pack:].reshape(token_devices, groups, SMALL_ROWS * block)
    small_full = jnp.swapaxes(small_full.astype(jnp.float32), 0, 1)

    def vector(start, size):
        return small_full[:, :, start : start + size].reshape(-1)

    gain_one, shift_one, query_offset, output_offset, gain_two, shift_two, down_offset = (
        vector(index * share_size, share_size) for index in range(7)
    )
    up_offset = vector(7 * share_size, up_bias.shape[0])
    count_at = 7 * share_size + up_bias.shape[0]
    counts = small_full[:, :, count_at : count_at + 2]
    valid_count = jnp.sum(counts[:, :, 0]) * 128.0 + jnp.sum(counts[:, :, 1])
    up_here = lax.dynamic_slice_in_dim(up_offset, ff_start, ff_here)

    scaled_one, inverse_one = norm_stats(inputs)
    normed_one = (scaled_one * gain_one + shift_one).astype(jnp.bfloat16)
    key_offset = jnp.concatenate(
        [jnp.zeros((HEAD_WIDTH,), jnp.float32), value_bias.astype(jnp.float32)]
    )
    key_value_rows = (plain_product(normed_one, keyval_full) + key_offset).astype(jnp.bfloat16)
    prompt_kv = tok_gather_small(
        key_value_rows[:own_prompt].reshape(prompt_count, prompt_rows, -1), 1, kernels
    )
    answer_kv = key_value_rows[own_prompt:]
    owning = answer_prompt - group_index * prompt_count
    owning = lax.dynamic_slice_in_dim(owning, token_index * answer_count, answer_count)
    place = jnp.reshape(token_index * prompt_rows, (1,)).astype(jnp.int32)
    if kernels:
        weights, queries, mixture, log_total, hidden, normed_two = gather_attention(
            owning,
            projections,
            normed_one,
            query_offset,
            prompt_kv,
            answer_kv,
            states,
            output_offset,
            gain_two,
            shift_two,
            prompt_count,
            answer_count,
            prompt_rows,
            8,
        )
    else:
        weights = lax.all_gather(projections, "tok", axis=0)
        weights = jnp.swapaxes(weights, 1, 2).reshape(token_devices, 2, model_width, block)
        queries, mixture, log_total, hidden, normed_two = attention_forward(
            place,
            owning,
            normed_one,
            weights[:, 0],
            weights[:, 1],
            query_offset,
            prompt_kv,
            answer_kv,
            states,
            output_offset,
            gain_two,
            shift_two,
            prompt_count,
            answer_count,
        )

    teacher = own_rows(prompt_teacher, answer_teacher)
    every_token = token_rows * groups * token_devices
    factors = (every_token / valid_count * valid_rows)[:, None]
    share = (owning[:, None] == jnp.arange(prompt_count)[None, :]).astype(jnp.float32).reshape(-1)
    if kernels:
        down_row, gain_row, share = lax.optimization_barrier(
            (down_offset.reshape(1, -1), gain_one.reshape(1, -1), share)
        )
        group_two, activated, slope = gather_and_up(normed_two, up_cols, up_here, 2)
        prompt_out, answer_out, grad_branch_two, grad_result, own_squares, grad_down_offset = (
            product_and_reduce(
                activated,
                down_cols,
                None,
                hidden,
                teacher,
                3,
                own_prompt,
                down_row,
                valid_rows[:, None],
                factors,
            )
        )
        _, grad_pre_active, grad_down_cols, grad_up_offset = gather_and_grad(
            grad_branch_two, down_cols, activated, slope, 4
        )
        grad_hidden, grad_up_cols, grad_branch_one, second_sums = product_and_reduce(
            grad_pre_active,
            up_cols,
            group_two,
            hidden,
            grad_result,
            5,
            own_prompt,
            gain_two.reshape(1, -1),
        )
        grad_up_offset = grad_up_offset.reshape(-1)
    else:
        group_two = lax.all_gather(normed_two, "tok", axis=0, tiled=True)
        pre_active = plain_product(group_two, up_cols) + up_here
        activated = jax.nn.gelu(pre_active, approximate=True).astype(jnp.bfloat16)
        feed_term = for_sending(transposed_product(activated, down_cols))
        feed_term = lax.psum_scatter(feed_term, "tok", scatter_dimension=0, tiled=True)
        result_rows = hidden + feed_term.astype(jnp.float32) + down_offset
        prompt_out, answer_out = result_rows[:own_prompt], result_rows[own_prompt:]
        differ = result_rows - teacher.astype(jnp.float32)
        own_squares = jnp.sum(valid_rows[:, None] * differ * differ)
        grad_result = factors * differ
        grad_branch_two = grad_result.astype(jnp.bfloat16)
        grad_down_offset = column_sums(grad_branch_two)
        group_grad_two = lax.all_gather(grad_branch_two, "tok", axis=0, tiled=True)
        grad_activated = plain_product(group_grad_two, down_cols)
        _, gelu_back = jax.vjp(
            lambda argument: jax.nn.gelu(argument, approximate=True), pre_active
        )
        grad_pre_active = gelu_back(grad_activated)[0].astype(jnp.bfloat16)
        grad_normed_two = for_sending(transposed_product(grad_pre_active, up_cols))
        grad_normed_two = lax.psum_scatter(
            grad_normed_two, "tok", scatter_dimension=0, tiled=True
        ).astype(jnp.float32)
        grad_down_cols = for_sending(weight_product(group_grad_two, activated))
        grad_up_cols = for_sending(weight_product(group_two, grad_pre_active))
        grad_up_offset = column_sums(grad_pre_active)
        scaled_two, inverse_two = norm_stats(hidden)
        grad_norm_two, grad_gain_two, grad_shift_two = norm_backward(
            grad_normed_two, gain_two, scaled_two, inverse_two
        )
        grad_hidden = grad_result + grad_norm_two
        grad_branch_one = grad_hidden.astype(jnp.bfloat16)
        grad_output_offset = column_sums(grad_branch_one)
    grad_down_weight = lax.psum_scatter(grad_down_cols, "grp", scatter_dimension=0, tiled=True)
    grad_down_weight, grad_up_cols = lax.optimization_barrier((grad_down_weight, grad_up_cols))
    grad_up_weight = lax.psum_scatter(grad_up_cols, "grp", scatter_dimension=0, tiled=True)

    grad_up_place = lax.dynamic_update_slice_in_dim(
        jnp.zeros((hidden_units,), jnp.float32), grad_up_offset, ff_start, 0
    )
    if kernels:
        (
            grad_query_own,
            grad_output_own,
            grad_keyval_own,
            vectors,
            mine,
            grad_up_own,
            prompt_grad,
            answer_grad,
        ) = backward_reduce(
            owning,
            share,
            weights,
            queries,
            mixture,
            grad_hidden,
            normed_one,
            grad_branch_one,
            log_total,
            prompt_kv,
            answer_kv,
            states,
            gain_row,
            keyval_full,
            grad_up_place.reshape(-1, model_width),
            second_sums,
            grad_down_offset,
            own_squares,
            groups,
            prompt_count,
            answer_count,
            prompt_rows,
            6,
        )
        (
            prompt_grad,
            answer_grad,
            grad_query_own,
            grad_output_own,
            grad_keyval_own,
            grad_up_weight,
            grad_down_weight,
            *own_vectors,
            grad_up_own,
            value_total,
            loss_value,
        ) = finish(
            share_size,
            vectors,
            mine,
            grad_up_own,
            valid_count,
            prompt_grad,
            answer_grad,
            grad_query_own,
            grad_output_own,
            grad_keyval_own,
            grad_up_weight,
            grad_down_weight,
        )
        own_vectors = [each.reshape(-1) for each in own_vectors]
        grad_up_own, value_total = grad_up_own.reshape(-1), value_total.reshape(-1)
        loss_value = loss_value.reshape(())
    else:
        grad_rows = keyval_start + keyval_pack
        grad_weights, grad_normed_one, grad_prompt_kv, grad_answer_kv, grad_query_offset = (
            attention_backward(
                place,
                owning,
                share,
                normed_one,
                weights,
                groups,
                grad_rows,
                prompt_kv,
                answer_kv,
                grad_branch_one,
                queries,
                mixture,
                log_total,
                prompt_count,
                answer_count,
            )
        )
        grad_prompt_kv = lax.psum_scatter(
            grad_prompt_kv, "tok", scatter_dimension=1, tiled=True
        ).astype(jnp.float32)
        grad_keyvals = jnp.concatenate(
            [grad_prompt_kv.reshape(own_prompt, -1), grad_answer_kv], axis=0
        ).astype(jnp.bfloat16)
        grad_keyval_full = weight_product(normed_one, grad_keyvals)
        grad_value_offset = column_sums(grad_keyvals[:, HEAD_WIDTH:])
        grad_normed_one = grad_normed_one + transposed_product(grad_keyvals, keyval_full)
        grad_norm_one, grad_gain_one, grad_shift_one = norm_backward(
            grad_normed_one, gain_one, scaled_one, inverse_one
        )
        grad_inputs = grad_hidden + grad_norm_one

        grad_keyval_blocks = jnp.swapaxes(
            grad_keyval_full.astype(jnp.bfloat16).reshape(groups, token_devices, -1, block), 0, 1
        )
        grad_weights = lax.dynamic_update_slice(
            grad_weights, grad_keyval_blocks, (0, 0, keyval_start, 0)
        )
        vectors = (
            grad_gain_one,
            grad_shift_one,
            grad_query_offset.reshape(-1),
            grad_output_offset,
            grad_gain_two,
            grad_shift_two,
            grad_down_offset,
            grad_up_place,
        )
        totals = jnp.concatenate([grad_value_offset, own_squares.reshape(1)])
        blocks = jnp.concatenate(
            [each.reshape(groups, token_devices, -1) for each in vectors]
            + [jnp.broadcast_to(totals, (groups, token_devices, totals.shape[0]))],
            axis=2,
        )
        blocks = jnp.pad(blocks, ((0, 0), (0, 0), (0, SMALL_SUMS - blocks.shape[2])))
        blocks = jnp.swapaxes(blocks, 0, 1).reshape(token_devices, -1, HEAD_WIDTH)
        grad_weights = lax.psum_scatter(
            grad_weights.reshape(token_devices, -1, block), "tok", scatter_dimension=0, tiled=False
        )
        grad_weights = lax.psum_scatter(grad_weights, "grp", scatter_dimension=0, tiled=True)
        grad_weights = grad_weights.astype(jnp.float32)
        small_sums = lax.psum_scatter(blocks, "tok", scatter_dimension=0, tiled=False)
        small_sums = lax.psum_scatter(small_sums, "grp", scatter_dimension=0, tiled=True)
        small_sums = small_sums.reshape(-1)
        up_share = up_bias.shape[0]
        totals_at = 7 * share_size + up_share
        value_total = small_sums[totals_at : totals_at + HEAD_WIDTH]
        squared_sum = small_sums[totals_at + HEAD_WIDTH]
        own_vectors = [
            small_sums[index * share_size : (index + 1) * share_size] for index in range(7)
        ]
        grad_up_own = small_sums[7 * share_size : totals_at]
        grad_query_own = grad_weights[:weight_rows]
        grad_output_own = grad_weights[weight_rows:keyval_start]
        grad_keyval_own = grad_weights[keyval_start:].reshape(keyval_rows, keyval_width)
        prompt_grad, answer_grad = grad_inputs[:own_prompt], grad_inputs[own_prompt:]
        loss_value = squared_sum / (valid_count * model_width)

    def row_outputs(prompt_part, answer_part):
        return (
            prompt_part.astype(jnp.bfloat16).reshape(prompt_states.shape),
            answer_part.astype(jnp.bfloat16).reshape(answer_states.shape),
        )

    prompt_out, answer_out = row_outputs(prompt_out, answer_out)
    prompt_grad, answer_grad = row_outputs(prompt_grad, answer_grad)
    pieces = own_vectors
    return (
        prompt_out,
        answer_out,
        prompt_grad,
        answer_grad,
        pieces[0],
        pieces[1],
        grad_query_own,
        pieces[2],
        grad_keyval_own,
        value_total,
        grad_output_own,
        pieces[3],
        pieces[4],
        pieces[5],
        grad_up_weight.astype(jnp.float32),
        grad_up_own,
        grad_down_weight.astype(jnp.float32),
        pieces[6],
        loss_value,
    )


def solution(mesh):
    rows = P(("grp", "tok"))
    table = P(("grp", "tok"), None)
    matrix = P("grp", "tok")
    prompt_part = P("grp", "tok", None)
    answer_part = P(("grp", "tok"), None, None)
    in_specs = (
        prompt_part,
        answer_part,
        P("grp"),
        prompt_part,
        answer_part,
        P("grp", "tok"),
        table,
        rows,
        rows,
        matrix,
        rows,
        table,
        P(),
        matrix,
        rows,
        rows,
        rows,
        matrix,
        rows,
        matrix,
        rows,
    )
    out_specs = (
        prompt_part,
        answer_part,
        prompt_part,
        answer_part,
        rows,
        rows,
        matrix,
        rows,
        table,
        P(),
        matrix,
        rows,
        rows,
        rows,
        matrix,
        rows,
        matrix,
        rows,
        P(),
    )
    kernels = mesh.shape["tok"] == 8 and mesh.shape["grp"] == 4
    return jax.shard_map(
        functools.partial(body, kernels),
        mesh=mesh,
        in_specs=in_specs,
        out_specs=out_specs,
        check_vma=False,
    )
```
